32 devices in a mesh: ctx: 8 (over y, x, core), fsdp: 4 (over z).
Axes of the slice: x: 2, y: 2, z: 4, core: 2. Of those that a mesh axis runs over, the one named last changes fastest.
Arguments:
- tokens: bfloat16 [4, 2048, 768], P('fsdp', 'ctx'), may hold values from -6 to 6
- prev_logits: float32 [4, 2048, 12], P('fsdp', 'ctx'), may hold values from -6 to 6
- routes: int32 [4, 2048, 2], P('fsdp', 'ctx'), may hold values from 0 to 11, all different within a row; in each aligned block of 256 rows (0 to 255, 256 to 511, ..., all dimensions but the last counted through in order) at most 64 rows name the same one
- lengths: int32 [4], P('fsdp'), may hold values from 512 to 2048, as said below
- cotangent: bfloat16 [4, 2048, 768], P('fsdp', 'ctx'), may hold values from -6 to 6
- w_qkv: bfloat16 [768, 2304], P('fsdp'), may hold values from -0.21875 to 0.21875
- w_out: bfloat16 [768, 768], P('fsdp'), may hold values from -4 to 4
- gain_attn: bfloat16 [768], replicated, may hold values from 0.25 to 1.75
- gain_moe: bfloat16 [768], replicated, may hold values from 0.25 to 1.75
- w_router: float32 [768, 12], replicated, may hold values from -0.15625 to 0.15625
- w_residual: float32 [12, 12], replicated, may hold values from -0.875 to 0.875
- const_vec: bfloat16 [2, 768], replicated, may hold values from -6 to 6
- w_expert: bfloat16 [8, 2048, 3, 768], P(None, 'fsdp'), may hold values from -0.21875 to 0.21875
Outputs:
- output: bfloat16 [4, 2048, 768], P('fsdp', 'ctx')
- grad_tokens: float32 [4, 2048, 768], P('fsdp', 'ctx')
- grad_prev_logits: float32 [4, 2048, 12], P('fsdp', 'ctx')
- grad_w_qkv: float32 [768, 2304], P('fsdp')
- grad_w_out: float32 [768, 768], P('fsdp')
- grad_gain_attn: float32 [768], replicated
- grad_gain_moe: float32 [768], replicated
- grad_w_router: float32 [768, 12], replicated
- grad_w_residual: float32 [12, 12], replicated
- grad_const_vec: float32 [2, 768], replicated
- grad_w_expert: float32 [8, 2048, 3, 768], P(None, 'fsdp')
The draws below stay inside these ranges and needn't reach their ends.
Inputs may be any that keep to these rules, and one draw needn't show every extreme that they name: `routes`: each row names two different ids. Ids 0 to 7 are feed-forward experts, 8 the zero expert, 9 the copy expert, 10 and 11 the constant experts. In the 256 positions of one slot on one device no id is named by more than 64 rows. `lengths`: one slot drawn from the seed has length 2048.
All inputs are finite; a program needn't handle non-finite values.
Results may differ from the reference program's by a relative error of at most 0.02.
Values may be sent and summed in bfloat16 or wider, within the bound.
A program may use at most 256 MiB of HBM per device.

```python
import math
import jax
import jax.numpy as jnp
import numpy as np
from jax import lax

HEAD_DIM = 64
D = 768
FF = 2048
FFN_EXPERTS = 8
EXPERT_IDS = 12
PIECE = 256
SLOT = 2048
SLOTS = 4
CAP = 64


def draw_lengths(key, part):
    key = jax.random.fold_in(key, 7)
    full_key, rest_key = jax.random.split(key)
    full_pick = jax.random.randint(full_key, (), 0, SLOTS)
    drawn = jax.random.randint(rest_key, (SLOTS,), SLOT // 4, SLOT + 1)
    which = jnp.arange(SLOTS, dtype=jnp.int32) == full_pick
    return jnp.where(which, SLOT, drawn).astype(jnp.int32)


def block_levels(key, shape, pieces, least, top_value):
    def one(dim, shards_of):
        heights = jax.random.uniform(jax.random.fold_in(jax.random.fold_in(key, 6), dim), (shards_of,), jnp.float32, least / len(pieces), top_value / len(pieces))
        return jnp.repeat(jnp.exp(heights), shape[dim] // shards_of).reshape((-1,) + (1,) * (len(shape) - dim - 1))

    level = one(*pieces[0])
    for cut in pieces[1:]:
        level = level * one(*cut)
    return level


def deal_out(own_key, own, number, rows, count, top, limit, slope):
    order = jax.random.permutation(own_key, count)
    packed, ordinary = shares(count, rows * top, limit, slope, True), shares(count, rows * top, limit, slope, False)
    places = jnp.arange(count)

    def named(sizes, turn):
        used = int((sizes > 0).sum())
        fixed = max(1, used // 4)
        shifted = fixed + (places - fixed + turn * (used - fixed)) % max(1, count - fixed)
        return jnp.zeros((count,), jnp.int32).at[order[jnp.where(places < fixed, places, shifted)]].set(jnp.asarray(sizes, jnp.int32))

    sizes = jnp.where(number % 4 == 0, named(packed, number // 4), named(ordinary, number - number // 4 - 1))
    mixed = jax.random.permutation(jax.random.fold_in(own, 3), count)
    giver, receiver = mixed[0:count // 2 * 2:2], mixed[1:count // 2 * 2:2]
    margin = jnp.minimum(sizes[giver] - 1, limit - sizes[receiver]) // 2
    margin = jnp.where((giver == order[0]) | (receiver == order[0]) | (sizes[receiver] == 0), 0, jnp.maximum(margin, 0))
    shifted = jax.random.randint(jax.random.fold_in(own, 4), (count // 2,), 0, 1 << 20) % (margin + 1)
    sizes = sizes.at[giver].add(-shifted).at[receiver].add(shifted)
    members = jnp.searchsorted(jnp.cumsum(sizes), jnp.arange(rows * top), side="right").astype(jnp.int32)
    table = members.reshape(top, rows).T
    table = table[jax.random.permutation(jax.random.fold_in(own, 1), rows)]
    turn = jax.random.randint(jax.random.fold_in(own, 2), (rows, 1), 0, top)
    return jnp.take_along_axis(table, (jnp.arange(top)[None, :] + turn) % top, axis=1)


def shares(amount, total, bound, skew, full):
    weights = [(1 << 20) // math.isqrt(rank ** skew) + 1 for rank in range(1, amount + 1)]
    largest = bound if full else min(bound, max(-(-total // amount), total * weights[0] // sum(weights)))
    least = 1 if total - largest >= amount - 1 else 0
    given, rest = [largest] + [least] * (amount - 1), total - largest - least * (amount - 1)
    while rest > 0:
        free = [i for i in range(1, amount) if given[i] < largest] or [i for i in range(1, amount) if given[i] < bound]
        mass, left = sum([weights[i] for i in free]), rest
        for i in free:
            extra = min(bound - given[i], max(1, left * weights[i] // mass), rest)
            given[i] = given[i] + extra
            rest = rest - extra
    return np.array(given)


def gaussian(stream_key, extent, scale, most, pieces=(), kind=jnp.bfloat16):
    values = scale * jax.random.normal(stream_key, extent, jnp.float32)
    if pieces:
        values = values * block_levels(stream_key, extent, pieces, -0.22, 0.18)
    return jnp.clip(values, -most, most).astype(kind)


def setup_inputs(seed: int = 0) -> dict:
    keys = jax.random.split(jax.random.key(seed), 14)
    tokens = gaussian(keys[0], (SLOTS, SLOT, D), 1.0, 6.0, ((0, 4), (1, 8)))
    prev_logits = gaussian(keys[1], (SLOTS, SLOT, EXPERT_IDS), 1.0, 6.0, ((0, 4), (1, 8)), jnp.float32)
    routes_keys = jax.random.split(jax.random.fold_in(keys[2], 1), SLOTS * SLOT // PIECE)
    routes_turns = jax.random.permutation(jax.random.fold_in(keys[2], 3), SLOTS * SLOT // PIECE)
    routes = jax.vmap(lambda own, number: deal_out(jax.random.fold_in(keys[2], 2), own, number, PIECE, EXPERT_IDS, 2, CAP, 1))(routes_keys, routes_turns).reshape((SLOTS, SLOT, 2))
    lengths = draw_lengths(jax.random.fold_in(keys[13], 71), 0)
    cotangent = gaussian(keys[4], (SLOTS, SLOT, D), 1.0, 6.0, ((0, 4), (1, 8)))
    w_qkv = gaussian(keys[5], (D, 3 * D), D ** -0.5, 0.21875, ((0, 4),))
    w_out = gaussian(keys[6], (D, D), 2 ** -0.5, 4.0, ((0, 4),))
    gain_attn = jnp.clip(1.0 + 0.15 * jax.random.normal(keys[7], (D,), jnp.float32), 0.25, 1.75).astype(jnp.bfloat16)
    gain_moe = jnp.clip(1.0 + 0.15 * jax.random.normal(keys[8], (D,), jnp.float32), 0.25, 1.75).astype(jnp.bfloat16)
    w_router = gaussian(keys[9], (D, EXPERT_IDS), (2 * D) ** -0.5, 0.15625, (), jnp.float32)
    w_residual = gaussian(keys[10], (EXPERT_IDS, EXPERT_IDS), 48 ** -0.5, 0.875, (), jnp.float32)
    const_vec = gaussian(keys[11], (2, D), 1.0, 6.0)
    w_expert = gaussian(keys[12], (FFN_EXPERTS, FF, 3, D), D ** -0.5, 0.21875, ((1, 4),))
    return dict(tokens=tokens, prev_logits=prev_logits, routes=routes, lengths=lengths, cotangent=cotangent, w_qkv=w_qkv, w_out=w_out, gain_attn=gain_attn, gain_moe=gain_moe, w_router=w_router, w_residual=w_residual, const_vec=const_vec, w_expert=w_expert)


EPSILON = 1e-05
MASKED = -1e+30
HIGHEST = lax.Precision.HIGHEST

@jax.custom_vjp
def low(v):
    return lax.optimization_barrier(v.astype(jnp.bfloat16)).astype(jnp.float32)

@jax.custom_vjp
def low_back(v):
    return v

def low_keep(v):
    return (low(v), None)

def low_pass(kept, grad):
    return (grad,)

def back_keep(v):
    return (v, None)

def back_low(kept, grad):
    return (low(grad),)
low.defvjp(low_keep, low_pass)
low_back.defvjp(back_keep, back_low)

def normalize(values, gain_row):
    return values * lax.rsqrt(lax.optimization_barrier(jnp.mean(values * values, axis=-1, keepdims=True)) + EPSILON) * gain_row

def rope_tables(positions, head_size):
    half_dim = head_size // 2
    frequency = jnp.exp(jnp.arange(half_dim, dtype=jnp.float32) * (-2.0 * math.log(10000.0) / head_size))
    angles = positions.astype(jnp.float32)[:, None] * frequency[None, :]
    return (jnp.cos(angles)[:, None, :], jnp.sin(angles)[:, None, :])

def rotate(values, cosine_table, sine_table):
    half_dim = values.shape[-1] // 2
    first_half = values[..., :half_dim]
    second_half = values[..., half_dim:]
    return jnp.concatenate([first_half * cosine_table - second_half * sine_table, second_half * cosine_table + first_half * sine_table], axis=-1)

def slot_attention(queries, key_rows, values, length):
    slot_len = queries.shape[0]
    block_len = min(512, slot_len)
    key_positions = jnp.arange(slot_len, dtype=jnp.int32)
    scaling = queries.shape[-1] ** (-0.5)

    def one_block(start_row):
        query_block = lax.dynamic_slice_in_dim(queries, start_row, block_len, 0)
        query_positions = start_row + jnp.arange(block_len, dtype=jnp.int32)
        allowed = (key_positions[None, :] <= query_positions[:, None]) & (key_positions[None, :] < length)
        scores = jnp.einsum('qhd,khd->hqk', query_block, key_rows, precision=HIGHEST) * scaling
        scores = jnp.where(allowed[None], low_back(scores), MASKED)
        row_max = lax.optimization_barrier(jnp.max(scores, axis=-1, keepdims=True))
        weights = jnp.exp(scores - row_max)
        probabilities = low(weights / lax.optimization_barrier(jnp.sum(weights, axis=-1, keepdims=True)))
        return jnp.einsum('hqk,khd->qhd', probabilities, values, precision=HIGHEST)
    starts = jnp.arange(slot_len // block_len, dtype=jnp.int32) * block_len
    blocks = lax.map(jax.checkpoint(one_block), starts)
    return blocks.reshape(queries.shape)

@jax.checkpoint
def expert_ffn(row_block, weights):
    gate_proj = low_back(jnp.dot(row_block, weights[:, 0].T, precision=HIGHEST, preferred_element_type=jnp.float32))
    up_proj = low_back(jnp.dot(row_block, weights[:, 1].T, precision=HIGHEST, preferred_element_type=jnp.float32))
    hidden = low(jax.nn.silu(gate_proj) * up_proj)
    return low_back(jnp.dot(hidden, weights[:, 2], precision=HIGHEST, preferred_element_type=jnp.float32))

def forward(inputs, prev_logits, routes, lengths, w_qkv, w_out, gain_attn, gain_moe, w_router, w_residual, const_vec, w_expert):
    slot_total, slot_len, model_width = inputs.shape
    head_count = model_width // HEAD_DIM
    experts = w_expert.shape[0]
    positions = jnp.arange(slot_len, dtype=jnp.int32)
    live_rows = (positions[None, :] < lengths[:, None]).astype(jnp.float32)[..., None]
    normed_one = low(normalize(inputs, gain_attn))
    projected = low_back(jnp.einsum('spd,de->spe', normed_one, w_qkv, precision=HIGHEST))
    cosine_table, sine_table = rope_tables(positions, HEAD_DIM)
    split_shape = (slot_total, slot_len, head_count, HEAD_DIM)
    queries = low(rotate(projected[..., :model_width].reshape(split_shape), cosine_table, sine_table))
    key_rows = low(rotate(projected[..., model_width:2 * model_width].reshape(split_shape), cosine_table, sine_table))
    values = low(projected[..., 2 * model_width:].reshape(split_shape))
    attended = lax.map(lambda items: slot_attention(*items), (queries, key_rows, values, lengths))
    mixed = low(low_back(attended.reshape(slot_total, slot_len, model_width)))
    attention = low_back(jnp.einsum('spd,de->spe', mixed, w_out, precision=HIGHEST))
    residual_sum = inputs + attention
    routed = low(normalize(residual_sum, gain_moe))
    logits = jnp.einsum('spd,de->spe', routed, w_router, precision=HIGHEST) + jnp.einsum('spi,ie->spe', prev_logits, w_residual, precision=HIGHEST)
    chosen = jnp.take_along_axis(logits, routes, axis=-1)
    chosen_exp = jnp.exp(chosen - lax.optimization_barrier(jnp.max(chosen, axis=-1, keepdims=True)))
    gate_weights = chosen_exp / lax.optimization_barrier(jnp.sum(chosen_exp, axis=-1, keepdims=True))
    id_range = jnp.arange(experts + 4, dtype=jnp.int32)
    route_hot = (routes[..., None] == id_range).astype(jnp.float32)
    per_id = lax.optimization_barrier(jnp.sum(gate_weights[..., None] * route_hot, axis=2))
    special = per_id[..., experts + 1:experts + 2] * routed + jnp.einsum('spj,jd->spd', per_id[..., experts + 2:], const_vec, precision=HIGHEST)
    flat_routed = routed.reshape(-1, model_width)
    flat_routes = routes.reshape(-1)
    flat_gates = gate_weights.reshape(-1)
    capacity = flat_routed.shape[0] // 4
    slots_used = jnp.arange(capacity, dtype=jnp.int32)
    ffn_sum = jnp.zeros_like(flat_routed)
    for expert in range(experts):
        matches = flat_routes == expert
        picked = jnp.nonzero(matches, size=capacity, fill_value=0)[0].astype(jnp.int32)
        counts = jnp.sum(matches.astype(jnp.int32))
        weight = jnp.where(slots_used < counts, flat_gates[picked], 0.0)
        token_index = picked // 2
        result = expert_ffn(flat_routed[token_index], w_expert[expert])
        ffn_sum = ffn_sum.at[token_index].add(weight[:, None] * result)
    moe_sum = special + ffn_sum.reshape(slot_total, slot_len, model_width)
    return live_rows * (residual_sum + moe_sum)

def reference(tokens, prev_logits, routes, lengths, cotangent, w_qkv, w_out, gain_attn, gain_moe, w_router, w_residual, const_vec, w_expert):
    floats = (tokens.astype(jnp.float32), prev_logits.astype(jnp.float32), w_qkv.astype(jnp.float32), w_out.astype(jnp.float32), gain_attn.astype(jnp.float32), gain_moe.astype(jnp.float32), w_router.astype(jnp.float32), w_residual.astype(jnp.float32), const_vec.astype(jnp.float32), w_expert.astype(jnp.float32))

    def forward_fn(inputs, previous, qkv_weight, out_weight, gain_one, gain_two, router, residual_map, constants, expert_weights):
        return forward(inputs, previous, routes, lengths, qkv_weight, out_weight, gain_one, gain_two, router, residual_map, constants, expert_weights)
    result, pullback = jax.vjp(forward_fn, *floats)
    gradients = pullback(cotangent.astype(jnp.float32))
    return (result.astype(jnp.bfloat16), gradients[0], gradients[1], gradients[2], gradients[3], gradients[4], gradients[5], gradients[6], gradients[7], gradients[8], gradients[9])
```

```python
import math

import jax
import jax.numpy as jnp
from jax import lax
from jax.sharding import PartitionSpec as P

HEAD_DIM = 64


EPSILON = 1e-05
MASKED = -1e30
HIGHEST = lax.Precision.HIGHEST


def normalize_rows(values, gain_row):
    scaling = lax.rsqrt(jnp.mean(values * values, axis=-1, keepdims=True) + EPSILON)
    return (values * scaling * gain_row, scaling)


def normalize_back(values, scaling, gain_row, grad_out):
    grad_hat = grad_out * gain_row
    grad_gain = jnp.sum(grad_out * values * scaling, axis=(0, 1))
    grad_values = scaling * grad_hat - values * scaling**3 * jnp.mean(
        grad_hat * values, axis=-1, keepdims=True
    )
    return (grad_values, grad_gain)


def rope_tables(positions, head_size):
    half_dim = head_size // 2
    frequency = jnp.exp(
        jnp.arange(half_dim, dtype=jnp.float32) * (-2.0 * math.log(10000.0) / head_size)
    )
    angles = positions.astype(jnp.float32)[:, None] * frequency[None, :]
    return (jnp.cos(angles)[:, None, :], jnp.sin(angles)[:, None, :])


def rotate(values, cosine_table, sine_table):
    half_dim = values.shape[-1] // 2
    first_half = values[..., :half_dim]
    second_half = values[..., half_dim:]
    return jnp.concatenate(
        [
            first_half * cosine_table - second_half * sine_table,
            second_half * cosine_table + first_half * sine_table,
        ],
        axis=-1,
    )


def masked_scores(queries, key_rows, allowed):
    scaling = queries.shape[-1] ** (-0.5)
    scores = (
        jnp.einsum("qhd,khd->hqk", queries, key_rows, preferred_element_type=jnp.float32) * scaling
    )
    return jnp.where(allowed[None], scores, MASKED)


def attend_forward(queries, key_rows, values, allowed):
    scores = masked_scores(queries, key_rows, allowed)
    row_max = jnp.max(scores, axis=-1, keepdims=True)
    weights = jnp.exp(scores - row_max)
    row_total = jnp.sum(weights, axis=-1, keepdims=True)
    probabilities = (weights / row_total).astype(jnp.bfloat16)
    attended = jnp.einsum("hqk,khd->qhd", probabilities, values, preferred_element_type=jnp.float32)
    return (attended, row_max, row_total)


def attend_backward(queries, key_rows, values, allowed, row_max, row_total, grad_out):
    scaling = queries.shape[-1] ** (-0.5)
    scores = masked_scores(queries, key_rows, allowed)
    probabilities = jnp.exp(scores - row_max) / row_total
    probs_low = probabilities.astype(jnp.bfloat16)
    grad_probs = jnp.einsum("qhd,khd->hqk", grad_out, values, preferred_element_type=jnp.float32)
    inner_sum = jnp.sum(probabilities * grad_probs, axis=-1, keepdims=True)
    grad_scores = (probabilities * (grad_probs - inner_sum)).astype(jnp.bfloat16)
    grad_queries = (
        jnp.einsum("hqk,khd->qhd", grad_scores, key_rows, preferred_element_type=jnp.float32)
        * scaling
    )
    grad_keys = (
        jnp.einsum("hqk,qhd->khd", grad_scores, queries, preferred_element_type=jnp.float32)
        * scaling
    )
    grad_values = jnp.einsum(
        "hqk,qhd->khd", probs_low, grad_out, preferred_element_type=jnp.float32
    )
    return (grad_queries, grad_keys, grad_values)


def per_device(
    tokens,
    prev_logits,
    routes,
    lengths,
    cotangent,
    w_qkv,
    w_out,
    gain_attn,
    gain_moe,
    w_router,
    w_residual,
    const_vec,
    w_expert,
):
    groups, piece_len, model_width = tokens.shape
    head_count = model_width // HEAD_DIM
    part_heads = 2
    part_count = head_count // part_heads
    slot_len = piece_len * lax.axis_size("ctx")
    positions = lax.axis_index("ctx") * piece_len + jnp.arange(piece_len, dtype=jnp.int32)
    key_positions = jnp.arange(slot_len, dtype=jnp.int32)
    live_rows = (positions[None, :] < lengths[:, None]).astype(jnp.float32)[..., None]
    experts = w_expert.shape[0]
    capacity = piece_len // 4
    slot_count = experts * capacity
    split_shape = (groups, piece_len, head_count, HEAD_DIM)
    full_qkv, full_out = (
        lax.all_gather(w_qkv, "fsdp", axis=0, tiled=True),
        lax.all_gather(w_out, "fsdp", axis=0, tiled=True),
    )
    inputs = tokens.astype(jnp.float32)
    gain_one = gain_attn.astype(jnp.float32)
    gain_two = gain_moe.astype(jnp.float32)
    normed_one, scale_one = normalize_rows(inputs, gain_one)
    normed_one_low = normed_one.astype(jnp.bfloat16)
    projected = jnp.einsum(
        "gpd,de->gpe", normed_one_low, full_qkv, preferred_element_type=jnp.float32
    )
    cosine_table, sine_table = rope_tables(positions, HEAD_DIM)
    queries = rotate(
        projected[..., :model_width].reshape(split_shape), cosine_table, sine_table
    ).astype(jnp.bfloat16)
    key_local = (
        rotate(
            projected[..., model_width : 2 * model_width].reshape(split_shape),
            cosine_table,
            sine_table,
        )
        .astype(jnp.bfloat16)
        .reshape(groups, piece_len, model_width)
    )
    value_local = projected[..., 2 * model_width :].astype(jnp.bfloat16)
    key_all, value_all = (
        lax.all_gather(key_local, "ctx", axis=1, tiled=True),
        lax.all_gather(value_local, "ctx", axis=1, tiled=True),
    )
    key_all = key_all.reshape(groups, slot_len, head_count, HEAD_DIM)
    value_all = value_all.reshape(groups, slot_len, head_count, HEAD_DIM)
    maxima_list = []
    totals_list = []
    group_index = 0
    allowed = (key_positions[None, :] <= positions[:, None]) & (
        key_positions[None, :] < lengths[group_index]
    )
    mask_list = [allowed]
    head_parts = []
    for part_index in range(part_count):
        first_head = part_index * part_heads
        last_head = first_head + part_heads
        attended, row_max, row_total = attend_forward(
            queries[group_index, :, first_head:last_head],
            key_all[group_index, :, first_head:last_head],
            value_all[group_index, :, first_head:last_head],
            allowed,
        )
        head_parts.append(attended)
        maxima_list.append(row_max)
        totals_list.append(row_total)
    attended_list = [jnp.concatenate(head_parts, axis=1)]
    mixed_low = (
        jnp.stack(attended_list).reshape(groups, piece_len, model_width).astype(jnp.bfloat16)
    )
    attention = jnp.einsum("gpd,de->gpe", mixed_low, full_out, preferred_element_type=jnp.float32)
    residual_sum = inputs + attention
    normed_two, scale_two = normalize_rows(residual_sum, gain_two)
    routed_low = normed_two.astype(jnp.bfloat16)
    routed = routed_low.astype(jnp.float32)
    logits = jnp.einsum("gpd,de->gpe", routed, w_router, precision=HIGHEST) + jnp.einsum(
        "gpi,ie->gpe", prev_logits, w_residual, precision=HIGHEST
    )
    id_range = jnp.arange(experts + 4, dtype=jnp.int32)
    route_hot = (routes[..., None] == id_range).astype(jnp.float32)
    chosen = jnp.sum(route_hot * logits[:, :, None, :], axis=-1)
    chosen_exp = jnp.exp(chosen - jnp.max(chosen, axis=-1, keepdims=True))
    gate_weights = chosen_exp / jnp.sum(chosen_exp, axis=-1, keepdims=True)
    assign_hot = route_hot[..., :experts].reshape(groups, 2 * piece_len, experts)
    earlier = jnp.cumsum(assign_hot, axis=1) - assign_hot
    order_in = jnp.sum(earlier * assign_hot, axis=-1)
    expert_of = jnp.sum(assign_hot * jnp.arange(experts, dtype=jnp.float32), axis=-1)
    is_ffn = jnp.sum(assign_hot, axis=-1)
    slot_of = jnp.where(is_ffn > 0.5, expert_of * capacity + order_in, -1.0).reshape(
        groups, piece_len, 2
    )
    slot_hot = slot_of[..., None] == jnp.arange(slot_count, dtype=jnp.float32)
    slot_gate = jnp.sum(jnp.where(slot_hot, gate_weights[..., None], 0.0), axis=(1, 2))
    cotangent_low = live_rows.astype(jnp.bfloat16) * cotangent
    row_pairs = lax.all_gather(
        jnp.concatenate([routed_low, cotangent_low], axis=-1), "fsdp", axis=0, tiled=True
    )
    all_slot_of = lax.all_gather(slot_of, "fsdp", axis=0, tiled=True)
    all_gate = lax.all_gather(slot_gate, "fsdp", axis=0, tiled=True)
    peers = row_pairs.shape[0]
    all_hot = (
        jnp.sum(
            (all_slot_of[..., None] == jnp.arange(slot_count, dtype=jnp.float32)).astype(
                jnp.float32
            ),
            axis=2,
        )
        .astype(jnp.bfloat16)
        .reshape(peers, piece_len, experts, capacity)
    )
    gate_rows = all_gate.reshape(peers, experts, capacity).swapaxes(0, 1)[..., None]
    buffers = jnp.einsum(
        "gpec,gpd->egcd", all_hot, row_pairs, preferred_element_type=jnp.float32
    ).astype(jnp.bfloat16)
    expert_in = buffers[..., :model_width].reshape(experts, peers * capacity, model_width)
    block_rows = buffers[..., model_width:].astype(jnp.float32)
    grad_out = (
        (gate_rows * block_rows)
        .astype(jnp.bfloat16)
        .reshape(experts, peers * capacity, model_width)
    )
    w_gate, w_up, w_down = w_expert[:, :, 0], w_expert[:, :, 1], w_expert[:, :, 2]

    def apply(spec, left, right):
        return jnp.einsum(spec, left, right, preferred_element_type=jnp.float32)

    gate_proj = apply("ecd,efd->ecf", expert_in, w_gate)
    up_proj = apply("ecd,efd->ecf", expert_in, w_up)
    sigmoid_gate = jax.nn.sigmoid(gate_proj)
    silu_gate = gate_proj * sigmoid_gate
    hidden = (silu_gate * up_proj).astype(jnp.bfloat16)
    expert_out = apply("ecf,efd->ecd", hidden, w_down).reshape(buffers.shape[:3] + (model_width,))
    grad_hidden = apply("ecd,efd->ecf", grad_out, w_down)
    grad_gate_proj = (
        grad_hidden * up_proj * sigmoid_gate * (1.0 + gate_proj * (1.0 - sigmoid_gate))
    ).astype(jnp.bfloat16)
    grad_up_proj = (grad_hidden * silu_gate).astype(jnp.bfloat16)
    grad_in = (
        apply("ecf,efd->ecd", grad_gate_proj, w_gate) + apply("ecf,efd->ecd", grad_up_proj, w_up)
    ).reshape(expert_out.shape)
    grad_weights = jnp.stack(
        [
            apply("ecf,ecd->efd", grad_gate_proj, expert_in).astype(jnp.bfloat16),
            apply("ecf,ecd->efd", grad_up_proj, expert_in).astype(jnp.bfloat16),
            apply("ecf,ecd->efd", hidden, grad_out).astype(jnp.bfloat16),
        ],
        axis=2,
    )
    returned = jnp.concatenate([gate_rows * expert_out, grad_in], axis=-1).astype(jnp.bfloat16)
    token_parts = apply("gpec,egcd->gpd", all_hot, returned).astype(jnp.bfloat16)
    token_sums = lax.psum_scatter(token_parts, "fsdp", scatter_dimension=0, tiled=True).astype(
        jnp.float32
    )
    ffn_sum, ffn_grad = token_sums[..., :model_width], token_sums[..., model_width:]
    slot_dot = lax.psum_scatter(
        jnp.sum(block_rows * expert_out, axis=-1).swapaxes(0, 1).reshape(peers, slot_count),
        "fsdp",
        scatter_dimension=0,
        tiled=True,
    )
    copy_hot = route_hot[..., experts + 1]
    const_hot = route_hot[..., experts + 2 :]
    constants = const_vec.astype(jnp.float32)
    gate_const = jnp.sum(gate_weights[..., None] * const_hot, axis=2)
    copy_gate = jnp.sum(gate_weights * copy_hot, axis=2, keepdims=True)
    moe_sum = (
        ffn_sum
        + copy_gate * routed
        + jnp.einsum("gpj,jd->gpd", gate_const, constants, precision=HIGHEST)
    )
    output = (live_rows * (residual_sum + moe_sum)).astype(jnp.bfloat16)
    grad_block = live_rows * cotangent.astype(jnp.float32)
    copy_dot = jnp.sum(grad_block * routed, axis=-1)[..., None]
    const_dot = jnp.einsum("gpd,jd->gpj", grad_block, constants, precision=HIGHEST)
    grad_gate = (
        jnp.sum(jnp.where(slot_hot, slot_dot[:, None, None, :], 0.0), axis=-1)
        + copy_hot * copy_dot
        + jnp.sum(const_hot * const_dot[:, :, None, :], axis=-1)
    )
    grad_chosen = gate_weights * (
        grad_gate - jnp.sum(gate_weights * grad_gate, axis=-1, keepdims=True)
    )
    grad_logits = jnp.sum(grad_chosen[..., None] * route_hot, axis=2)
    grad_router = jnp.einsum("gpd,gpe->de", routed, grad_logits, precision=HIGHEST)
    grad_mixing = jnp.einsum("gpi,gpe->ie", prev_logits, grad_logits, precision=HIGHEST)
    grad_previous = jnp.einsum("gpe,ie->gpi", grad_logits, w_residual, precision=HIGHEST)
    grad_const = jnp.einsum("gpd,gpj->jd", grad_block, gate_const, precision=HIGHEST)
    grad_routed = (
        jnp.einsum("gpe,de->gpd", grad_logits, w_router, precision=HIGHEST)
        + copy_gate * grad_block
        + ffn_grad
    )
    grad_norm_two, grad_gain_two = normalize_back(residual_sum, scale_two, gain_two, grad_routed)
    grad_residual = grad_block + grad_norm_two
    grad_attention = grad_residual.astype(jnp.bfloat16)
    grad_wout = jnp.einsum(
        "gpd,gpe->de", mixed_low, grad_attention, preferred_element_type=jnp.float32
    )
    grad_mixed = (
        jnp.einsum("gpe,de->gpd", grad_attention, full_out, preferred_element_type=jnp.float32)
        .astype(jnp.bfloat16)
        .reshape(split_shape)
    )
    group_index = 0
    query_parts = []
    key_parts = []
    value_parts = []
    for part_index in range(part_count):
        first_head = part_index * part_heads
        last_head = first_head + part_heads
        grad_query, grad_key, grad_value = attend_backward(
            queries[group_index, :, first_head:last_head],
            key_all[group_index, :, first_head:last_head],
            value_all[group_index, :, first_head:last_head],
            mask_list[group_index],
            maxima_list[part_count * group_index + part_index],
            totals_list[part_count * group_index + part_index],
            grad_mixed[group_index, :, first_head:last_head],
        )
        query_parts.append(grad_query)
        key_parts.append(grad_key)
        value_parts.append(grad_value)
    query_grads = [jnp.concatenate(query_parts, axis=1)]
    key_grads_list = [jnp.concatenate(key_parts, axis=1)]
    value_grads_list = [jnp.concatenate(value_parts, axis=1)]
    key_grad_all = jnp.stack(key_grads_list).reshape(groups, slot_len, model_width)
    value_grad_all = jnp.stack(value_grads_list).reshape(groups, slot_len, model_width)
    key_grad, value_grad = (
        lax.psum_scatter(
            key_grad_all.astype(jnp.bfloat16), "ctx", scatter_dimension=1, tiled=True
        ).astype(jnp.float32),
        lax.psum_scatter(
            value_grad_all.astype(jnp.bfloat16), "ctx", scatter_dimension=1, tiled=True
        ).astype(jnp.float32),
    )
    query_back = rotate(jnp.stack(query_grads), cosine_table, -sine_table).reshape(
        groups, piece_len, model_width
    )
    key_back = rotate(key_grad.reshape(split_shape), cosine_table, -sine_table).reshape(
        groups, piece_len, model_width
    )
    grad_projected = jnp.concatenate([query_back, key_back, value_grad], axis=-1).astype(
        jnp.bfloat16
    )
    grad_wqkv = jnp.einsum(
        "gpd,gpe->de", normed_one_low, grad_projected, preferred_element_type=jnp.float32
    )
    grad_normed_one = jnp.einsum(
        "gpe,de->gpd", grad_projected, full_qkv, preferred_element_type=jnp.float32
    )
    grad_norm_one, grad_gain_one = normalize_back(inputs, scale_one, gain_one, grad_normed_one)
    grad_inputs = grad_residual + grad_norm_one
    wqkv_part, wout_part = (
        lax.psum_scatter(
            grad_wqkv.astype(jnp.bfloat16), "fsdp", scatter_dimension=0, tiled=True
        ).astype(jnp.float32),
        lax.psum_scatter(
            grad_wout.astype(jnp.bfloat16), "fsdp", scatter_dimension=0, tiled=True
        ).astype(jnp.float32),
    )
    wqkv_sum, wout_sum, expert_sum = (
        lax.psum(wqkv_part.astype(jnp.bfloat16), "ctx").astype(jnp.float32),
        lax.psum(wout_part.astype(jnp.bfloat16), "ctx").astype(jnp.float32),
        lax.psum(grad_weights, "ctx").astype(jnp.float32),
    )
    gain_one_sum, gain_two_sum, router_sum, mixing_sum, const_sum = lax.psum(
        (grad_gain_one, grad_gain_two, grad_router, grad_mixing, grad_const), ("ctx", "fsdp")
    )
    return (
        output,
        grad_inputs,
        grad_previous,
        wqkv_sum,
        wout_sum,
        gain_one_sum,
        gain_two_sum,
        router_sum,
        mixing_sum,
        const_sum,
        expert_sum,
    )


def solution(mesh):
    return jax.shard_map(
        per_device,
        mesh=mesh,
        in_specs=(
            P("fsdp", "ctx", None),
            P("fsdp", "ctx", None),
            P("fsdp", "ctx", None),
            P("fsdp"),
            P("fsdp", "ctx", None),
            P("fsdp", None),
            P("fsdp", None),
            P(),
            P(),
            P(),
            P(),
            P(),
            P(None, "fsdp", None, None),
        ),
        out_specs=(
            P("fsdp", "ctx", None),
            P("fsdp", "ctx", None),
            P("fsdp", "ctx", None),
            P("fsdp", None),
            P("fsdp", None),
            P(),
            P(),
            P(),
            P(),
            P(),
            P(None, "fsdp", None, None),
        ),
        check_vma=False,
    )
```

```python
import itertools
import math

import jax
import jax.numpy as jnp
from jax import lax
from jax.experimental import pallas as pl
from jax.experimental.pallas import tpu as pltpu

from jax.sharding import PartitionSpec as P

HEAD_DIM = 64


EPSILON = 1e-05
MASKED = -1e30
HIGHEST = lax.Precision.HIGHEST


LOGICAL = pl.DeviceIdType.MESH
VMEM_LIMIT = 56 * 1024 * 1024


class Copies:
    def __init__(self, send, recv):
        self.send, self.recv, self.used = send, recv, 0

    def make(self, source, target, peer):
        index = self.used
        self.used += 1
        return pltpu.make_async_remote_copy(
            source, target, self.send.at[index], self.recv.at[index],
            device_id=peer, device_id_type=LOGICAL,
        )


def meet(peers):
    barrier = pltpu.get_barrier_semaphore()
    for allowed, peer in peers:
        @pl.when(allowed)
        def _():
            pl.semaphore_signal(barrier, 1, device_id=peer, device_id_type=LOGICAL)
    awaited = sum(jnp.where(allowed, 1, 0) for allowed, _ in peers)
    pl.semaphore_wait(barrier, awaited)


def together(*streams):
    for _ in itertools.zip_longest(*streams):
        pass


def within(value, count):
    return (value >= 0) & (value < count)


def bounded(value, count):
    return jnp.minimum(jnp.maximum(value, 0), count - 1)


def line_peers(count):
    rank = lax.axis_index("fsdp")
    return [
        (within(rank + way, count), {"fsdp": bounded(rank + way, count)}) for way in (1, -1)
    ]


def ring_peers(axis, count, stride=1):
    rank = lax.axis_index(axis)
    return [
        (rank >= 0, {axis: lax.rem(rank + stride * step, count)})
        for step in range(1, count // stride)
    ]


def own_place(count):
    rank = lax.axis_index("ctx")
    core = lax.rem(rank, 2)
    return rank, core, rank // 2, count // 2, rank + 1 - 2 * core


def plane_peers(count):
    rank, core, chip, chips, sibling = own_place(count)
    peers = [(rank >= 0, {"ctx": sibling})]
    if chips == 4:
        across, along, _ = square(chip)
        return peers + [(rank >= 0, {"ctx": 2 * c + core}) for c in (across, along)]
    return peers + ring_peers("ctx", count, 2)


def square(chip):
    side, row = lax.rem(chip, 2), chip // 2
    across = chip + 1 - 2 * side
    along = chip + 2 - 4 * row
    return across, along, across + 2 - 4 * row


def line_gather(copies, own, slot, count, arrived=None):
    rank = lax.axis_index("fsdp")
    sent, latest = [], {}
    for hop in range(1, count + 1):
        for way in (1, -1):
            origin = rank - way * (hop - 1)
            held = slot(bounded(origin, count))
            if hop > 1:
                earlier = latest[way]

                @pl.when(within(origin, count))
                def _():
                    earlier.wait_recv()

                if arrived is not None:
                    arrived(within(origin, count), bounded(origin, count), held)
            if hop < count:
                copy = copies.make(
                    own if hop == 1 else held, held, {"fsdp": bounded(rank + way, count)}
                )
                allowed = within(origin, count) & within(rank + way, count)

                @pl.when(allowed)
                def _():
                    copy.start()

                sent.append((allowed, copy))
                latest[way] = copy
        yield
    for allowed, copy in sent:

        @pl.when(allowed)
        def _():
            copy.wait_send()


def line_reduce(copies, part, passing, landing, count, total):
    rank = lax.axis_index("fsdp")
    sent, arriving = [], {}
    for step in range(count - 1, 0, -1):
        for side, way in enumerate((1, -1)):
            goal = rank + way * step
            allowed = within(goal, count)
            copy = copies.make(
                passing.at[side, step - 1],
                landing.at[side, step - 1],
                {"fsdp": bounded(rank + way, count)},
            )
            arriving[side, step - 1] = copy
            own = part(bounded(goal, count))
            has_earlier = allowed & within(rank - way, count)
            if step < count - 1:
                earlier = arriving[side, step]

                @pl.when(has_earlier)
                def _():
                    earlier.wait_recv()
                    passing[side, step - 1] = (
                        own[...].astype(jnp.float32) + landing[side, step].astype(jnp.float32)
                    ).astype(passing.dtype)

                @pl.when(allowed & jnp.logical_not(within(rank - way, count)))
                def _():
                    passing[side, step - 1] = own[...]
            else:

                @pl.when(allowed)
                def _():
                    passing[side, step - 1] = own[...]

            @pl.when(allowed)
            def _():
                copy.start()

            sent.append((allowed, copy))
        yield
    total[...] = part(rank)[...].astype(jnp.float32)
    for side, way in enumerate((1, -1)):
        last = arriving[side, 0]

        @pl.when(within(rank - way, count))
        def _():
            last.wait_recv()
            total[...] += landing[side, 0].astype(jnp.float32)
    for allowed, copy in sent:

        @pl.when(allowed)
        def _():
            copy.wait_send()


def push_gather(copies, own, slot, axis, count, stride=1):
    rank = lax.axis_index(axis)
    sent = []
    for step in range(1, count // stride):
        copy = copies.make(own, slot(step), {axis: lax.rem(rank + stride * step, count)})
        copy.start()
        sent.append(copy)
    yield
    for copy in sent:
        copy.wait()


def plane_gather(copies, own, slot, count):
    rank, core, chip, chips, sibling = own_place(count)
    sent, forwarded = [], []

    def send(source, target, peer):
        copy = copies.make(source, target, {"ctx": peer})
        copy.start()
        sent.append(copy)
        return copy

    def forward(index, part):
        copy = copies.make(slot(index, part), slot(index, part), {"ctx": sibling})
        copy.start()
        forwarded.append(copy)

    if chips == 4:
        across, along, _ = square(chip)
        side_x, side_y = 2 * across + core, 2 * along + core
        corner = 2 * square(chip)[2] + core
        first_x = send(own(1), slot(rank, 1), side_x)
        second_y = send(own(2), slot(rank, 2), side_y)
        second_x = send(own(2), slot(rank, 2), side_x)
        first_y = send(own(1), slot(rank, 1), side_y)
        copy = copies.make(own(0), slot(rank, 0), {"ctx": sibling})
        copy.start()
        forwarded.append(copy)
        yield
        first_x.wait_recv()
        corner_first = send(slot(side_x, 1), slot(side_x, 1), side_y)
        forward(side_x, 1)
        second_y.wait_recv()
        corner_second = send(slot(side_y, 2), slot(side_y, 2), side_x)
        forward(side_y, 2)
        yield
        second_x.wait_recv()
        forward(side_x, 2)
        first_y.wait_recv()
        forward(side_y, 1)
        yield
        corner_first.wait_recv()
        forward(corner, 1)
        corner_second.wait_recv()
        forward(corner, 2)
        yield
    else:
        pending = []
        for step in range(1, chips):
            peer = lax.rem(rank + 2 * step, count)
            pending.append((lax.rem(rank + count - 2 * step, count), send(own(0), slot(rank, 0), peer)))
        copy = copies.make(own(0), slot(rank, 0), {"ctx": sibling})
        copy.start()
        forwarded.append(copy)
        yield
        for origin, copy in pending:
            copy.wait_recv()
            forward(origin, 0)
        yield
    for copy in sent:
        copy.wait_send()
    for copy in forwarded:
        copy.wait()


def plane_reduce(copies, paired, passing, landing, count, finish):
    rank, core, chip, chips, sibling = own_place(count)
    sent = []

    def send(source, target, peer_chip):
        copy = copies.make(source, target, {"ctx": 2 * peer_chip + core})
        copy.start()
        sent.append(copy)
        return copy

    if chips == 4:
        across, along, corner = square(chip)
        via_x = send(paired(corner, 1), landing.at[0], across)
        via_y = send(paired(corner, 2), landing.at[1], along)
        own_x = send(paired(across, 1), landing.at[2], across)
        own_y = send(paired(along, 2), landing.at[3], along)
        yield
        via_x.wait_recv()
        passing[0] = (
            paired(along, 1)[...].astype(jnp.float32) + landing[0].astype(jnp.float32)
        ).astype(passing.dtype)
        last_first = send(passing.at[0], landing.at[4], along)
        via_y.wait_recv()
        passing[1] = (
            paired(across, 2)[...].astype(jnp.float32) + landing[1].astype(jnp.float32)
        ).astype(passing.dtype)
        last_second = send(passing.at[1], landing.at[5], across)
        yield
        own_x.wait_recv()
        own_y.wait_recv()
        last_first.wait_recv()
        last_second.wait_recv()
        for half in (1, 2):
            total = paired(chip, half)[...].astype(jnp.float32)
            total = total + landing[1 + half].astype(jnp.float32)
            total = total + landing[3 + half].astype(jnp.float32)
            finish(half, total)
    else:
        for step in range(1, chips):
            send(paired(lax.rem(chip + step, chips), 0), landing.at[step - 1], lax.rem(chip + step, chips))
        yield
        total = paired(chip, 0)[...].astype(jnp.float32)
        for step, copy in enumerate(sent):
            copy.wait_recv()
            total = total + landing[step].astype(jnp.float32)
        finish(0, total)
    for copy in sent:
        copy.wait_send()


def remote_call(kernel, name, results, operands, in_spaces, out_spaces, scratch, copies, cost):
    ids = ("weights", "keys", "rows", "row_sums", "key_sums", "totals")
    return pl.pallas_call(
        kernel,
        out_shape=results,
        in_specs=[pl.BlockSpec(memory_space=space) for space in in_spaces],
        out_specs=[pl.BlockSpec(memory_space=space) for space in out_spaces],
        scratch_shapes=list(scratch)
        + [pltpu.SemaphoreType.DMA((copies,)), pltpu.SemaphoreType.DMA((copies,))],
        compiler_params=pltpu.CompilerParams(
            collective_id=ids.index(name), has_side_effects=True, vmem_limit_bytes=VMEM_LIMIT
        ),
        cost_estimate=pl.CostEstimate(flops=0, bytes_accessed=cost, transcendentals=0),
        name=name,
    )(*operands)


def struct(shape, dtype):
    return jax.ShapeDtypeStruct(shape, dtype)


class SharedBlock:
    def __init__(self, copies, source, target, count, ctx_count):
        _, core, _, _, self.sibling = own_place(ctx_count)
        half = source.shape[0] // 2
        rows = pl.ds(pl.multiple_of(core * half, math.gcd(half, 256)), half)
        self.copies, self.forwarded = copies, []
        self.stream = line_gather(
            copies, source.at[rows], lambda i: target.at[i, rows], count, self.arrived
        )

    def arrived(self, allowed, _, held):
        copy = self.copies.make(held, held, {"ctx": self.sibling})

        @pl.when(allowed)
        def _():
            copy.start()

        self.forwarded.append((allowed, copy))

    def wait(self):
        for allowed, copy in self.forwarded:

            @pl.when(allowed)
            def _():
                copy.wait()


def gather_weights(weight, count, ctx_count):
    rows, width = weight.shape

    def kernel(source, target, local, send, recv):
        copies = Copies(send, recv)
        rank = lax.axis_index("fsdp")
        meet(line_peers(count) + plane_peers(ctx_count)[:1])
        keep = pltpu.make_async_copy(source, target.at[rank], local)
        keep.start()
        block = SharedBlock(copies, source, target, count, ctx_count)
        together(block.stream)
        block.wait()
        keep.wait()

    (full,) = remote_call(
        kernel, "weights", [struct((count, rows, width), weight.dtype)], [weight],
        [pl.ANY], [pl.ANY], [pltpu.SemaphoreType.DMA], 4 * count, count * rows * width * 4,
    )
    return full.reshape(count * rows, width)


def gather_keys(block, weights, count, ctx_count):
    rows, width = block.shape
    half = rows // 2

    def kernel(*refs):
        own, *sources = refs[: 1 + len(weights)]
        gathered, *targets = refs[1 + len(weights) : 2 + 2 * len(weights)]
        local, send, recv = refs[2 + 2 * len(weights) :]
        copies = Copies(send, recv)
        rank, place = lax.axis_index("fsdp"), lax.axis_index("ctx")
        spans = (pl.ds(0, rows), pl.ds(0, half), pl.ds(half, half))
        meet(line_peers(count) + plane_peers(ctx_count))
        kept = [pltpu.make_async_copy(own, gathered.at[place], local.at[0])]
        kept += [
            pltpu.make_async_copy(source, target.at[rank], local.at[1 + i])
            for i, (source, target) in enumerate(zip(sources, targets))
        ]
        for copy in kept:
            copy.start()
        blocks = [SharedBlock(copies, s, t, count, ctx_count) for s, t in zip(sources, targets)]
        together(
            plane_gather(
                copies,
                lambda part: own.at[spans[part]],
                lambda i, part: gathered.at[i, spans[part]],
                ctx_count,
            ),
            *[b.stream for b in blocks],
        )
        for b in blocks:
            b.wait()
        for copy in kept:
            copy.wait()

    results = [struct((ctx_count, rows, width), block.dtype)]
    results += [struct((count,) + w.shape, w.dtype) for w in weights]
    gathered, *full = remote_call(
        kernel, "keys", results, [block, *weights],
        [pl.ANY] * (1 + len(weights)), [pl.ANY] * (1 + len(weights)),
        [pltpu.SemaphoreType.DMA((1 + len(weights),))],
        16 + 2 * ctx_count + 4 * count * len(weights),
        ctx_count * rows * width * 4,
    )
    return gathered.reshape(ctx_count * rows, width), [
        f.reshape(count * f.shape[1], f.shape[2]) for f in full
    ]


def gather_rows(block, notes, count):
    def kernel(own, own_notes, gathered, all_notes, local, send, recv):
        copies = Copies(send, recv)
        rank = lax.axis_index("fsdp")
        meet(ring_peers("fsdp", count))
        kept = [
            pltpu.make_async_copy(own, gathered.at[rank], local.at[0]),
            pltpu.make_async_copy(own_notes, all_notes.at[rank], local.at[1]),
        ]
        for copy in kept:
            copy.start()
        together(
            push_gather(copies, own_notes, lambda step: all_notes.at[rank], "fsdp", count),
            line_gather(copies, own, lambda i: gathered.at[i], count),
        )
        for copy in kept:
            copy.wait()

    return remote_call(
        kernel, "rows",
        [struct((count,) + block.shape, block.dtype), struct((count,) + notes.shape, notes.dtype)],
        [block, notes], [pl.ANY] * 2, [pl.ANY] * 2, [pltpu.SemaphoreType.DMA((2,))],
        4 * count, count * block.size * 4,
    )


def reduce_rows(parts, notes, count):
    _, rows, width = parts.shape

    def kernel(given, given_notes, total, notes_total, passing, landing, noted, send, recv):
        copies = Copies(send, recv)
        rank = lax.axis_index("fsdp")
        meet(ring_peers("fsdp", count))
        pushes = []
        for step in range(1, count):
            peer = lax.rem(rank + step, count)
            copy = copies.make(given_notes.at[peer], noted.at[step - 1], {"fsdp": peer})
            copy.start()
            pushes.append(copy)
        together(
            line_reduce(copies, lambda d: given.at[d], passing, landing, count, total)
        )
        sums = given_notes[rank]
        for step, copy in enumerate(pushes):
            copy.wait()
            sums = sums + noted[step]
        notes_total[...] = sums

    return remote_call(
        kernel, "row_sums",
        [struct((rows, width), jnp.float32), struct(notes.shape[1:], notes.dtype)],
        [parts, notes], [pltpu.VMEM] * 2, [pltpu.VMEM] * 2,
        [
            pltpu.VMEM((2, count - 1, rows, width), parts.dtype),
            pltpu.VMEM((2, count - 1, rows, width), parts.dtype),
            pltpu.VMEM((count - 1,) + notes.shape[1:], notes.dtype),
        ],
        4 * count, count * rows * width * 4,
    )


def reduce_keys(parts, row_parts, count, ctx_count):
    _, rows, width = parts.shape
    chips = ctx_count // 2
    half = rows // 2
    lands = (6, half, width) if chips == 4 else (chips - 1, rows, width)

    def kernel(given, given_rows, total, rows_total, met, paired, passing, landing,
               row_passing, row_landing, send, recv):
        copies = Copies(send, recv)
        _, core, _, _, sibling = own_place(ctx_count)
        spans = (pl.ds(0, rows), pl.ds(0, half), pl.ds(half, half))
        meet(ring_peers("fsdp", count) + plane_peers(ctx_count))
        exchanged = []
        for q in range(chips):
            copy = copies.make(given.at[2 * q + 1 - core], met.at[q], {"ctx": sibling})
            copy.start()
            exchanged.append(copy)

        def finish(part, value):
            total[spans[part], :] = value

        def planes():
            yield
            for q, copy in enumerate(exchanged):
                copy.wait_recv()
                paired[q] = (
                    given[2 * q + core].astype(jnp.float32) + met[q].astype(jnp.float32)
                ).astype(paired.dtype)
            yield from plane_reduce(
                copies, lambda q, part: paired.at[q, spans[part]],
                passing, landing, ctx_count, finish,
            )

        together(
            planes(),
            line_reduce(
                copies, lambda d: given_rows.at[d], row_passing, row_landing, count, rows_total
            ),
        )
        for copy in exchanged:
            copy.wait_send()

    _, row_count, row_width = row_parts.shape
    return remote_call(
        kernel, "key_sums",
        [struct((rows, width), jnp.float32), struct((row_count, row_width), jnp.float32)],
        [parts, row_parts], [pltpu.VMEM] * 2, [pltpu.VMEM] * 2,
        [
            pltpu.VMEM((chips, rows, width), parts.dtype),
            pltpu.VMEM((chips, rows, width), parts.dtype),
            pltpu.VMEM((2, half, width), parts.dtype),
            pltpu.VMEM(lands, parts.dtype),
            pltpu.VMEM((2, count - 1, row_count, row_width), parts.dtype),
            pltpu.VMEM((2, count - 1, row_count, row_width), parts.dtype),
        ],
        2 * chips + 8 + 2 * count, ctx_count * rows * width * 4,
    )


def reduce_weights(parts, small, count, ctx_count):
    _, rows, width = parts.shape
    chips = ctx_count // 2
    half, share = rows // 2, width // chips
    row_unit = math.gcd(half, 256)
    first = max(count // 2, 1)
    lands = (6, first, half, share) if chips == 4 else (chips - 1, count, half, share)

    def kernel(given, given_small, total, small_total, met, paired, passing, landing, merged,
               line_passing, line_landing, line_total, own_total, small_met, small_sum,
               small_plane, small_plane_sum, small_line, send, recv):
        copies = Copies(send, recv)
        rank = lax.axis_index("fsdp")
        place, core, chip, _, sibling = own_place(ctx_count)
        spans = (pl.ds(0, count), pl.ds(0, first), pl.ds(first, count - first))
        mine = pl.ds(pl.multiple_of(core * half, row_unit), half)
        theirs = pl.ds(pl.multiple_of((1 - core) * half, row_unit), half)

        def columns(q):
            return pl.ds(pl.multiple_of(q * share, 128), share)

        meet(
            ring_peers("fsdp", count)
            + ring_peers("ctx", ctx_count, 2)
            + plane_peers(ctx_count)[:1]
        )
        small_pair = copies.make(given_small, small_met, {"ctx": sibling})
        small_pair.start()
        exchanged = []
        for d in range(count):
            copy = copies.make(given.at[d, theirs], met.at[d], {"ctx": sibling})
            copy.start()
            exchanged.append(copy)

        def small_stream():
            small_pair.wait()
            small_sum[...] = given_small[...] + small_met[...]
            pushes = []
            for step in range(1, chips):
                copy = copies.make(
                    small_sum, small_plane.at[step - 1],
                    {"ctx": lax.rem(place + 2 * step, ctx_count)},
                )
                copy.start()
                pushes.append(copy)
            yield
            for copy in pushes:
                copy.wait()
            small_plane_sum[...] = small_sum[...] + jnp.sum(small_plane[...], axis=0)
            pushes = []
            for step in range(1, count):
                copy = copies.make(
                    small_plane_sum, small_line.at[step - 1],
                    {"fsdp": lax.rem(rank + step, count)},
                )
                copy.start()
                pushes.append(copy)
            yield
            yield
            for copy in pushes:
                copy.wait()
            small_total[...] = small_plane_sum[...] + jnp.sum(small_line[...], axis=0)

        def finish(part, value):
            merged[spans[part]] = value.astype(merged.dtype)

        def large_stream():
            for d, copy in enumerate(exchanged):
                copy.wait_recv()
                for q in range(chips):
                    paired[q, d] = (
                        given[d, mine, q * share : (q + 1) * share].astype(jnp.float32)
                        + met[d, :, q * share : (q + 1) * share].astype(jnp.float32)
                    ).astype(paired.dtype)
            yield from plane_reduce(
                copies, lambda q, part: paired.at[q, spans[part]],
                passing, landing, ctx_count, finish,
            )
            yield from line_reduce(
                copies, lambda d: merged.at[d], line_passing, line_landing, count, line_total
            )
            own_total[...] = line_total[...].astype(own_total.dtype)
            sent = []
            forwarded = []
            copy = copies.make(own_total, total.at[mine, columns(chip)], {"ctx": sibling})
            copy.start()
            forwarded.append(copy)
            for step in range(1, chips):
                copy = copies.make(
                    own_total, total.at[mine, columns(chip)],
                    {"ctx": lax.rem(place + 2 * step, ctx_count)},
                )
                copy.start()
                sent.append(copy)
            total[mine, columns(chip)] = own_total[...]
            for step, copy in enumerate(sent, 1):
                copy.wait_recv()
                held = total.at[mine, columns(lax.rem(chip + chips - step, chips))]
                copy = copies.make(held, held, {"ctx": sibling})
                copy.start()
                forwarded.append(copy)
            for copy in sent:
                copy.wait_send()
            for copy in forwarded:
                copy.wait()

        together(small_stream(), large_stream())
        for copy in exchanged:
            copy.wait_send()

    kind = parts.dtype
    f32 = jnp.float32
    return remote_call(
        kernel, "totals",
        [struct((rows, width), kind), struct(small.shape, f32)],
        [parts, small], [pltpu.VMEM] * 2, [pltpu.VMEM] * 2,
        [
            pltpu.VMEM((count, half, width), kind),
            pltpu.VMEM((chips, count, half, share), kind),
            pltpu.VMEM((2, first, half, share), kind),
            pltpu.VMEM(lands, kind),
            pltpu.VMEM((count, half, share), kind),
            pltpu.VMEM((2, count - 1, half, share), kind),
            pltpu.VMEM((2, count - 1, half, share), kind),
            pltpu.VMEM((half, share), f32),
            pltpu.VMEM((half, share), kind),
            pltpu.VMEM(small.shape, f32),
            pltpu.VMEM(small.shape, f32),
            pltpu.VMEM((chips - 1,) + small.shape, f32),
            pltpu.VMEM(small.shape, f32),
            pltpu.VMEM((count - 1,) + small.shape, f32),
        ],
        count + 8 + 3 * count + 4 * chips, parts.size * 8,
    )


def normalize_rows(values, gain_row):
    scaling = lax.rsqrt(jnp.mean(values * values, axis=-1, keepdims=True) + EPSILON)
    return (values * scaling * gain_row, scaling)


def normalize_back(values, scaling, gain_row, grad_out):
    grad_hat = grad_out * gain_row
    grad_gain = jnp.sum(grad_out * values * scaling, axis=(0, 1))
    grad_values = scaling * grad_hat - values * scaling**3 * jnp.mean(
        grad_hat * values, axis=-1, keepdims=True
    )
    return (grad_values, grad_gain)


def rope_tables(positions, head_size):
    half_dim = head_size // 2
    frequency = jnp.exp(
        jnp.arange(half_dim, dtype=jnp.float32) * (-2.0 * math.log(10000.0) / head_size)
    )
    angles = positions.astype(jnp.float32)[:, None] * frequency[None, :]
    return (jnp.cos(angles)[:, None, :], jnp.sin(angles)[:, None, :])


def rotate(values, cosine_table, sine_table):
    half_dim = values.shape[-1] // 2
    first_half = values[..., :half_dim]
    second_half = values[..., half_dim:]
    return jnp.concatenate(
        [
            first_half * cosine_table - second_half * sine_table,
            second_half * cosine_table + first_half * sine_table,
        ],
        axis=-1,
    )


def masked_scores(queries, key_rows, allowed):
    scaling = queries.shape[-1] ** (-0.5)
    scores = (
        jnp.einsum("qhd,khd->hqk", queries, key_rows, preferred_element_type=jnp.float32) * scaling
    )
    return jnp.where(allowed[None], scores, MASKED)


def attend_forward(queries, key_rows, values, allowed):
    scores = masked_scores(queries, key_rows, allowed)
    row_max = jnp.max(scores, axis=-1, keepdims=True)
    weights = jnp.exp(scores - row_max)
    row_total = jnp.sum(weights, axis=-1, keepdims=True)
    probabilities = (weights / row_total).astype(jnp.bfloat16)
    attended = jnp.einsum("hqk,khd->qhd", probabilities, values, preferred_element_type=jnp.float32)
    return (attended, row_max, row_total)


def attend_backward(queries, key_rows, values, allowed, row_max, row_total, grad_out):
    scaling = queries.shape[-1] ** (-0.5)
    scores = masked_scores(queries, key_rows, allowed)
    probabilities = jnp.exp(scores - row_max) / row_total
    probs_low = probabilities.astype(jnp.bfloat16)
    grad_probs = jnp.einsum("qhd,khd->hqk", grad_out, values, preferred_element_type=jnp.float32)
    inner_sum = jnp.sum(probabilities * grad_probs, axis=-1, keepdims=True)
    grad_scores = (probabilities * (grad_probs - inner_sum)).astype(jnp.bfloat16)
    grad_queries = (
        jnp.einsum("hqk,khd->qhd", grad_scores, key_rows, preferred_element_type=jnp.float32)
        * scaling
    )
    grad_keys = (
        jnp.einsum("hqk,qhd->khd", grad_scores, queries, preferred_element_type=jnp.float32)
        * scaling
    )
    grad_values = jnp.einsum(
        "hqk,qhd->khd", probs_low, grad_out, preferred_element_type=jnp.float32
    )
    return (grad_queries, grad_keys, grad_values)


def per_device(
    tokens,
    prev_logits,
    routes,
    lengths,
    cotangent,
    w_qkv,
    w_out,
    gain_attn,
    gain_moe,
    w_router,
    w_residual,
    const_vec,
    w_expert,
):
    groups, piece_len, model_width = tokens.shape
    head_count = model_width // HEAD_DIM
    part_heads = 2
    part_count = head_count // part_heads
    slot_len = piece_len * lax.axis_size("ctx")
    positions = lax.axis_index("ctx") * piece_len + jnp.arange(piece_len, dtype=jnp.int32)
    key_positions = jnp.arange(slot_len, dtype=jnp.int32)
    live_rows = (positions[None, :] < lengths[:, None]).astype(jnp.float32)[..., None]
    experts = w_expert.shape[0]
    capacity = piece_len // 4
    slot_count = experts * capacity
    split_shape = (groups, piece_len, head_count, HEAD_DIM)
    fsdp_count, ctx_count = lax.axis_size("fsdp"), lax.axis_size("ctx")
    full_kv = gather_weights(w_qkv[:, model_width:], fsdp_count, ctx_count)
    inputs = tokens.astype(jnp.float32)
    gain_one = gain_attn.astype(jnp.float32)
    gain_two = gain_moe.astype(jnp.float32)
    normed_one, scale_one = normalize_rows(inputs, gain_one)
    normed_one_low = normed_one.astype(jnp.bfloat16)
    projected = jnp.einsum("gpd,de->gpe", normed_one_low, full_kv, preferred_element_type=jnp.float32)
    cosine_table, sine_table = rope_tables(positions, HEAD_DIM)
    key_local = (
        rotate(projected[..., :model_width].reshape(split_shape), cosine_table, sine_table)
        .astype(jnp.bfloat16)
        .reshape(piece_len, model_width)
    )
    value_local = projected[0, :, model_width:].astype(jnp.bfloat16)
    all_pairs, (full_query, full_out) = gather_keys(
        jnp.concatenate([key_local, value_local], axis=-1),
        [w_qkv[:, :model_width], w_out],
        fsdp_count,
        ctx_count,
    )
    cotangent_low = live_rows.astype(jnp.bfloat16) * cotangent
    cotangent_own, all_pairs = lax.optimization_barrier((cotangent_low, all_pairs))
    cotangent_rows = lax.all_gather(cotangent_own, "fsdp", axis=0, tiled=True)
    queries = rotate(
        jnp.einsum(
            "gpd,de->gpe", normed_one_low, full_query, preferred_element_type=jnp.float32
        ).reshape(split_shape),
        cosine_table,
        sine_table,
    ).astype(jnp.bfloat16)
    key_all = all_pairs[:, :model_width].reshape(groups, slot_len, head_count, HEAD_DIM)
    value_all = all_pairs[:, model_width:].reshape(groups, slot_len, head_count, HEAD_DIM)
    maxima_list = []
    totals_list = []
    group_index = 0
    allowed = (key_positions[None, :] <= positions[:, None]) & (
        key_positions[None, :] < lengths[group_index]
    )
    mask_list = [allowed]
    head_parts = []
    for part_index in range(part_count):
        first_head = part_index * part_heads
        last_head = first_head + part_heads
        attended, row_max, row_total = attend_forward(
            queries[group_index, :, first_head:last_head],
            key_all[group_index, :, first_head:last_head],
            value_all[group_index, :, first_head:last_head],
            allowed,
        )
        head_parts.append(attended)
        maxima_list.append(row_max)
        totals_list.append(row_total)
    attended_list = [jnp.concatenate(head_parts, axis=1)]
    mixed_low = (
        jnp.stack(attended_list).reshape(groups, piece_len, model_width).astype(jnp.bfloat16)
    )
    attention = jnp.einsum("gpd,de->gpe", mixed_low, full_out, preferred_element_type=jnp.float32)
    residual_sum = inputs + attention
    normed_two, scale_two = normalize_rows(residual_sum, gain_two)
    routed_low = normed_two.astype(jnp.bfloat16)
    routed = routed_low.astype(jnp.float32)
    logits = jnp.einsum("gpd,de->gpe", routed, w_router, precision=HIGHEST) + jnp.einsum(
        "gpi,ie->gpe", prev_logits, w_residual, precision=HIGHEST
    )
    id_range = jnp.arange(experts + 4, dtype=jnp.int32)
    route_hot = (routes[..., None] == id_range).astype(jnp.float32)
    chosen = jnp.sum(route_hot * logits[:, :, None, :], axis=-1)
    chosen_exp = jnp.exp(chosen - jnp.max(chosen, axis=-1, keepdims=True))
    gate_weights = chosen_exp / jnp.sum(chosen_exp, axis=-1, keepdims=True)
    assign_hot = route_hot[..., :experts].reshape(groups, 2 * piece_len, experts)
    earlier = jnp.cumsum(assign_hot, axis=1) - assign_hot
    order_in = jnp.sum(earlier * assign_hot, axis=-1)
    expert_of = jnp.sum(assign_hot * jnp.arange(experts, dtype=jnp.float32), axis=-1)
    is_ffn = jnp.sum(assign_hot, axis=-1)
    slot_of = jnp.where(is_ffn > 0.5, expert_of * capacity + order_in, -1.0).reshape(
        groups, piece_len, 2
    )
    notes = jnp.concatenate([slot_of[0].T, gate_weights[0].T, jnp.zeros((4, piece_len))], axis=0)
    routed_rows, all_notes = gather_rows(routed_low[0], notes, fsdp_count)
    peers = fsdp_count
    all_slot_of = all_notes[:, :2].swapaxes(1, 2)
    slot_hot = all_slot_of[..., None] == jnp.arange(slot_count, dtype=jnp.float32)
    all_gate = jnp.sum(
        jnp.where(slot_hot, all_notes[:, 2:4].swapaxes(1, 2)[..., None], 0.0), axis=(1, 2)
    )
    all_hot = (
        jnp.sum(slot_hot.astype(jnp.float32), axis=2)
        .astype(jnp.bfloat16)
        .reshape(peers, piece_len, experts, capacity)
    )
    gate_rows = all_gate.reshape(peers, experts, capacity).swapaxes(0, 1)[..., None]
    row_pairs = jnp.concatenate([routed_rows, cotangent_rows], axis=-1)
    buffers = jnp.einsum(
        "gpec,gpd->egcd", all_hot, row_pairs, preferred_element_type=jnp.float32
    ).astype(jnp.bfloat16)
    expert_in = buffers[..., :model_width].reshape(experts, peers * capacity, model_width)
    block_rows = buffers[..., model_width:].astype(jnp.float32)
    grad_out = (
        (gate_rows * block_rows)
        .astype(jnp.bfloat16)
        .reshape(experts, peers * capacity, model_width)
    )
    w_gate, w_up, w_down = w_expert[:, :, 0], w_expert[:, :, 1], w_expert[:, :, 2]

    def apply(spec, left, right):
        return jnp.einsum(spec, left, right, preferred_element_type=jnp.float32)

    gate_proj = apply("ecd,efd->ecf", expert_in, w_gate)
    up_proj = apply("ecd,efd->ecf", expert_in, w_up)
    sigmoid_gate = jax.nn.sigmoid(gate_proj)
    silu_gate = gate_proj * sigmoid_gate
    hidden = (silu_gate * up_proj).astype(jnp.bfloat16)
    expert_out = apply("ecf,efd->ecd", hidden, w_down).reshape(buffers.shape[:3] + (model_width,))
    grad_hidden = apply("ecd,efd->ecf", grad_out, w_down)
    grad_gate_proj = (
        grad_hidden * up_proj * sigmoid_gate * (1.0 + gate_proj * (1.0 - sigmoid_gate))
    ).astype(jnp.bfloat16)
    grad_up_proj = (grad_hidden * silu_gate).astype(jnp.bfloat16)
    grad_in = (
        apply("ecf,efd->ecd", grad_gate_proj, w_gate) + apply("ecf,efd->ecd", grad_up_proj, w_up)
    ).reshape(expert_out.shape)
    slot_dot = jnp.sum(block_rows * expert_out, axis=-1).swapaxes(0, 1).reshape(peers, slot_count)
    route_dot = jnp.sum(jnp.where(slot_hot, slot_dot[:, None, None, :], 0.0), axis=-1)
    dot_notes = jnp.concatenate(
        [route_dot.swapaxes(1, 2), jnp.zeros((peers, 6, piece_len), jnp.float32)], axis=1
    )
    grad_parts = apply("gpec,egcd->gpd", all_hot, grad_in.astype(jnp.bfloat16)).astype(jnp.bfloat16)
    out_parts = apply(
        "gpec,egcd->gpd", all_hot, (gate_rows * expert_out).astype(jnp.bfloat16)
    ).astype(jnp.bfloat16)
    grad_weights = jnp.stack(
        [
            apply("ecf,ecd->efd", grad_gate_proj, expert_in).astype(jnp.bfloat16),
            apply("ecf,ecd->efd", grad_up_proj, expert_in).astype(jnp.bfloat16),
            apply("ecf,ecd->efd", hidden, grad_out).astype(jnp.bfloat16),
        ],
        axis=2,
    )
    grad_weights, grad_parts = lax.optimization_barrier((grad_weights, grad_parts))
    expert_sum = lax.psum(grad_weights, "ctx").astype(jnp.float32)
    ffn_grad, dot_sums = reduce_rows(grad_parts, dot_notes, fsdp_count)
    ffn_grad = ffn_grad[None]
    copy_hot = route_hot[..., experts + 1]
    const_hot = route_hot[..., experts + 2 :]
    constants = const_vec.astype(jnp.float32)
    gate_const = jnp.sum(gate_weights[..., None] * const_hot, axis=2)
    copy_gate = jnp.sum(gate_weights * copy_hot, axis=2, keepdims=True)
    special_sum = copy_gate * routed + jnp.einsum(
        "gpj,jd->gpd", gate_const, constants, precision=HIGHEST
    )
    grad_block = live_rows * cotangent.astype(jnp.float32)
    copy_dot = jnp.sum(grad_block * routed, axis=-1)[..., None]
    const_dot = jnp.einsum("gpd,jd->gpj", grad_block, constants, precision=HIGHEST)
    grad_gate = (
        dot_sums[:2].T[None]
        + copy_hot * copy_dot
        + jnp.sum(const_hot * const_dot[:, :, None, :], axis=-1)
    )
    grad_chosen = gate_weights * (
        grad_gate - jnp.sum(gate_weights * grad_gate, axis=-1, keepdims=True)
    )
    grad_logits = jnp.sum(grad_chosen[..., None] * route_hot, axis=2)
    grad_router = jnp.einsum("gpd,gpe->de", routed, grad_logits, precision=HIGHEST)
    grad_mixing = jnp.einsum("gpi,gpe->ie", prev_logits, grad_logits, precision=HIGHEST)
    grad_previous = jnp.einsum("gpe,ie->gpi", grad_logits, w_residual, precision=HIGHEST)
    grad_const = jnp.einsum("gpd,gpj->jd", grad_block, gate_const, precision=HIGHEST)
    grad_routed = (
        jnp.einsum("gpe,de->gpd", grad_logits, w_router, precision=HIGHEST)
        + copy_gate * grad_block
        + ffn_grad
    )
    grad_norm_two, grad_gain_two = normalize_back(residual_sum, scale_two, gain_two, grad_routed)
    grad_residual = grad_block + grad_norm_two
    grad_attention = grad_residual.astype(jnp.bfloat16)
    grad_wout = jnp.einsum(
        "gpd,gpe->de", mixed_low, grad_attention, preferred_element_type=jnp.float32
    )
    grad_mixed = (
        jnp.einsum("gpe,de->gpd", grad_attention, full_out, preferred_element_type=jnp.float32)
        .astype(jnp.bfloat16)
        .reshape(split_shape)
    )
    group_index = 0
    query_parts = []
    key_parts = []
    value_parts = []
    for part_index in range(part_count):
        first_head = part_index * part_heads
        last_head = first_head + part_heads
        grad_query, grad_key, grad_value = attend_backward(
            queries[group_index, :, first_head:last_head],
            key_all[group_index, :, first_head:last_head],
            value_all[group_index, :, first_head:last_head],
            mask_list[group_index],
            maxima_list[part_count * group_index + part_index],
            totals_list[part_count * group_index + part_index],
            grad_mixed[group_index, :, first_head:last_head],
        )
        query_parts.append(grad_query)
        key_parts.append(grad_key)
        value_parts.append(grad_value)
    query_grads = [jnp.concatenate(query_parts, axis=1)]
    key_grads_list = [jnp.concatenate(key_parts, axis=1)]
    value_grads_list = [jnp.concatenate(value_parts, axis=1)]
    pair_grads = jnp.concatenate(
        [
            key_grads_list[0].reshape(ctx_count, piece_len, model_width),
            value_grads_list[0].reshape(ctx_count, piece_len, model_width),
        ],
        axis=-1,
    ).astype(jnp.bfloat16)
    pair_grad, ffn_sum = reduce_keys(pair_grads, out_parts, fsdp_count, ctx_count)
    output = (live_rows * (residual_sum + special_sum + ffn_sum[None])).astype(jnp.bfloat16)
    key_grad = pair_grad[None, :, :model_width]
    value_grad = pair_grad[None, :, model_width:]
    query_back = rotate(jnp.stack(query_grads), cosine_table, -sine_table).reshape(
        groups, piece_len, model_width
    )
    key_back = rotate(key_grad.reshape(split_shape), cosine_table, -sine_table).reshape(
        groups, piece_len, model_width
    )
    grad_projected = jnp.concatenate([query_back, key_back, value_grad], axis=-1).astype(
        jnp.bfloat16
    )
    grad_wqkv = jnp.einsum(
        "gpd,gpe->de", normed_one_low, grad_projected, preferred_element_type=jnp.float32
    )
    grad_normed_one = jnp.einsum(
        "gpe,de->gpd",
        grad_projected[..., :model_width],
        full_query,
        preferred_element_type=jnp.float32,
    ) + jnp.einsum(
        "gpe,de->gpd",
        grad_projected[..., model_width:],
        full_kv,
        preferred_element_type=jnp.float32,
    )
    grad_norm_one, grad_gain_one = normalize_back(inputs, scale_one, gain_one, grad_normed_one)
    grad_inputs = grad_residual + grad_norm_one
    weight_parts = (
        jnp.concatenate([grad_wqkv, grad_wout], axis=-1)
        .astype(jnp.bfloat16)
        .reshape(fsdp_count, -1, 4 * model_width)
    )
    few = experts + 4
    mixing_row = jnp.pad(grad_mixing.reshape(1, -1), ((0, 0), (0, model_width - few * few)))
    small = jnp.concatenate(
        [grad_router.T, grad_const, grad_gain_one[None], grad_gain_two[None], mixing_row], axis=0
    )
    small = jnp.pad(small, ((0, -small.shape[0] % 8), (0, 0)))
    weight_sum, small_sum = reduce_weights(weight_parts, small, fsdp_count, ctx_count)
    weight_sum = weight_sum.astype(jnp.float32)
    wqkv_sum, wout_sum = weight_sum[:, : 3 * model_width], weight_sum[:, 3 * model_width :]
    router_sum, const_sum = small_sum[:few].T, small_sum[few : few + 2]
    gain_one_sum, gain_two_sum = small_sum[few + 2], small_sum[few + 3]
    mixing_sum = small_sum[few + 4, : few * few].reshape(few, few)
    return (
        output,
        grad_inputs,
        grad_previous,
        wqkv_sum,
        wout_sum,
        gain_one_sum,
        gain_two_sum,
        router_sum,
        mixing_sum,
        const_sum,
        expert_sum,
    )


def solution(mesh):
    return jax.shard_map(
        per_device,
        mesh=mesh,
        in_specs=(
            P("fsdp", "ctx", None),
            P("fsdp", "ctx", None),
            P("fsdp", "ctx", None),
            P("fsdp"),
            P("fsdp", "ctx", None),
            P("fsdp", None),
            P("fsdp", None),
            P(),
            P(),
            P(),
            P(),
            P(),
            P(None, "fsdp", None, None),
        ),
        out_specs=(
            P("fsdp", "ctx", None),
            P("fsdp", "ctx", None),
            P("fsdp", "ctx", None),
            P("fsdp", None),
            P("fsdp", None),
            P(),
            P(),
            P(),
            P(),
            P(),
            P(None, "fsdp", None, None),
        ),
        check_vma=False,
    )
```

```python
import itertools
import math

import jax
import jax.numpy as jnp
from jax import lax
from jax.experimental import pallas as pl
from jax.experimental.pallas import tpu as pltpu

from jax.sharding import PartitionSpec as P

HEAD_DIM = 64


EPSILON = 1e-05
MASKED = -1e30
HIGHEST = lax.Precision.HIGHEST


LOGICAL = pl.DeviceIdType.MESH
VMEM_LIMIT = 56 * 1024 * 1024


class Copies:
    def __init__(self, send, recv):
        self.send, self.recv, self.used = send, recv, 0

    def make(self, source, target, peer):
        index = self.used
        self.used += 1
        return pltpu.make_async_remote_copy(
            source, target, self.send.at[index], self.recv.at[index],
            device_id=peer, device_id_type=LOGICAL,
        )


def meet(peers):
    barrier = pltpu.get_barrier_semaphore()
    for allowed, peer in peers:
        @pl.when(allowed)
        def _():
            pl.semaphore_signal(barrier, 1, device_id=peer, device_id_type=LOGICAL)
    awaited = sum(jnp.where(allowed, 1, 0) for allowed, _ in peers)
    pl.semaphore_wait(barrier, awaited)


def together(*streams):
    for _ in itertools.zip_longest(*streams):
        pass


def within(value, count):
    return (value >= 0) & (value < count)


def bounded(value, count):
    return jnp.minimum(jnp.maximum(value, 0), count - 1)


def line_peers(count):
    rank = lax.axis_index("fsdp")
    return [
        (within(rank + way, count), {"fsdp": bounded(rank + way, count)}) for way in (1, -1)
    ]


def ring_peers(axis, count, stride=1):
    rank = lax.axis_index(axis)
    return [
        (rank >= 0, {axis: lax.rem(rank + stride * step, count)})
        for step in range(1, count // stride)
    ]


def own_place(count):
    rank = lax.axis_index("ctx")
    core = lax.rem(rank, 2)
    return rank, core, rank // 2, count // 2, rank + 1 - 2 * core


def plane_peers(count):
    rank, core, chip, chips, sibling = own_place(count)
    peers = [(rank >= 0, {"ctx": sibling})]
    if chips == 4:
        across, along, _ = square(chip)
        return peers + [(rank >= 0, {"ctx": 2 * c + core}) for c in (across, along)]
    return peers + ring_peers("ctx", count, 2)


def square(chip):
    side, row = lax.rem(chip, 2), chip // 2
    across = chip + 1 - 2 * side
    along = chip + 2 - 4 * row
    return across, along, across + 2 - 4 * row


def line_gather(copies, own, slot, count, arrived=None):
    rank = lax.axis_index("fsdp")
    sent, latest = [], {}
    for hop in range(1, count + 1):
        for way in (1, -1):
            origin = rank - way * (hop - 1)
            held = slot(bounded(origin, count))
            if hop > 1:
                earlier = latest[way]

                @pl.when(within(origin, count))
                def _():
                    earlier.wait_recv()

                if arrived is not None:
                    arrived(within(origin, count), bounded(origin, count), held)
            if hop < count:
                copy = copies.make(
                    own if hop == 1 else held, held, {"fsdp": bounded(rank + way, count)}
                )
                allowed = within(origin, count) & within(rank + way, count)

                @pl.when(allowed)
                def _():
                    copy.start()

                sent.append((allowed, copy))
                latest[way] = copy
        yield
    for allowed, copy in sent:

        @pl.when(allowed)
        def _():
            copy.wait_send()


def line_reduce(copies, part, passing, landing, count, total):
    rank = lax.axis_index("fsdp")
    sent, arriving = [], {}
    for step in range(count - 1, 0, -1):
        for side, way in enumerate((1, -1)):
            goal = rank + way * step
            allowed = within(goal, count)
            copy = copies.make(
                passing.at[side, step - 1],
                landing.at[side, step - 1],
                {"fsdp": bounded(rank + way, count)},
            )
            arriving[side, step - 1] = copy
            own = part(bounded(goal, count))
            has_earlier = allowed & within(rank - way, count)
            if step < count - 1:
                earlier = arriving[side, step]

                @pl.when(has_earlier)
                def _():
                    earlier.wait_recv()
                    passing[side, step - 1] = (
                        own[...].astype(jnp.float32) + landing[side, step].astype(jnp.float32)
                    ).astype(passing.dtype)

                @pl.when(allowed & jnp.logical_not(within(rank - way, count)))
                def _():
                    passing[side, step - 1] = own[...]
            else:

                @pl.when(allowed)
                def _():
                    passing[side, step - 1] = own[...]

            @pl.when(allowed)
            def _():
                copy.start()

            sent.append((allowed, copy))
        yield
    total[...] = part(rank)[...].astype(jnp.float32)
    for side, way in enumerate((1, -1)):
        last = arriving[side, 0]

        @pl.when(within(rank - way, count))
        def _():
            last.wait_recv()
            total[...] += landing[side, 0].astype(jnp.float32)
    for allowed, copy in sent:

        @pl.when(allowed)
        def _():
            copy.wait_send()


def push_gather(copies, own, slot, axis, count, stride=1):
    rank = lax.axis_index(axis)
    sent = []
    for step in range(1, count // stride):
        copy = copies.make(own, slot(step), {axis: lax.rem(rank + stride * step, count)})
        copy.start()
        sent.append(copy)
    yield
    for copy in sent:
        copy.wait()


def plane_gather(copies, own, slot, count):
    rank, core, chip, chips, sibling = own_place(count)
    sent, forwarded = [], []

    def send(source, target, peer):
        copy = copies.make(source, target, {"ctx": peer})
        copy.start()
        sent.append(copy)
        return copy

    def forward(index, part):
        copy = copies.make(slot(index, part), slot(index, part), {"ctx": sibling})
        copy.start()
        forwarded.append(copy)

    if chips == 4:
        across, along, _ = square(chip)
        side_x, side_y = 2 * across + core, 2 * along + core
        corner = 2 * square(chip)[2] + core
        first_x = send(own(1), slot(rank, 1), side_x)
        second_y = send(own(2), slot(rank, 2), side_y)
        second_x = send(own(2), slot(rank, 2), side_x)
        first_y = send(own(1), slot(rank, 1), side_y)
        copy = copies.make(own(0), slot(rank, 0), {"ctx": sibling})
        copy.start()
        forwarded.append(copy)
        yield
        first_x.wait_recv()
        corner_first = send(slot(side_x, 1), slot(side_x, 1), side_y)
        forward(side_x, 1)
        second_y.wait_recv()
        corner_second = send(slot(side_y, 2), slot(side_y, 2), side_x)
        forward(side_y, 2)
        yield
        second_x.wait_recv()
        forward(side_x, 2)
        first_y.wait_recv()
        forward(side_y, 1)
        yield
        corner_first.wait_recv()
        forward(corner, 1)
        corner_second.wait_recv()
        forward(corner, 2)
        yield
    else:
        pending = []
        for step in range(1, chips):
            peer = lax.rem(rank + 2 * step, count)
            pending.append((lax.rem(rank + count - 2 * step, count), send(own(0), slot(rank, 0), peer)))
        copy = copies.make(own(0), slot(rank, 0), {"ctx": sibling})
        copy.start()
        forwarded.append(copy)
        yield
        for origin, copy in pending:
            copy.wait_recv()
            forward(origin, 0)
        yield
    for copy in sent:
        copy.wait_send()
    for copy in forwarded:
        copy.wait()


def plane_reduce(copies, paired, passing, landing, count, finish):
    rank, core, chip, chips, sibling = own_place(count)
    sent = []

    def send(source, target, peer_chip):
        copy = copies.make(source, target, {"ctx": 2 * peer_chip + core})
        copy.start()
        sent.append(copy)
        return copy

    if chips == 4:
        across, along, corner = square(chip)
        via_x = send(paired(corner, 1), landing.at[0], across)
        via_y = send(paired(corner, 2), landing.at[1], along)
        own_x = send(paired(across, 1), landing.at[2], across)
        own_y = send(paired(along, 2), landing.at[3], along)
        yield
        via_x.wait_recv()
        passing[0] = (
            paired(along, 1)[...].astype(jnp.float32) + landing[0].astype(jnp.float32)
        ).astype(passing.dtype)
        last_first = send(passing.at[0], landing.at[4], along)
        via_y.wait_recv()
        passing[1] = (
            paired(across, 2)[...].astype(jnp.float32) + landing[1].astype(jnp.float32)
        ).astype(passing.dtype)
        last_second = send(passing.at[1], landing.at[5], across)
        yield
        own_x.wait_recv()
        own_y.wait_recv()
        last_first.wait_recv()
        last_second.wait_recv()
        for half in (1, 2):
            total = paired(chip, half)[...].astype(jnp.float32)
            total = total + landing[1 + half].astype(jnp.float32)
            total = total + landing[3 + half].astype(jnp.float32)
            finish(half, total)
    else:
        for step in range(1, chips):
            send(paired(lax.rem(chip + step, chips), 0), landing.at[step - 1], lax.rem(chip + step, chips))
        yield
        total = paired(chip, 0)[...].astype(jnp.float32)
        for step, copy in enumerate(sent):
            copy.wait_recv()
            total = total + landing[step].astype(jnp.float32)
        finish(0, total)
    for copy in sent:
        copy.wait_send()


def remote_call(kernel, name, results, operands, in_spaces, out_spaces, scratch, copies, cost):
    ids = ("weights", "keys", "rows", "row_sums", "key_sums", "totals")
    return pl.pallas_call(
        kernel,
        out_shape=results,
        in_specs=[pl.BlockSpec(memory_space=space) for space in in_spaces],
        out_specs=[pl.BlockSpec(memory_space=space) for space in out_spaces],
        scratch_shapes=list(scratch)
        + [pltpu.SemaphoreType.DMA((copies,)), pltpu.SemaphoreType.DMA((copies,))],
        compiler_params=pltpu.CompilerParams(
            collective_id=ids.index(name), has_side_effects=True, vmem_limit_bytes=VMEM_LIMIT
        ),
        cost_estimate=pl.CostEstimate(flops=0, bytes_accessed=cost, transcendentals=0),
        name=name,
    )(*operands)


def struct(shape, dtype):
    return jax.ShapeDtypeStruct(shape, dtype)


class SharedBlock:
    def __init__(self, copies, source, target, count, ctx_count):
        _, core, _, _, self.sibling = own_place(ctx_count)
        half = source.shape[0] // 2
        rows = pl.ds(pl.multiple_of(core * half, math.gcd(half, 256)), half)
        self.copies, self.forwarded = copies, []
        self.stream = line_gather(
            copies, source.at[rows], lambda i: target.at[i, rows], count, self.arrived
        )

    def arrived(self, allowed, _, held):
        copy = self.copies.make(held, held, {"ctx": self.sibling})

        @pl.when(allowed)
        def _():
            copy.start()

        self.forwarded.append((allowed, copy))

    def wait(self):
        for allowed, copy in self.forwarded:

            @pl.when(allowed)
            def _():
                copy.wait()


def gather_weights(weight, count, ctx_count):
    rows, width = weight.shape

    def kernel(source, target, local, send, recv):
        copies = Copies(send, recv)
        rank = lax.axis_index("fsdp")
        meet(line_peers(count) + plane_peers(ctx_count)[:1])
        keep = pltpu.make_async_copy(source, target.at[rank], local)
        keep.start()
        block = SharedBlock(copies, source, target, count, ctx_count)
        together(block.stream)
        block.wait()
        keep.wait()

    (full,) = remote_call(
        kernel, "weights", [struct((count, rows, width), weight.dtype)], [weight],
        [pl.ANY], [pl.ANY], [pltpu.SemaphoreType.DMA], 4 * count, count * rows * width * 4,
    )
    return full.reshape(count * rows, width)


def gather_keys(block, weights, count, ctx_count):
    rows, width = block.shape
    half = rows // 2

    def kernel(*refs):
        own, *sources = refs[: 1 + len(weights)]
        gathered, *targets = refs[1 + len(weights) : 2 + 2 * len(weights)]
        local, send, recv = refs[2 + 2 * len(weights) :]
        copies = Copies(send, recv)
        rank, place = lax.axis_index("fsdp"), lax.axis_index("ctx")
        spans = (pl.ds(0, rows), pl.ds(0, half), pl.ds(half, half))
        meet(line_peers(count) + plane_peers(ctx_count))
        kept = [pltpu.make_async_copy(own, gathered.at[place], local.at[0])]
        kept += [
            pltpu.make_async_copy(source, target.at[rank], local.at[1 + i])
            for i, (source, target) in enumerate(zip(sources, targets))
        ]
        for copy in kept:
            copy.start()
        blocks = [SharedBlock(copies, s, t, count, ctx_count) for s, t in zip(sources, targets)]
        together(
            plane_gather(
                copies,
                lambda part: own.at[spans[part]],
                lambda i, part: gathered.at[i, spans[part]],
                ctx_count,
            ),
            *[b.stream for b in blocks],
        )
        for b in blocks:
            b.wait()
        for copy in kept:
            copy.wait()

    results = [struct((ctx_count, rows, width), block.dtype)]
    results += [struct((count,) + w.shape, w.dtype) for w in weights]
    gathered, *full = remote_call(
        kernel, "keys", results, [block, *weights],
        [pl.ANY] * (1 + len(weights)), [pl.ANY] * (1 + len(weights)),
        [pltpu.SemaphoreType.DMA((1 + len(weights),))],
        16 + 2 * ctx_count + 4 * count * len(weights),
        ctx_count * rows * width * 4,
    )
    return gathered.reshape(ctx_count * rows, width), [
        f.reshape(count * f.shape[1], f.shape[2]) for f in full
    ]


def gather_rows(block, notes, count):
    def kernel(own, own_notes, gathered, all_notes, local, send, recv):
        copies = Copies(send, recv)
        rank = lax.axis_index("fsdp")
        meet(ring_peers("fsdp", count))
        kept = [
            pltpu.make_async_copy(own, gathered.at[rank], local.at[0]),
            pltpu.make_async_copy(own_notes, all_notes.at[rank], local.at[1]),
        ]
        for copy in kept:
            copy.start()
        together(
            push_gather(copies, own_notes, lambda step: all_notes.at[rank], "fsdp", count),
            line_gather(copies, own, lambda i: gathered.at[i], count),
        )
        for copy in kept:
            copy.wait()

    return remote_call(
        kernel, "rows",
        [struct((count,) + block.shape, block.dtype), struct((count,) + notes.shape, notes.dtype)],
        [block, notes], [pl.ANY] * 2, [pl.ANY] * 2, [pltpu.SemaphoreType.DMA((2,))],
        4 * count, count * block.size * 4,
    )


def reduce_rows(parts, notes, count):
    _, rows, width = parts.shape

    def kernel(given, given_notes, total, notes_total, passing, landing, noted, send, recv):
        copies = Copies(send, recv)
        rank = lax.axis_index("fsdp")
        meet(ring_peers("fsdp", count))
        pushes = []
        for step in range(1, count):
            peer = lax.rem(rank + step, count)
            copy = copies.make(given_notes.at[peer], noted.at[step - 1], {"fsdp": peer})
            copy.start()
            pushes.append(copy)
        together(
            line_reduce(copies, lambda d: given.at[d], passing, landing, count, total)
        )
        sums = given_notes[rank]
        for step, copy in enumerate(pushes):
            copy.wait()
            sums = sums + noted[step]
        notes_total[...] = sums

    return remote_call(
        kernel, "row_sums",
        [struct((rows, width), jnp.float32), struct(notes.shape[1:], notes.dtype)],
        [parts, notes], [pltpu.VMEM] * 2, [pltpu.VMEM] * 2,
        [
            pltpu.VMEM((2, count - 1, rows, width), parts.dtype),
            pltpu.VMEM((2, count - 1, rows, width), parts.dtype),
            pltpu.VMEM((count - 1,) + notes.shape[1:], notes.dtype),
        ],
        4 * count, count * rows * width * 4,
    )


def reduce_keys(parts, row_parts, count, ctx_count):
    _, _, rows, width = parts.shape
    chips = ctx_count // 2
    lands = (6, 1, rows, width) if chips == 4 else (chips - 1, 2, rows, width)

    def kernel(given, given_rows, total, rows_total, met, paired, passing, landing,
               row_passing, row_landing, send, recv):
        copies = Copies(send, recv)
        _, core, _, _, sibling = own_place(ctx_count)
        spans = (pl.ds(0, 2), pl.ds(0, 1), pl.ds(1, 1))
        meet(ring_peers("fsdp", count) + plane_peers(ctx_count))
        exchanged = []
        for q in range(chips):
            for kind in range(2):
                copy = copies.make(
                    given.at[kind, 2 * q + 1 - core], met.at[q, kind], {"ctx": sibling}
                )
                copy.start()
                exchanged.append((q, kind, copy))

        def finish(part, value):
            total[spans[part]] = value

        def planes():
            yield
            for q, kind, copy in exchanged:
                copy.wait_recv()
                paired[q, kind] = (
                    given[kind, 2 * q + core].astype(jnp.float32)
                    + met[q, kind].astype(jnp.float32)
                ).astype(paired.dtype)
            yield from plane_reduce(
                copies, lambda q, part: paired.at[q, spans[part]],
                passing, landing, ctx_count, finish,
            )

        together(
            planes(),
            line_reduce(
                copies, lambda d: given_rows.at[d], row_passing, row_landing, count, rows_total
            ),
        )
        for _, _, copy in exchanged:
            copy.wait_send()

    _, row_count, row_width = row_parts.shape
    return remote_call(
        kernel, "key_sums",
        [struct((2, rows, width), jnp.float32), struct((row_count, row_width), jnp.float32)],
        [parts, row_parts], [pltpu.VMEM] * 2, [pltpu.VMEM] * 2,
        [
            pltpu.VMEM((chips, 2, rows, width), parts.dtype),
            pltpu.VMEM((chips, 2, rows, width), parts.dtype),
            pltpu.VMEM((2, 1, rows, width), parts.dtype),
            pltpu.VMEM(lands, parts.dtype),
            pltpu.VMEM((2, count - 1, row_count, row_width), parts.dtype),
            pltpu.VMEM((2, count - 1, row_count, row_width), parts.dtype),
        ],
        3 * chips + 8 + 2 * count, ctx_count * rows * width * 8,
    )


def reduce_weights(parts, small, count, ctx_count):
    _, rows, width = parts.shape
    chips = ctx_count // 2
    half, share = rows // 2, width // chips
    row_unit = math.gcd(half, 256)
    first = max(count // 2, 1)
    lands = (6, first, half, share) if chips == 4 else (chips - 1, count, half, share)

    def kernel(given, given_small, total, small_total, met, paired, passing, landing, merged,
               line_passing, line_landing, line_total, own_total, small_met, small_sum,
               small_plane, small_plane_sum, small_line, send, recv):
        copies = Copies(send, recv)
        rank = lax.axis_index("fsdp")
        place, core, chip, _, sibling = own_place(ctx_count)
        spans = (pl.ds(0, count), pl.ds(0, first), pl.ds(first, count - first))
        mine = pl.ds(pl.multiple_of(core * half, row_unit), half)
        theirs = pl.ds(pl.multiple_of((1 - core) * half, row_unit), half)

        def columns(q):
            return pl.ds(pl.multiple_of(q * share, 128), share)

        meet(
            ring_peers("fsdp", count)
            + ring_peers("ctx", ctx_count, 2)
            + plane_peers(ctx_count)[:1]
        )
        small_pair = copies.make(given_small, small_met, {"ctx": sibling})
        small_pair.start()
        exchanged = []
        for d in range(count):
            copy = copies.make(given.at[d, theirs], met.at[d], {"ctx": sibling})
            copy.start()
            exchanged.append(copy)

        def small_stream():
            small_pair.wait()
            small_sum[...] = given_small[...] + small_met[...]
            pushes = []
            for step in range(1, chips):
                copy = copies.make(
                    small_sum, small_plane.at[step - 1],
                    {"ctx": lax.rem(place + 2 * step, ctx_count)},
                )
                copy.start()
                pushes.append(copy)
            yield
            for copy in pushes:
                copy.wait()
            small_plane_sum[...] = small_sum[...] + jnp.sum(small_plane[...], axis=0)
            pushes = []
            for step in range(1, count):
                copy = copies.make(
                    small_plane_sum, small_line.at[step - 1],
                    {"fsdp": lax.rem(rank + step, count)},
                )
                copy.start()
                pushes.append(copy)
            yield
            yield
            for copy in pushes:
                copy.wait()
            small_total[...] = small_plane_sum[...] + jnp.sum(small_line[...], axis=0)

        def finish(part, value):
            merged[spans[part]] = value.astype(merged.dtype)

        def large_stream():
            for d, copy in enumerate(exchanged):
                copy.wait_recv()
                for q in range(chips):
                    paired[q, d] = (
                        given[d, mine, q * share : (q + 1) * share].astype(jnp.float32)
                        + met[d, :, q * share : (q + 1) * share].astype(jnp.float32)
                    ).astype(paired.dtype)
            yield from plane_reduce(
                copies, lambda q, part: paired.at[q, spans[part]],
                passing, landing, ctx_count, finish,
            )
            yield from line_reduce(
                copies, lambda d: merged.at[d], line_passing, line_landing, count, line_total
            )
            own_total[...] = line_total[...].astype(own_total.dtype)
            sent = []
            forwarded = []
            copy = copies.make(own_total, total.at[mine, columns(chip)], {"ctx": sibling})
            copy.start()
            forwarded.append(copy)
            for step in range(1, chips):
                copy = copies.make(
                    own_total, total.at[mine, columns(chip)],
                    {"ctx": lax.rem(place + 2 * step, ctx_count)},
                )
                copy.start()
                sent.append(copy)
            total[mine, columns(chip)] = own_total[...]
            for step, copy in enumerate(sent, 1):
                copy.wait_recv()
                held = total.at[mine, columns(lax.rem(chip + chips - step, chips))]
                copy = copies.make(held, held, {"ctx": sibling})
                copy.start()
                forwarded.append(copy)
            for copy in sent:
                copy.wait_send()
            for copy in forwarded:
                copy.wait()

        together(small_stream(), large_stream())
        for copy in exchanged:
            copy.wait_send()

    kind = parts.dtype
    f32 = jnp.float32
    return remote_call(
        kernel, "totals",
        [struct((rows, width), kind), struct(small.shape, f32)],
        [parts, small], [pltpu.VMEM] * 2, [pltpu.VMEM] * 2,
        [
            pltpu.VMEM((count, half, width), kind),
            pltpu.VMEM((chips, count, half, share), kind),
            pltpu.VMEM((2, first, half, share), kind),
            pltpu.VMEM(lands, kind),
            pltpu.VMEM((count, half, share), kind),
            pltpu.VMEM((2, count - 1, half, share), kind),
            pltpu.VMEM((2, count - 1, half, share), kind),
            pltpu.VMEM((half, share), f32),
            pltpu.VMEM((half, share), kind),
            pltpu.VMEM(small.shape, f32),
            pltpu.VMEM(small.shape, f32),
            pltpu.VMEM((chips - 1,) + small.shape, f32),
            pltpu.VMEM(small.shape, f32),
            pltpu.VMEM((count - 1,) + small.shape, f32),
        ],
        count + 8 + 3 * count + 4 * chips, parts.size * 8,
    )


def local_call(kernel, name, grid, results, operands, in_specs, out_specs, scratch, flops, cost):
    return pl.pallas_call(
        kernel,
        grid=grid,
        out_shape=results,
        in_specs=in_specs,
        out_specs=out_specs,
        scratch_shapes=scratch,
        compiler_params=pltpu.CompilerParams(vmem_limit_bytes=VMEM_LIMIT),
        cost_estimate=pl.CostEstimate(flops=flops, bytes_accessed=cost, transcendentals=0),
        name=name,
    )(*operands)


def whole_block(shape):
    return pl.BlockSpec(shape, lambda *_: (0,) * len(shape))


def product(left, right, left_dim=1, right_dim=0):
    return lax.dot_general(
        left, right, (((left_dim,), (right_dim,)), ((), ())), preferred_element_type=jnp.float32
    )


def expert_layers(routed_rows, block_rows, notes, weights):
    peers, piece_len, width = routed_rows.shape
    experts, _, units, _ = weights.shape
    capacity = piece_len // 4
    count = peers * capacity

    def kernel(routed, block, note, w, grads, out_parts, grad_parts, dots, out_sum, grad_sum):
        expert = pl.program_id(0)
        low = jnp.bfloat16

        @pl.when(expert == 0)
        def _():
            out_sum[...] = jnp.zeros_like(out_sum)
            grad_sum[...] = jnp.zeros_like(grad_sum)
            dots[...] = jnp.zeros_like(dots)

        slots = (
            lax.broadcasted_iota(jnp.int32, (capacity, piece_len), 0) + expert * capacity
        ).astype(jnp.float32)
        hots, firsts, seconds, gates, taken, blocks = [], [], [], [], [], []
        for g in range(peers):
            first = note[g, 0:1, :] == slots
            second = note[g, 1:2, :] == slots
            gates.append(
                jnp.sum(
                    jnp.where(first, note[g, 2:3, :], 0.0)
                    + jnp.where(second, note[g, 3:4, :], 0.0),
                    axis=1,
                    keepdims=True,
                )
            )
            first, second = jnp.where(first, 1.0, 0.0), jnp.where(second, 1.0, 0.0)
            hot = (first + second).astype(low)
            taken.append(product(hot, routed[g]).astype(low))
            blocks.append(product(hot, block[g]))
            hots.append(hot)
            firsts.append(first)
            seconds.append(second)
        rows = jnp.concatenate(taken, axis=0)
        block_part = jnp.concatenate(blocks, axis=0)
        gate = jnp.concatenate(gates, axis=0)
        grad_out = (gate * block_part).astype(low)
        w_gate, w_up, w_down = w[0, 0], w[0, 1], w[0, 2]
        gate_proj = product(rows, w_gate, 1, 1)
        up_proj = product(rows, w_up, 1, 1)
        grad_hidden = product(grad_out, w_down, 1, 1)
        sigmoid = 1.0 / (1.0 + jnp.exp(-gate_proj))
        silu = gate_proj * sigmoid
        hidden = (silu * up_proj).astype(low)
        grad_gate_proj = (
            grad_hidden * up_proj * sigmoid * (1.0 + gate_proj * (1.0 - sigmoid))
        ).astype(low)
        grad_up_proj = (grad_hidden * silu).astype(low)
        grads[0, 0] = product(grad_gate_proj, rows, 0, 0).astype(low)
        grads[0, 1] = product(grad_up_proj, rows, 0, 0).astype(low)
        grads[0, 2] = product(hidden, grad_out, 0, 0).astype(low)
        expert_out = product(hidden, w_down)
        grad_in = (product(grad_gate_proj, w_gate) + product(grad_up_proj, w_up)).astype(low)
        row_dots = jnp.sum(block_part * expert_out, axis=1, keepdims=True)
        gated = (gate * expert_out).astype(low)
        for g in range(peers):
            span = slice(g * capacity, (g + 1) * capacity)
            out_sum[g] += product(hots[g], gated[span], 0, 0)
            grad_sum[g] += product(hots[g], grad_in[span], 0, 0)
            dots[g, 0:1, :] += jnp.sum(firsts[g] * row_dots[span], axis=0, keepdims=True)
            dots[g, 1:2, :] += jnp.sum(seconds[g] * row_dots[span], axis=0, keepdims=True)

        @pl.when(expert == experts - 1)
        def _():
            out_parts[...] = out_sum[...].astype(low)
            grad_parts[...] = grad_sum[...].astype(low)

    rows_shape = (peers, piece_len, width)
    low = jnp.bfloat16
    expert_block = pl.BlockSpec((1, 3, units, width), lambda e: (e, 0, 0, 0))
    return local_call(
        kernel, "experts", (experts,),
        [struct(weights.shape, low), struct(rows_shape, low), struct(rows_shape, low),
         struct(notes.shape, jnp.float32)],
        [routed_rows, block_rows, notes, weights],
        [whole_block(rows_shape), whole_block(rows_shape), whole_block(notes.shape), expert_block],
        [expert_block, whole_block(rows_shape), whole_block(rows_shape), whole_block(notes.shape)],
        [pltpu.VMEM(rows_shape, jnp.float32), pltpu.VMEM(rows_shape, jnp.float32)],
        18 * experts * count * units * width, 4 * weights.size,
    )


def score_bias(length, first_row, rows, keys):
    key_place = lax.broadcasted_iota(jnp.int32, (keys, rows), 0)
    query_place = first_row + lax.broadcasted_iota(jnp.int32, (keys, rows), 1)
    return jnp.where(key_place <= jnp.minimum(query_place, length - 1), 0.0, MASKED)


def head_masks(shape):
    lane = lax.broadcasted_iota(jnp.int32, shape, 1)
    return [lane < HEAD_DIM, lane >= HEAD_DIM]


def attention_forward(places, queries, pairs):
    rows, width = queries.shape
    keys = pairs.shape[0]
    tile = 2 * HEAD_DIM
    tiles = width // tile

    def kernel(place, query, key, value, mixed, sums, bias):
        step = pl.program_id(0)

        @pl.when(step == 0)
        def _():
            bias[...] = score_bias(place[0], place[1], rows, keys)

        own_masks = head_masks((rows, tile))
        scaled = query[...] * HEAD_DIM**-0.5
        outs = []
        for head in range(2):
            chosen = jnp.where(own_masks[head], scaled, 0)
            scores = product(key[...], chosen, 1, 1) + bias[...]
            top = jnp.max(scores, axis=0, keepdims=True)
            weights = jnp.exp(scores - top)
            total = jnp.sum(weights, axis=0, keepdims=True)
            probabilities = (weights * (1.0 / total)).astype(jnp.bfloat16)
            outs.append(product(probabilities, value[...], 0, 0))
            sums[0, head : head + 1, :] = top + jnp.log(total)
        mixed[...] = jnp.where(own_masks[0], outs[0], outs[1]).astype(mixed.dtype)

    return pl.pallas_call(
        kernel,
        grid_spec=pltpu.PrefetchScalarGridSpec(
            num_scalar_prefetch=1,
            grid=(tiles,),
            in_specs=[
                pl.BlockSpec((rows, tile), lambda i, _: (0, i)),
                pl.BlockSpec((keys, tile), lambda i, _: (0, i)),
                pl.BlockSpec((keys, tile), lambda i, _: (0, i + tiles)),
            ],
            out_specs=[
                pl.BlockSpec((rows, tile), lambda i, _: (0, i)),
                pl.BlockSpec((1, 8, rows), lambda i, _: (i, 0, 0)),
            ],
            scratch_shapes=[pltpu.VMEM((keys, rows), jnp.float32)],
        ),
        out_shape=[struct((rows, width), jnp.bfloat16), struct((tiles, 8, rows), jnp.float32)],
        compiler_params=pltpu.CompilerParams(vmem_limit_bytes=VMEM_LIMIT),
        cost_estimate=pl.CostEstimate(
            flops=4 * rows * keys * width, bytes_accessed=pairs.size * 2, transcendentals=0
        ),
        name="attention",
    )(places, queries, pairs, pairs)


def attention_backward(places, queries, pairs, sums, mixed, grad_mixed):
    rows, width = queries.shape
    keys = pairs.shape[0]
    tile = 2 * HEAD_DIM
    tiles = width // tile
    scaling = HEAD_DIM**-0.5

    def kernel(place, query, key, value, total, out, grad_out, grad_query, grad_pair, bias):
        step = pl.program_id(0)

        @pl.when(step == 0)
        def _():
            bias[...] = score_bias(place[0], place[1], rows, keys)

        own_masks = head_masks((rows, tile))
        scaled = query[...] * scaling
        inner = out[...].astype(jnp.float32) * grad_out[...].astype(jnp.float32)
        grads, key_sum, value_sum = [], None, None
        for head in range(2):
            chosen = jnp.where(own_masks[head], scaled, 0)
            upstream = jnp.where(own_masks[head], grad_out[...], 0)
            ones = jnp.where(own_masks[head][:8], 1.0, 0.0)
            inner_row = lax.dot_general(
                ones, inner, (((1,), (1,)), ((), ())),
                precision=HIGHEST, preferred_element_type=jnp.float32,
            )[0:1]
            scores = product(key[...], chosen, 1, 1) + bias[...]
            probabilities = jnp.exp(scores - total[0, head : head + 1, :])
            grad_probs = product(value[...], upstream, 1, 1)
            grad_scores = (probabilities * (grad_probs - inner_row)).astype(jnp.bfloat16)
            key_part = product(grad_scores, chosen)
            value_part = product(probabilities.astype(jnp.bfloat16), upstream)
            key_sum = key_part if key_sum is None else key_sum + key_part
            value_sum = value_part if value_sum is None else value_sum + value_part
            grads.append(product(grad_scores, key[...], 0, 0) * scaling)
        grad_query[...] = jnp.where(own_masks[0], grads[0], grads[1])
        grad_pair[0] = key_sum.astype(grad_pair.dtype)
        grad_pair[1] = value_sum.astype(grad_pair.dtype)

    own_block = pl.BlockSpec((rows, tile), lambda i, _: (0, i))
    key_block = pl.BlockSpec((keys, tile), lambda i, _: (0, i))
    low = jnp.bfloat16
    return pl.pallas_call(
        kernel,
        grid_spec=pltpu.PrefetchScalarGridSpec(
            num_scalar_prefetch=1,
            grid=(tiles,),
            in_specs=[
                own_block,
                key_block,
                pl.BlockSpec((keys, tile), lambda i, _: (0, i + tiles)),
                pl.BlockSpec((1, 8, rows), lambda i, _: (i, 0, 0)),
                own_block,
                own_block,
            ],
            out_specs=[own_block, pl.BlockSpec((2, keys, tile), lambda i, _: (0, 0, i))],
            scratch_shapes=[pltpu.VMEM((keys, rows), jnp.float32)],
        ),
        out_shape=[
            struct((rows, width), jnp.float32),
            struct((2, keys, width), low),
        ],
        compiler_params=pltpu.CompilerParams(vmem_limit_bytes=VMEM_LIMIT),
        cost_estimate=pl.CostEstimate(
            flops=10 * rows * keys * width, bytes_accessed=pairs.size * 4, transcendentals=0
        ),
        name="attention_back",
    )(places, queries, pairs, pairs, sums, mixed, grad_mixed)


def normalize_rows(values, gain_row):
    scaling = lax.rsqrt(jnp.mean(values * values, axis=-1, keepdims=True) + EPSILON)
    return (values * scaling * gain_row, scaling)


def normalize_back(values, scaling, gain_row, grad_out):
    grad_hat = grad_out * gain_row
    grad_gain = jnp.sum(grad_out * values * scaling, axis=(0, 1))
    grad_values = scaling * grad_hat - values * scaling**3 * jnp.mean(
        grad_hat * values, axis=-1, keepdims=True
    )
    return (grad_values, grad_gain)


def rope_tables(positions, head_size):
    half_dim = head_size // 2
    frequency = jnp.exp(
        jnp.arange(half_dim, dtype=jnp.float32) * (-2.0 * math.log(10000.0) / head_size)
    )
    angles = positions.astype(jnp.float32)[:, None] * frequency[None, :]
    return (jnp.cos(angles)[:, None, :], jnp.sin(angles)[:, None, :])


def rotate(values, cosine_table, sine_table):
    half_dim = values.shape[-1] // 2
    first_half = values[..., :half_dim]
    second_half = values[..., half_dim:]
    return jnp.concatenate(
        [
            first_half * cosine_table - second_half * sine_table,
            second_half * cosine_table + first_half * sine_table,
        ],
        axis=-1,
    )


def per_device(
    tokens,
    prev_logits,
    routes,
    lengths,
    cotangent,
    w_qkv,
    w_out,
    gain_attn,
    gain_moe,
    w_router,
    w_residual,
    const_vec,
    w_expert,
):
    groups, piece_len, model_width = tokens.shape
    head_count = model_width // HEAD_DIM
    part_heads = 2
    part_count = head_count // part_heads
    slot_len = piece_len * lax.axis_size("ctx")
    positions = lax.axis_index("ctx") * piece_len + jnp.arange(piece_len, dtype=jnp.int32)
    key_positions = jnp.arange(slot_len, dtype=jnp.int32)
    live_rows = (positions[None, :] < lengths[:, None]).astype(jnp.float32)[..., None]
    experts = w_expert.shape[0]
    capacity = piece_len // 4
    slot_count = experts * capacity
    split_shape = (groups, piece_len, head_count, HEAD_DIM)
    fsdp_count, ctx_count = lax.axis_size("fsdp"), lax.axis_size("ctx")
    full_kv = gather_weights(w_qkv[:, model_width:], fsdp_count, ctx_count)
    inputs = tokens.astype(jnp.float32)
    gain_one = gain_attn.astype(jnp.float32)
    gain_two = gain_moe.astype(jnp.float32)
    normed_one, scale_one = normalize_rows(inputs, gain_one)
    normed_one_low = normed_one.astype(jnp.bfloat16)
    projected = jnp.einsum("gpd,de->gpe", normed_one_low, full_kv, preferred_element_type=jnp.float32)
    cosine_table, sine_table = rope_tables(positions, HEAD_DIM)
    key_local = (
        rotate(projected[..., :model_width].reshape(split_shape), cosine_table, sine_table)
        .astype(jnp.bfloat16)
        .reshape(piece_len, model_width)
    )
    value_local = projected[0, :, model_width:].astype(jnp.bfloat16)
    all_pairs, (full_query, full_out) = gather_keys(
        jnp.concatenate([key_local, value_local], axis=-1),
        [w_qkv[:, :model_width], w_out],
        fsdp_count,
        ctx_count,
    )
    cotangent_low = live_rows.astype(jnp.bfloat16) * cotangent
    cotangent_own, all_pairs = lax.optimization_barrier((cotangent_low, all_pairs))
    cotangent_rows = lax.all_gather(cotangent_own, "fsdp", axis=0, tiled=True)
    queries = rotate(
        jnp.einsum(
            "gpd,de->gpe", normed_one_low, full_query, preferred_element_type=jnp.float32
        ).reshape(split_shape),
        cosine_table,
        sine_table,
    ).astype(jnp.bfloat16)
    places = jnp.stack([lengths[0], lax.axis_index("ctx") * piece_len]).astype(jnp.int32)
    query_rows = queries.reshape(piece_len, model_width)
    mixed_rows, score_sums = attention_forward(places, query_rows, all_pairs)
    mixed_low = mixed_rows[None]
    attention = jnp.einsum("gpd,de->gpe", mixed_low, full_out, preferred_element_type=jnp.float32)
    residual_sum = inputs + attention
    normed_two, scale_two = normalize_rows(residual_sum, gain_two)
    routed_low = normed_two.astype(jnp.bfloat16)
    routed = routed_low.astype(jnp.float32)
    logits = jnp.einsum("gpd,de->gpe", routed, w_router, precision=HIGHEST) + jnp.einsum(
        "gpi,ie->gpe", prev_logits, w_residual, precision=HIGHEST
    )
    id_range = jnp.arange(experts + 4, dtype=jnp.int32)
    route_hot = (routes[..., None] == id_range).astype(jnp.float32)
    chosen = jnp.sum(route_hot * logits[:, :, None, :], axis=-1)
    chosen_exp = jnp.exp(chosen - jnp.max(chosen, axis=-1, keepdims=True))
    gate_weights = chosen_exp / jnp.sum(chosen_exp, axis=-1, keepdims=True)
    assign_hot = route_hot[..., :experts].reshape(groups, 2 * piece_len, experts)
    earlier = jnp.cumsum(assign_hot, axis=1) - assign_hot
    order_in = jnp.sum(earlier * assign_hot, axis=-1)
    expert_of = jnp.sum(assign_hot * jnp.arange(experts, dtype=jnp.float32), axis=-1)
    is_ffn = jnp.sum(assign_hot, axis=-1)
    slot_of = jnp.where(is_ffn > 0.5, expert_of * capacity + order_in, -1.0).reshape(
        groups, piece_len, 2
    )
    notes = jnp.concatenate([slot_of[0].T, gate_weights[0].T, jnp.zeros((4, piece_len))], axis=0)
    routed_rows, all_notes = gather_rows(routed_low[0], notes, fsdp_count)
    grad_weights, out_parts, grad_parts, dot_notes = expert_layers(
        routed_rows, cotangent_rows, all_notes, w_expert.swapaxes(1, 2)
    )
    expert_sum = lax.psum(grad_weights, "ctx").astype(jnp.float32).swapaxes(1, 2)
    ffn_grad, dot_sums = reduce_rows(grad_parts, dot_notes, fsdp_count)
    ffn_grad = ffn_grad[None]
    copy_hot = route_hot[..., experts + 1]
    const_hot = route_hot[..., experts + 2 :]
    constants = const_vec.astype(jnp.float32)
    gate_const = jnp.sum(gate_weights[..., None] * const_hot, axis=2)
    copy_gate = jnp.sum(gate_weights * copy_hot, axis=2, keepdims=True)
    special_sum = copy_gate * routed + jnp.einsum(
        "gpj,jd->gpd", gate_const, constants, precision=HIGHEST
    )
    grad_block = live_rows * cotangent.astype(jnp.float32)
    copy_dot = jnp.sum(grad_block * routed, axis=-1)[..., None]
    const_dot = jnp.einsum("gpd,jd->gpj", grad_block, constants, precision=HIGHEST)
    grad_gate = (
        dot_sums[:2].T[None]
        + copy_hot * copy_dot
        + jnp.sum(const_hot * const_dot[:, :, None, :], axis=-1)
    )
    grad_chosen = gate_weights * (
        grad_gate - jnp.sum(gate_weights * grad_gate, axis=-1, keepdims=True)
    )
    grad_logits = jnp.sum(grad_chosen[..., None] * route_hot, axis=2)
    grad_router = jnp.einsum("gpd,gpe->de", routed, grad_logits, precision=HIGHEST)
    grad_mixing = jnp.einsum("gpi,gpe->ie", prev_logits, grad_logits, precision=HIGHEST)
    grad_previous = jnp.einsum("gpe,ie->gpi", grad_logits, w_residual, precision=HIGHEST)
    grad_const = jnp.einsum("gpd,gpj->jd", grad_block, gate_const, precision=HIGHEST)
    grad_routed = (
        jnp.einsum("gpe,de->gpd", grad_logits, w_router, precision=HIGHEST)
        + copy_gate * grad_block
        + ffn_grad
    )
    grad_norm_two, grad_gain_two = normalize_back(residual_sum, scale_two, gain_two, grad_routed)
    grad_residual = grad_block + grad_norm_two
    grad_attention = grad_residual.astype(jnp.bfloat16)
    grad_wout = jnp.einsum(
        "gpd,gpe->de", mixed_low, grad_attention, preferred_element_type=jnp.float32
    )
    grad_mixed = jnp.einsum(
        "gpe,de->gpd", grad_attention, full_out, preferred_element_type=jnp.float32
    ).astype(jnp.bfloat16)
    query_grad, pair_grads = attention_backward(
        places, query_rows, all_pairs, score_sums, mixed_rows, grad_mixed[0]
    )
    pair_grads = pair_grads.reshape(2, ctx_count, piece_len, model_width)
    pair_grad, ffn_sum = reduce_keys(pair_grads, out_parts, fsdp_count, ctx_count)
    output = (live_rows * (residual_sum + special_sum + ffn_sum[None])).astype(jnp.bfloat16)
    key_grad, value_grad = pair_grad[:1], pair_grad[1:]
    query_back = rotate(query_grad.reshape(split_shape), cosine_table, -sine_table).reshape(
        groups, piece_len, model_width
    )
    key_back = rotate(key_grad.reshape(split_shape), cosine_table, -sine_table).reshape(
        groups, piece_len, model_width
    )
    grad_projected = jnp.concatenate([query_back, key_back, value_grad], axis=-1).astype(
        jnp.bfloat16
    )
    grad_wqkv = jnp.einsum(
        "gpd,gpe->de", normed_one_low, grad_projected, preferred_element_type=jnp.float32
    )
    grad_normed_one = jnp.einsum(
        "gpe,de->gpd",
        grad_projected[..., :model_width],
        full_query,
        preferred_element_type=jnp.float32,
    ) + jnp.einsum(
        "gpe,de->gpd",
        grad_projected[..., model_width:],
        full_kv,
        preferred_element_type=jnp.float32,
    )
    grad_norm_one, grad_gain_one = normalize_back(inputs, scale_one, gain_one, grad_normed_one)
    grad_inputs = grad_residual + grad_norm_one
    weight_parts = (
        jnp.concatenate([grad_wqkv, grad_wout], axis=-1)
        .astype(jnp.bfloat16)
        .reshape(fsdp_count, -1, 4 * model_width)
    )
    few = experts + 4
    mixing_row = jnp.pad(grad_mixing.reshape(1, -1), ((0, 0), (0, model_width - few * few)))
    small = jnp.concatenate(
        [grad_router.T, grad_const, grad_gain_one[None], grad_gain_two[None], mixing_row], axis=0
    )
    small = jnp.pad(small, ((0, -small.shape[0] % 8), (0, 0)))
    weight_sum, small_sum = reduce_weights(weight_parts, small, fsdp_count, ctx_count)
    weight_sum = weight_sum.astype(jnp.float32)
    wqkv_sum, wout_sum = weight_sum[:, : 3 * model_width], weight_sum[:, 3 * model_width :]
    router_sum, const_sum = small_sum[:few].T, small_sum[few : few + 2]
    gain_one_sum, gain_two_sum = small_sum[few + 2], small_sum[few + 3]
    mixing_sum = small_sum[few + 4, : few * few].reshape(few, few)
    return (
        output,
        grad_inputs,
        grad_previous,
        wqkv_sum,
        wout_sum,
        gain_one_sum,
        gain_two_sum,
        router_sum,
        mixing_sum,
        const_sum,
        expert_sum,
    )


def solution(mesh):
    return jax.shard_map(
        per_device,
        mesh=mesh,
        in_specs=(
            P("fsdp", "ctx", None),
            P("fsdp", "ctx", None),
            P("fsdp", "ctx", None),
            P("fsdp"),
            P("fsdp", "ctx", None),
            P("fsdp", None),
            P("fsdp", None),
            P(),
            P(),
            P(),
            P(),
            P(),
            P(None, "fsdp", None, None),
        ),
        out_specs=(
            P("fsdp", "ctx", None),
            P("fsdp", "ctx", None),
            P("fsdp", "ctx", None),
            P("fsdp", None),
            P("fsdp", None),
            P(),
            P(),
            P(),
            P(),
            P(),
            P(None, "fsdp", None, None),
        ),
        check_vma=False,
    )
```

```python
import itertools
import math

import jax
import jax.numpy as jnp
from jax import lax
from jax.experimental import pallas as pl
from jax.experimental.pallas import tpu as pltpu

from jax.sharding import PartitionSpec as P

HEAD_DIM = 64


EPSILON = 1e-05
MASKED = -1e30
HIGHEST = lax.Precision.HIGHEST


LOGICAL = pl.DeviceIdType.MESH
VMEM_LIMIT = 56 * 1024 * 1024


class Copies:
    def __init__(self, send, recv):
        self.send, self.recv, self.used = send, recv, 0

    def make(self, source, target, peer):
        index = self.used
        self.used += 1
        return pltpu.make_async_remote_copy(
            source, target, self.send.at[index], self.recv.at[index],
            device_id=peer, device_id_type=LOGICAL,
        )


def meet(peers):
    barrier = pltpu.get_barrier_semaphore()
    for allowed, peer in peers:
        @pl.when(allowed)
        def _():
            pl.semaphore_signal(barrier, 1, device_id=peer, device_id_type=LOGICAL)
    awaited = sum(jnp.where(allowed, 1, 0) for allowed, _ in peers)
    pl.semaphore_wait(barrier, awaited)


def together(*streams):
    for _ in itertools.zip_longest(*streams):
        pass


def within(value, count):
    return (value >= 0) & (value < count)


def bounded(value, count):
    return jnp.minimum(jnp.maximum(value, 0), count - 1)


def line_peers(count):
    rank = lax.axis_index("fsdp")
    return [
        (within(rank + way, count), {"fsdp": bounded(rank + way, count)}) for way in (1, -1)
    ]


def ring_peers(axis, count, stride=1):
    rank = lax.axis_index(axis)
    return [
        (rank >= 0, {axis: lax.rem(rank + stride * step, count)})
        for step in range(1, count // stride)
    ]


def own_place(count):
    rank = lax.axis_index("ctx")
    core = lax.rem(rank, 2)
    return rank, core, rank // 2, count // 2, rank + 1 - 2 * core


def plane_peers(count):
    rank, core, chip, chips, sibling = own_place(count)
    peers = [(rank >= 0, {"ctx": sibling})]
    if chips == 4:
        across, along, _ = square(chip)
        return peers + [(rank >= 0, {"ctx": 2 * c + core}) for c in (across, along)]
    return peers + ring_peers("ctx", count, 2)


def square(chip):
    side, row = lax.rem(chip, 2), chip // 2
    across = chip + 1 - 2 * side
    along = chip + 2 - 4 * row
    return across, along, across + 2 - 4 * row


def line_gather(copies, own, slot, count, arrived=None):
    rank = lax.axis_index("fsdp")
    sent, latest = [], {}
    for hop in range(1, count + 1):
        for way in (1, -1):
            origin = rank - way * (hop - 1)
            held = slot(bounded(origin, count))
            if hop > 1:
                earlier = latest[way]

                @pl.when(within(origin, count))
                def _():
                    earlier.wait_recv()

                if arrived is not None:
                    arrived(within(origin, count), bounded(origin, count), held)
            if hop < count:
                copy = copies.make(
                    own if hop == 1 else held, held, {"fsdp": bounded(rank + way, count)}
                )
                allowed = within(origin, count) & within(rank + way, count)

                @pl.when(allowed)
                def _():
                    copy.start()

                sent.append((allowed, copy))
                latest[way] = copy
        yield
    for allowed, copy in sent:

        @pl.when(allowed)
        def _():
            copy.wait_send()


def line_reduce(copies, part, passing, landing, count, total):
    rank = lax.axis_index("fsdp")
    sent, arriving = [], {}
    for step in range(count - 1, 0, -1):
        for side, way in enumerate((1, -1)):
            goal = rank + way * step
            allowed = within(goal, count)
            copy = copies.make(
                passing.at[side, step - 1],
                landing.at[side, step - 1],
                {"fsdp": bounded(rank + way, count)},
            )
            arriving[side, step - 1] = copy
            own = part(bounded(goal, count))
            has_earlier = allowed & within(rank - way, count)
            if step < count - 1:
                earlier = arriving[side, step]

                @pl.when(has_earlier)
                def _():
                    earlier.wait_recv()
                    passing[side, step - 1] = (
                        own[...].astype(jnp.float32) + landing[side, step].astype(jnp.float32)
                    ).astype(passing.dtype)

                @pl.when(allowed & jnp.logical_not(within(rank - way, count)))
                def _():
                    passing[side, step - 1] = own[...]
            else:

                @pl.when(allowed)
                def _():
                    passing[side, step - 1] = own[...]

            @pl.when(allowed)
            def _():
                copy.start()

            sent.append((allowed, copy))
        yield
    total[...] = part(rank)[...].astype(jnp.float32)
    for side, way in enumerate((1, -1)):
        last = arriving[side, 0]

        @pl.when(within(rank - way, count))
        def _():
            last.wait_recv()
            total[...] += landing[side, 0].astype(jnp.float32)
    for allowed, copy in sent:

        @pl.when(allowed)
        def _():
            copy.wait_send()


def push_gather(copies, own, slot, axis, count, stride=1):
    rank = lax.axis_index(axis)
    sent = []
    for step in range(1, count // stride):
        copy = copies.make(own, slot(step), {axis: lax.rem(rank + stride * step, count)})
        copy.start()
        sent.append(copy)
    yield
    for copy in sent:
        copy.wait()


def plane_gather(copies, own, slot, count):
    rank, core, chip, chips, sibling = own_place(count)
    sent, forwarded = [], []

    def send(source, target, peer):
        copy = copies.make(source, target, {"ctx": peer})
        copy.start()
        sent.append(copy)
        return copy

    def forward(index, part):
        copy = copies.make(slot(index, part), slot(index, part), {"ctx": sibling})
        copy.start()
        forwarded.append(copy)

    if chips == 4:
        across, along, _ = square(chip)
        side_x, side_y = 2 * across + core, 2 * along + core
        corner = 2 * square(chip)[2] + core
        first_x = send(own(1), slot(rank, 1), side_x)
        second_y = send(own(2), slot(rank, 2), side_y)
        second_x = send(own(2), slot(rank, 2), side_x)
        first_y = send(own(1), slot(rank, 1), side_y)
        copy = copies.make(own(0), slot(rank, 0), {"ctx": sibling})
        copy.start()
        forwarded.append(copy)
        yield
        first_x.wait_recv()
        corner_first = send(slot(side_x, 1), slot(side_x, 1), side_y)
        forward(side_x, 1)
        second_y.wait_recv()
        corner_second = send(slot(side_y, 2), slot(side_y, 2), side_x)
        forward(side_y, 2)
        yield
        second_x.wait_recv()
        forward(side_x, 2)
        first_y.wait_recv()
        forward(side_y, 1)
        yield
        corner_first.wait_recv()
        forward(corner, 1)
        corner_second.wait_recv()
        forward(corner, 2)
        yield
    else:
        pending = []
        for step in range(1, chips):
            peer = lax.rem(rank + 2 * step, count)
            pending.append((lax.rem(rank + count - 2 * step, count), send(own(0), slot(rank, 0), peer)))
        copy = copies.make(own(0), slot(rank, 0), {"ctx": sibling})
        copy.start()
        forwarded.append(copy)
        yield
        for origin, copy in pending:
            copy.wait_recv()
            forward(origin, 0)
        yield
    for copy in sent:
        copy.wait_send()
    for copy in forwarded:
        copy.wait()


def plane_reduce(copies, paired, passing, landing, count, finish):
    rank, core, chip, chips, sibling = own_place(count)
    sent = []

    def send(source, target, peer_chip):
        copy = copies.make(source, target, {"ctx": 2 * peer_chip + core})
        copy.start()
        sent.append(copy)
        return copy

    if chips == 4:
        across, along, corner = square(chip)
        via_x = send(paired(corner, 1), landing.at[0], across)
        via_y = send(paired(corner, 2), landing.at[1], along)
        own_x = send(paired(across, 1), landing.at[2], across)
        own_y = send(paired(along, 2), landing.at[3], along)
        yield
        via_x.wait_recv()
        passing[0] = (
            paired(along, 1)[...].astype(jnp.float32) + landing[0].astype(jnp.float32)
        ).astype(passing.dtype)
        last_first = send(passing.at[0], landing.at[4], along)
        via_y.wait_recv()
        passing[1] = (
            paired(across, 2)[...].astype(jnp.float32) + landing[1].astype(jnp.float32)
        ).astype(passing.dtype)
        last_second = send(passing.at[1], landing.at[5], across)
        yield
        own_x.wait_recv()
        own_y.wait_recv()
        last_first.wait_recv()
        last_second.wait_recv()
        for half in (1, 2):
            total = paired(chip, half)[...].astype(jnp.float32)
            total = total + landing[1 + half].astype(jnp.float32)
            total = total + landing[3 + half].astype(jnp.float32)
            finish(half, total)
    else:
        for step in range(1, chips):
            send(paired(lax.rem(chip + step, chips), 0), landing.at[step - 1], lax.rem(chip + step, chips))
        yield
        total = paired(chip, 0)[...].astype(jnp.float32)
        for step, copy in enumerate(sent):
            copy.wait_recv()
            total = total + landing[step].astype(jnp.float32)
        finish(0, total)
    for copy in sent:
        copy.wait_send()


def remote_call(kernel, name, results, operands, in_spaces, out_spaces, scratch, copies, cost):
    ids = ("weights", "keys", "rows", "row_sums", "key_sums", "totals")
    return pl.pallas_call(
        kernel,
        out_shape=results,
        in_specs=[pl.BlockSpec(memory_space=space) for space in in_spaces],
        out_specs=[pl.BlockSpec(memory_space=space) for space in out_spaces],
        scratch_shapes=list(scratch)
        + [pltpu.SemaphoreType.DMA((copies,)), pltpu.SemaphoreType.DMA((copies,))],
        compiler_params=pltpu.CompilerParams(
            collective_id=ids.index(name), has_side_effects=True, vmem_limit_bytes=VMEM_LIMIT
        ),
        cost_estimate=pl.CostEstimate(flops=0, bytes_accessed=cost, transcendentals=0),
        name=name,
    )(*operands)


def struct(shape, dtype):
    return jax.ShapeDtypeStruct(shape, dtype)


class SharedBlock:
    def __init__(self, copies, source, target, count, ctx_count):
        _, core, _, _, self.sibling = own_place(ctx_count)
        half = source.shape[0] // 2
        rows = pl.ds(pl.multiple_of(core * half, math.gcd(half, 256)), half)
        self.copies, self.forwarded = copies, []
        self.stream = line_gather(
            copies, source.at[rows], lambda i: target.at[i, rows], count, self.arrived
        )

    def arrived(self, allowed, _, held):
        copy = self.copies.make(held, held, {"ctx": self.sibling})

        @pl.when(allowed)
        def _():
            copy.start()

        self.forwarded.append((allowed, copy))

    def wait(self):
        for allowed, copy in self.forwarded:

            @pl.when(allowed)
            def _():
                copy.wait()


def gather_weights(weight, count, ctx_count):
    rows, width = weight.shape

    def kernel(source, target, local, send, recv):
        copies = Copies(send, recv)
        rank = lax.axis_index("fsdp")
        meet(line_peers(count) + plane_peers(ctx_count)[:1])
        keep = pltpu.make_async_copy(source, target.at[rank], local)
        keep.start()
        block = SharedBlock(copies, source, target, count, ctx_count)
        together(block.stream)
        block.wait()
        keep.wait()

    (full,) = remote_call(
        kernel, "weights", [struct((count, rows, width), weight.dtype)], [weight],
        [pl.ANY], [pl.ANY], [pltpu.SemaphoreType.DMA], 4 * count, count * rows * width * 4,
    )
    return full.reshape(count * rows, width)


def gather_keys(block, weights, count, ctx_count):
    rows, width = block.shape
    half = rows // 2

    def kernel(*refs):
        own, *sources = refs[: 1 + len(weights)]
        gathered, *targets = refs[1 + len(weights) : 2 + 2 * len(weights)]
        local, send, recv = refs[2 + 2 * len(weights) :]
        copies = Copies(send, recv)
        rank, place = lax.axis_index("fsdp"), lax.axis_index("ctx")
        spans = (pl.ds(0, rows), pl.ds(0, half), pl.ds(half, half))
        meet(line_peers(count) + plane_peers(ctx_count))
        kept = [pltpu.make_async_copy(own, gathered.at[place], local.at[0])]
        kept += [
            pltpu.make_async_copy(source, target.at[rank], local.at[1 + i])
            for i, (source, target) in enumerate(zip(sources, targets))
        ]
        for copy in kept:
            copy.start()
        blocks = [SharedBlock(copies, s, t, count, ctx_count) for s, t in zip(sources, targets)]
        together(
            plane_gather(
                copies,
                lambda part: own.at[spans[part]],
                lambda i, part: gathered.at[i, spans[part]],
                ctx_count,
            ),
            *[b.stream for b in blocks],
        )
        for b in blocks:
            b.wait()
        for copy in kept:
            copy.wait()

    results = [struct((ctx_count, rows, width), block.dtype)]
    results += [struct((count,) + w.shape, w.dtype) for w in weights]
    gathered, *full = remote_call(
        kernel, "keys", results, [block, *weights],
        [pl.ANY] * (1 + len(weights)), [pl.ANY] * (1 + len(weights)),
        [pltpu.SemaphoreType.DMA((1 + len(weights),))],
        16 + 2 * ctx_count + 4 * count * len(weights),
        ctx_count * rows * width * 4,
    )
    return gathered.reshape(ctx_count * rows, width), [
        f.reshape(count * f.shape[1], f.shape[2]) for f in full
    ]


def gather_rows(block, notes, count):
    def kernel(own, own_notes, gathered, all_notes, local, send, recv):
        copies = Copies(send, recv)
        rank = lax.axis_index("fsdp")
        meet(ring_peers("fsdp", count))
        kept = [
            pltpu.make_async_copy(own, gathered.at[rank], local.at[0]),
            pltpu.make_async_copy(own_notes, all_notes.at[rank], local.at[1]),
        ]
        for copy in kept:
            copy.start()
        together(
            push_gather(copies, own_notes, lambda step: all_notes.at[rank], "fsdp", count),
            line_gather(copies, own, lambda i: gathered.at[i], count),
        )
        for copy in kept:
            copy.wait()

    return remote_call(
        kernel, "rows",
        [struct((count,) + block.shape, block.dtype), struct((count,) + notes.shape, notes.dtype)],
        [block, notes], [pl.ANY] * 2, [pl.ANY] * 2, [pltpu.SemaphoreType.DMA((2,))],
        4 * count, count * block.size * 4,
    )


def reduce_rows(parts, notes, shared, count, ctx_count):
    _, rows, width = parts.shape

    def kernel(given, given_notes, own, total, notes_total, all_shared,
               passing, landing, noted, send, recv):
        copies = Copies(send, recv)
        rank, place = lax.axis_index("fsdp"), lax.axis_index("ctx")
        meet(ring_peers("fsdp", count) + ring_peers("ctx", ctx_count))
        pushes, spread = [], []
        for step in range(1, count):
            peer = lax.rem(rank + step, count)
            copy = copies.make(given_notes.at[peer], noted.at[step - 1], {"fsdp": peer})
            copy.start()
            pushes.append(copy)
        for step in range(1, ctx_count):
            copy = copies.make(own, all_shared.at[place], {"ctx": lax.rem(place + step, ctx_count)})
            copy.start()
            spread.append(copy)
        all_shared[place] = own[...]
        together(
            line_reduce(copies, lambda d: given.at[d], passing, landing, count, total)
        )
        sums = given_notes[rank]
        for step, copy in enumerate(pushes):
            copy.wait()
            sums = sums + noted[step]
        notes_total[...] = sums
        for copy in spread:
            copy.wait()

    return remote_call(
        kernel, "row_sums",
        [
            struct((rows, width), jnp.float32),
            struct(notes.shape[1:], notes.dtype),
            struct((ctx_count,) + shared.shape, shared.dtype),
        ],
        [parts, notes, shared], [pltpu.VMEM] * 3, [pltpu.VMEM] * 3,
        [
            pltpu.VMEM((2, count - 1, rows, width), parts.dtype),
            pltpu.VMEM((2, count - 1, rows, width), parts.dtype),
            pltpu.VMEM((count - 1,) + notes.shape[1:], notes.dtype),
        ],
        4 * count + ctx_count, count * rows * width * 4,
    )


def reduce_keys(parts, row_parts, count, ctx_count):
    _, _, rows, width = parts.shape
    chips = ctx_count // 2
    lands = (6, 1, rows, width) if chips == 4 else (chips - 1, 2, rows, width)

    def kernel(given, given_rows, total, rows_total, met, paired, passing, landing,
               row_passing, row_landing, send, recv):
        copies = Copies(send, recv)
        _, core, _, _, sibling = own_place(ctx_count)
        spans = (pl.ds(0, 2), pl.ds(0, 1), pl.ds(1, 1))
        meet(ring_peers("fsdp", count) + plane_peers(ctx_count))
        exchanged = []
        for q in range(chips):
            for kind in range(2):
                copy = copies.make(
                    given.at[kind, 2 * q + 1 - core], met.at[q, kind], {"ctx": sibling}
                )
                copy.start()
                exchanged.append((q, kind, copy))

        def finish(part, value):
            total[spans[part]] = value

        def planes():
            yield
            for q, kind, copy in exchanged:
                copy.wait_recv()
                paired[q, kind] = (
                    given[kind, 2 * q + core].astype(jnp.float32)
                    + met[q, kind].astype(jnp.float32)
                ).astype(paired.dtype)
            yield from plane_reduce(
                copies, lambda q, part: paired.at[q, spans[part]],
                passing, landing, ctx_count, finish,
            )

        together(
            planes(),
            line_reduce(
                copies, lambda d: given_rows.at[d], row_passing, row_landing, count, rows_total
            ),
        )
        for _, _, copy in exchanged:
            copy.wait_send()

    _, row_count, row_width = row_parts.shape
    return remote_call(
        kernel, "key_sums",
        [struct((2, rows, width), jnp.float32), struct((row_count, row_width), jnp.float32)],
        [parts, row_parts], [pltpu.VMEM] * 2, [pltpu.VMEM] * 2,
        [
            pltpu.VMEM((chips, 2, rows, width), parts.dtype),
            pltpu.VMEM((chips, 2, rows, width), parts.dtype),
            pltpu.VMEM((2, 1, rows, width), parts.dtype),
            pltpu.VMEM(lands, parts.dtype),
            pltpu.VMEM((2, count - 1, row_count, row_width), parts.dtype),
            pltpu.VMEM((2, count - 1, row_count, row_width), parts.dtype),
        ],
        3 * chips + 8 + 2 * count, ctx_count * rows * width * 8,
    )


def reduce_weights(parts, small, half_grads, row_parts, count, ctx_count):
    _, rows, width = parts.shape
    chips = ctx_count // 2
    half, share = rows // 2, width // chips
    row_unit = math.gcd(half, 256)
    first = max(count // 2, 1)
    lands = (6, first, half, share) if chips == 4 else (chips - 1, count, half, share)

    own = half_grads.shape[0]

    def kernel(given, given_small, half_ref, given_rows, total, small_total, grads_ref, rows_total,
               row_passing, row_landing, met, paired, passing, landing, merged,
               line_passing, line_landing, line_total, own_total, small_met, small_sum,
               small_plane, small_plane_sum, small_line, send, recv):
        copies = Copies(send, recv)
        rank = lax.axis_index("fsdp")
        place, core, chip, _, sibling = own_place(ctx_count)
        spans = (pl.ds(0, count), pl.ds(0, first), pl.ds(first, count - first))
        mine = pl.ds(pl.multiple_of(core * half, row_unit), half)
        theirs = pl.ds(pl.multiple_of((1 - core) * half, row_unit), half)

        def columns(q):
            return pl.ds(pl.multiple_of(q * share, 128), share)

        meet(
            ring_peers("fsdp", count)
            + ring_peers("ctx", ctx_count, 2)
            + plane_peers(ctx_count)[:1]
        )
        small_pair = copies.make(given_small, small_met, {"ctx": sibling})
        small_pair.start()
        exchanged = []
        for d in range(count):
            copy = copies.make(given.at[d, theirs], met.at[d], {"ctx": sibling})
            copy.start()
            exchanged.append(copy)

        for i in range(own):
            copy = copies.make(half_ref.at[i], grads_ref.at[i], {"ctx": sibling})
            copy.start()
            exchanged.append(copy)

        def small_stream():
            small_pair.wait()
            small_sum[...] = given_small[...] + small_met[...]
            pushes = []
            for step in range(1, chips):
                copy = copies.make(
                    small_sum, small_plane.at[step - 1],
                    {"ctx": lax.rem(place + 2 * step, ctx_count)},
                )
                copy.start()
                pushes.append(copy)
            yield
            for copy in pushes:
                copy.wait()
            small_plane_sum[...] = small_sum[...] + jnp.sum(small_plane[...], axis=0)
            pushes = []
            for step in range(1, count):
                copy = copies.make(
                    small_plane_sum, small_line.at[step - 1],
                    {"fsdp": lax.rem(rank + step, count)},
                )
                copy.start()
                pushes.append(copy)
            yield
            yield
            for copy in pushes:
                copy.wait()
            small_total[...] = small_plane_sum[...] + jnp.sum(small_line[...], axis=0)

        def finish(part, value):
            merged[spans[part]] = value.astype(merged.dtype)

        def large_stream():
            for d, copy in enumerate(exchanged[:count]):
                copy.wait_recv()
                for q in range(chips):
                    paired[q, d] = (
                        given[d, mine, q * share : (q + 1) * share].astype(jnp.float32)
                        + met[d, :, q * share : (q + 1) * share].astype(jnp.float32)
                    ).astype(paired.dtype)
            yield from plane_reduce(
                copies, lambda q, part: paired.at[q, spans[part]],
                passing, landing, ctx_count, finish,
            )
            yield from line_reduce(
                copies, lambda d: merged.at[d], line_passing, line_landing, count, line_total
            )
            own_total[...] = line_total[...].astype(own_total.dtype)
            sent = []
            forwarded = []
            copy = copies.make(own_total, total.at[mine, columns(chip)], {"ctx": sibling})
            copy.start()
            forwarded.append(copy)
            for step in range(1, chips):
                copy = copies.make(
                    own_total, total.at[mine, columns(chip)],
                    {"ctx": lax.rem(place + 2 * step, ctx_count)},
                )
                copy.start()
                sent.append(copy)
            total[mine, columns(chip)] = own_total[...]
            for step, copy in enumerate(sent, 1):
                copy.wait_recv()
                held = total.at[mine, columns(lax.rem(chip + chips - step, chips))]
                copy = copies.make(held, held, {"ctx": sibling})
                copy.start()
                forwarded.append(copy)
            for copy in sent:
                copy.wait_send()
            for copy in forwarded:
                copy.wait()

        together(
            line_reduce(
                copies, lambda d: given_rows.at[d], row_passing, row_landing, count, rows_total
            ),
            small_stream(),
            large_stream(),
        )
        for copy in exchanged:
            copy.wait_send()
        for copy in exchanged[count:]:
            copy.wait_recv()

    kind = parts.dtype
    f32 = jnp.float32
    return remote_call(
        kernel, "totals",
        [
            struct((rows, width), kind),
            struct(small.shape, f32),
            struct(half_grads.shape, kind),
            struct(row_parts.shape[1:], f32),
        ],
        [parts, small, half_grads, row_parts],
        [pltpu.VMEM, pltpu.VMEM, pl.ANY, pltpu.VMEM],
        [pltpu.VMEM, pltpu.VMEM, pl.ANY, pltpu.VMEM],
        [
            pltpu.VMEM((2, count - 1) + row_parts.shape[1:], kind),
            pltpu.VMEM((2, count - 1) + row_parts.shape[1:], kind),
            pltpu.VMEM((count, half, width), kind),
            pltpu.VMEM((chips, count, half, share), kind),
            pltpu.VMEM((2, first, half, share), kind),
            pltpu.VMEM(lands, kind),
            pltpu.VMEM((count, half, share), kind),
            pltpu.VMEM((2, count - 1, half, share), kind),
            pltpu.VMEM((2, count - 1, half, share), kind),
            pltpu.VMEM((half, share), f32),
            pltpu.VMEM((half, share), kind),
            pltpu.VMEM(small.shape, f32),
            pltpu.VMEM(small.shape, f32),
            pltpu.VMEM((chips - 1,) + small.shape, f32),
            pltpu.VMEM(small.shape, f32),
            pltpu.VMEM((count - 1,) + small.shape, f32),
        ],
        count + 8 + 5 * count + 4 * chips + own, parts.size * 8,
    )


def local_call(kernel, name, grid, results, operands, in_specs, out_specs, scratch, flops, cost):
    return pl.pallas_call(
        kernel,
        grid=grid,
        out_shape=results,
        in_specs=in_specs,
        out_specs=out_specs,
        scratch_shapes=scratch,
        compiler_params=pltpu.CompilerParams(vmem_limit_bytes=VMEM_LIMIT),
        cost_estimate=pl.CostEstimate(flops=flops, bytes_accessed=cost, transcendentals=0),
        name=name,
    )(*operands)


def whole_block(shape):
    return pl.BlockSpec(shape, lambda *_: (0,) * len(shape))


def product(left, right, left_dim=1, right_dim=0):
    return lax.dot_general(
        left, right, (((left_dim,), (right_dim,)), ((), ())), preferred_element_type=jnp.float32
    )


def expert_layers(routed_rows, block_rows, notes, weights):
    peers, piece_len, width = routed_rows.shape
    experts, _, units, _ = weights.shape
    capacity = piece_len // 4
    count = peers * capacity

    def kernel(routed, block, note, w, out_parts, grad_parts, dots, out_sum, grad_sum):
        expert = pl.program_id(0)
        low = jnp.bfloat16

        @pl.when(expert == 0)
        def _():
            out_sum[...] = jnp.zeros_like(out_sum)
            grad_sum[...] = jnp.zeros_like(grad_sum)
            dots[...] = jnp.zeros_like(dots)

        slots = (
            lax.broadcasted_iota(jnp.int32, (capacity, piece_len), 0) + expert * capacity
        ).astype(jnp.float32)
        hots, firsts, seconds, gates, taken, blocks = [], [], [], [], [], []
        for g in range(peers):
            first = note[g, 0:1, :] == slots
            second = note[g, 1:2, :] == slots
            gates.append(
                jnp.sum(
                    jnp.where(first, note[g, 2:3, :], 0.0)
                    + jnp.where(second, note[g, 3:4, :], 0.0),
                    axis=1,
                    keepdims=True,
                )
            )
            first, second = jnp.where(first, 1.0, 0.0), jnp.where(second, 1.0, 0.0)
            hot = (first + second).astype(low)
            taken.append(product(hot, routed[g]).astype(low))
            blocks.append(product(hot, block[g]))
            hots.append(hot)
            firsts.append(first)
            seconds.append(second)
        rows = jnp.concatenate(taken, axis=0)
        block_part = jnp.concatenate(blocks, axis=0)
        gate = jnp.concatenate(gates, axis=0)
        grad_out = (gate * block_part).astype(low)
        w_gate, w_up, w_down = w[0, 0], w[0, 1], w[0, 2]
        gate_proj = product(rows, w_gate, 1, 1)
        up_proj = product(rows, w_up, 1, 1)
        grad_hidden = product(grad_out, w_down, 1, 1)
        sigmoid = 1.0 / (1.0 + jnp.exp(-gate_proj))
        silu = gate_proj * sigmoid
        hidden = (silu * up_proj).astype(low)
        grad_gate_proj = (
            grad_hidden * up_proj * sigmoid * (1.0 + gate_proj * (1.0 - sigmoid))
        ).astype(low)
        grad_up_proj = (grad_hidden * silu).astype(low)
        expert_out = product(hidden, w_down)
        grad_in = (product(grad_gate_proj, w_gate) + product(grad_up_proj, w_up)).astype(low)
        row_dots = jnp.sum(block_part * expert_out, axis=1, keepdims=True)
        gated = (gate * expert_out).astype(low)
        for g in range(peers):
            span = slice(g * capacity, (g + 1) * capacity)
            out_sum[g] += product(hots[g], gated[span], 0, 0)
            grad_sum[g] += product(hots[g], grad_in[span], 0, 0)
            dots[g, 0:1, :] += jnp.sum(firsts[g] * row_dots[span], axis=0, keepdims=True)
            dots[g, 1:2, :] += jnp.sum(seconds[g] * row_dots[span], axis=0, keepdims=True)

        @pl.when(expert == experts - 1)
        def _():
            out_parts[...] = out_sum[...].astype(low)
            grad_parts[...] = grad_sum[...].astype(low)

    rows_shape = (peers, piece_len, width)
    low = jnp.bfloat16
    expert_block = pl.BlockSpec((1, 3, units, width), lambda e: (e, 0, 0, 0))
    return local_call(
        kernel, "experts", (experts,),
        [struct(rows_shape, low), struct(rows_shape, low),
         struct(notes.shape, jnp.float32)],
        [routed_rows, block_rows, notes, weights],
        [whole_block(rows_shape), whole_block(rows_shape), whole_block(notes.shape), expert_block],
        [whole_block(rows_shape), whole_block(rows_shape), whole_block(notes.shape)],
        [pltpu.VMEM(rows_shape, jnp.float32), pltpu.VMEM(rows_shape, jnp.float32)],
        12 * experts * count * units * width, 2 * weights.size,
    )


def expert_gradients(first, counts, routed_rows, block_rows, notes, weights):
    pieces, piece_len, width = routed_rows.shape
    experts, _, units, _ = weights.shape
    capacity = piece_len // 4
    own = experts // 2
    tile = 256
    room = pieces * capacity + tile
    batch = max(d for d in range(1, own + 1) if own % d == 0 and (d == 1 or d * room * width * 4 <= 30 << 20))
    low = jnp.bfloat16

    def kernel(start, count, routed, block, note, w, grads, final, rows, grad_rows, ends):
        turn, step = pl.program_id(0), pl.program_id(1)
        expert = start[0] + turn * batch

        @pl.when(step == 0)
        def _():
            for j in range(batch):
                ends[j] = 0

        piece = jnp.minimum(step, pieces - 1)
        numbers = [count[piece * experts + expert + j] for j in range(batch)]

        @pl.when((step < pieces) & (sum(numbers) > 0))
        def _():
            slots = (
                lax.broadcasted_iota(jnp.int32, (batch * capacity, piece_len), 0)
                + expert * capacity
            ).astype(jnp.float32)
            first = note[0, 0:1, :] == slots
            second = note[0, 1:2, :] == slots
            gate = jnp.sum(
                jnp.where(first, note[0, 2:3, :], 0.0) + jnp.where(second, note[0, 3:4, :], 0.0),
                axis=1,
                keepdims=True,
            )
            hot = (jnp.where(first, 1.0, 0.0) + jnp.where(second, 1.0, 0.0)).astype(low)
            taken = product(hot, routed[0]).astype(low)
            grad_out = (gate * product(hot, block[0])).astype(low)
            for j in range(batch):
                place = pl.ds(pl.multiple_of(ends[j], 16), capacity)
                span = slice(j * capacity, (j + 1) * capacity)
                rows[j, place, :] = taken[span]
                grad_rows[j, place, :] = grad_out[span]
                ends[j] += (numbers[j] + 15) // 16 * 16

        @pl.when(step >= pieces)
        def _():
            j = jnp.maximum(step - pieces, 0)
            end = pl.multiple_of(ends[j], 16)
            rest = pl.ds(end, tile)
            rows[j, rest, :] = jnp.zeros((tile, width), low)
            grad_rows[j, rest, :] = jnp.zeros((tile, width), low)
            final[...] = jnp.zeros_like(final)

            def one_tile(index, _):
                place = pl.ds(pl.multiple_of(index * tile, tile), tile)
                x = rows[j, place, :]
                grad_out = grad_rows[j, place, :]
                gate_proj = product(x, w[0, 0], 1, 1)
                up_proj = product(x, w[0, 1], 1, 1)
                grad_hidden = product(grad_out, w[0, 2], 1, 1)
                sigmoid = 1.0 / (1.0 + jnp.exp(-gate_proj))
                silu = gate_proj * sigmoid
                hidden = (silu * up_proj).astype(low)
                grad_gate_proj = (
                    grad_hidden * up_proj * sigmoid * (1.0 + gate_proj * (1.0 - sigmoid))
                ).astype(low)
                grad_up_proj = (grad_hidden * silu).astype(low)
                final[0, 0] += product(grad_gate_proj, x, 0, 0)
                final[0, 1] += product(grad_up_proj, x, 0, 0)
                final[0, 2] += product(hidden, grad_out, 0, 0)
                return 0

            lax.fori_loop(0, (end + tile - 1) // tile, one_tile, 0)
            grads[...] = final[...].astype(low)

    def piece_block(shape):
        return pl.BlockSpec(
            (1,) + shape[1:], lambda turn, step, *_: (jnp.minimum(step, pieces - 1), 0, 0)
        )

    def local(turn, step):
        return turn * batch + jnp.maximum(step - pieces, 0)

    return pl.pallas_call(
        kernel,
        grid_spec=pltpu.PrefetchScalarGridSpec(
            num_scalar_prefetch=2,
            grid=(own // batch, pieces + batch),
            in_specs=[
                piece_block(routed_rows.shape),
                piece_block(block_rows.shape),
                piece_block(notes.shape),
                pl.BlockSpec(
                    (1, 3, units, width),
                    lambda turn, step, start, _: (start[0] + local(turn, step), 0, 0, 0),
                ),
            ],
            out_specs=[
                pl.BlockSpec(
                    (1, 3, units, width), lambda turn, step, *_: (local(turn, step), 0, 0, 0)
                ),
                pl.BlockSpec(
                    (1, 3, units, width),
                    lambda turn, step, start, _: (start[0] + local(turn, step), 0, 0, 0),
                ),
            ],
            scratch_shapes=[
                pltpu.VMEM((batch, room, width), low),
                pltpu.VMEM((batch, room, width), low),
                pltpu.SMEM((batch,), jnp.int32),
            ],
        ),
        out_shape=[
            struct((own, 3, units, width), low),
            struct((experts, 3, units, width), jnp.float32),
        ],
        compiler_params=pltpu.CompilerParams(vmem_limit_bytes=VMEM_LIMIT),
        cost_estimate=pl.CostEstimate(
            flops=12 * own * pieces * capacity * units * width // 2,
            bytes_accessed=routed_rows.size * 4 + weights.size * 2,
            transcendentals=0,
        ),
        name="expert_gradients",
    )(first, counts, routed_rows, block_rows, notes, weights)


def other_gradients(first, received, final):
    own, _, units, width = received.shape
    block = (1, 1, units, width)

    def kernel(start, given, _, result):
        result[...] = given[...].astype(jnp.float32)

    return pl.pallas_call(
        kernel,
        grid_spec=pltpu.PrefetchScalarGridSpec(
            num_scalar_prefetch=1,
            grid=(own, 3),
            in_specs=[
                pl.BlockSpec(block, lambda i, k, _: (i, k, 0, 0)),
                pl.BlockSpec(memory_space=pl.ANY),
            ],
            out_specs=pl.BlockSpec(block, lambda i, k, start: (start[0] + i, k, 0, 0)),
        ),
        out_shape=struct(final.shape, jnp.float32),
        input_output_aliases={2: 0},
        compiler_params=pltpu.CompilerParams(vmem_limit_bytes=VMEM_LIMIT),
        name="other_gradients",
    )(first, received, final)


def score_bias(length, first_row, rows, keys):
    key_place = lax.broadcasted_iota(jnp.int32, (keys, rows), 0)
    query_place = first_row + lax.broadcasted_iota(jnp.int32, (keys, rows), 1)
    return jnp.where(key_place <= jnp.minimum(query_place, length - 1), 0.0, MASKED)


def head_masks(shape):
    lane = lax.broadcasted_iota(jnp.int32, shape, 1)
    return [lane < HEAD_DIM, lane >= HEAD_DIM]


def attention_forward(places, queries, pairs):
    rows, width = queries.shape
    keys = pairs.shape[0]
    tile = 2 * HEAD_DIM
    tiles = width // tile

    def kernel(place, query, key, value, mixed, sums, bias):
        step = pl.program_id(0)

        @pl.when(step == 0)
        def _():
            bias[...] = score_bias(place[0], place[1], rows, keys)

        own_masks = head_masks((rows, tile))
        scaled = query[...] * HEAD_DIM**-0.5
        outs = []
        for head in range(2):
            chosen = jnp.where(own_masks[head], scaled, 0)
            scores = product(key[...], chosen, 1, 1) + bias[...]
            top = jnp.max(scores, axis=0, keepdims=True)
            weights = jnp.exp(scores - top)
            total = jnp.sum(weights, axis=0, keepdims=True)
            probabilities = (weights * (1.0 / total)).astype(jnp.bfloat16)
            outs.append(product(probabilities, value[...], 0, 0))
            sums[0, head : head + 1, :] = top + jnp.log(total)
        mixed[...] = jnp.where(own_masks[0], outs[0], outs[1]).astype(mixed.dtype)

    return pl.pallas_call(
        kernel,
        grid_spec=pltpu.PrefetchScalarGridSpec(
            num_scalar_prefetch=1,
            grid=(tiles,),
            in_specs=[
                pl.BlockSpec((rows, tile), lambda i, _: (0, i)),
                pl.BlockSpec((keys, tile), lambda i, _: (0, i)),
                pl.BlockSpec((keys, tile), lambda i, _: (0, i + tiles)),
            ],
            out_specs=[
                pl.BlockSpec((rows, tile), lambda i, _: (0, i)),
                pl.BlockSpec((1, 8, rows), lambda i, _: (i, 0, 0)),
            ],
            scratch_shapes=[pltpu.VMEM((keys, rows), jnp.float32)],
        ),
        out_shape=[struct((rows, width), jnp.bfloat16), struct((tiles, 8, rows), jnp.float32)],
        compiler_params=pltpu.CompilerParams(vmem_limit_bytes=VMEM_LIMIT),
        cost_estimate=pl.CostEstimate(
            flops=4 * rows * keys * width, bytes_accessed=pairs.size * 2, transcendentals=0
        ),
        name="attention",
    )(places, queries, pairs, pairs)


def attention_backward(places, queries, pairs, sums, mixed, grad_mixed):
    rows, width = queries.shape
    keys = pairs.shape[0]
    pieces = keys // rows
    tile = 2 * HEAD_DIM
    tiles = width // tile
    scaling = HEAD_DIM**-0.5

    def kernel(place, query, key, value, total, out, grad_out, grad_query, grad_pair, bias):
        step = pl.program_id(0)

        @pl.when(step == 0)
        def _():
            bias[...] = score_bias(place[0], place[1], rows, keys)

        own_masks = head_masks((rows, tile))
        scaled = query[...] * scaling
        inner = out[...].astype(jnp.float32) * grad_out[...].astype(jnp.float32)
        grads, key_sum, value_sum = [], None, None
        for head in range(2):
            chosen = jnp.where(own_masks[head], scaled, 0)
            upstream = jnp.where(own_masks[head], grad_out[...], 0)
            ones = jnp.where(own_masks[head][:8], 1.0, 0.0)
            inner_row = lax.dot_general(
                ones, inner, (((1,), (1,)), ((), ())),
                precision=HIGHEST, preferred_element_type=jnp.float32,
            )[0:1]
            scores = product(key[...], chosen, 1, 1) + bias[...]
            probabilities = jnp.exp(scores - total[0, head : head + 1, :])
            grad_probs = product(value[...], upstream, 1, 1)
            grad_scores = (probabilities * (grad_probs - inner_row)).astype(jnp.bfloat16)
            key_part = product(grad_scores, chosen)
            value_part = product(probabilities.astype(jnp.bfloat16), upstream)
            key_sum = key_part if key_sum is None else key_sum + key_part
            value_sum = value_part if value_sum is None else value_sum + value_part
            grads.append(product(grad_scores, key[...], 0, 0) * scaling)
        grad_query[...] = jnp.where(own_masks[0], grads[0], grads[1])
        grad_pair[:, 0] = key_sum.astype(grad_pair.dtype).reshape(pieces, rows, tile)
        grad_pair[:, 1] = value_sum.astype(grad_pair.dtype).reshape(pieces, rows, tile)

    own_block = pl.BlockSpec((rows, tile), lambda i, _: (0, i))
    key_block = pl.BlockSpec((keys, tile), lambda i, _: (0, i))
    low = jnp.bfloat16
    return pl.pallas_call(
        kernel,
        grid_spec=pltpu.PrefetchScalarGridSpec(
            num_scalar_prefetch=1,
            grid=(tiles,),
            in_specs=[
                own_block,
                key_block,
                pl.BlockSpec((keys, tile), lambda i, _: (0, i + tiles)),
                pl.BlockSpec((1, 8, rows), lambda i, _: (i, 0, 0)),
                own_block,
                own_block,
            ],
            out_specs=[
                own_block,
                pl.BlockSpec((pieces, 2, rows, tile), lambda i, _: (0, 0, 0, i)),
            ],
            scratch_shapes=[pltpu.VMEM((keys, rows), jnp.float32)],
        ),
        out_shape=[
            struct((rows, width), jnp.float32),
            struct((pieces, 2, rows, width), low),
        ],
        compiler_params=pltpu.CompilerParams(vmem_limit_bytes=VMEM_LIMIT),
        cost_estimate=pl.CostEstimate(
            flops=10 * rows * keys * width, bytes_accessed=pairs.size * 4, transcendentals=0
        ),
        name="attention_back",
    )(places, queries, pairs, pairs, sums, mixed, grad_mixed)


def normalize_rows(values, gain_row):
    scaling = lax.rsqrt(jnp.mean(values * values, axis=-1, keepdims=True) + EPSILON)
    return (values * scaling * gain_row, scaling)


def normalize_back(values, scaling, gain_row, grad_out):
    grad_hat = grad_out * gain_row
    grad_gain = jnp.sum(grad_out * values * scaling, axis=(0, 1))
    grad_values = scaling * grad_hat - values * scaling**3 * jnp.mean(
        grad_hat * values, axis=-1, keepdims=True
    )
    return (grad_values, grad_gain)


def rope_tables(positions, head_size):
    half_dim = head_size // 2
    frequency = jnp.exp(
        jnp.arange(half_dim, dtype=jnp.float32) * (-2.0 * math.log(10000.0) / head_size)
    )
    angles = positions.astype(jnp.float32)[:, None] * frequency[None, :]
    return (jnp.cos(angles)[:, None, :], jnp.sin(angles)[:, None, :])


def rotate(values, cosine_table, sine_table):
    half_dim = values.shape[-1] // 2
    first_half = values[..., :half_dim]
    second_half = values[..., half_dim:]
    return jnp.concatenate(
        [
            first_half * cosine_table - second_half * sine_table,
            second_half * cosine_table + first_half * sine_table,
        ],
        axis=-1,
    )


def per_device(
    tokens,
    prev_logits,
    routes,
    lengths,
    cotangent,
    w_qkv,
    w_out,
    gain_attn,
    gain_moe,
    w_router,
    w_residual,
    const_vec,
    w_expert,
):
    groups, piece_len, model_width = tokens.shape
    head_count = model_width // HEAD_DIM
    part_heads = 2
    part_count = head_count // part_heads
    slot_len = piece_len * lax.axis_size("ctx")
    positions = lax.axis_index("ctx") * piece_len + jnp.arange(piece_len, dtype=jnp.int32)
    key_positions = jnp.arange(slot_len, dtype=jnp.int32)
    live_rows = (positions[None, :] < lengths[:, None]).astype(jnp.float32)[..., None]
    experts = w_expert.shape[0]
    capacity = piece_len // 4
    slot_count = experts * capacity
    split_shape = (groups, piece_len, head_count, HEAD_DIM)
    fsdp_count, ctx_count = lax.axis_size("fsdp"), lax.axis_size("ctx")
    full_kv = gather_weights(w_qkv[:, model_width:], fsdp_count, ctx_count)
    inputs = tokens.astype(jnp.float32)
    gain_one = gain_attn.astype(jnp.float32)
    gain_two = gain_moe.astype(jnp.float32)
    normed_one, scale_one = normalize_rows(inputs, gain_one)
    normed_one_low = normed_one.astype(jnp.bfloat16)
    projected = jnp.einsum("gpd,de->gpe", normed_one_low, full_kv, preferred_element_type=jnp.float32)
    cosine_table, sine_table = rope_tables(positions, HEAD_DIM)
    key_local = (
        rotate(projected[..., :model_width].reshape(split_shape), cosine_table, sine_table)
        .astype(jnp.bfloat16)
        .reshape(piece_len, model_width)
    )
    value_local = projected[0, :, model_width:].astype(jnp.bfloat16)
    cotangent_low = live_rows.astype(jnp.bfloat16) * cotangent
    own_pairs = jnp.concatenate([key_local, value_local], axis=-1)
    cotangent_low, own_pairs = lax.optimization_barrier((cotangent_low, own_pairs))
    cotangent_rows = lax.all_gather(cotangent_low, "fsdp", axis=0, tiled=True)
    all_pairs, (full_query, full_out) = gather_keys(
        own_pairs, [w_qkv[:, :model_width], w_out], fsdp_count, ctx_count
    )
    cotangent_rows, all_pairs = lax.optimization_barrier((cotangent_rows, all_pairs))
    slot_block = lax.all_gather(cotangent_rows, "ctx", axis=0, tiled=True)
    queries = rotate(
        jnp.einsum(
            "gpd,de->gpe", normed_one_low, full_query, preferred_element_type=jnp.float32
        ).reshape(split_shape),
        cosine_table,
        sine_table,
    ).astype(jnp.bfloat16)
    places = jnp.stack([lengths[0], lax.axis_index("ctx") * piece_len]).astype(jnp.int32)
    query_rows = queries.reshape(piece_len, model_width)
    mixed_rows, score_sums = attention_forward(places, query_rows, all_pairs)
    mixed_low = mixed_rows[None]
    attention = jnp.einsum("gpd,de->gpe", mixed_low, full_out, preferred_element_type=jnp.float32)
    residual_sum = inputs + attention
    normed_two, scale_two = normalize_rows(residual_sum, gain_two)
    routed_low = normed_two.astype(jnp.bfloat16)
    routed = routed_low.astype(jnp.float32)
    logits = jnp.einsum("gpd,de->gpe", routed, w_router, precision=HIGHEST) + jnp.einsum(
        "gpi,ie->gpe", prev_logits, w_residual, precision=HIGHEST
    )
    id_range = jnp.arange(experts + 4, dtype=jnp.int32)
    route_hot = (routes[..., None] == id_range).astype(jnp.float32)
    chosen = jnp.sum(route_hot * logits[:, :, None, :], axis=-1)
    chosen_exp = jnp.exp(chosen - jnp.max(chosen, axis=-1, keepdims=True))
    gate_weights = chosen_exp / jnp.sum(chosen_exp, axis=-1, keepdims=True)
    assign_hot = route_hot[..., :experts].reshape(groups, 2 * piece_len, experts)
    earlier = jnp.cumsum(assign_hot, axis=1) - assign_hot
    order_in = jnp.sum(earlier * assign_hot, axis=-1)
    expert_of = jnp.sum(assign_hot * jnp.arange(experts, dtype=jnp.float32), axis=-1)
    is_ffn = jnp.sum(assign_hot, axis=-1)
    slot_of = jnp.where(is_ffn > 0.5, expert_of * capacity + order_in, -1.0).reshape(
        groups, piece_len, 2
    )
    live_counts = jnp.sum(
        assign_hot * jnp.repeat(live_rows[..., 0], 2, axis=1)[..., None], axis=(0, 1)
    )
    notes = jnp.concatenate(
        [
            slot_of[0].T,
            gate_weights[0].T,
            jnp.pad(live_counts[None], ((0, 3), (0, piece_len - experts))),
        ],
        axis=0,
    )
    routed_rows, all_notes = gather_rows(routed_low[0], notes, fsdp_count)
    expert_weights = w_expert.swapaxes(1, 2)
    out_parts, grad_parts, dot_notes = expert_layers(
        routed_rows, cotangent_rows, all_notes, expert_weights
    )
    slot_block, routed_rows, out_parts = lax.optimization_barrier(
        (slot_block, routed_rows, out_parts)
    )
    slot_routed = lax.all_gather(routed_rows, "ctx", axis=0, tiled=True)
    ffn_grad, dot_sums, slot_notes = reduce_rows(
        grad_parts, dot_notes, all_notes, fsdp_count, ctx_count
    )
    slot_notes = slot_notes.reshape((ctx_count * fsdp_count,) + notes.shape)
    ffn_grad = ffn_grad[None]
    copy_hot = route_hot[..., experts + 1]
    const_hot = route_hot[..., experts + 2 :]
    constants = const_vec.astype(jnp.float32)
    gate_const = jnp.sum(gate_weights[..., None] * const_hot, axis=2)
    copy_gate = jnp.sum(gate_weights * copy_hot, axis=2, keepdims=True)
    special_sum = copy_gate * routed + jnp.einsum(
        "gpj,jd->gpd", gate_const, constants, precision=HIGHEST
    )
    grad_block = live_rows * cotangent.astype(jnp.float32)
    copy_dot = jnp.sum(grad_block * routed, axis=-1)[..., None]
    const_dot = jnp.einsum("gpd,jd->gpj", grad_block, constants, precision=HIGHEST)
    grad_gate = (
        dot_sums[:2].T[None]
        + copy_hot * copy_dot
        + jnp.sum(const_hot * const_dot[:, :, None, :], axis=-1)
    )
    grad_chosen = gate_weights * (
        grad_gate - jnp.sum(gate_weights * grad_gate, axis=-1, keepdims=True)
    )
    grad_logits = jnp.sum(grad_chosen[..., None] * route_hot, axis=2)
    grad_router = jnp.einsum("gpd,gpe->de", routed, grad_logits, precision=HIGHEST)
    grad_mixing = jnp.einsum("gpi,gpe->ie", prev_logits, grad_logits, precision=HIGHEST)
    grad_previous = jnp.einsum("gpe,ie->gpi", grad_logits, w_residual, precision=HIGHEST)
    grad_const = jnp.einsum("gpd,gpj->jd", grad_block, gate_const, precision=HIGHEST)
    grad_routed = (
        jnp.einsum("gpe,de->gpd", grad_logits, w_router, precision=HIGHEST)
        + copy_gate * grad_block
        + ffn_grad
    )
    grad_norm_two, grad_gain_two = normalize_back(residual_sum, scale_two, gain_two, grad_routed)
    grad_residual = grad_block + grad_norm_two
    grad_attention = grad_residual.astype(jnp.bfloat16)
    grad_wout = jnp.einsum(
        "gpd,gpe->de", mixed_low, grad_attention, preferred_element_type=jnp.float32
    )
    grad_mixed = jnp.einsum(
        "gpe,de->gpd", grad_attention, full_out, preferred_element_type=jnp.float32
    ).astype(jnp.bfloat16)
    query_grad, pair_grads = attention_backward(
        places, query_rows, all_pairs, score_sums, mixed_rows, grad_mixed[0]
    )
    counts = slot_notes[:, 4, :experts].astype(jnp.int32).reshape(-1)
    counts, slot_routed, pair_grads = lax.optimization_barrier((counts, slot_routed, pair_grads))
    first_expert = lax.rem(lax.axis_index("ctx"), 2) * (experts // 2)
    half_grads, expert_half = expert_gradients(
        first_expert.astype(jnp.int32)[None], counts, slot_routed, slot_block, slot_notes, expert_weights
    )
    pair_grad = lax.psum_scatter(
        pair_grads.reshape(1, -1, model_width), "ctx", scatter_dimension=1, tiled=True
    )
    pair_grad = pair_grad.astype(jnp.float32).reshape(2, piece_len, model_width)
    key_grad, value_grad = pair_grad[:1], pair_grad[1:]
    query_back = rotate(query_grad.reshape(split_shape), cosine_table, -sine_table).reshape(
        groups, piece_len, model_width
    )
    key_back = rotate(key_grad.reshape(split_shape), cosine_table, -sine_table).reshape(
        groups, piece_len, model_width
    )
    grad_projected = jnp.concatenate([query_back, key_back, value_grad], axis=-1).astype(
        jnp.bfloat16
    )
    grad_wqkv = jnp.einsum(
        "gpd,gpe->de", normed_one_low, grad_projected, preferred_element_type=jnp.float32
    )
    grad_normed_one = jnp.einsum(
        "gpe,de->gpd",
        grad_projected[..., :model_width],
        full_query,
        preferred_element_type=jnp.float32,
    ) + jnp.einsum(
        "gpe,de->gpd",
        grad_projected[..., model_width:],
        full_kv,
        preferred_element_type=jnp.float32,
    )
    grad_norm_one, grad_gain_one = normalize_back(inputs, scale_one, gain_one, grad_normed_one)
    grad_inputs = grad_residual + grad_norm_one
    weight_parts = (
        jnp.concatenate([grad_wqkv, grad_wout], axis=-1)
        .astype(jnp.bfloat16)
        .reshape(fsdp_count, -1, 4 * model_width)
    )
    few = experts + 4
    mixing_row = jnp.pad(grad_mixing.reshape(1, -1), ((0, 0), (0, model_width - few * few)))
    small = jnp.concatenate(
        [grad_router.T, grad_const, grad_gain_one[None], grad_gain_two[None], mixing_row], axis=0
    )
    small = jnp.pad(small, ((0, -small.shape[0] % 8), (0, 0)))
    weight_sum, small_sum, expert_grads, ffn_sum = reduce_weights(
        weight_parts, small, half_grads, out_parts, fsdp_count, ctx_count
    )
    other_first = (experts // 2 - first_expert).astype(jnp.int32)[None]
    expert_sum = other_gradients(other_first, expert_grads, expert_half).swapaxes(1, 2)
    output = (live_rows * (residual_sum + special_sum + ffn_sum[None])).astype(jnp.bfloat16)
    weight_sum = weight_sum.astype(jnp.float32)
    wqkv_sum, wout_sum = weight_sum[:, : 3 * model_width], weight_sum[:, 3 * model_width :]
    router_sum, const_sum = small_sum[:few].T, small_sum[few : few + 2]
    gain_one_sum, gain_two_sum = small_sum[few + 2], small_sum[few + 3]
    mixing_sum = small_sum[few + 4, : few * few].reshape(few, few)
    return (
        output,
        grad_inputs,
        grad_previous,
        wqkv_sum,
        wout_sum,
        gain_one_sum,
        gain_two_sum,
        router_sum,
        mixing_sum,
        const_sum,
        expert_sum,
    )


def solution(mesh):
    return jax.shard_map(
        per_device,
        mesh=mesh,
        in_specs=(
            P("fsdp", "ctx", None),
            P("fsdp", "ctx", None),
            P("fsdp", "ctx", None),
            P("fsdp"),
            P("fsdp", "ctx", None),
            P("fsdp", None),
            P("fsdp", None),
            P(),
            P(),
            P(),
            P(),
            P(),
            P(None, "fsdp", None, None),
        ),
        out_specs=(
            P("fsdp", "ctx", None),
            P("fsdp", "ctx", None),
            P("fsdp", "ctx", None),
            P("fsdp", None),
            P("fsdp", None),
            P(),
            P(),
            P(),
            P(),
            P(),
            P(None, "fsdp", None, None),
        ),
        check_vma=False,
    )
```

```python
import itertools
import math

import jax
import jax.numpy as jnp
from jax import lax
from jax.experimental import pallas as pl
from jax.experimental.pallas import tpu as pltpu

from jax.sharding import PartitionSpec as P

HEAD_DIM = 64


EPSILON = 1e-05
MASKED = -1e30
HIGHEST = lax.Precision.HIGHEST


LOGICAL = pl.DeviceIdType.MESH
VMEM_LIMIT = 56 * 1024 * 1024


class Copies:
    def __init__(self, send, recv):
        self.send, self.recv, self.used = send, recv, 0

    def make(self, source, target, peer):
        index = self.used
        self.used += 1
        return pltpu.make_async_remote_copy(
            source, target, self.send.at[index], self.recv.at[index],
            device_id=peer, device_id_type=LOGICAL,
        )


def meet(peers):
    barrier = pltpu.get_barrier_semaphore()
    for allowed, peer in peers:
        @pl.when(allowed)
        def _():
            pl.semaphore_signal(barrier, 1, device_id=peer, device_id_type=LOGICAL)
    awaited = sum(jnp.where(allowed, 1, 0) for allowed, _ in peers)
    pl.semaphore_wait(barrier, awaited)


def together(*streams):
    for _ in itertools.zip_longest(*streams):
        pass


def within(value, count):
    return (value >= 0) & (value < count)


def bounded(value, count):
    return jnp.minimum(jnp.maximum(value, 0), count - 1)


def line_peers(count):
    rank = lax.axis_index("fsdp")
    return [
        (within(rank + way, count), {"fsdp": bounded(rank + way, count)}) for way in (1, -1)
    ]


def ring_peers(axis, count, stride=1):
    rank = lax.axis_index(axis)
    return [
        (rank >= 0, {axis: lax.rem(rank + stride * step, count)})
        for step in range(1, count // stride)
    ]


def own_place(count):
    rank = lax.axis_index("ctx")
    core = lax.rem(rank, 2)
    return rank, core, rank // 2, count // 2, rank + 1 - 2 * core


def plane_peers(count):
    rank, core, chip, chips, sibling = own_place(count)
    peers = [(rank >= 0, {"ctx": sibling})]
    if chips == 4:
        across, along, _ = square(chip)
        return peers + [(rank >= 0, {"ctx": 2 * c + core}) for c in (across, along)]
    return peers + ring_peers("ctx", count, 2)


def square(chip):
    side, row = lax.rem(chip, 2), chip // 2
    across = chip + 1 - 2 * side
    along = chip + 2 - 4 * row
    return across, along, across + 2 - 4 * row


def line_gather(copies, own, slot, count, arrived=None):
    rank = lax.axis_index("fsdp")
    sent, latest = [], {}
    for hop in range(1, count + 1):
        for way in (1, -1):
            origin = rank - way * (hop - 1)
            held = slot(bounded(origin, count))
            if hop > 1:
                earlier = latest[way]

                @pl.when(within(origin, count))
                def _():
                    earlier.wait_recv()

                if arrived is not None:
                    arrived(within(origin, count), bounded(origin, count), held)
            if hop < count:
                copy = copies.make(
                    own if hop == 1 else held, held, {"fsdp": bounded(rank + way, count)}
                )
                allowed = within(origin, count) & within(rank + way, count)

                @pl.when(allowed)
                def _():
                    copy.start()

                sent.append((allowed, copy))
                latest[way] = copy
        yield
    for allowed, copy in sent:

        @pl.when(allowed)
        def _():
            copy.wait_send()


def line_reduce(copies, part, passing, landing, count, total):
    rank = lax.axis_index("fsdp")
    sent, arriving = [], {}
    for step in range(count - 1, 0, -1):
        for side, way in enumerate((1, -1)):
            goal = rank + way * step
            allowed = within(goal, count)
            copy = copies.make(
                passing.at[side, step - 1],
                landing.at[side, step - 1],
                {"fsdp": bounded(rank + way, count)},
            )
            arriving[side, step - 1] = copy
            own = part(bounded(goal, count))
            has_earlier = allowed & within(rank - way, count)
            if step < count - 1:
                earlier = arriving[side, step]

                @pl.when(has_earlier)
                def _():
                    earlier.wait_recv()
                    passing[side, step - 1] = (
                        own[...].astype(jnp.float32) + landing[side, step].astype(jnp.float32)
                    ).astype(passing.dtype)

                @pl.when(allowed & jnp.logical_not(within(rank - way, count)))
                def _():
                    passing[side, step - 1] = own[...]
            else:

                @pl.when(allowed)
                def _():
                    passing[side, step - 1] = own[...]

            @pl.when(allowed)
            def _():
                copy.start()

            sent.append((allowed, copy))
        yield
    total[...] = part(rank)[...].astype(jnp.float32)
    for side, way in enumerate((1, -1)):
        last = arriving[side, 0]

        @pl.when(within(rank - way, count))
        def _():
            last.wait_recv()
            total[...] += landing[side, 0].astype(jnp.float32)
    for allowed, copy in sent:

        @pl.when(allowed)
        def _():
            copy.wait_send()


def push_gather(copies, own, slot, axis, count, stride=1):
    rank = lax.axis_index(axis)
    sent = []
    for step in range(1, count // stride):
        copy = copies.make(own, slot(step), {axis: lax.rem(rank + stride * step, count)})
        copy.start()
        sent.append(copy)
    yield
    for copy in sent:
        copy.wait()


def plane_gather(copies, own, slot, count):
    rank, core, chip, chips, sibling = own_place(count)
    sent, forwarded = [], []

    def send(source, target, peer):
        copy = copies.make(source, target, {"ctx": peer})
        copy.start()
        sent.append(copy)
        return copy

    def forward(index, part):
        copy = copies.make(slot(index, part), slot(index, part), {"ctx": sibling})
        copy.start()
        forwarded.append(copy)

    if chips == 4:
        across, along, _ = square(chip)
        side_x, side_y = 2 * across + core, 2 * along + core
        corner = 2 * square(chip)[2] + core
        first_x = send(own(1), slot(rank, 1), side_x)
        second_y = send(own(2), slot(rank, 2), side_y)
        second_x = send(own(2), slot(rank, 2), side_x)
        first_y = send(own(1), slot(rank, 1), side_y)
        copy = copies.make(own(0), slot(rank, 0), {"ctx": sibling})
        copy.start()
        forwarded.append(copy)
        yield
        first_x.wait_recv()
        corner_first = send(slot(side_x, 1), slot(side_x, 1), side_y)
        forward(side_x, 1)
        second_y.wait_recv()
        corner_second = send(slot(side_y, 2), slot(side_y, 2), side_x)
        forward(side_y, 2)
        yield
        second_x.wait_recv()
        forward(side_x, 2)
        first_y.wait_recv()
        forward(side_y, 1)
        yield
        corner_first.wait_recv()
        forward(corner, 1)
        corner_second.wait_recv()
        forward(corner, 2)
        yield
    else:
        pending = []
        for step in range(1, chips):
            peer = lax.rem(rank + 2 * step, count)
            pending.append((lax.rem(rank + count - 2 * step, count), send(own(0), slot(rank, 0), peer)))
        copy = copies.make(own(0), slot(rank, 0), {"ctx": sibling})
        copy.start()
        forwarded.append(copy)
        yield
        for origin, copy in pending:
            copy.wait_recv()
            forward(origin, 0)
        yield
    for copy in sent:
        copy.wait_send()
    for copy in forwarded:
        copy.wait()


def plane_reduce(copies, paired, passing, landing, count, finish):
    rank, core, chip, chips, sibling = own_place(count)
    sent = []

    def send(source, target, peer_chip):
        copy = copies.make(source, target, {"ctx": 2 * peer_chip + core})
        copy.start()
        sent.append(copy)
        return copy

    if chips == 4:
        across, along, corner = square(chip)
        via_x = send(paired(corner, 1), landing.at[0], across)
        via_y = send(paired(corner, 2), landing.at[1], along)
        own_x = send(paired(across, 1), landing.at[2], across)
        own_y = send(paired(along, 2), landing.at[3], along)
        yield
        via_x.wait_recv()
        passing[0] = (
            paired(along, 1)[...].astype(jnp.float32) + landing[0].astype(jnp.float32)
        ).astype(passing.dtype)
        last_first = send(passing.at[0], landing.at[4], along)
        via_y.wait_recv()
        passing[1] = (
            paired(across, 2)[...].astype(jnp.float32) + landing[1].astype(jnp.float32)
        ).astype(passing.dtype)
        last_second = send(passing.at[1], landing.at[5], across)
        yield
        own_x.wait_recv()
        own_y.wait_recv()
        last_first.wait_recv()
        last_second.wait_recv()
        for half in (1, 2):
            total = paired(chip, half)[...].astype(jnp.float32)
            total = total + landing[1 + half].astype(jnp.float32)
            total = total + landing[3 + half].astype(jnp.float32)
            finish(half, total)
    else:
        for step in range(1, chips):
            send(paired(lax.rem(chip + step, chips), 0), landing.at[step - 1], lax.rem(chip + step, chips))
        yield
        total = paired(chip, 0)[...].astype(jnp.float32)
        for step, copy in enumerate(sent):
            copy.wait_recv()
            total = total + landing[step].astype(jnp.float32)
        finish(0, total)
    for copy in sent:
        copy.wait_send()


def remote_call(kernel, name, results, operands, in_spaces, out_spaces, scratch, copies, cost):
    ids = ("weights", "keys", "rows", "row_sums", "key_sums", "totals")
    return pl.pallas_call(
        kernel,
        out_shape=results,
        in_specs=[pl.BlockSpec(memory_space=space) for space in in_spaces],
        out_specs=[pl.BlockSpec(memory_space=space) for space in out_spaces],
        scratch_shapes=list(scratch)
        + [pltpu.SemaphoreType.DMA((copies,)), pltpu.SemaphoreType.DMA((copies,))],
        compiler_params=pltpu.CompilerParams(
            collective_id=ids.index(name), has_side_effects=True, vmem_limit_bytes=VMEM_LIMIT
        ),
        cost_estimate=pl.CostEstimate(flops=0, bytes_accessed=cost, transcendentals=0),
        name=name,
    )(*operands)


def struct(shape, dtype):
    return jax.ShapeDtypeStruct(shape, dtype)


class SharedBlock:
    def __init__(self, copies, source, target, count, ctx_count):
        _, core, _, _, self.sibling = own_place(ctx_count)
        half = source.shape[0] // 2
        rows = pl.ds(pl.multiple_of(core * half, math.gcd(half, 256)), half)
        self.copies, self.forwarded = copies, []
        self.stream = line_gather(
            copies, source.at[rows], lambda i: target.at[i, rows], count, self.arrived
        )

    def arrived(self, allowed, _, held):
        copy = self.copies.make(held, held, {"ctx": self.sibling})

        @pl.when(allowed)
        def _():
            copy.start()

        self.forwarded.append((allowed, copy))

    def wait(self):
        for allowed, copy in self.forwarded:

            @pl.when(allowed)
            def _():
                copy.wait()


def gather_weights(weight, count, ctx_count):
    rows, width = weight.shape
    chips = ctx_count // 2
    parts = chips if chips == 4 and width % (128 * chips) == 0 else 1
    half, share = rows // 2, width // parts

    def kernel(source, target, send, recv):
        copies = Copies(send, recv)
        rank = lax.axis_index("fsdp")
        place, core, chip, _, sibling = own_place(ctx_count)
        span = pl.ds(pl.multiple_of(core * half, math.gcd(half, 256)), half)
        meet(
            (ring_peers("fsdp", count) if parts > 1 else line_peers(count))
            + plane_peers(ctx_count)[:1]
            + (ring_peers("ctx", ctx_count, 2) if parts > 1 else [])
        )

        def held(origin, part):
            return target.at[origin, span, pl.ds(pl.multiple_of(part * share, 128), share)]

        mine = chip if parts > 1 else 0
        received, forwarded = [], []

        def hand(allowed, ref):
            copy = copies.make(ref, ref, {"ctx": sibling})

            @pl.when(allowed)
            def _():
                copy.start()

            forwarded.append((allowed, copy))

        def arrived(allowed, origin, ref):
            for step in range(1, parts):
                copy = copies.make(ref, ref, {"ctx": lax.rem(place + 2 * step, ctx_count)})

                @pl.when(allowed)
                def _():
                    copy.start()

                received.append((allowed, origin, lax.rem(chip + chips - step, chips), copy))
            hand(allowed, ref)

        if parts > 1:
            pushes = []
            for step in range(1, count):
                copy = copies.make(
                    source.at[span, pl.ds(pl.multiple_of(mine * share, 128), share)],
                    held(rank, mine),
                    {"fsdp": lax.rem(rank + step, count)},
                )
                copy.start()
                pushes.append(copy)
            target[rank] = source[...]
            for step, copy in enumerate(pushes, 1):
                copy.wait()
                origin = lax.rem(rank + count - step, count)
                arrived(rank >= 0, origin, held(origin, mine))
        else:
            target[rank] = source[...]
            together(
                line_gather(copies, held(rank, mine), lambda i: held(i, mine), count, arrived)
            )
        for allowed, origin, part, copy in received:

            @pl.when(allowed)
            def _():
                copy.wait()

            hand(allowed, held(origin, part))
        for allowed, copy in forwarded:

            @pl.when(allowed)
            def _():
                copy.wait()

    (full,) = remote_call(
        kernel, "weights", [struct((count, rows, width), weight.dtype)], [weight],
        [pltpu.VMEM], [pltpu.VMEM], [], 2 * count + 4 * count * (2 * parts - 1),
        count * rows * width * 4,
    )
    return full.reshape(count * rows, width)


def gather_keys(block, weights, count, ctx_count):
    rows, width = block.shape
    half = rows // 2

    def kernel(*refs):
        own, *sources = refs[: 1 + len(weights)]
        gathered, *targets = refs[1 + len(weights) : 2 + 2 * len(weights)]
        local, send, recv = refs[2 + 2 * len(weights) :]
        copies = Copies(send, recv)
        rank, place = lax.axis_index("fsdp"), lax.axis_index("ctx")
        spans = (pl.ds(0, rows), pl.ds(0, half), pl.ds(half, half))
        meet(line_peers(count) + plane_peers(ctx_count))
        kept = [pltpu.make_async_copy(own, gathered.at[place], local.at[0])]
        kept += [
            pltpu.make_async_copy(source, target.at[rank], local.at[1 + i])
            for i, (source, target) in enumerate(zip(sources, targets))
        ]
        for copy in kept:
            copy.start()
        blocks = [SharedBlock(copies, s, t, count, ctx_count) for s, t in zip(sources, targets)]
        together(
            plane_gather(
                copies,
                lambda part: own.at[spans[part]],
                lambda i, part: gathered.at[i, spans[part]],
                ctx_count,
            ),
            *[b.stream for b in blocks],
        )
        for b in blocks:
            b.wait()
        for copy in kept:
            copy.wait()

    results = [struct((ctx_count, rows, width), block.dtype)]
    results += [struct((count,) + w.shape, w.dtype) for w in weights]
    gathered, *full = remote_call(
        kernel, "keys", results, [block, *weights],
        [pltpu.VMEM] * (1 + len(weights)), [pl.ANY] * (1 + len(weights)),
        [pltpu.SemaphoreType.DMA((1 + len(weights),))],
        16 + 2 * ctx_count + 4 * count * len(weights),
        ctx_count * rows * width * 4,
    )
    return gathered.reshape(ctx_count * rows, width), [
        f.reshape(count * f.shape[1], f.shape[2]) for f in full
    ]


def gather_rows(block, notes, count):
    def kernel(own, own_notes, gathered, all_notes, local, send, recv):
        copies = Copies(send, recv)
        rank = lax.axis_index("fsdp")
        meet(ring_peers("fsdp", count))
        kept = [
            pltpu.make_async_copy(own, gathered.at[rank], local.at[0]),
            pltpu.make_async_copy(own_notes, all_notes.at[rank], local.at[1]),
        ]
        for copy in kept:
            copy.start()
        together(
            push_gather(copies, own_notes, lambda step: all_notes.at[rank], "fsdp", count),
            line_gather(copies, own, lambda i: gathered.at[i], count),
        )
        for copy in kept:
            copy.wait()

    return remote_call(
        kernel, "rows",
        [struct((count,) + block.shape, block.dtype), struct((count,) + notes.shape, notes.dtype)],
        [block, notes], [pltpu.VMEM] * 2, [pl.ANY] * 2, [pltpu.SemaphoreType.DMA((2,))],
        4 * count, count * block.size * 4,
    )


def reduce_rows(parts, notes, shared, count, ctx_count):
    _, rows, width = parts.shape

    def kernel(given, given_notes, own, total, notes_total, all_shared,
               passing, landing, noted, send, recv):
        copies = Copies(send, recv)
        rank, place = lax.axis_index("fsdp"), lax.axis_index("ctx")
        meet(ring_peers("fsdp", count) + ring_peers("ctx", ctx_count))
        pushes, spread = [], []
        for step in range(1, count):
            peer = lax.rem(rank + step, count)
            copy = copies.make(given_notes.at[peer], noted.at[step - 1], {"fsdp": peer})
            copy.start()
            pushes.append(copy)
        for step in range(1, ctx_count):
            copy = copies.make(own, all_shared.at[place], {"ctx": lax.rem(place + step, ctx_count)})
            copy.start()
            spread.append(copy)
        all_shared[place] = own[...]
        together(
            line_reduce(copies, lambda d: given.at[d], passing, landing, count, total)
        )
        sums = given_notes[rank]
        for step, copy in enumerate(pushes):
            copy.wait()
            sums = sums + noted[step]
        notes_total[...] = sums
        for copy in spread:
            copy.wait()

    return remote_call(
        kernel, "row_sums",
        [
            struct((rows, width), jnp.float32),
            struct(notes.shape[1:], notes.dtype),
            struct((ctx_count,) + shared.shape, shared.dtype),
        ],
        [parts, notes, shared], [pltpu.VMEM] * 3, [pltpu.VMEM] * 3,
        [
            pltpu.VMEM((2, count - 1, rows, width), parts.dtype),
            pltpu.VMEM((2, count - 1, rows, width), parts.dtype),
            pltpu.VMEM((count - 1,) + notes.shape[1:], notes.dtype),
        ],
        4 * count + ctx_count, count * rows * width * 4,
    )


def reduce_keys(parts, row_parts, count, ctx_count):
    _, _, rows, width = parts.shape
    chips = ctx_count // 2
    lands = (6, 1, rows, width) if chips == 4 else (chips - 1, 2, rows, width)

    def kernel(given, given_rows, total, rows_total, met, paired, passing, landing,
               row_passing, row_landing, send, recv):
        copies = Copies(send, recv)
        _, core, _, _, sibling = own_place(ctx_count)
        spans = (pl.ds(0, 2), pl.ds(0, 1), pl.ds(1, 1))
        meet(ring_peers("fsdp", count) + plane_peers(ctx_count))
        exchanged = []
        for q in range(chips):
            for kind in range(2):
                copy = copies.make(
                    given.at[kind, 2 * q + 1 - core], met.at[q, kind], {"ctx": sibling}
                )
                copy.start()
                exchanged.append((q, kind, copy))

        def finish(part, value):
            total[spans[part]] = value

        def planes():
            yield
            for q, kind, copy in exchanged:
                copy.wait_recv()
                paired[q, kind] = (
                    given[kind, 2 * q + core].astype(jnp.float32)
                    + met[q, kind].astype(jnp.float32)
                ).astype(paired.dtype)
            yield from plane_reduce(
                copies, lambda q, part: paired.at[q, spans[part]],
                passing, landing, ctx_count, finish,
            )

        together(
            planes(),
            line_reduce(
                copies, lambda d: given_rows.at[d], row_passing, row_landing, count, rows_total
            ),
        )
        for _, _, copy in exchanged:
            copy.wait_send()

    _, row_count, row_width = row_parts.shape
    return remote_call(
        kernel, "key_sums",
        [struct((2, rows, width), jnp.float32), struct((row_count, row_width), jnp.float32)],
        [parts, row_parts], [pltpu.VMEM] * 2, [pltpu.VMEM] * 2,
        [
            pltpu.VMEM((chips, 2, rows, width), parts.dtype),
            pltpu.VMEM((chips, 2, rows, width), parts.dtype),
            pltpu.VMEM((2, 1, rows, width), parts.dtype),
            pltpu.VMEM(lands, parts.dtype),
            pltpu.VMEM((2, count - 1, row_count, row_width), parts.dtype),
            pltpu.VMEM((2, count - 1, row_count, row_width), parts.dtype),
        ],
        3 * chips + 8 + 2 * count, ctx_count * rows * width * 8,
    )


def reduce_weights(parts, small, half_grads, row_parts, count, ctx_count):
    _, rows, width = parts.shape
    chips = ctx_count // 2
    half, share = rows // 2, width // chips
    row_unit = math.gcd(half, 256)
    first = max(count // 2, 1)
    lands = (6, first, half, share) if chips == 4 else (chips - 1, count, half, share)

    own = half_grads.shape[0]

    def kernel(given, given_small, half_ref, given_rows, total, small_total, grads_ref, rows_total,
               row_passing, row_landing, met, paired, passing, landing, merged,
               line_passing, line_landing, line_total, own_total, small_met, small_sum,
               small_plane, small_plane_sum, small_line, send, recv):
        copies = Copies(send, recv)
        rank = lax.axis_index("fsdp")
        place, core, chip, _, sibling = own_place(ctx_count)
        spans = (pl.ds(0, count), pl.ds(0, first), pl.ds(first, count - first))
        mine = pl.ds(pl.multiple_of(core * half, row_unit), half)
        theirs = pl.ds(pl.multiple_of((1 - core) * half, row_unit), half)

        def columns(q):
            return pl.ds(pl.multiple_of(q * share, 128), share)

        meet(
            ring_peers("fsdp", count)
            + ring_peers("ctx", ctx_count, 2)
            + plane_peers(ctx_count)[:1]
        )
        small_pair = copies.make(given_small, small_met, {"ctx": sibling})
        small_pair.start()
        exchanged = []
        for d in range(count):
            copy = copies.make(given.at[d, theirs], met.at[d], {"ctx": sibling})
            copy.start()
            exchanged.append(copy)

        for i in range(own):
            copy = copies.make(half_ref.at[i], grads_ref.at[i], {"ctx": sibling})
            copy.start()
            exchanged.append(copy)

        def small_stream():
            small_pair.wait()
            small_sum[...] = given_small[...] + small_met[...]
            pushes = []
            for step in range(1, chips):
                copy = copies.make(
                    small_sum, small_plane.at[step - 1],
                    {"ctx": lax.rem(place + 2 * step, ctx_count)},
                )
                copy.start()
                pushes.append(copy)
            yield
            for copy in pushes:
                copy.wait()
            small_plane_sum[...] = small_sum[...] + jnp.sum(small_plane[...], axis=0)
            pushes = []
            for step in range(1, count):
                copy = copies.make(
                    small_plane_sum, small_line.at[step - 1],
                    {"fsdp": lax.rem(rank + step, count)},
                )
                copy.start()
                pushes.append(copy)
            yield
            yield
            for copy in pushes:
                copy.wait()
            small_total[...] = small_plane_sum[...] + jnp.sum(small_line[...], axis=0)

        def finish(part, value):
            merged[spans[part]] = value.astype(merged.dtype)

        def large_stream():
            for d, copy in enumerate(exchanged[:count]):
                copy.wait_recv()
                for q in range(chips):
                    paired[q, d] = (
                        given[d, mine, q * share : (q + 1) * share].astype(jnp.float32)
                        + met[d, :, q * share : (q + 1) * share].astype(jnp.float32)
                    ).astype(paired.dtype)
            yield from plane_reduce(
                copies, lambda q, part: paired.at[q, spans[part]],
                passing, landing, ctx_count, finish,
            )
            yield from line_reduce(
                copies, lambda d: merged.at[d], line_passing, line_landing, count, line_total
            )
            own_total[...] = line_total[...].astype(own_total.dtype)
            sent = []
            forwarded = []
            copy = copies.make(own_total, total.at[mine, columns(chip)], {"ctx": sibling})
            copy.start()
            forwarded.append(copy)
            for step in range(1, chips):
                copy = copies.make(
                    own_total, total.at[mine, columns(chip)],
                    {"ctx": lax.rem(place + 2 * step, ctx_count)},
                )
                copy.start()
                sent.append(copy)
            total[mine, columns(chip)] = own_total[...]
            for step, copy in enumerate(sent, 1):
                copy.wait_recv()
                held = total.at[mine, columns(lax.rem(chip + chips - step, chips))]
                copy = copies.make(held, held, {"ctx": sibling})
                copy.start()
                forwarded.append(copy)
            for copy in sent:
                copy.wait_send()
            for copy in forwarded:
                copy.wait()

        together(
            line_reduce(
                copies, lambda d: given_rows.at[d], row_passing, row_landing, count, rows_total
            ),
            small_stream(),
            large_stream(),
        )
        for copy in exchanged:
            copy.wait_send()
        for copy in exchanged[count:]:
            copy.wait_recv()

    kind = parts.dtype
    f32 = jnp.float32
    return remote_call(
        kernel, "totals",
        [
            struct((rows, width), kind),
            struct(small.shape, f32),
            struct(half_grads.shape, kind),
            struct(row_parts.shape[1:], f32),
        ],
        [parts, small, half_grads, row_parts],
        [pltpu.VMEM, pltpu.VMEM, pl.ANY, pltpu.VMEM],
        [pltpu.VMEM, pltpu.VMEM, pl.ANY, pltpu.VMEM],
        [
            pltpu.VMEM((2, count - 1) + row_parts.shape[1:], kind),
            pltpu.VMEM((2, count - 1) + row_parts.shape[1:], kind),
            pltpu.VMEM((count, half, width), kind),
            pltpu.VMEM((chips, count, half, share), kind),
            pltpu.VMEM((2, first, half, share), kind),
            pltpu.VMEM(lands, kind),
            pltpu.VMEM((count, half, share), kind),
            pltpu.VMEM((2, count - 1, half, share), kind),
            pltpu.VMEM((2, count - 1, half, share), kind),
            pltpu.VMEM((half, share), f32),
            pltpu.VMEM((half, share), kind),
            pltpu.VMEM(small.shape, f32),
            pltpu.VMEM(small.shape, f32),
            pltpu.VMEM((chips - 1,) + small.shape, f32),
            pltpu.VMEM(small.shape, f32),
            pltpu.VMEM((count - 1,) + small.shape, f32),
        ],
        count + 8 + 5 * count + 4 * chips + own, parts.size * 8,
    )


def local_call(kernel, name, grid, results, operands, in_specs, out_specs, scratch, flops, cost):
    return pl.pallas_call(
        kernel,
        grid=grid,
        out_shape=results,
        in_specs=in_specs,
        out_specs=out_specs,
        scratch_shapes=scratch,
        compiler_params=pltpu.CompilerParams(vmem_limit_bytes=60 * 1024 * 1024),
        cost_estimate=pl.CostEstimate(flops=flops, bytes_accessed=cost, transcendentals=0),
        name=name,
    )(*operands)


def whole_block(shape):
    return pl.BlockSpec(shape, lambda *_: (0,) * len(shape))


def product(left, right, left_dim=1, right_dim=0):
    return lax.dot_general(
        left, right, (((left_dim,), (right_dim,)), ((), ())), preferred_element_type=jnp.float32
    )


def expert_layers(routed_rows, block_rows, notes, weights):
    peers, piece_len, width = routed_rows.shape
    experts, _, units, _ = weights.shape
    capacity = piece_len // 4
    count = peers * capacity

    def kernel(routed, block, note, w, out_parts, grad_parts, dots, out_sum, grad_sum):
        expert = pl.program_id(0)
        low = jnp.bfloat16

        @pl.when(expert == 0)
        def _():
            out_sum[...] = jnp.zeros_like(out_sum)
            grad_sum[...] = jnp.zeros_like(grad_sum)
            dots[...] = jnp.zeros_like(dots)

        slots = (
            lax.broadcasted_iota(jnp.int32, (capacity, piece_len), 0) + expert * capacity
        ).astype(jnp.float32)
        hots, firsts, seconds, gates, taken, blocks = [], [], [], [], [], []
        for g in range(peers):
            first = note[g, 0:1, :] == slots
            second = note[g, 1:2, :] == slots
            gates.append(
                jnp.sum(
                    jnp.where(first, note[g, 2:3, :], 0.0)
                    + jnp.where(second, note[g, 3:4, :], 0.0),
                    axis=1,
                    keepdims=True,
                )
            )
            first, second = jnp.where(first, 1.0, 0.0), jnp.where(second, 1.0, 0.0)
            hot = (first + second).astype(low)
            taken.append(product(hot, routed[g]).astype(low))
            blocks.append(product(hot, block[g]))
            hots.append(hot)
            firsts.append(first)
            seconds.append(second)
        rows = jnp.concatenate(taken, axis=0)
        block_part = jnp.concatenate(blocks, axis=0)
        gate = jnp.concatenate(gates, axis=0)
        grad_out = (gate * block_part).astype(low)
        w_gate, w_up, w_down = w[0, 0], w[0, 1], w[0, 2]
        gate_proj = product(rows, w_gate, 1, 1)
        up_proj = product(rows, w_up, 1, 1)
        grad_hidden = product(grad_out, w_down, 1, 1)
        sigmoid = 1.0 / (1.0 + jnp.exp(-gate_proj))
        silu = gate_proj * sigmoid
        hidden = (silu * up_proj).astype(low)
        grad_gate_proj = (
            grad_hidden * up_proj * sigmoid * (1.0 + gate_proj * (1.0 - sigmoid))
        ).astype(low)
        grad_up_proj = (grad_hidden * silu).astype(low)
        expert_out = product(hidden, w_down)
        grad_in = (product(grad_gate_proj, w_gate) + product(grad_up_proj, w_up)).astype(low)
        row_dots = jnp.sum(block_part * expert_out, axis=1, keepdims=True)
        gated = (gate * expert_out).astype(low)
        for g in range(peers):
            span = slice(g * capacity, (g + 1) * capacity)
            out_sum[g] += product(hots[g], gated[span], 0, 0)
            grad_sum[g] += product(hots[g], grad_in[span], 0, 0)
            dots[g, 0:1, :] += jnp.sum(firsts[g] * row_dots[span], axis=0, keepdims=True)
            dots[g, 1:2, :] += jnp.sum(seconds[g] * row_dots[span], axis=0, keepdims=True)

        @pl.when(expert == experts - 1)
        def _():
            out_parts[...] = out_sum[...].astype(low)
            grad_parts[...] = grad_sum[...].astype(low)

    rows_shape = (peers, piece_len, width)
    low = jnp.bfloat16
    expert_block = pl.BlockSpec((1, 3, units, width), lambda e: (e, 0, 0, 0))
    return local_call(
        kernel, "experts", (experts,),
        [struct(rows_shape, low), struct(rows_shape, low),
         struct(notes.shape, jnp.float32)],
        [routed_rows, block_rows, notes, weights],
        [whole_block(rows_shape), whole_block(rows_shape), whole_block(notes.shape), expert_block],
        [whole_block(rows_shape), whole_block(rows_shape), whole_block(notes.shape)],
        [pltpu.VMEM(rows_shape, jnp.float32), pltpu.VMEM(rows_shape, jnp.float32)],
        12 * experts * count * units * width, 2 * weights.size,
    )


def expert_gradients(first, counts, routed_rows, block_rows, notes, weights):
    pieces, piece_len, width = routed_rows.shape
    experts, _, units, _ = weights.shape
    capacity = piece_len // 4
    own = experts // 2
    tile = 256
    room = pieces * capacity + tile
    batch = max(d for d in range(1, own + 1) if own % d == 0 and (d == 1 or d * room * width * 4 <= 30 << 20))
    low = jnp.bfloat16
    group = 4
    steps = pieces // group

    def kernel(start, count, routed, block, note, w, grads, final, rows, grad_rows, ends):
        turn, step = pl.program_id(0), pl.program_id(1)
        expert = start[0] + turn * batch

        @pl.when(step == 0)
        def _():
            for j in range(batch):
                ends[j] = 0

        for part in range(group):
            piece = jnp.minimum(step * group + part, pieces - 1)
            numbers = [count[piece * experts + expert + j] for j in range(batch)]

            @pl.when((step < steps) & (sum(numbers) > 0))
            def _():
                slots = (
                    lax.broadcasted_iota(jnp.int32, (batch * capacity, piece_len), 0)
                    + expert * capacity
                ).astype(jnp.float32)
                first = note[part, 0:1, :] == slots
                second = note[part, 1:2, :] == slots
                gate = jnp.sum(
                    jnp.where(first, note[part, 2:3, :], jnp.where(second, note[part, 3:4, :], 0.0)),
                    axis=1,
                    keepdims=True,
                )
                hot = jnp.where(first | second, 1.0, 0.0).astype(low)
                taken = product(hot, routed[part]).astype(low)
                grad_out = (gate * product(hot, block[part])).astype(low)
                for j in range(batch):
                    place = pl.ds(pl.multiple_of(ends[j], 16), capacity)
                    span = slice(j * capacity, (j + 1) * capacity)
                    rows[j, place, :] = taken[span]
                    grad_rows[j, place, :] = grad_out[span]
                    ends[j] += (numbers[j] + 15) // 16 * 16

        @pl.when(step >= steps)
        def _():
            j = jnp.maximum(step - steps, 0)
            end = pl.multiple_of(ends[j], 16)
            rest = pl.ds(end, tile)
            rows[j, rest, :] = jnp.zeros((tile, width), low)
            grad_rows[j, rest, :] = jnp.zeros((tile, width), low)
            def terms(index):
                place = pl.ds(pl.multiple_of(index * tile, tile), tile)
                x = rows[j, place, :]
                grad_out = grad_rows[j, place, :]
                gate_proj = product(x, w[0, 0], 1, 1)
                up_proj = product(x, w[0, 1], 1, 1)
                grad_hidden = product(grad_out, w[0, 2], 1, 1)
                sigmoid = 1.0 / (1.0 + jnp.exp(-gate_proj))
                silu = gate_proj * sigmoid
                hidden = (silu * up_proj).astype(low)
                grad_gate_proj = (
                    grad_hidden * up_proj * sigmoid * (1.0 + gate_proj * (1.0 - sigmoid))
                ).astype(low)
                grad_up_proj = (grad_hidden * silu).astype(low)
                return (
                    product(grad_gate_proj, x, 0, 0),
                    product(grad_up_proj, x, 0, 0),
                    product(hidden, grad_out, 0, 0),
                )

            for k, term in enumerate(terms(0)):
                final[0, k] = term

            def one_tile(index, _):
                for k, term in enumerate(terms(index)):
                    final[0, k] += term
                return 0

            lax.fori_loop(1, (end + tile - 1) // tile, one_tile, 0)
            grads[...] = final[...].astype(low)

    def piece_block(shape):
        return pl.BlockSpec(
            (group,) + shape[1:], lambda turn, step, *_: (jnp.minimum(step, steps - 1), 0, 0)
        )

    def local(turn, step):
        return turn * batch + jnp.maximum(step - steps, 0)

    return pl.pallas_call(
        kernel,
        grid_spec=pltpu.PrefetchScalarGridSpec(
            num_scalar_prefetch=2,
            grid=(own // batch, steps + batch),
            in_specs=[
                piece_block(routed_rows.shape),
                piece_block(block_rows.shape),
                piece_block(notes.shape),
                pl.BlockSpec(
                    (1, 3, units, width),
                    lambda turn, step, start, _: (start[0] + local(turn, step), 0, 0, 0),
                ),
            ],
            out_specs=[
                pl.BlockSpec(
                    (1, 3, units, width), lambda turn, step, *_: (local(turn, step), 0, 0, 0)
                ),
                pl.BlockSpec(
                    (1, 3, units, width),
                    lambda turn, step, start, _: (start[0] + local(turn, step), 0, 0, 0),
                ),
            ],
            scratch_shapes=[
                pltpu.VMEM((batch, room, width), low),
                pltpu.VMEM((batch, room, width), low),
                pltpu.SMEM((batch,), jnp.int32),
            ],
        ),
        out_shape=[
            struct((own, 3, units, width), low),
            struct((experts, 3, units, width), jnp.float32),
        ],
        compiler_params=pltpu.CompilerParams(vmem_limit_bytes=60 * 1024 * 1024),
        cost_estimate=pl.CostEstimate(
            flops=12 * own * pieces * capacity * units * width // 2,
            bytes_accessed=routed_rows.size * 4 + weights.size * 2,
            transcendentals=0,
        ),
        name="expert_gradients",
    )(first, counts, routed_rows, block_rows, notes, weights)


def other_gradients(first, received, final):
    own, _, units, width = received.shape
    block = (1, 1, units, width)

    def kernel(start, given, _, result):
        result[...] = given[...].astype(jnp.float32)

    return pl.pallas_call(
        kernel,
        grid_spec=pltpu.PrefetchScalarGridSpec(
            num_scalar_prefetch=1,
            grid=(own, 3),
            in_specs=[
                pl.BlockSpec(block, lambda i, k, _: (i, k, 0, 0)),
                pl.BlockSpec(memory_space=pl.ANY),
            ],
            out_specs=pl.BlockSpec(block, lambda i, k, start: (start[0] + i, k, 0, 0)),
        ),
        out_shape=struct(final.shape, jnp.float32),
        input_output_aliases={2: 0},
        compiler_params=pltpu.CompilerParams(vmem_limit_bytes=60 * 1024 * 1024),
        name="other_gradients",
    )(first, received, final)


def score_bias(length, first_row, rows, keys):
    key_place = lax.broadcasted_iota(jnp.int32, (keys, rows), 0)
    query_place = first_row + lax.broadcasted_iota(jnp.int32, (keys, rows), 1)
    return jnp.where(key_place <= jnp.minimum(query_place, length - 1), 0.0, MASKED)


def head_masks(shape):
    lane = lax.broadcasted_iota(jnp.int32, shape, 1)
    return [lane < HEAD_DIM, lane >= HEAD_DIM]


def turn_halves(values, cosines, sines):
    lane = lax.broadcasted_iota(jnp.int32, values.shape, 1)
    half = HEAD_DIM // 2
    swapped = jnp.where(
        lax.rem(lane, HEAD_DIM) < half,
        pltpu.roll(values, 2 * HEAD_DIM - half, 1),
        pltpu.roll(values, half, 1),
    )
    return values * cosines + swapped * sines


def project_keys(tokens, gain, weights, turns):
    rows, width = tokens.shape
    tile = 2 * HEAD_DIM

    def kernel(token, gain_row, weight, turn, normed, pairs):
        x = token[...].astype(jnp.float32)
        scaling = lax.rsqrt(jnp.mean(x * x, axis=1, keepdims=True) + EPSILON)
        normed[...] = (x * scaling * gain_row[...]).astype(jnp.bfloat16)
        for i in range(2 * width // tile):
            span = slice(i * tile, (i + 1) * tile)
            values = product(normed[...], weight[:, span])
            if i < width // tile:
                values = turn_halves(values, turn[0], turn[1])
            pairs[:, span] = values.astype(jnp.bfloat16)

    return pl.pallas_call(
        kernel,
        out_shape=[struct((rows, width), jnp.bfloat16), struct((rows, 2 * width), jnp.bfloat16)],
        compiler_params=pltpu.CompilerParams(vmem_limit_bytes=VMEM_LIMIT),
        name="project_keys",
    )(tokens, gain, weights, turns)


def projection_gradients(
    pair_grad, query_grad, normed, tokens, gain, turns, full_query, full_kv, mixed, grad_attention,
    grad_residual,
):
    rows, width = tokens.shape
    tile = 2 * HEAD_DIM
    low = jnp.bfloat16

    def kernel(pair, query, normed_ref, token, gain_row, turn, w_query, w_kv, mix, attention,
               residual, weight_grad, token_grad, gain_grad, projected):
        for i in range(width // tile):
            span = slice(i * tile, (i + 1) * tile)
            projected[:, span] = turn_halves(query[:, span], turn[0], -turn[1]).astype(low)
            keys = pair[0:rows, span].astype(jnp.float32)
            projected[:, width + i * tile : width + (i + 1) * tile] = turn_halves(
                keys, turn[0], -turn[1]
            ).astype(low)
        projected[:, 2 * width :] = pair[rows:, :]
        for i in range(3):
            span = slice(i * width, (i + 1) * width)
            weight_grad[:, span] = product(normed_ref[...], projected[:, span], 0, 0).astype(low)
        weight_grad[:, 3 * width :] = product(mix[...], attention[...], 0, 0).astype(low)
        grad_normed = product(projected[:, :width], w_query[...], 1, 1) + product(
            projected[:, width:], w_kv[...], 1, 1
        )
        x = token[...].astype(jnp.float32)
        scaling = lax.rsqrt(jnp.mean(x * x, axis=1, keepdims=True) + EPSILON)
        scaled = x * scaling
        gain_grad[...] = jnp.broadcast_to(
            jnp.sum(grad_normed * scaled, axis=0, keepdims=True), gain_grad.shape
        )
        grad_hat = grad_normed * gain_row[...]
        inner = jnp.mean(grad_hat * x, axis=1, keepdims=True)
        token_grad[...] = residual[...] + scaling * grad_hat - scaled * (scaling * scaling * inner)

    return pl.pallas_call(
        kernel,
        out_shape=[
            struct((width, 4 * width), low),
            struct((rows, width), jnp.float32),
            struct((8, width), jnp.float32),
        ],
        scratch_shapes=[pltpu.VMEM((rows, 3 * width), low)],
        compiler_params=pltpu.CompilerParams(vmem_limit_bytes=VMEM_LIMIT),
        name="projection_gradients",
    )(pair_grad, query_grad, normed, tokens, gain, turns, full_query, full_kv, mixed,
      grad_attention, grad_residual)


def attention_forward(places, normed, w_query, turns, pairs):
    rows, width = normed.shape
    keys = pairs.shape[0]
    tile = 2 * HEAD_DIM
    tiles = width // tile

    def kernel(place, normed_ref, weight, turn, key, value, mixed, query, sums, bias):
        step = pl.program_id(0)

        @pl.when(step == 0)
        def _():
            bias[...] = score_bias(place[0], place[1], rows, keys)

        query[...] = turn_halves(
            product(normed_ref[...], weight[...]), turn[0], turn[1]
        ).astype(query.dtype)
        own_masks = head_masks((rows, tile))
        scaled = query[...] * HEAD_DIM**-0.5
        outs = []
        for head in range(2):
            chosen = jnp.where(own_masks[head], scaled, 0)
            scores = product(key[...], chosen, 1, 1) + bias[...]
            top = jnp.max(scores, axis=0, keepdims=True)
            weights = jnp.exp(scores - top)
            total = jnp.sum(weights, axis=0, keepdims=True)
            probabilities = (weights * (1.0 / total)).astype(jnp.bfloat16)
            outs.append(product(probabilities, value[...], 0, 0))
            sums[0, head : head + 1, :] = top + jnp.log(total)
        mixed[...] = jnp.where(own_masks[0], outs[0], outs[1]).astype(mixed.dtype)

    return pl.pallas_call(
        kernel,
        grid_spec=pltpu.PrefetchScalarGridSpec(
            num_scalar_prefetch=1,
            grid=(tiles,),
            in_specs=[
                whole_block((rows, width)),
                pl.BlockSpec((width, tile), lambda i, _: (0, i)),
                whole_block(turns.shape),
                pl.BlockSpec((keys, tile), lambda i, _: (0, i)),
                pl.BlockSpec((keys, tile), lambda i, _: (0, i + tiles)),
            ],
            out_specs=[
                pl.BlockSpec((rows, tile), lambda i, _: (0, i)),
                pl.BlockSpec((rows, tile), lambda i, _: (0, i)),
                pl.BlockSpec((1, 8, rows), lambda i, _: (i, 0, 0)),
            ],
            scratch_shapes=[pltpu.VMEM((keys, rows), jnp.float32)],
        ),
        out_shape=[
            struct((rows, width), jnp.bfloat16),
            struct((rows, width), jnp.bfloat16),
            struct((tiles, 8, rows), jnp.float32),
        ],
        compiler_params=pltpu.CompilerParams(vmem_limit_bytes=60 * 1024 * 1024),
        cost_estimate=pl.CostEstimate(
            flops=4 * rows * keys * width, bytes_accessed=pairs.size * 2, transcendentals=0
        ),
        name="attention",
    )(places, normed, w_query, turns, pairs, pairs)


def attention_backward(places, queries, pairs, sums, mixed, grad_mixed):
    rows, width = queries.shape
    keys = pairs.shape[0]
    pieces = keys // rows
    tile = 2 * HEAD_DIM
    tiles = width // tile
    scaling = HEAD_DIM**-0.5

    def kernel(place, query, key, value, total, out, grad_out, grad_query, grad_pair, bias):
        step = pl.program_id(0)

        @pl.when(step == 0)
        def _():
            bias[...] = score_bias(place[0], place[1], rows, keys)

        own_masks = head_masks((rows, tile))
        scaled = query[...] * scaling
        inner = out[...].astype(jnp.float32) * grad_out[...].astype(jnp.float32)
        grads, key_sum, value_sum = [], None, None
        for head in range(2):
            chosen = jnp.where(own_masks[head], scaled, 0)
            upstream = jnp.where(own_masks[head], grad_out[...], 0)
            ones = jnp.where(own_masks[head][:8], 1.0, 0.0)
            inner_row = lax.dot_general(
                ones, inner, (((1,), (1,)), ((), ())),
                precision=HIGHEST, preferred_element_type=jnp.float32,
            )[0:1]
            scores = product(key[...], chosen, 1, 1) + bias[...]
            probabilities = jnp.exp(scores - total[0, head : head + 1, :])
            grad_probs = product(value[...], upstream, 1, 1)
            grad_scores = (probabilities * (grad_probs - inner_row)).astype(jnp.bfloat16)
            key_part = product(grad_scores, chosen)
            value_part = product(probabilities.astype(jnp.bfloat16), upstream)
            key_sum = key_part if key_sum is None else key_sum + key_part
            value_sum = value_part if value_sum is None else value_sum + value_part
            grads.append(product(grad_scores, key[...], 0, 0) * scaling)
        grad_query[...] = jnp.where(own_masks[0], grads[0], grads[1])
        grad_pair[:, 0] = key_sum.astype(grad_pair.dtype).reshape(pieces, rows, tile)
        grad_pair[:, 1] = value_sum.astype(grad_pair.dtype).reshape(pieces, rows, tile)

    own_block = pl.BlockSpec((rows, tile), lambda i, _: (0, i))
    key_block = pl.BlockSpec((keys, tile), lambda i, _: (0, i))
    low = jnp.bfloat16
    return pl.pallas_call(
        kernel,
        grid_spec=pltpu.PrefetchScalarGridSpec(
            num_scalar_prefetch=1,
            grid=(tiles,),
            in_specs=[
                own_block,
                key_block,
                pl.BlockSpec((keys, tile), lambda i, _: (0, i + tiles)),
                pl.BlockSpec((1, 8, rows), lambda i, _: (i, 0, 0)),
                own_block,
                own_block,
            ],
            out_specs=[
                own_block,
                pl.BlockSpec((pieces, 2, rows, tile), lambda i, _: (0, 0, 0, i)),
            ],
            scratch_shapes=[pltpu.VMEM((keys, rows), jnp.float32)],
        ),
        out_shape=[
            struct((rows, width), jnp.float32),
            struct((pieces, 2, rows, width), low),
        ],
        compiler_params=pltpu.CompilerParams(vmem_limit_bytes=60 * 1024 * 1024),
        cost_estimate=pl.CostEstimate(
            flops=10 * rows * keys * width, bytes_accessed=pairs.size * 4, transcendentals=0
        ),
        name="attention_back",
    )(places, queries, pairs, pairs, sums, mixed, grad_mixed)


def normalize_rows(values, gain_row):
    scaling = lax.rsqrt(jnp.mean(values * values, axis=-1, keepdims=True) + EPSILON)
    return (values * scaling * gain_row, scaling)


def normalize_back(values, scaling, gain_row, grad_out):
    grad_hat = grad_out * gain_row
    grad_gain = jnp.sum(grad_out * values * scaling, axis=(0, 1))
    grad_values = scaling * grad_hat - values * scaling**3 * jnp.mean(
        grad_hat * values, axis=-1, keepdims=True
    )
    return (grad_values, grad_gain)


def rope_angles(positions, head_size):
    half_dim = head_size // 2
    frequency = jnp.exp(
        jnp.arange(half_dim, dtype=jnp.float32) * (-2.0 * math.log(10000.0) / head_size)
    )
    return positions.astype(jnp.float32)[:, None] * frequency[None, :]


def per_device(
    tokens,
    prev_logits,
    routes,
    lengths,
    cotangent,
    w_qkv,
    w_out,
    gain_attn,
    gain_moe,
    w_router,
    w_residual,
    const_vec,
    w_expert,
):
    groups, piece_len, model_width = tokens.shape
    positions = lax.axis_index("ctx") * piece_len + jnp.arange(piece_len, dtype=jnp.int32)
    live_rows = (positions[None, :] < lengths[:, None]).astype(jnp.float32)[..., None]
    experts = w_expert.shape[0]
    capacity = piece_len // 4
    slot_count = experts * capacity
    fsdp_count, ctx_count = lax.axis_size("fsdp"), lax.axis_size("ctx")
    full_kv = gather_weights(w_qkv[:, model_width:], fsdp_count, ctx_count)
    inputs = tokens.astype(jnp.float32)
    gain_one = gain_attn.astype(jnp.float32)
    gain_two = gain_moe.astype(jnp.float32)
    angles = rope_angles(positions, HEAD_DIM)
    cosines, sines = jnp.cos(angles), jnp.sin(angles)
    turns = jnp.stack(
        [jnp.tile(cosines, (1, 4)), jnp.concatenate([-sines, sines, -sines, sines], axis=1)]
    )
    normed_one_low, own_pairs = project_keys(tokens[0], gain_one[None], full_kv, turns)
    cotangent_low = live_rows.astype(jnp.bfloat16) * cotangent
    all_pairs, (full_query, full_out) = gather_keys(
        own_pairs, [w_qkv[:, :model_width], w_out], fsdp_count, ctx_count
    )
    cotangent_rows = lax.all_gather(cotangent_low, "fsdp", axis=0, tiled=True)
    cotangent_rows, all_pairs = lax.optimization_barrier((cotangent_rows, all_pairs))
    slot_block = lax.all_gather(cotangent_rows, "ctx", axis=0, tiled=True)
    places = jnp.stack([lengths[0], lax.axis_index("ctx") * piece_len]).astype(jnp.int32)
    mixed_rows, query_rows, score_sums = attention_forward(
        places, normed_one_low, full_query, turns, all_pairs
    )
    mixed_low = mixed_rows[None]
    attention = jnp.einsum("gpd,de->gpe", mixed_low, full_out, preferred_element_type=jnp.float32)
    residual_sum = inputs + attention
    normed_two, scale_two = normalize_rows(residual_sum, gain_two)
    routed_low = normed_two.astype(jnp.bfloat16)
    routed = routed_low.astype(jnp.float32)
    logits = jnp.einsum("gpd,de->gpe", routed, w_router, precision=HIGHEST) + jnp.einsum(
        "gpi,ie->gpe", prev_logits, w_residual, precision=HIGHEST
    )
    id_range = jnp.arange(experts + 4, dtype=jnp.int32)
    route_hot = (routes[..., None] == id_range).astype(jnp.float32)
    chosen = jnp.sum(route_hot * logits[:, :, None, :], axis=-1)
    chosen_exp = jnp.exp(chosen - jnp.max(chosen, axis=-1, keepdims=True))
    gate_weights = chosen_exp / jnp.sum(chosen_exp, axis=-1, keepdims=True)
    assign_hot = route_hot[..., :experts].reshape(groups, 2 * piece_len, experts)
    earlier = jnp.cumsum(assign_hot, axis=1) - assign_hot
    order_in = jnp.sum(earlier * assign_hot, axis=-1)
    expert_of = jnp.sum(assign_hot * jnp.arange(experts, dtype=jnp.float32), axis=-1)
    is_ffn = jnp.sum(assign_hot, axis=-1)
    slot_of = jnp.where(is_ffn > 0.5, expert_of * capacity + order_in, -1.0).reshape(
        groups, piece_len, 2
    )
    live_counts = jnp.sum(
        assign_hot * jnp.repeat(live_rows[..., 0], 2, axis=1)[..., None], axis=(0, 1)
    )
    notes = jnp.concatenate(
        [
            slot_of[0].T,
            gate_weights[0].T,
            jnp.pad(live_counts[None], ((0, 3), (0, piece_len - experts))),
        ],
        axis=0,
    )
    routed_rows, all_notes = gather_rows(routed_low[0], notes, fsdp_count)
    expert_weights = w_expert.swapaxes(1, 2)
    slot_block, routed_rows = lax.optimization_barrier((slot_block, routed_rows))
    slot_routed = lax.all_gather(routed_rows, "ctx", axis=0, tiled=True)
    out_parts, grad_parts, dot_notes = expert_layers(
        routed_rows, cotangent_rows, all_notes, expert_weights
    )
    ffn_grad, dot_sums, slot_notes = reduce_rows(
        grad_parts, dot_notes, all_notes, fsdp_count, ctx_count
    )
    slot_notes = slot_notes.reshape((ctx_count * fsdp_count,) + notes.shape)
    ffn_grad = ffn_grad[None]
    copy_hot = route_hot[..., experts + 1]
    const_hot = route_hot[..., experts + 2 :]
    constants = const_vec.astype(jnp.float32)
    gate_const = jnp.sum(gate_weights[..., None] * const_hot, axis=2)
    copy_gate = jnp.sum(gate_weights * copy_hot, axis=2, keepdims=True)
    special_sum = copy_gate * routed + jnp.einsum(
        "gpj,jd->gpd", gate_const, constants, precision=HIGHEST
    )
    grad_block = live_rows * cotangent.astype(jnp.float32)
    copy_dot = jnp.sum(grad_block * routed, axis=-1)[..., None]
    const_dot = jnp.einsum("gpd,jd->gpj", grad_block, constants, precision=HIGHEST)
    grad_gate = (
        dot_sums[:2].T[None]
        + copy_hot * copy_dot
        + jnp.sum(const_hot * const_dot[:, :, None, :], axis=-1)
    )
    grad_chosen = gate_weights * (
        grad_gate - jnp.sum(gate_weights * grad_gate, axis=-1, keepdims=True)
    )
    grad_logits = jnp.sum(grad_chosen[..., None] * route_hot, axis=2)
    grad_router = jnp.einsum("gpd,gpe->de", routed, grad_logits, precision=HIGHEST)
    grad_mixing = jnp.einsum("gpi,gpe->ie", prev_logits, grad_logits, precision=HIGHEST)
    grad_previous = jnp.einsum("gpe,ie->gpi", grad_logits, w_residual, precision=HIGHEST)
    grad_const = jnp.einsum("gpd,gpj->jd", grad_block, gate_const, precision=HIGHEST)
    grad_routed = (
        jnp.einsum("gpe,de->gpd", grad_logits, w_router, precision=HIGHEST)
        + copy_gate * grad_block
        + ffn_grad
    )
    grad_norm_two, grad_gain_two = normalize_back(residual_sum, scale_two, gain_two, grad_routed)
    grad_residual = grad_block + grad_norm_two
    grad_attention = grad_residual.astype(jnp.bfloat16)
    grad_mixed = jnp.einsum(
        "gpe,de->gpd", grad_attention, full_out, preferred_element_type=jnp.float32
    ).astype(jnp.bfloat16)
    query_grad, pair_grads = attention_backward(
        places, query_rows, all_pairs, score_sums, mixed_rows, grad_mixed[0]
    )
    counts = slot_notes[:, 4, :experts].astype(jnp.int32).reshape(-1)
    counts, slot_routed, pair_grads = lax.optimization_barrier((counts, slot_routed, pair_grads))
    first_expert = lax.rem(lax.axis_index("ctx"), 2) * (experts // 2)
    half_grads, expert_half = expert_gradients(
        first_expert.astype(jnp.int32)[None], counts, slot_routed, slot_block, slot_notes, expert_weights
    )
    pair_grad = lax.psum_scatter(
        pair_grads.reshape(1, -1, model_width), "ctx", scatter_dimension=1, tiled=True
    )
    weight_parts, grad_inputs, grad_gain_one = projection_gradients(
        pair_grad[0],
        query_grad,
        normed_one_low,
        tokens[0],
        gain_one[None],
        turns,
        full_query,
        full_kv,
        mixed_rows,
        grad_attention[0],
        grad_residual[0],
    )
    grad_inputs = grad_inputs[None]
    weight_parts = weight_parts.reshape(fsdp_count, -1, 4 * model_width)
    few = experts + 4
    mixing_row = jnp.pad(grad_mixing.reshape(1, -1), ((0, 0), (0, model_width - few * few)))
    small = jnp.concatenate(
        [grad_router.T, grad_const, grad_gain_one[:1], grad_gain_two[None], mixing_row], axis=0
    )
    small = jnp.pad(small, ((0, -small.shape[0] % 8), (0, 0)))
    weight_sum, small_sum, expert_grads, ffn_sum = reduce_weights(
        weight_parts, small, half_grads, out_parts, fsdp_count, ctx_count
    )
    other_first = (experts // 2 - first_expert).astype(jnp.int32)[None]
    expert_sum = other_gradients(other_first, expert_grads, expert_half).swapaxes(1, 2)
    output = (live_rows * (residual_sum + special_sum + ffn_sum[None])).astype(jnp.bfloat16)
    weight_sum = weight_sum.astype(jnp.float32)
    wqkv_sum, wout_sum = weight_sum[:, : 3 * model_width], weight_sum[:, 3 * model_width :]
    router_sum, const_sum = small_sum[:few].T, small_sum[few : few + 2]
    gain_one_sum, gain_two_sum = small_sum[few + 2], small_sum[few + 3]
    mixing_sum = small_sum[few + 4, : few * few].reshape(few, few)
    return (
        output,
        grad_inputs,
        grad_previous,
        wqkv_sum,
        wout_sum,
        gain_one_sum,
        gain_two_sum,
        router_sum,
        mixing_sum,
        const_sum,
        expert_sum,
    )


def solution(mesh):
    return jax.shard_map(
        per_device,
        mesh=mesh,
        in_specs=(
            P("fsdp", "ctx", None),
            P("fsdp", "ctx", None),
            P("fsdp", "ctx", None),
            P("fsdp"),
            P("fsdp", "ctx", None),
            P("fsdp", None),
            P("fsdp", None),
            P(),
            P(),
            P(),
            P(),
            P(),
            P(None, "fsdp", None, None),
        ),
        out_specs=(
            P("fsdp", "ctx", None),
            P("fsdp", "ctx", None),
            P("fsdp", "ctx", None),
            P("fsdp", None),
            P("fsdp", None),
            P(),
            P(),
            P(),
            P(),
            P(),
            P(None, "fsdp", None, None),
        ),
        check_vma=False,
    )
```

```python
import itertools
import math

import jax
import jax.numpy as jnp
from jax import lax
from jax.experimental import pallas as pl
from jax.experimental.pallas import tpu as pltpu

from jax.sharding import PartitionSpec as P

HEAD_DIM = 64


EPSILON = 1e-05
MASKED = -1e30
HIGHEST = lax.Precision.HIGHEST


LOGICAL = pl.DeviceIdType.MESH
VMEM_LIMIT = 56 * 1024 * 1024


class Copies:
    def __init__(self, send, recv):
        self.send, self.recv, self.used = send, recv, 0

    def make(self, source, target, peer):
        index = self.used
        self.used += 1
        return pltpu.make_async_remote_copy(
            source, target, self.send.at[index], self.recv.at[index],
            device_id=peer, device_id_type=LOGICAL,
        )


def meet(peers):
    barrier = pltpu.get_barrier_semaphore()
    for allowed, peer in peers:
        @pl.when(allowed)
        def _():
            pl.semaphore_signal(barrier, 1, device_id=peer, device_id_type=LOGICAL)
    awaited = sum(jnp.where(allowed, 1, 0) for allowed, _ in peers)
    pl.semaphore_wait(barrier, awaited)


def together(*streams):
    for _ in itertools.zip_longest(*streams):
        pass


def within(value, count):
    return (value >= 0) & (value < count)


def bounded(value, count):
    return jnp.minimum(jnp.maximum(value, 0), count - 1)


def line_peers(count):
    rank = lax.axis_index("fsdp")
    return [
        (within(rank + way, count), {"fsdp": bounded(rank + way, count)}) for way in (1, -1)
    ]


def ring_peers(axis, count, stride=1):
    rank = lax.axis_index(axis)
    return [
        (rank >= 0, {axis: lax.rem(rank + stride * step, count)})
        for step in range(1, count // stride)
    ]


def own_place(count):
    rank = lax.axis_index("ctx")
    core = lax.rem(rank, 2)
    return rank, core, rank // 2, count // 2, rank + 1 - 2 * core


def plane_peers(count):
    rank, core, chip, chips, sibling = own_place(count)
    peers = [(rank >= 0, {"ctx": sibling})]
    if chips == 4:
        across, along, _ = square(chip)
        return peers + [(rank >= 0, {"ctx": 2 * c + core}) for c in (across, along)]
    return peers + ring_peers("ctx", count, 2)


def square(chip):
    side, row = lax.rem(chip, 2), chip // 2
    across = chip + 1 - 2 * side
    along = chip + 2 - 4 * row
    return across, along, across + 2 - 4 * row


def line_gather(copies, own, slot, count, arrived=None):
    rank = lax.axis_index("fsdp")
    sent, latest = [], {}
    for hop in range(1, count + 1):
        for way in (1, -1):
            origin = rank - way * (hop - 1)
            held = slot(bounded(origin, count))
            if hop > 1:
                earlier = latest[way]

                @pl.when(within(origin, count))
                def _():
                    earlier.wait_recv()

                if arrived is not None:
                    arrived(within(origin, count), bounded(origin, count), held)
            if hop < count:
                copy = copies.make(
                    own if hop == 1 else held, held, {"fsdp": bounded(rank + way, count)}
                )
                allowed = within(origin, count) & within(rank + way, count)

                @pl.when(allowed)
                def _():
                    copy.start()

                sent.append((allowed, copy))
                latest[way] = copy
        yield
    for allowed, copy in sent:

        @pl.when(allowed)
        def _():
            copy.wait_send()


def line_reduce(copies, part, passing, landing, count, total):
    rank = lax.axis_index("fsdp")
    sent, arriving = [], {}
    for step in range(count - 1, 0, -1):
        for side, way in enumerate((1, -1)):
            goal = rank + way * step
            allowed = within(goal, count)
            copy = copies.make(
                passing.at[side, step - 1],
                landing.at[side, step - 1],
                {"fsdp": bounded(rank + way, count)},
            )
            arriving[side, step - 1] = copy
            own = part(bounded(goal, count))
            has_earlier = allowed & within(rank - way, count)
            if step < count - 1:
                earlier = arriving[side, step]

                @pl.when(has_earlier)
                def _():
                    earlier.wait_recv()
                    passing[side, step - 1] = (
                        own[...].astype(jnp.float32) + landing[side, step].astype(jnp.float32)
                    ).astype(passing.dtype)

                @pl.when(allowed & jnp.logical_not(within(rank - way, count)))
                def _():
                    passing[side, step - 1] = own[...]
            else:

                @pl.when(allowed)
                def _():
                    passing[side, step - 1] = own[...]

            @pl.when(allowed)
            def _():
                copy.start()

            sent.append((allowed, copy))
        yield
    total[...] = part(rank)[...].astype(jnp.float32)
    for side, way in enumerate((1, -1)):
        last = arriving[side, 0]

        @pl.when(within(rank - way, count))
        def _():
            last.wait_recv()
            total[...] += landing[side, 0].astype(jnp.float32)
    for allowed, copy in sent:

        @pl.when(allowed)
        def _():
            copy.wait_send()


def push_reduce(copies, part, landing, count, total):
    rank = lax.axis_index("fsdp")
    sent = []
    for step in range(1, count):
        peer = lax.rem(rank + step, count)
        copy = copies.make(part(peer), landing.at[step - 1], {"fsdp": peer})
        copy.start()
        sent.append(copy)
    yield
    value = part(rank)[...].astype(jnp.float32)
    for step, copy in enumerate(sent):
        copy.wait_recv()
        value = value + landing[step].astype(jnp.float32)
    total[...] = value
    for copy in sent:
        copy.wait_send()


def push_gather(copies, own, slot, axis, count, stride=1):
    rank = lax.axis_index(axis)
    sent = []
    for step in range(1, count // stride):
        copy = copies.make(own, slot(step), {axis: lax.rem(rank + stride * step, count)})
        copy.start()
        sent.append(copy)
    yield
    for copy in sent:
        copy.wait()


def plane_gather(copies, own, slot, count):
    rank, core, chip, chips, sibling = own_place(count)
    sent, forwarded = [], []

    def send(source, target, peer):
        copy = copies.make(source, target, {"ctx": peer})
        copy.start()
        sent.append(copy)
        return copy

    def forward(index, part):
        copy = copies.make(slot(index, part), slot(index, part), {"ctx": sibling})
        copy.start()
        forwarded.append(copy)

    if chips == 4:
        across, along, _ = square(chip)
        side_x, side_y = 2 * across + core, 2 * along + core
        corner = 2 * square(chip)[2] + core
        first_x = send(own(1), slot(rank, 1), side_x)
        second_y = send(own(2), slot(rank, 2), side_y)
        second_x = send(own(2), slot(rank, 2), side_x)
        first_y = send(own(1), slot(rank, 1), side_y)
        copy = copies.make(own(0), slot(rank, 0), {"ctx": sibling})
        copy.start()
        forwarded.append(copy)
        yield
        first_x.wait_recv()
        corner_first = send(slot(side_x, 1), slot(side_x, 1), side_y)
        forward(side_x, 1)
        second_y.wait_recv()
        corner_second = send(slot(side_y, 2), slot(side_y, 2), side_x)
        forward(side_y, 2)
        yield
        second_x.wait_recv()
        forward(side_x, 2)
        first_y.wait_recv()
        forward(side_y, 1)
        yield
        corner_first.wait_recv()
        forward(corner, 1)
        corner_second.wait_recv()
        forward(corner, 2)
        yield
    else:
        pending = []
        for step in range(1, chips):
            peer = lax.rem(rank + 2 * step, count)
            pending.append((lax.rem(rank + count - 2 * step, count), send(own(0), slot(rank, 0), peer)))
        copy = copies.make(own(0), slot(rank, 0), {"ctx": sibling})
        copy.start()
        forwarded.append(copy)
        yield
        for origin, copy in pending:
            copy.wait_recv()
            forward(origin, 0)
        yield
    for copy in sent:
        copy.wait_send()
    for copy in forwarded:
        copy.wait()


def plane_reduce(copies, paired, passing, landing, count, finish):
    rank, core, chip, chips, sibling = own_place(count)
    sent = []

    def send(source, target, peer_chip):
        copy = copies.make(source, target, {"ctx": 2 * peer_chip + core})
        copy.start()
        sent.append(copy)
        return copy

    if chips == 4:
        across, along, corner = square(chip)
        via_x = send(paired(corner, 1), landing.at[0], across)
        via_y = send(paired(corner, 2), landing.at[1], along)
        own_x = send(paired(across, 1), landing.at[2], across)
        own_y = send(paired(along, 2), landing.at[3], along)
        yield
        via_x.wait_recv()
        passing[0] = (
            paired(along, 1)[...].astype(jnp.float32) + landing[0].astype(jnp.float32)
        ).astype(passing.dtype)
        last_first = send(passing.at[0], landing.at[4], along)
        via_y.wait_recv()
        passing[1] = (
            paired(across, 2)[...].astype(jnp.float32) + landing[1].astype(jnp.float32)
        ).astype(passing.dtype)
        last_second = send(passing.at[1], landing.at[5], across)
        yield
        own_x.wait_recv()
        own_y.wait_recv()
        last_first.wait_recv()
        last_second.wait_recv()
        for half in (1, 2):
            total = paired(chip, half)[...].astype(jnp.float32)
            total = total + landing[1 + half].astype(jnp.float32)
            total = total + landing[3 + half].astype(jnp.float32)
            finish(half, total)
    else:
        for step in range(1, chips):
            send(paired(lax.rem(chip + step, chips), 0), landing.at[step - 1], lax.rem(chip + step, chips))
        yield
        total = paired(chip, 0)[...].astype(jnp.float32)
        for step, copy in enumerate(sent):
            copy.wait_recv()
            total = total + landing[step].astype(jnp.float32)
        finish(0, total)
    for copy in sent:
        copy.wait_send()


def remote_call(kernel, name, results, operands, in_spaces, out_spaces, scratch, copies, cost):
    ids = ("weights", "keys", "rows", "row_sums", "pair_sums", "totals")
    return pl.pallas_call(
        kernel,
        out_shape=results,
        in_specs=[pl.BlockSpec(memory_space=space) for space in in_spaces],
        out_specs=[pl.BlockSpec(memory_space=space) for space in out_spaces],
        scratch_shapes=list(scratch)
        + [pltpu.SemaphoreType.DMA((copies,)), pltpu.SemaphoreType.DMA((copies,))],
        compiler_params=pltpu.CompilerParams(
            collective_id=ids.index(name), has_side_effects=True, vmem_limit_bytes=VMEM_LIMIT
        ),
        cost_estimate=pl.CostEstimate(flops=0, bytes_accessed=cost, transcendentals=0),
        name=name,
    )(*operands)


def struct(shape, dtype):
    return jax.ShapeDtypeStruct(shape, dtype)


class SharedBlock:
    def __init__(self, copies, source, target, count, ctx_count):
        _, core, _, _, self.sibling = own_place(ctx_count)
        half = source.shape[0] // 2
        rows = pl.ds(pl.multiple_of(core * half, math.gcd(half, 256)), half)
        self.copies, self.forwarded = copies, []
        self.stream = line_gather(
            copies, source.at[rows], lambda i: target.at[i, rows], count, self.arrived
        )

    def arrived(self, allowed, _, held):
        copy = self.copies.make(held, held, {"ctx": self.sibling})

        @pl.when(allowed)
        def _():
            copy.start()

        self.forwarded.append((allowed, copy))

    def wait(self):
        for allowed, copy in self.forwarded:

            @pl.when(allowed)
            def _():
                copy.wait()


def gather_weights(weight, skip, count, ctx_count):
    rows, width = weight.shape[0], weight.shape[1] - skip
    chips = ctx_count // 2
    parts = chips if chips == 4 and width % (128 * chips) == 0 else 1
    half, share = rows // 2, width // parts

    def kernel(source, target, send, recv):
        copies = Copies(send, recv)
        rank = lax.axis_index("fsdp")
        place, core, chip, _, sibling = own_place(ctx_count)
        span = pl.ds(pl.multiple_of(core * half, math.gcd(half, 256)), half)
        meet(
            (ring_peers("fsdp", count) if parts > 1 else line_peers(count))
            + plane_peers(ctx_count)[:1]
            + (ring_peers("ctx", ctx_count, 2) if parts > 1 else [])
        )

        def held(origin, part):
            return target.at[origin, span, pl.ds(pl.multiple_of(part * share, 128), share)]

        mine = chip if parts > 1 else 0
        received, forwarded = [], []

        def hand(allowed, ref):
            copy = copies.make(ref, ref, {"ctx": sibling})

            @pl.when(allowed)
            def _():
                copy.start()

            forwarded.append((allowed, copy))

        def arrived(allowed, origin, ref):
            for step in range(1, parts):
                copy = copies.make(ref, ref, {"ctx": lax.rem(place + 2 * step, ctx_count)})

                @pl.when(allowed)
                def _():
                    copy.start()

                received.append((allowed, origin, lax.rem(chip + chips - step, chips), copy))
            hand(allowed, ref)

        if parts > 1:
            pushes = []
            for step in range(1, count):
                copy = copies.make(
                    source.at[span, pl.ds(pl.multiple_of(skip + mine * share, 128), share)],
                    held(rank, mine),
                    {"fsdp": lax.rem(rank + step, count)},
                )
                copy.start()
                pushes.append(copy)
            target[rank] = source[:, skip:]
            for step, copy in enumerate(pushes, 1):
                copy.wait()
                origin = lax.rem(rank + count - step, count)
                arrived(rank >= 0, origin, held(origin, mine))
        else:
            target[rank] = source[:, skip:]
            together(
                line_gather(copies, source.at[span, pl.ds(skip, width)], lambda i: held(i, mine), count, arrived)
            )
        for allowed, origin, part, copy in received:

            @pl.when(allowed)
            def _():
                copy.wait()

            hand(allowed, held(origin, part))
        for allowed, copy in forwarded:

            @pl.when(allowed)
            def _():
                copy.wait()

    (full,) = remote_call(
        kernel, "weights", [struct((count, rows, width), weight.dtype)], [weight],
        [pltpu.VMEM], [pltpu.VMEM], [], 2 * count + 4 * count * (2 * parts - 1),
        count * rows * width * 4,
    )
    return full.reshape(count * rows, width)


def gather_keys(block, weights, wide, count, ctx_count):
    rows, width = block.shape
    half = rows // 2

    def kernel(*refs):
        own, *sources = refs[: 1 + len(weights)]
        sources = [source.at[:, pl.ds(0, wide)] for source in sources]
        gathered, *targets = refs[1 + len(weights) : 2 + 2 * len(weights)]
        local, send, recv = refs[2 + 2 * len(weights) :]
        copies = Copies(send, recv)
        rank, place = lax.axis_index("fsdp"), lax.axis_index("ctx")
        spans = (pl.ds(0, rows), pl.ds(0, half), pl.ds(half, half))
        meet(line_peers(count) + plane_peers(ctx_count))
        kept = [pltpu.make_async_copy(own, gathered.at[place], local.at[0])]
        kept += [
            pltpu.make_async_copy(source, target.at[rank], local.at[1 + i])
            for i, (source, target) in enumerate(zip(sources, targets))
        ]
        for copy in kept:
            copy.start()
        blocks = [SharedBlock(copies, s, t, count, ctx_count) for s, t in zip(sources, targets)]
        together(
            plane_gather(
                copies,
                lambda part: own.at[spans[part]],
                lambda i, part: gathered.at[i, spans[part]],
                ctx_count,
            ),
            *[b.stream for b in blocks],
        )
        for b in blocks:
            b.wait()
        for copy in kept:
            copy.wait()

    results = [struct((ctx_count, rows, width), block.dtype)]
    results += [struct((count, w.shape[0], wide), w.dtype) for w in weights]
    gathered, *full = remote_call(
        kernel, "keys", results, [block, *weights],
        [pltpu.VMEM] * (1 + len(weights)), [pl.ANY] * (1 + len(weights)),
        [pltpu.SemaphoreType.DMA((1 + len(weights),))],
        16 + 2 * ctx_count + 4 * count * len(weights),
        ctx_count * rows * width * 4,
    )
    return gathered.reshape(ctx_count * rows, width), [
        f.reshape(count * f.shape[1], f.shape[2]) for f in full
    ]


def gather_rows(block, notes, count):
    def kernel(own, own_notes, gathered, all_notes, local, send, recv):
        copies = Copies(send, recv)
        rank = lax.axis_index("fsdp")
        meet(ring_peers("fsdp", count))
        kept = [
            pltpu.make_async_copy(own, gathered.at[rank], local.at[0]),
            pltpu.make_async_copy(own_notes, all_notes.at[rank], local.at[1]),
        ]
        for copy in kept:
            copy.start()
        together(
            push_gather(copies, own_notes, lambda step: all_notes.at[rank], "fsdp", count),
            line_gather(copies, own, lambda i: gathered.at[i], count),
        )
        for copy in kept:
            copy.wait()

    return remote_call(
        kernel, "rows",
        [struct((count,) + block.shape, block.dtype), struct((count,) + notes.shape, notes.dtype)],
        [block, notes], [pltpu.VMEM] * 2, [pl.ANY] * 2, [pltpu.SemaphoreType.DMA((2,))],
        4 * count, count * block.size * 4,
    )


def reduce_rows(parts, notes, shared, count, ctx_count):
    _, rows, width = parts.shape

    def kernel(given, given_notes, own, total, notes_total, all_shared,
               passing, landing, noted, send, recv):
        copies = Copies(send, recv)
        rank, place = lax.axis_index("fsdp"), lax.axis_index("ctx")
        meet(ring_peers("fsdp", count) + ring_peers("ctx", ctx_count))
        pushes, spread = [], []
        for step in range(1, count):
            peer = lax.rem(rank + step, count)
            copy = copies.make(given_notes.at[peer], noted.at[step - 1], {"fsdp": peer})
            copy.start()
            pushes.append(copy)
        for step in range(1, ctx_count):
            copy = copies.make(own, all_shared.at[place], {"ctx": lax.rem(place + step, ctx_count)})
            copy.start()
            spread.append(copy)
        all_shared[place] = own[...]
        together(
            line_reduce(copies, lambda d: given.at[d], passing, landing, count, total)
        )
        sums = given_notes[rank]
        for step, copy in enumerate(pushes):
            copy.wait()
            sums = sums + noted[step]
        notes_total[...] = sums
        for copy in spread:
            copy.wait()

    return remote_call(
        kernel, "row_sums",
        [
            struct((rows, width), jnp.float32),
            struct(notes.shape[1:], notes.dtype),
            struct((ctx_count,) + shared.shape, shared.dtype),
        ],
        [parts, notes, shared], [pltpu.VMEM] * 3, [pltpu.VMEM] * 3,
        [
            pltpu.VMEM((2, count - 1, rows, width), parts.dtype),
            pltpu.VMEM((2, count - 1, rows, width), parts.dtype),
            pltpu.VMEM((count - 1,) + notes.shape[1:], notes.dtype),
        ],
        4 * count + ctx_count, count * rows * width * 4,
    )


def pair_sums(parts, ctx_count):
    chips = ctx_count // 2

    def kernel(given, total, met, send, recv):
        copies = Copies(send, recv)
        _, core, _, _, sibling = own_place(ctx_count)
        meet(plane_peers(ctx_count)[:1])
        exchanged = []
        for q in range(chips):
            copy = copies.make(given.at[2 * q + 1 - core], met.at[q], {"ctx": sibling})
            copy.start()
            exchanged.append(copy)
        for q, copy in enumerate(exchanged):
            copy.wait_recv()
            total[q] = (
                given[2 * q + core].astype(jnp.float32) + met[q].astype(jnp.float32)
            ).astype(total.dtype)
        for copy in exchanged:
            copy.wait_send()

    shape = (chips,) + parts.shape[1:]
    (sums,) = remote_call(
        kernel, "pair_sums", [struct(shape, parts.dtype)], [parts], [pltpu.VMEM], [pltpu.VMEM],
        [pltpu.VMEM(shape, parts.dtype)], chips, parts.size * 4,
    )
    return sums


def reduce_weights(parts, small, half_grads, row_parts, count, ctx_count):
    _, rows, width = parts.shape
    chips = ctx_count // 2
    half, share = rows // 2, width // chips
    chunks = 2 if share % 256 == 0 else 1
    piece = share // chunks
    row_unit = math.gcd(half, 256)
    first = max(count // 2, 1)
    lands = (6, first, half, piece) if chips == 4 else (chips - 1, count, half, piece)

    own = half_grads.shape[0]

    def kernel(given, given_small, half_ref, given_rows, total, small_total, grads_ref, rows_total,
               row_passing, row_landing, met, paired, passing, landing, merged,
               line_landing, line_total, own_total, small_met, small_sum,
               small_plane, small_plane_sum, small_line, send, recv):
        copies = Copies(send, recv)
        rank = lax.axis_index("fsdp")
        place, core, chip, _, sibling = own_place(ctx_count)
        spans = (pl.ds(0, count), pl.ds(0, first), pl.ds(first, count - first))
        mine = pl.ds(pl.multiple_of(core * half, row_unit), half)
        theirs = pl.ds(pl.multiple_of((1 - core) * half, row_unit), half)

        def columns(q, c):
            return pl.ds(pl.multiple_of(q * share + c * piece, 128), piece)

        meet(
            ring_peers("fsdp", count)
            + ring_peers("ctx", ctx_count, 2)
            + plane_peers(ctx_count)[:1]
        )
        small_pair = copies.make(given_small, small_met, {"ctx": sibling})
        small_pair.start()
        exchanged = []
        for d in range(count):
            copy = copies.make(given.at[d, theirs], met.at[d], {"ctx": sibling})
            copy.start()
            exchanged.append(copy)

        for i in range(own):
            copy = copies.make(half_ref.at[i], grads_ref.at[i], {"ctx": sibling})
            copy.start()
            exchanged.append(copy)

        def small_stream():
            small_pair.wait()
            small_sum[...] = given_small[...] + small_met[...]
            pushes = []
            for step in range(1, chips):
                copy = copies.make(
                    small_sum, small_plane.at[step - 1],
                    {"ctx": lax.rem(place + 2 * step, ctx_count)},
                )
                copy.start()
                pushes.append(copy)
            yield
            for copy in pushes:
                copy.wait()
            small_plane_sum[...] = small_sum[...] + jnp.sum(small_plane[...], axis=0)
            pushes = []
            for step in range(1, count):
                copy = copies.make(
                    small_plane_sum, small_line.at[step - 1],
                    {"fsdp": lax.rem(rank + step, count)},
                )
                copy.start()
                pushes.append(copy)
            yield
            yield
            for copy in pushes:
                copy.wait()
            small_total[...] = small_plane_sum[...] + jnp.sum(small_line[...], axis=0)

        def large_stream(c):
            def finish(part, value):
                merged[c, spans[part]] = value.astype(merged.dtype)

            for d, copy in enumerate(exchanged[:count]):
                if c == 0:
                    copy.wait_recv()
                for q in range(chips):
                    span = slice(q * share + c * piece, q * share + (c + 1) * piece)
                    paired[c, q, d] = (
                        given[d, mine, span].astype(jnp.float32)
                        + met[d, :, span].astype(jnp.float32)
                    ).astype(paired.dtype)
            yield from plane_reduce(
                copies, lambda q, part: paired.at[c, q, spans[part]],
                passing.at[c], landing.at[c], ctx_count, finish,
            )
            yield from push_reduce(
                copies, lambda d: merged.at[c, d], line_landing.at[c], count, line_total.at[c]
            )
            own_total[c] = line_total[c].astype(own_total.dtype)
            sent = []
            forwarded = []
            target = total.at[mine, columns(chip, c)]
            copy = copies.make(own_total.at[c], target, {"ctx": sibling})
            copy.start()
            forwarded.append(copy)
            for step in range(1, chips):
                copy = copies.make(
                    own_total.at[c], target, {"ctx": lax.rem(place + 2 * step, ctx_count)}
                )
                copy.start()
                sent.append(copy)
            total[mine, columns(chip, c)] = own_total[c]
            yield
            for step, copy in enumerate(sent, 1):
                copy.wait_recv()
                held = total.at[mine, columns(lax.rem(chip + chips - step, chips), c)]
                copy = copies.make(held, held, {"ctx": sibling})
                copy.start()
                forwarded.append(copy)
            yield
            for copy in sent:
                copy.wait_send()
            for copy in forwarded:
                copy.wait()

        together(
            line_reduce(
                copies, lambda d: given_rows.at[d], row_passing, row_landing, count, rows_total
            ),
            small_stream(),
            *[large_stream(c) for c in range(chunks)],
        )
        for copy in exchanged:
            copy.wait_send()
        for copy in exchanged[count:]:
            copy.wait_recv()

    kind = parts.dtype
    f32 = jnp.float32
    return remote_call(
        kernel, "totals",
        [
            struct((rows, width), kind),
            struct(small.shape, f32),
            struct(half_grads.shape, kind),
            struct(row_parts.shape[1:], f32),
        ],
        [parts, small, half_grads, row_parts],
        [pltpu.VMEM, pltpu.VMEM, pl.ANY, pltpu.VMEM],
        [pltpu.VMEM, pltpu.VMEM, pl.ANY, pltpu.VMEM],
        [
            pltpu.VMEM((2, count - 1) + row_parts.shape[1:], kind),
            pltpu.VMEM((2, count - 1) + row_parts.shape[1:], kind),
            pltpu.VMEM((count, half, width), kind),
            pltpu.VMEM((chunks, chips, count, half, piece), kind),
            pltpu.VMEM((chunks, 2, first, half, piece), kind),
            pltpu.VMEM((chunks,) + lands, kind),
            pltpu.VMEM((chunks, count, half, piece), kind),
            pltpu.VMEM((chunks, count - 1, half, piece), kind),
            pltpu.VMEM((chunks, half, piece), f32),
            pltpu.VMEM((chunks, half, piece), kind),
            pltpu.VMEM(small.shape, f32),
            pltpu.VMEM(small.shape, f32),
            pltpu.VMEM((chips - 1,) + small.shape, f32),
            pltpu.VMEM(small.shape, f32),
            pltpu.VMEM((count - 1,) + small.shape, f32),
        ],
        8 + 8 * count + 6 * chips + own + chunks * (8 + 2 * count + 3 * chips), parts.size * 8,
    )


def local_call(kernel, name, grid, results, operands, in_specs, out_specs, scratch, flops, cost):
    return pl.pallas_call(
        kernel,
        grid=grid,
        out_shape=results,
        in_specs=in_specs,
        out_specs=out_specs,
        scratch_shapes=scratch,
        compiler_params=pltpu.CompilerParams(vmem_limit_bytes=60 * 1024 * 1024),
        cost_estimate=pl.CostEstimate(flops=flops, bytes_accessed=cost, transcendentals=0),
        name=name,
    )(*operands)


def whole_block(shape):
    return pl.BlockSpec(shape, lambda *_: (0,) * len(shape))


def product(left, right, left_dim=1, right_dim=0):
    return lax.dot_general(
        left, right, (((left_dim,), (right_dim,)), ((), ())), preferred_element_type=jnp.float32
    )


def expert_layers(routed_rows, block_rows, notes, weights):
    peers, piece_len, width = routed_rows.shape
    experts, _, units, _ = weights.shape
    capacity = piece_len // 4
    count = peers * capacity

    slots = experts * capacity

    def kernel(routed, block, note, w, out_parts, grad_parts, dots, hots, taken, blocks, outs, ins):
        expert = pl.program_id(0)
        low = jnp.bfloat16

        def chosen(g, first_slot, number):
            places = (
                lax.broadcasted_iota(jnp.int32, (number, piece_len), 0) + first_slot
            ).astype(jnp.float32)
            return note[g, 0:1, :] == places, note[g, 1:2, :] == places

        @pl.when(expert == 0)
        def _():
            dots[...] = jnp.zeros_like(dots)
            for g in range(peers):
                first, second = chosen(g, 0, slots)
                hots[g] = jnp.where(first | second, 1.0, 0.0).astype(low)
                taken[g] = product(hots[g], routed[g]).astype(low)
                blocks[g] = product(hots[g], block[g]).astype(low)

        span = pl.ds(pl.multiple_of(expert * capacity, 16), capacity)
        firsts, seconds, gates = [], [], []
        for g in range(peers):
            first, second = chosen(g, expert * capacity, capacity)
            gates.append(
                jnp.sum(
                    jnp.where(first, note[g, 2:3, :], jnp.where(second, note[g, 3:4, :], 0.0)),
                    axis=1,
                    keepdims=True,
                )
            )
            firsts.append(first)
            seconds.append(second)
        rows = jnp.concatenate([taken[g, span, :] for g in range(peers)], axis=0)
        block_part = jnp.concatenate(
            [blocks[g, span, :] for g in range(peers)], axis=0
        ).astype(jnp.float32)
        gate = jnp.concatenate(gates, axis=0)
        grad_out = (gate * block_part).astype(low)
        w_gate, w_up, w_down = w[0, 0], w[0, 1], w[0, 2]
        gate_proj = product(rows, w_gate, 1, 1)
        up_proj = product(rows, w_up, 1, 1)
        grad_hidden = product(grad_out, w_down, 1, 1)
        sigmoid = 1.0 / (1.0 + jnp.exp(-gate_proj))
        silu = gate_proj * sigmoid
        hidden = (silu * up_proj).astype(low)
        grad_gate_proj = (
            grad_hidden * up_proj * sigmoid * (1.0 + gate_proj * (1.0 - sigmoid))
        ).astype(low)
        grad_up_proj = (grad_hidden * silu).astype(low)
        expert_out = product(hidden, w_down)
        grad_in = (product(grad_gate_proj, w_gate) + product(grad_up_proj, w_up)).astype(low)
        row_dots = jnp.sum(block_part * expert_out, axis=1, keepdims=True)
        gated = (gate * expert_out).astype(low)
        for g in range(peers):
            part = slice(g * capacity, (g + 1) * capacity)
            outs[g, span, :] = gated[part]
            ins[g, span, :] = grad_in[part]
            for k, hit in enumerate((firsts[g], seconds[g])):
                dots[g, k : k + 1, :] += jnp.sum(
                    jnp.where(hit, row_dots[part], 0.0), axis=0, keepdims=True
                )

        @pl.when(expert == experts - 1)
        def _():
            for g in range(peers):
                out_parts[g] = product(hots[g], outs[g], 0, 0).astype(low)
                grad_parts[g] = product(hots[g], ins[g], 0, 0).astype(low)

    rows_shape = (peers, piece_len, width)
    low = jnp.bfloat16
    expert_block = pl.BlockSpec((1, 3, units, width), lambda e: (e, 0, 0, 0))
    return local_call(
        kernel, "experts", (experts,),
        [struct(rows_shape, low), struct(rows_shape, low),
         struct(notes.shape, jnp.float32)],
        [routed_rows, block_rows, notes, weights],
        [whole_block(rows_shape), whole_block(rows_shape), whole_block(notes.shape), expert_block],
        [whole_block(rows_shape), whole_block(rows_shape), whole_block(notes.shape)],
        [pltpu.VMEM((peers, slots, piece_len), low)]
        + [pltpu.VMEM((peers, slots, width), low)] * 4,
        12 * experts * count * units * width, 2 * weights.size,
    )


def expert_gradients(first, counts, routed_rows, block_rows, notes, weights):
    pieces, piece_len, width = routed_rows.shape
    experts, _, units, _ = weights.shape
    capacity = piece_len // 4
    own = experts // 2
    tile = 256
    room = pieces * capacity + tile
    batch = max(d for d in range(1, own + 1) if own % d == 0 and (d == 1 or d * room * width * 4 <= 30 << 20))
    low = jnp.bfloat16
    group = 4
    steps = pieces // group

    def kernel(start, count, routed, block, note, w, grads, final, rows, grad_rows, ends):
        turn, step = pl.program_id(0), pl.program_id(1)
        expert = start[0] + turn * batch

        @pl.when(step == 0)
        def _():
            for j in range(batch):
                ends[j] = 0

        for part in range(group):
            piece = jnp.minimum(step * group + part, pieces - 1)
            numbers = [count[piece * experts + expert + j] for j in range(batch)]

            @pl.when((step < steps) & (sum(numbers) > 0))
            def _():
                slots = (
                    lax.broadcasted_iota(jnp.int32, (batch * capacity, piece_len), 0)
                    + expert * capacity
                ).astype(jnp.float32)
                first = note[part, 0:1, :] == slots
                second = note[part, 1:2, :] == slots
                gate = jnp.sum(
                    jnp.where(first, note[part, 2:3, :], jnp.where(second, note[part, 3:4, :], 0.0)),
                    axis=1,
                    keepdims=True,
                )
                hot = jnp.where(first | second, 1.0, 0.0).astype(low)
                taken = product(hot, routed[part]).astype(low)
                grad_out = (gate * product(hot, block[part])).astype(low)
                for j in range(batch):
                    place = pl.ds(pl.multiple_of(ends[j], 16), capacity)
                    span = slice(j * capacity, (j + 1) * capacity)
                    rows[j, place, :] = taken[span]
                    grad_rows[j, place, :] = grad_out[span]
                    ends[j] += (numbers[j] + 15) // 16 * 16

        @pl.when(step >= steps)
        def _():
            j = jnp.maximum(step - steps, 0)
            end = pl.multiple_of(ends[j], 16)
            rest = pl.ds(end, tile)
            rows[j, rest, :] = jnp.zeros((tile, width), low)
            grad_rows[j, rest, :] = jnp.zeros((tile, width), low)
            def terms(index):
                place = pl.ds(pl.multiple_of(index * tile, tile), tile)
                x = rows[j, place, :]
                grad_out = grad_rows[j, place, :]
                gate_proj = product(x, w[0, 0], 1, 1)
                up_proj = product(x, w[0, 1], 1, 1)
                grad_hidden = product(grad_out, w[0, 2], 1, 1)
                sigmoid = 1.0 / (1.0 + jnp.exp(-gate_proj))
                silu = gate_proj * sigmoid
                hidden = (silu * up_proj).astype(low)
                grad_gate_proj = (
                    grad_hidden * up_proj * sigmoid * (1.0 + gate_proj * (1.0 - sigmoid))
                ).astype(low)
                grad_up_proj = (grad_hidden * silu).astype(low)
                return (
                    product(grad_gate_proj, x, 0, 0),
                    product(grad_up_proj, x, 0, 0),
                    product(hidden, grad_out, 0, 0),
                )

            for k, term in enumerate(terms(0)):
                final[0, k] = term

            def one_tile(index, _):
                for k, term in enumerate(terms(index)):
                    final[0, k] += term
                return 0

            lax.fori_loop(1, (end + tile - 1) // tile, one_tile, 0)
            grads[...] = final[...].astype(low)

    def piece_block(shape):
        return pl.BlockSpec(
            (group,) + shape[1:], lambda turn, step, *_: (jnp.minimum(step, steps - 1), 0, 0)
        )

    def local(turn, step):
        return turn * batch + jnp.maximum(step - steps, 0)

    return pl.pallas_call(
        kernel,
        grid_spec=pltpu.PrefetchScalarGridSpec(
            num_scalar_prefetch=2,
            grid=(own // batch, steps + batch),
            in_specs=[
                piece_block(routed_rows.shape),
                piece_block(block_rows.shape),
                piece_block(notes.shape),
                pl.BlockSpec(
                    (1, 3, units, width),
                    lambda turn, step, start, _: (start[0] + local(turn, step), 0, 0, 0),
                ),
            ],
            out_specs=[
                pl.BlockSpec(
                    (1, 3, units, width), lambda turn, step, *_: (local(turn, step), 0, 0, 0)
                ),
                pl.BlockSpec(
                    (1, 3, units, width),
                    lambda turn, step, start, _: (start[0] + local(turn, step), 0, 0, 0),
                ),
            ],
            scratch_shapes=[
                pltpu.VMEM((batch, room, width), low),
                pltpu.VMEM((batch, room, width), low),
                pltpu.SMEM((batch,), jnp.int32),
            ],
        ),
        out_shape=[
            struct((own, 3, units, width), low),
            struct((experts, 3, units, width), jnp.float32),
        ],
        compiler_params=pltpu.CompilerParams(vmem_limit_bytes=60 * 1024 * 1024),
        cost_estimate=pl.CostEstimate(
            flops=12 * own * pieces * capacity * units * width // 2,
            bytes_accessed=routed_rows.size * 4 + weights.size * 2,
            transcendentals=0,
        ),
        name="expert_gradients",
    )(first, counts, routed_rows, block_rows, notes, weights)


def last_results(first, received, final, weight_sums, small, base, live, ffn_sum, few):
    own, _, units, width = received.shape
    rows = weight_sums.shape[0]
    block = (1, 3, units, width)
    shapes = [(rows, 3 * width), (rows, width), base.shape, (few, width), (2, width)]
    shapes += [(width,), (width,), (1, width)]

    def kernel(start, given, _, sums, few_sums, base_ref, live_ref, ffn, result, qkv, out, output,
               router, const, gain_one, gain_two, mixing):
        result[...] = given[...].astype(jnp.float32)

        @pl.when(pl.program_id(0) == 0)
        def _():
            qkv[...] = sums[:, : 3 * width].astype(jnp.float32)
            out[...] = sums[:, 3 * width :].astype(jnp.float32)
            output[...] = (base_ref[...] + live_ref[...] * ffn[...]).astype(output.dtype)
            router[...] = few_sums[0:few, :]
            const[...] = few_sums[few : few + 2, :]
            gain_one[...] = few_sums[few + 2, :]
            gain_two[...] = few_sums[few + 3, :]
            mixing[...] = few_sums[few + 4 : few + 5, :]

    return pl.pallas_call(
        kernel,
        grid_spec=pltpu.PrefetchScalarGridSpec(
            num_scalar_prefetch=1,
            grid=(own,),
            in_specs=[
                pl.BlockSpec(block, lambda i, _: (i, 0, 0, 0)),
                pl.BlockSpec(memory_space=pl.ANY),
                whole_block(weight_sums.shape),
                whole_block(small.shape),
                whole_block(base.shape),
                whole_block(live.shape),
                whole_block(ffn_sum.shape),
            ],
            out_specs=[pl.BlockSpec(block, lambda i, start: (start[0] + i, 0, 0, 0))]
            + [whole_block(shape) for shape in shapes],
        ),
        out_shape=[
            struct(final.shape, jnp.float32),
            struct(shapes[0], jnp.float32),
            struct(shapes[1], jnp.float32),
            struct(shapes[2], jnp.bfloat16),
        ]
        + [struct(shape, jnp.float32) for shape in shapes[3:]],
        input_output_aliases={2: 0},
        compiler_params=pltpu.CompilerParams(vmem_limit_bytes=VMEM_LIMIT),
        name="last_results",
    )(first, received, final, weight_sums, small, base, live, ffn_sum)


def score_bias(length, first_row, rows, keys):
    key_place = lax.broadcasted_iota(jnp.int32, (keys, rows), 0)
    query_place = first_row + lax.broadcasted_iota(jnp.int32, (keys, rows), 1)
    return jnp.where(key_place <= jnp.minimum(query_place, length - 1), 0.0, MASKED)


def head_masks(shape):
    lane = lax.broadcasted_iota(jnp.int32, shape, 1)
    return [lane < HEAD_DIM, lane >= HEAD_DIM]


def turn_halves(values, cosines, sines):
    lane = lax.broadcasted_iota(jnp.int32, values.shape, 1)
    half = HEAD_DIM // 2
    swapped = jnp.where(
        lax.rem(lane, HEAD_DIM) < half,
        pltpu.roll(values, 2 * HEAD_DIM - half, 1),
        pltpu.roll(values, half, 1),
    )
    return values * cosines + swapped * sines


def project_keys(tokens, gain, weights, turns):
    rows, width = tokens.shape
    tile = 2 * HEAD_DIM

    def kernel(token, gain_row, weight, turn, normed, pairs):
        x = token[...].astype(jnp.float32)
        scaling = lax.rsqrt(jnp.mean(x * x, axis=1, keepdims=True) + EPSILON)
        normed[...] = (x * scaling * gain_row[...]).astype(jnp.bfloat16)
        for i in range(2 * width // tile):
            span = slice(i * tile, (i + 1) * tile)
            values = product(normed[...], weight[:, span])
            if i < width // tile:
                values = turn_halves(values, turn[0], turn[1])
            pairs[:, span] = values.astype(jnp.bfloat16)

    return pl.pallas_call(
        kernel,
        out_shape=[struct((rows, width), jnp.bfloat16), struct((rows, 2 * width), jnp.bfloat16)],
        compiler_params=pltpu.CompilerParams(vmem_limit_bytes=VMEM_LIMIT),
        name="project_keys",
    )(tokens, gain, weights, turns)


def projection_gradients(
    pair_grads, query_grad, normed, tokens, gain, turns, full_query, full_kv, mixed, grad_attention,
    grad_residual,
):
    rows, width = tokens.shape
    tile = 2 * HEAD_DIM
    low = jnp.bfloat16

    def kernel(*refs):
        pairs = refs[: len(pair_grads)]
        (query, normed_ref, token, gain_row, turn, w_query, w_kv, mix, attention, residual, weight_grad,
         token_grad, gain_grad, projected) = refs[len(pair_grads) :]

        def summed(kind, span):
            return sum(pair[kind, :, span].astype(jnp.float32) for pair in pairs)

        for i in range(width // tile):
            span = slice(i * tile, (i + 1) * tile)
            projected[:, span] = turn_halves(query[:, span], turn[0], -turn[1]).astype(low)
            projected[:, width + i * tile : width + (i + 1) * tile] = turn_halves(
                summed(0, span), turn[0], -turn[1]
            ).astype(low)
            projected[:, 2 * width + i * tile : 2 * width + (i + 1) * tile] = summed(
                1, span
            ).astype(low)
        for i in range(3):
            span = slice(i * width, (i + 1) * width)
            weight_grad[:, span] = product(normed_ref[...], projected[:, span], 0, 0).astype(low)
        weight_grad[:, 3 * width :] = product(mix[...], attention[...], 0, 0).astype(low)
        grad_normed = product(projected[:, :width], w_query[...], 1, 1) + product(
            projected[:, width:], w_kv[...], 1, 1
        )
        x = token[...].astype(jnp.float32)
        scaling = lax.rsqrt(jnp.mean(x * x, axis=1, keepdims=True) + EPSILON)
        scaled = x * scaling
        gain_grad[...] = jnp.broadcast_to(
            jnp.sum(grad_normed * scaled, axis=0, keepdims=True), gain_grad.shape
        )
        grad_hat = grad_normed * gain_row[...]
        inner = jnp.mean(grad_hat * x, axis=1, keepdims=True)
        token_grad[...] = residual[...] + scaling * grad_hat - scaled * (scaling * scaling * inner)

    return pl.pallas_call(
        kernel,
        out_shape=[
            struct((width, 4 * width), low),
            struct((rows, width), jnp.float32),
            struct((8, width), jnp.float32),
        ],
        scratch_shapes=[pltpu.VMEM((rows, 3 * width), low)],
        compiler_params=pltpu.CompilerParams(vmem_limit_bytes=VMEM_LIMIT),
        name="projection_gradients",
    )(*pair_grads, query_grad, normed, tokens, gain, turns, full_query, full_kv, mixed,
      grad_attention, grad_residual)


def attention_forward(places, normed, w_query, turns, pairs):
    rows, width = normed.shape
    keys = pairs.shape[0]
    tile = 2 * HEAD_DIM
    tiles = width // tile

    def kernel(place, normed_ref, weight, turn, key, value, mixed, query, sums, bias):
        step = pl.program_id(0)

        @pl.when(step == 0)
        def _():
            bias[...] = score_bias(place[0], place[1], rows, keys)

        query[...] = turn_halves(
            product(normed_ref[...], weight[...]), turn[0], turn[1]
        ).astype(query.dtype)
        own_masks = head_masks((rows, tile))
        scaled = query[...] * HEAD_DIM**-0.5
        outs = []
        for head in range(2):
            chosen = jnp.where(own_masks[head], scaled, 0)
            scores = product(key[...], chosen, 1, 1) + bias[...]
            top = jnp.max(scores, axis=0, keepdims=True)
            weights = jnp.exp(scores - top)
            total = jnp.sum(weights, axis=0, keepdims=True)
            probabilities = (weights * (1.0 / total)).astype(jnp.bfloat16)
            outs.append(product(probabilities, value[...], 0, 0))
            sums[0, head : head + 1, :] = top + jnp.log(total)
        mixed[...] = jnp.where(own_masks[0], outs[0], outs[1]).astype(mixed.dtype)

    return pl.pallas_call(
        kernel,
        grid_spec=pltpu.PrefetchScalarGridSpec(
            num_scalar_prefetch=1,
            grid=(tiles,),
            in_specs=[
                whole_block((rows, width)),
                pl.BlockSpec((width, tile), lambda i, _: (0, i)),
                whole_block(turns.shape),
                pl.BlockSpec((keys, tile), lambda i, _: (0, i)),
                pl.BlockSpec((keys, tile), lambda i, _: (0, i + tiles)),
            ],
            out_specs=[
                pl.BlockSpec((rows, tile), lambda i, _: (0, i)),
                pl.BlockSpec((rows, tile), lambda i, _: (0, i)),
                pl.BlockSpec((1, 8, rows), lambda i, _: (i, 0, 0)),
            ],
            scratch_shapes=[pltpu.VMEM((keys, rows), jnp.float32)],
        ),
        out_shape=[
            struct((rows, width), jnp.bfloat16),
            struct((rows, width), jnp.bfloat16),
            struct((tiles, 8, rows), jnp.float32),
        ],
        compiler_params=pltpu.CompilerParams(vmem_limit_bytes=60 * 1024 * 1024),
        cost_estimate=pl.CostEstimate(
            flops=4 * rows * keys * width, bytes_accessed=pairs.size * 2, transcendentals=0
        ),
        name="attention",
    )(places, normed, w_query, turns, pairs, pairs)


def attention_backward(places, queries, pairs, sums, mixed, grad_mixed, start, stop):
    rows, width = queries.shape
    keys = pairs.shape[0]
    pieces = keys // rows
    tile = 2 * HEAD_DIM
    tiles = width // tile
    scaling = HEAD_DIM**-0.5

    def kernel(place, query, key, value, total, out, grad_out, grad_query, grad_pair, bias):
        step = pl.program_id(0)

        @pl.when(step == 0)
        def _():
            bias[...] = score_bias(place[0], place[1], rows, keys)

        own_masks = head_masks((rows, tile))
        scaled = query[...] * scaling
        inner = out[...].astype(jnp.float32) * grad_out[...].astype(jnp.float32)
        grads, key_sum, value_sum = [], None, None
        for head in range(2):
            chosen = jnp.where(own_masks[head], scaled, 0)
            upstream = jnp.where(own_masks[head], grad_out[...], 0)
            ones = jnp.where(own_masks[head][:8], 1.0, 0.0)
            inner_row = lax.dot_general(
                ones, inner, (((1,), (1,)), ((), ())),
                precision=HIGHEST, preferred_element_type=jnp.float32,
            )[0:1]
            scores = product(key[...], chosen, 1, 1) + bias[...]
            probabilities = jnp.exp(scores - total[0, head : head + 1, :])
            grad_probs = product(value[...], upstream, 1, 1)
            grad_scores = (probabilities * (grad_probs - inner_row)).astype(jnp.bfloat16)
            key_part = product(grad_scores, chosen)
            value_part = product(probabilities.astype(jnp.bfloat16), upstream)
            key_sum = key_part if key_sum is None else key_sum + key_part
            value_sum = value_part if value_sum is None else value_sum + value_part
            grads.append(product(grad_scores, key[...], 0, 0) * scaling)
        grad_query[...] = jnp.where(own_masks[0], grads[0], grads[1])
        grad_pair[:, 0] = key_sum.astype(grad_pair.dtype).reshape(pieces, rows, tile)
        grad_pair[:, 1] = value_sum.astype(grad_pair.dtype).reshape(pieces, rows, tile)

    own_block = pl.BlockSpec((rows, tile), lambda i, _: (0, i + start))
    key_block = pl.BlockSpec((keys, tile), lambda i, _: (0, i + start))
    number = stop - start
    low = jnp.bfloat16
    return pl.pallas_call(
        kernel,
        grid_spec=pltpu.PrefetchScalarGridSpec(
            num_scalar_prefetch=1,
            grid=(number,),
            in_specs=[
                own_block,
                key_block,
                pl.BlockSpec((keys, tile), lambda i, _: (0, i + start + tiles)),
                pl.BlockSpec((1, 8, rows), lambda i, _: (i + start, 0, 0)),
                own_block,
                own_block,
            ],
            out_specs=[
                pl.BlockSpec((rows, tile), lambda i, _: (0, i)),
                pl.BlockSpec((pieces, 2, rows, tile), lambda i, _: (0, 0, 0, i)),
            ],
            scratch_shapes=[pltpu.VMEM((keys, rows), jnp.float32)],
        ),
        out_shape=[
            struct((rows, number * tile), jnp.float32),
            struct((pieces, 2, rows, number * tile), low),
        ],
        compiler_params=pltpu.CompilerParams(vmem_limit_bytes=60 * 1024 * 1024),
        cost_estimate=pl.CostEstimate(
            flops=10 * rows * keys * number * tile, bytes_accessed=pairs.size * 2, transcendentals=0
        ),
        name="attention_back",
    )(places, queries, pairs, pairs, sums, mixed, grad_mixed)


def normalize_rows(values, gain_row):
    scaling = lax.rsqrt(jnp.mean(values * values, axis=-1, keepdims=True) + EPSILON)
    return (values * scaling * gain_row, scaling)


def normalize_back(values, scaling, gain_row, grad_out):
    grad_hat = grad_out * gain_row
    grad_gain = jnp.sum(grad_out * values * scaling, axis=(0, 1))
    grad_values = scaling * grad_hat - values * scaling**3 * jnp.mean(
        grad_hat * values, axis=-1, keepdims=True
    )
    return (grad_values, grad_gain)


def rope_angles(positions, head_size):
    half_dim = head_size // 2
    frequency = jnp.exp(
        jnp.arange(half_dim, dtype=jnp.float32) * (-2.0 * math.log(10000.0) / head_size)
    )
    return positions.astype(jnp.float32)[:, None] * frequency[None, :]


def per_device(
    tokens,
    prev_logits,
    routes,
    lengths,
    cotangent,
    w_qkv,
    w_out,
    gain_attn,
    gain_moe,
    w_router,
    w_residual,
    const_vec,
    w_expert,
):
    groups, piece_len, model_width = tokens.shape
    positions = lax.axis_index("ctx") * piece_len + jnp.arange(piece_len, dtype=jnp.int32)
    live_rows = (positions[None, :] < lengths[:, None]).astype(jnp.float32)[..., None]
    experts = w_expert.shape[0]
    capacity = piece_len // 4
    slot_count = experts * capacity
    fsdp_count, ctx_count = lax.axis_size("fsdp"), lax.axis_size("ctx")
    full_kv = gather_weights(w_qkv, model_width, fsdp_count, ctx_count)
    inputs = tokens.astype(jnp.float32)
    gain_one = gain_attn.astype(jnp.float32)
    gain_two = gain_moe.astype(jnp.float32)
    angles = rope_angles(positions, HEAD_DIM)
    cosines, sines = jnp.cos(angles), jnp.sin(angles)
    turns = jnp.stack(
        [jnp.tile(cosines, (1, 4)), jnp.concatenate([-sines, sines, -sines, sines], axis=1)]
    )
    normed_one_low, own_pairs = project_keys(tokens[0], gain_one[None], full_kv, turns)
    cotangent_low = live_rows.astype(jnp.bfloat16) * cotangent
    all_pairs, (full_query, full_out) = gather_keys(
        own_pairs, [w_qkv, w_out], model_width, fsdp_count, ctx_count
    )
    cotangent_rows = lax.all_gather(cotangent_low, "fsdp", axis=0, tiled=True)
    cotangent_rows, all_pairs = lax.optimization_barrier((cotangent_rows, all_pairs))
    slot_block = lax.all_gather(cotangent_rows, "ctx", axis=0, tiled=True)
    places = jnp.stack([lengths[0], lax.axis_index("ctx") * piece_len]).astype(jnp.int32)
    mixed_rows, query_rows, score_sums = attention_forward(
        places, normed_one_low, full_query, turns, all_pairs
    )
    mixed_low = mixed_rows[None]
    attention = jnp.einsum("gpd,de->gpe", mixed_low, full_out, preferred_element_type=jnp.float32)
    residual_sum = inputs + attention
    normed_two, scale_two = normalize_rows(residual_sum, gain_two)
    routed_low = normed_two.astype(jnp.bfloat16)
    routed = routed_low.astype(jnp.float32)
    logits = jnp.einsum("gpd,de->gpe", routed, w_router, precision=HIGHEST) + jnp.einsum(
        "gpi,ie->gpe", prev_logits, w_residual, precision=HIGHEST
    )
    id_range = jnp.arange(experts + 4, dtype=jnp.int32)
    route_hot = (routes[..., None] == id_range).astype(jnp.float32)
    chosen = jnp.sum(route_hot * logits[:, :, None, :], axis=-1)
    chosen_exp = jnp.exp(chosen - jnp.max(chosen, axis=-1, keepdims=True))
    gate_weights = chosen_exp / jnp.sum(chosen_exp, axis=-1, keepdims=True)
    assign_hot = route_hot[..., :experts].reshape(groups, 2 * piece_len, experts)
    earlier = jnp.cumsum(assign_hot, axis=1) - assign_hot
    order_in = jnp.sum(earlier * assign_hot, axis=-1)
    expert_of = jnp.sum(assign_hot * jnp.arange(experts, dtype=jnp.float32), axis=-1)
    is_ffn = jnp.sum(assign_hot, axis=-1)
    slot_of = jnp.where(is_ffn > 0.5, expert_of * capacity + order_in, -1.0).reshape(
        groups, piece_len, 2
    )
    live_counts = jnp.sum(
        assign_hot * jnp.repeat(live_rows[..., 0], 2, axis=1)[..., None], axis=(0, 1)
    )
    notes = jnp.concatenate(
        [
            slot_of[0].T,
            gate_weights[0].T,
            jnp.pad(live_counts[None], ((0, 3), (0, piece_len - experts))),
        ],
        axis=0,
    )
    routed_rows, all_notes = gather_rows(routed_low[0], notes, fsdp_count)
    expert_weights = w_expert.swapaxes(1, 2)
    out_parts, grad_parts, dot_notes = expert_layers(
        routed_rows, cotangent_rows, all_notes, expert_weights
    )
    slot_block, routed_rows, grad_parts = lax.optimization_barrier(
        (slot_block, routed_rows, grad_parts)
    )
    slot_routed = lax.all_gather(routed_rows, "ctx", axis=0, tiled=True)
    ffn_grad, dot_sums, slot_notes = reduce_rows(
        grad_parts, dot_notes, all_notes, fsdp_count, ctx_count
    )
    slot_notes = slot_notes.reshape((ctx_count * fsdp_count,) + notes.shape)
    ffn_grad = ffn_grad[None]
    copy_hot = route_hot[..., experts + 1]
    const_hot = route_hot[..., experts + 2 :]
    constants = const_vec.astype(jnp.float32)
    gate_const = jnp.sum(gate_weights[..., None] * const_hot, axis=2)
    copy_gate = jnp.sum(gate_weights * copy_hot, axis=2, keepdims=True)
    special_sum = copy_gate * routed + jnp.einsum(
        "gpj,jd->gpd", gate_const, constants, precision=HIGHEST
    )
    grad_block = live_rows * cotangent.astype(jnp.float32)
    copy_dot = jnp.sum(grad_block * routed, axis=-1)[..., None]
    const_dot = jnp.einsum("gpd,jd->gpj", grad_block, constants, precision=HIGHEST)
    grad_gate = (
        dot_sums[:2].T[None]
        + copy_hot * copy_dot
        + jnp.sum(const_hot * const_dot[:, :, None, :], axis=-1)
    )
    grad_chosen = gate_weights * (
        grad_gate - jnp.sum(gate_weights * grad_gate, axis=-1, keepdims=True)
    )
    grad_logits = jnp.sum(grad_chosen[..., None] * route_hot, axis=2)
    grad_router = jnp.einsum("gpd,gpe->de", routed, grad_logits, precision=HIGHEST)
    grad_mixing = jnp.einsum("gpi,gpe->ie", prev_logits, grad_logits, precision=HIGHEST)
    grad_previous = jnp.einsum("gpe,ie->gpi", grad_logits, w_residual, precision=HIGHEST)
    grad_const = jnp.einsum("gpd,gpj->jd", grad_block, gate_const, precision=HIGHEST)
    grad_routed = (
        jnp.einsum("gpe,de->gpd", grad_logits, w_router, precision=HIGHEST)
        + copy_gate * grad_block
        + ffn_grad
    )
    grad_norm_two, grad_gain_two = normalize_back(residual_sum, scale_two, gain_two, grad_routed)
    grad_residual = grad_block + grad_norm_two
    grad_attention = grad_residual.astype(jnp.bfloat16)
    grad_mixed = jnp.einsum(
        "gpe,de->gpd", grad_attention, full_out, preferred_element_type=jnp.float32
    ).astype(jnp.bfloat16)
    counts = slot_notes[:, 4, :experts].astype(jnp.int32).reshape(-1)
    first_expert = lax.rem(lax.axis_index("ctx"), 2) * (experts // 2)
    tiles = model_width // (2 * HEAD_DIM)
    query_grad, pair_grads = attention_backward(
        places, query_rows, all_pairs, score_sums, mixed_rows, grad_mixed[0], 0, tiles
    )
    chip_grads = pair_sums(pair_grads, ctx_count)
    counts, chip_grads = lax.optimization_barrier((counts, chip_grads))
    chips = ctx_count // 2
    chip = lax.axis_index("ctx") // 2
    arrived = [lax.dynamic_index_in_dim(chip_grads, chip, 0, keepdims=False)]
    for step in range(1, chips):
        block = lax.dynamic_index_in_dim(chip_grads, lax.rem(chip + step, chips), 0, keepdims=False)
        ring = [(i, (i + 2 * step) % ctx_count) for i in range(ctx_count)]
        arrived.append(lax.ppermute(block, "ctx", ring))
    half_grads, expert_half = expert_gradients(
        first_expert.astype(jnp.int32)[None], counts, slot_routed, slot_block, slot_notes, expert_weights
    )
    half_grads, query_grad = lax.optimization_barrier((half_grads, query_grad))
    weight_parts, grad_inputs, grad_gain_one = projection_gradients(
        arrived,
        query_grad,
        normed_one_low,
        tokens[0],
        gain_one[None],
        turns,
        full_query,
        full_kv,
        mixed_rows,
        grad_attention[0],
        grad_residual[0],
    )
    grad_inputs = grad_inputs[None]
    weight_parts = weight_parts.reshape(fsdp_count, -1, 4 * model_width)
    few = experts + 4
    mixing_row = jnp.pad(grad_mixing.reshape(1, -1), ((0, 0), (0, model_width - few * few)))
    small = jnp.concatenate(
        [grad_router.T, grad_const, grad_gain_one[:1], grad_gain_two[None], mixing_row], axis=0
    )
    small = jnp.pad(small, ((0, -small.shape[0] % 8), (0, 0)))
    weight_sum, small_sum, expert_grads, ffn_sum = reduce_weights(
        weight_parts, small, half_grads, out_parts, fsdp_count, ctx_count
    )
    other_first = (experts // 2 - first_expert).astype(jnp.int32)[None]
    expert_sum, wqkv_sum, wout_sum, output, router_sum, const_sum, *rest = last_results(
        other_first, expert_grads, expert_half, weight_sum, small_sum,
        (live_rows * (residual_sum + special_sum))[0], live_rows[0], ffn_sum, few,
    )
    expert_sum, output, router_sum = expert_sum.swapaxes(1, 2), output[None], router_sum.T
    gain_one_sum, gain_two_sum, mixing_row = rest
    mixing_sum = mixing_row[0, : few * few].reshape(few, few)
    return (
        output,
        grad_inputs,
        grad_previous,
        wqkv_sum,
        wout_sum,
        gain_one_sum,
        gain_two_sum,
        router_sum,
        mixing_sum,
        const_sum,
        expert_sum,
    )


def solution(mesh):
    return jax.shard_map(
        per_device,
        mesh=mesh,
        in_specs=(
            P("fsdp", "ctx", None),
            P("fsdp", "ctx", None),
            P("fsdp", "ctx", None),
            P("fsdp"),
            P("fsdp", "ctx", None),
            P("fsdp", None),
            P("fsdp", None),
            P(),
            P(),
            P(),
            P(),
            P(),
            P(None, "fsdp", None, None),
        ),
        out_specs=(
            P("fsdp", "ctx", None),
            P("fsdp", "ctx", None),
            P("fsdp", "ctx", None),
            P("fsdp", None),
            P("fsdp", None),
            P(),
            P(),
            P(),
            P(),
            P(),
            P(None, "fsdp", None, None),
        ),
        check_vma=False,
    )
```

```python
import itertools
import math

import jax
import jax.numpy as jnp
from jax import lax
from jax.experimental import pallas as pl
from jax.experimental.pallas import tpu as pltpu

from jax.sharding import PartitionSpec as P

HEAD_DIM = 64


EPSILON = 1e-05
MASKED = -1e30
HIGHEST = lax.Precision.HIGHEST


LOGICAL = pl.DeviceIdType.MESH
VMEM_LIMIT = 56 * 1024 * 1024


class Copies:
    def __init__(self, send, recv):
        self.send, self.recv, self.used = send, recv, 0

    def make(self, source, target, peer):
        index = self.used
        self.used += 1
        return pltpu.make_async_remote_copy(
            source, target, self.send.at[index], self.recv.at[index],
            device_id=peer, device_id_type=LOGICAL,
        )


def meet(peers):
    barrier = pltpu.get_barrier_semaphore()
    for allowed, peer in peers:
        @pl.when(allowed)
        def _():
            pl.semaphore_signal(barrier, 1, device_id=peer, device_id_type=LOGICAL)
    awaited = sum(jnp.where(allowed, 1, 0) for allowed, _ in peers)
    pl.semaphore_wait(barrier, awaited)


def together(*streams):
    for _ in itertools.zip_longest(*streams):
        pass


def within(value, count):
    return (value >= 0) & (value < count)


def bounded(value, count):
    return jnp.minimum(jnp.maximum(value, 0), count - 1)


def line_peers(count):
    rank = lax.axis_index("fsdp")
    return [
        (within(rank + way, count), {"fsdp": bounded(rank + way, count)}) for way in (1, -1)
    ]


def ring_peers(axis, count, stride=1):
    rank = lax.axis_index(axis)
    return [
        (rank >= 0, {axis: lax.rem(rank + stride * step, count)})
        for step in range(1, count // stride)
    ]


def own_place(count):
    rank = lax.axis_index("ctx")
    core = lax.rem(rank, 2)
    return rank, core, rank // 2, count // 2, rank + 1 - 2 * core


def plane_peers(count):
    rank, core, chip, chips, sibling = own_place(count)
    peers = [(rank >= 0, {"ctx": sibling})]
    if chips == 4:
        across, along, _ = square(chip)
        return peers + [(rank >= 0, {"ctx": 2 * c + core}) for c in (across, along)]
    return peers + ring_peers("ctx", count, 2)


def square(chip):
    side, row = lax.rem(chip, 2), chip // 2
    across = chip + 1 - 2 * side
    along = chip + 2 - 4 * row
    return across, along, across + 2 - 4 * row


def line_gather(copies, own, slot, count, arrived=None):
    rank = lax.axis_index("fsdp")
    sent, latest = [], {}
    for hop in range(1, count + 1):
        for way in (1, -1):
            origin = rank - way * (hop - 1)
            held = slot(bounded(origin, count))
            if hop > 1:
                earlier = latest[way]

                @pl.when(within(origin, count))
                def _():
                    earlier.wait_recv()

                if arrived is not None:
                    arrived(within(origin, count), bounded(origin, count), held)
            if hop < count:
                copy = copies.make(
                    own if hop == 1 else held, held, {"fsdp": bounded(rank + way, count)}
                )
                allowed = within(origin, count) & within(rank + way, count)

                @pl.when(allowed)
                def _():
                    copy.start()

                sent.append((allowed, copy))
                latest[way] = copy
        yield
    for allowed, copy in sent:

        @pl.when(allowed)
        def _():
            copy.wait_send()


def line_reduce(copies, part, passing, landing, count, total):
    rank = lax.axis_index("fsdp")
    sent, arriving = [], {}
    for step in range(count - 1, 0, -1):
        for side, way in enumerate((1, -1)):
            goal = rank + way * step
            allowed = within(goal, count)
            copy = copies.make(
                passing.at[side, step - 1],
                landing.at[side, step - 1],
                {"fsdp": bounded(rank + way, count)},
            )
            arriving[side, step - 1] = copy
            own = part(bounded(goal, count))
            has_earlier = allowed & within(rank - way, count)
            if step < count - 1:
                earlier = arriving[side, step]

                @pl.when(has_earlier)
                def _():
                    earlier.wait_recv()
                    passing[side, step - 1] = (
                        own[...].astype(jnp.float32) + landing[side, step].astype(jnp.float32)
                    ).astype(passing.dtype)

                @pl.when(allowed & jnp.logical_not(within(rank - way, count)))
                def _():
                    passing[side, step - 1] = own[...]
            else:

                @pl.when(allowed)
                def _():
                    passing[side, step - 1] = own[...]

            @pl.when(allowed)
            def _():
                copy.start()

            sent.append((allowed, copy))
        yield
    total[...] = part(rank)[...].astype(jnp.float32)
    for side, way in enumerate((1, -1)):
        last = arriving[side, 0]

        @pl.when(within(rank - way, count))
        def _():
            last.wait_recv()
            total[...] += landing[side, 0].astype(jnp.float32)
    for allowed, copy in sent:

        @pl.when(allowed)
        def _():
            copy.wait_send()


def push_reduce(copies, part, landing, count, total):
    rank = lax.axis_index("fsdp")
    sent = []
    for step in range(1, count):
        peer = lax.rem(rank + step, count)
        copy = copies.make(part(peer), landing.at[step - 1], {"fsdp": peer})
        copy.start()
        sent.append(copy)
    yield
    value = part(rank)[...].astype(jnp.float32)
    for step, copy in enumerate(sent):
        copy.wait_recv()
        value = value + landing[step].astype(jnp.float32)
    total[...] = value
    for copy in sent:
        copy.wait_send()


def push_gather(copies, own, slot, axis, count, stride=1):
    rank = lax.axis_index(axis)
    sent = []
    for step in range(1, count // stride):
        copy = copies.make(own, slot(step), {axis: lax.rem(rank + stride * step, count)})
        copy.start()
        sent.append(copy)
    yield
    for copy in sent:
        copy.wait()


def plane_gather(copies, own, slot, count):
    rank, core, chip, chips, sibling = own_place(count)
    sent, forwarded = [], []

    def send(source, target, peer):
        copy = copies.make(source, target, {"ctx": peer})
        copy.start()
        sent.append(copy)
        return copy

    def forward(index, part):
        copy = copies.make(slot(index, part), slot(index, part), {"ctx": sibling})
        copy.start()
        forwarded.append(copy)

    if chips == 4:
        across, along, _ = square(chip)
        side_x, side_y = 2 * across + core, 2 * along + core
        corner = 2 * square(chip)[2] + core
        first_x = send(own(1), slot(rank, 1), side_x)
        second_y = send(own(2), slot(rank, 2), side_y)
        second_x = send(own(2), slot(rank, 2), side_x)
        first_y = send(own(1), slot(rank, 1), side_y)
        copy = copies.make(own(0), slot(rank, 0), {"ctx": sibling})
        copy.start()
        forwarded.append(copy)
        yield
        first_x.wait_recv()
        corner_first = send(slot(side_x, 1), slot(side_x, 1), side_y)
        forward(side_x, 1)
        second_y.wait_recv()
        corner_second = send(slot(side_y, 2), slot(side_y, 2), side_x)
        forward(side_y, 2)
        yield
        second_x.wait_recv()
        forward(side_x, 2)
        first_y.wait_recv()
        forward(side_y, 1)
        yield
        corner_first.wait_recv()
        forward(corner, 1)
        corner_second.wait_recv()
        forward(corner, 2)
        yield
    else:
        pending = []
        for step in range(1, chips):
            peer = lax.rem(rank + 2 * step, count)
            pending.append((lax.rem(rank + count - 2 * step, count), send(own(0), slot(rank, 0), peer)))
        copy = copies.make(own(0), slot(rank, 0), {"ctx": sibling})
        copy.start()
        forwarded.append(copy)
        yield
        for origin, copy in pending:
            copy.wait_recv()
            forward(origin, 0)
        yield
    for copy in sent:
        copy.wait_send()
    for copy in forwarded:
        copy.wait()


def plane_reduce(copies, paired, passing, landing, count, finish):
    rank, core, chip, chips, sibling = own_place(count)
    sent = []

    def send(source, target, peer_chip):
        copy = copies.make(source, target, {"ctx": 2 * peer_chip + core})
        copy.start()
        sent.append(copy)
        return copy

    if chips == 4:
        across, along, corner = square(chip)
        via_x = send(paired(corner, 1), landing.at[0], across)
        via_y = send(paired(corner, 2), landing.at[1], along)
        own_x = send(paired(across, 1), landing.at[2], across)
        own_y = send(paired(along, 2), landing.at[3], along)
        yield
        via_x.wait_recv()
        passing[0] = (
            paired(along, 1)[...].astype(jnp.float32) + landing[0].astype(jnp.float32)
        ).astype(passing.dtype)
        last_first = send(passing.at[0], landing.at[4], along)
        via_y.wait_recv()
        passing[1] = (
            paired(across, 2)[...].astype(jnp.float32) + landing[1].astype(jnp.float32)
        ).astype(passing.dtype)
        last_second = send(passing.at[1], landing.at[5], across)
        yield
        own_x.wait_recv()
        own_y.wait_recv()
        last_first.wait_recv()
        last_second.wait_recv()
        for half in (1, 2):
            total = paired(chip, half)[...].astype(jnp.float32)
            total = total + landing[1 + half].astype(jnp.float32)
            total = total + landing[3 + half].astype(jnp.float32)
            finish(half, total)
    else:
        for step in range(1, chips):
            send(paired(lax.rem(chip + step, chips), 0), landing.at[step - 1], lax.rem(chip + step, chips))
        yield
        total = paired(chip, 0)[...].astype(jnp.float32)
        for step, copy in enumerate(sent):
            copy.wait_recv()
            total = total + landing[step].astype(jnp.float32)
        finish(0, total)
    for copy in sent:
        copy.wait_send()


def remote_call(kernel, name, results, operands, in_spaces, out_spaces, scratch, copies, cost):
    ids = ("weights", "keys", "rows", "row_sums", "pair_sums", "totals")
    return pl.pallas_call(
        kernel,
        out_shape=results,
        in_specs=[pl.BlockSpec(memory_space=space) for space in in_spaces],
        out_specs=[pl.BlockSpec(memory_space=space) for space in out_spaces],
        scratch_shapes=list(scratch)
        + [pltpu.SemaphoreType.DMA((copies,)), pltpu.SemaphoreType.DMA((copies,))],
        compiler_params=pltpu.CompilerParams(
            collective_id=ids.index(name), has_side_effects=True, vmem_limit_bytes=VMEM_LIMIT
        ),
        cost_estimate=pl.CostEstimate(flops=0, bytes_accessed=cost, transcendentals=0),
        name=name,
    )(*operands)


def struct(shape, dtype):
    return jax.ShapeDtypeStruct(shape, dtype)


class SharedBlock:
    def __init__(self, copies, source, target, count, ctx_count):
        _, core, _, _, self.sibling = own_place(ctx_count)
        half = source.shape[0] // 2
        rows = pl.ds(pl.multiple_of(core * half, math.gcd(half, 256)), half)
        self.copies, self.forwarded = copies, []
        self.stream = line_gather(
            copies, source.at[rows], lambda i: target.at[i, rows], count, self.arrived
        )

    def arrived(self, allowed, _, held):
        copy = self.copies.make(held, held, {"ctx": self.sibling})

        @pl.when(allowed)
        def _():
            copy.start()

        self.forwarded.append((allowed, copy))

    def wait(self):
        for allowed, copy in self.forwarded:

            @pl.when(allowed)
            def _():
                copy.wait()


def gather_weights(weight, skip, count, ctx_count):
    rows, width = weight.shape[0], weight.shape[1] - skip
    chips = ctx_count // 2
    parts = chips if chips == 4 and width % (128 * chips) == 0 else 1
    half, share = rows // 2, width // parts

    def kernel(source, target, send, recv):
        copies = Copies(send, recv)
        rank = lax.axis_index("fsdp")
        place, core, chip, _, sibling = own_place(ctx_count)
        span = pl.ds(pl.multiple_of(core * half, math.gcd(half, 256)), half)
        meet(
            (ring_peers("fsdp", count) if parts > 1 else line_peers(count))
            + plane_peers(ctx_count)[:1]
            + (ring_peers("ctx", ctx_count, 2) if parts > 1 else [])
        )

        def held(origin, part):
            return target.at[origin, span, pl.ds(pl.multiple_of(part * share, 128), share)]

        mine = chip if parts > 1 else 0
        received, forwarded = [], []

        def hand(allowed, ref):
            copy = copies.make(ref, ref, {"ctx": sibling})

            @pl.when(allowed)
            def _():
                copy.start()

            forwarded.append((allowed, copy))

        def arrived(allowed, origin, ref):
            for step in range(1, parts):
                copy = copies.make(ref, ref, {"ctx": lax.rem(place + 2 * step, ctx_count)})

                @pl.when(allowed)
                def _():
                    copy.start()

                received.append((allowed, origin, lax.rem(chip + chips - step, chips), copy))
            hand(allowed, ref)

        if parts > 1:
            pushes = []
            for step in range(1, count):
                copy = copies.make(
                    source.at[span, pl.ds(pl.multiple_of(skip + mine * share, 128), share)],
                    held(rank, mine),
                    {"fsdp": lax.rem(rank + step, count)},
                )
                copy.start()
                pushes.append(copy)
            target[rank] = source[:, skip:]
            for step, copy in enumerate(pushes, 1):
                copy.wait()
                origin = lax.rem(rank + count - step, count)
                arrived(rank >= 0, origin, held(origin, mine))
        else:
            target[rank] = source[:, skip:]
            together(
                line_gather(copies, source.at[span, pl.ds(skip, width)], lambda i: held(i, mine), count, arrived)
            )
        for allowed, origin, part, copy in received:

            @pl.when(allowed)
            def _():
                copy.wait()

            hand(allowed, held(origin, part))
        for allowed, copy in forwarded:

            @pl.when(allowed)
            def _():
                copy.wait()

    (full,) = remote_call(
        kernel, "weights", [struct((count, rows, width), weight.dtype)], [weight],
        [pltpu.VMEM], [pltpu.VMEM], [], 2 * count + 4 * count * (2 * parts - 1),
        count * rows * width * 4,
    )
    return full.reshape(count * rows, width)


def gather_keys(block, weights, wide, count, ctx_count):
    rows, width = block.shape
    half = rows // 2

    def kernel(*refs):
        own, *sources = refs[: 1 + len(weights)]
        sources = [source.at[:, pl.ds(0, wide)] for source in sources]
        gathered, *targets = refs[1 + len(weights) : 2 + 2 * len(weights)]
        local, send, recv = refs[2 + 2 * len(weights) :]
        copies = Copies(send, recv)
        rank, place = lax.axis_index("fsdp"), lax.axis_index("ctx")
        spans = (pl.ds(0, rows), pl.ds(0, half), pl.ds(half, half))
        meet(line_peers(count) + plane_peers(ctx_count))
        kept = [pltpu.make_async_copy(own, gathered.at[place], local.at[0])]
        kept += [
            pltpu.make_async_copy(source, target.at[rank], local.at[1 + i])
            for i, (source, target) in enumerate(zip(sources, targets))
        ]
        for copy in kept:
            copy.start()
        blocks = [SharedBlock(copies, s, t, count, ctx_count) for s, t in zip(sources, targets)]
        together(
            plane_gather(
                copies,
                lambda part: own.at[spans[part]],
                lambda i, part: gathered.at[i, spans[part]],
                ctx_count,
            ),
            *[b.stream for b in blocks],
        )
        for b in blocks:
            b.wait()
        for copy in kept:
            copy.wait()

    results = [struct((ctx_count, rows, width), block.dtype)]
    results += [struct((count, w.shape[0], wide), w.dtype) for w in weights]
    gathered, *full = remote_call(
        kernel, "keys", results, [block, *weights],
        [pltpu.VMEM] * (1 + len(weights)), [pl.ANY] * (1 + len(weights)),
        [pltpu.SemaphoreType.DMA((1 + len(weights),))],
        16 + 2 * ctx_count + 4 * count * len(weights),
        ctx_count * rows * width * 4,
    )
    return gathered.reshape(ctx_count * rows, width), [
        f.reshape(count * f.shape[1], f.shape[2]) for f in full
    ]


def gather_rows(block, notes, count):
    def kernel(own, own_notes, gathered, all_notes, local, send, recv):
        copies = Copies(send, recv)
        rank = lax.axis_index("fsdp")
        meet(ring_peers("fsdp", count))
        kept = [
            pltpu.make_async_copy(own, gathered.at[rank], local.at[0]),
            pltpu.make_async_copy(own_notes, all_notes.at[rank], local.at[1]),
        ]
        for copy in kept:
            copy.start()
        together(
            push_gather(copies, own_notes, lambda step: all_notes.at[rank], "fsdp", count),
            line_gather(copies, own, lambda i: gathered.at[i], count),
        )
        for copy in kept:
            copy.wait()

    return remote_call(
        kernel, "rows",
        [struct((count,) + block.shape, block.dtype), struct((count,) + notes.shape, notes.dtype)],
        [block, notes], [pltpu.VMEM] * 2, [pl.ANY] * 2, [pltpu.SemaphoreType.DMA((2,))],
        4 * count, count * block.size * 4,
    )


def reduce_rows(parts, notes, shared, count, ctx_count):
    _, rows, width = parts.shape

    def kernel(given, given_notes, own, total, notes_total, all_shared,
               passing, landing, noted, send, recv):
        copies = Copies(send, recv)
        rank, place = lax.axis_index("fsdp"), lax.axis_index("ctx")
        meet(ring_peers("fsdp", count) + ring_peers("ctx", ctx_count))
        pushes, spread = [], []
        for step in range(1, count):
            peer = lax.rem(rank + step, count)
            copy = copies.make(given_notes.at[peer], noted.at[step - 1], {"fsdp": peer})
            copy.start()
            pushes.append(copy)
        for step in range(1, ctx_count):
            copy = copies.make(own, all_shared.at[place], {"ctx": lax.rem(place + step, ctx_count)})
            copy.start()
            spread.append(copy)
        all_shared[place] = own[...]
        together(
            line_reduce(copies, lambda d: given.at[d], passing, landing, count, total)
        )
        sums = given_notes[rank]
        for step, copy in enumerate(pushes):
            copy.wait()
            sums = sums + noted[step]
        notes_total[...] = sums
        for copy in spread:
            copy.wait()

    return remote_call(
        kernel, "row_sums",
        [
            struct((rows, width), jnp.float32),
            struct(notes.shape[1:], notes.dtype),
            struct((ctx_count,) + shared.shape, shared.dtype),
        ],
        [parts, notes, shared], [pltpu.VMEM] * 3, [pltpu.VMEM] * 3,
        [
            pltpu.VMEM((2, count - 1, rows, width), parts.dtype),
            pltpu.VMEM((2, count - 1, rows, width), parts.dtype),
            pltpu.VMEM((count - 1,) + notes.shape[1:], notes.dtype),
        ],
        4 * count + ctx_count, count * rows * width * 4,
    )


def pair_sums(parts, early, ctx_count):
    chips = ctx_count // 2
    shape, kind = parts.shape[1:], parts.dtype
    _, rows, width = shape
    number = 0 if early is None else early.shape[1]
    if number:
        half, share = early.shape[2] // 2, width // 2
        low_half = half // 2
    else:
        low_half = 0

    def kernel(*refs):
        given, refs = refs[0], refs[1:]
        if number:
            given_early, refs = refs[0], refs[1:]
        totals, refs = refs[:chips], refs[chips:]
        met, *met_early, send, recv = refs
        copies = Copies(send, recv)
        _, core, chip, _, sibling = own_place(ctx_count)
        meet(plane_peers(ctx_count)[:1])
        exchanged = []
        for k in range(chips):
            q = lax.rem(chip + k, chips)
            copy = copies.make(given.at[2 * q + 1 - core], met.at[q], {"ctx": sibling})
            copy.start()
            exchanged.append(copy)
        if number:
            mine = pl.ds(pl.multiple_of(core * half, 16), half)
            theirs = pl.ds(pl.multiple_of((1 - core) * half, 16), half)
            for which in range(2):
                for d in range(number):
                    copy = copies.make(
                        given_early.at[which, d, theirs], met_early[0].at[which, d], {"ctx": sibling}
                    )
                    copy.start()
                    exchanged.append(copy)
        for k in range(chips):
            q = lax.rem(chip + k, chips)
            exchanged[k].wait_recv()
            for which in range(2):
                totals[k][which * rows : (which + 1) * rows, :] = (
                    given[2 * q + core, which].astype(jnp.float32)
                    + met[q, which].astype(jnp.float32)
                ).astype(kind)
        for copy in exchanged[chips:]:
            copy.wait_recv()
        if number:
            for k in range(chips):
                q = lax.rem(chip + k, chips)
                which = q // 2
                columns = pl.ds(pl.multiple_of(lax.rem(q, 2) * share, 128), share)
                for d in range(number):
                    value = (
                        given_early[which, d, mine, columns].astype(jnp.float32)
                        + met_early[0][which, d, :, columns].astype(jnp.float32)
                    ).astype(kind)
                    place = 2 * rows + d * low_half
                    totals[k][place : place + low_half, :share] = value[:low_half]
                    totals[k][place : place + low_half, share:] = value[low_half:]
        for copy in exchanged:
            copy.wait_send()

    results = [struct((2 * rows + number * low_half, width), kind)] * chips
    operands, scratch = [parts], [pltpu.VMEM((chips,) + shape, kind)]
    if number:
        operands = operands + [early]
        scratch = scratch + [pltpu.VMEM((2, number, half, width), kind)]
    return remote_call(
        kernel, "pair_sums", results, operands, [pltpu.VMEM] * len(operands),
        [pltpu.VMEM] * len(results), scratch, chips + 2 * number, parts.size * 4,
    )


def reduce_weights(parts, early, small, half_grads, row_parts, count, ctx_count):
    _, rows, width = parts.shape
    chips = ctx_count // 2
    half, share = rows // 2, width // chips
    chunks = 2 if early else 1
    row_unit = math.gcd(half, 256)
    first = max(count // 2, 1)
    lands = (6, first, half, share) if chips == 4 else (chips - 1, count, half, share)

    own = half_grads.shape[0]

    def kernel(*refs):
        early_refs, refs = refs[: len(early)], refs[len(early) :]
        (given, given_small, half_ref, given_rows, total, small_total, grads_ref, rows_total,
         row_passing, row_landing, met, paired, passing, landing, merged, line_landing, line_total,
         own_total, small_met, small_sum, small_plane, small_plane_sum, small_line, send, recv) = refs
        copies = Copies(send, recv)
        rank = lax.axis_index("fsdp")
        place, core, chip, _, sibling = own_place(ctx_count)
        spans = (pl.ds(0, count), pl.ds(0, first), pl.ds(first, count - first))
        mine = pl.ds(pl.multiple_of(core * half, row_unit), half)
        theirs = pl.ds(pl.multiple_of((1 - core) * half, row_unit), half)

        def columns(q):
            return pl.ds(pl.multiple_of(q * share, 128), share)

        meet(
            ring_peers("fsdp", count)
            + ring_peers("ctx", ctx_count, 2)
            + plane_peers(ctx_count)[:1]
        )
        small_pair = copies.make(given_small, small_met, {"ctx": sibling})
        small_pair.start()
        exchanged = []
        for d in range(count):
            copy = copies.make(given.at[d, theirs], met.at[d], {"ctx": sibling})
            copy.start()
            exchanged.append(copy)

        for i in range(own):
            copy = copies.make(half_ref.at[i], grads_ref.at[i], {"ctx": sibling})
            copy.start()
            exchanged.append(copy)

        def small_stream():
            small_pair.wait()
            small_sum[...] = given_small[...] + small_met[...]
            pushes = []
            for step in range(1, chips):
                copy = copies.make(
                    small_sum, small_plane.at[step - 1],
                    {"ctx": lax.rem(place + 2 * step, ctx_count)},
                )
                copy.start()
                pushes.append(copy)
            yield
            for copy in pushes:
                copy.wait()
            small_plane_sum[...] = small_sum[...] + jnp.sum(small_plane[...], axis=0)
            pushes = []
            for step in range(1, count):
                copy = copies.make(
                    small_plane_sum, small_line.at[step - 1],
                    {"fsdp": lax.rem(rank + step, count)},
                )
                copy.start()
                pushes.append(copy)
            yield
            yield
            for copy in pushes:
                copy.wait()
            small_total[...] = small_plane_sum[...] + jnp.sum(small_line[...], axis=0)

        def large_stream(c):
            def finish(part, value):
                merged[c, spans[part]] = value.astype(merged.dtype)

            if c > 0:
                merged[c] = early_refs[0][...]
            else:
                for d, copy in enumerate(exchanged[:count]):
                    copy.wait_recv()
                    for q in range(chips):
                        span = slice(q * share, (q + 1) * share)
                        paired[q, d] = (
                            given[d, mine, span].astype(jnp.float32)
                            + met[d, :, span].astype(jnp.float32)
                        ).astype(paired.dtype)
                yield from plane_reduce(
                    copies, lambda q, part: paired.at[q, spans[part]],
                    passing, landing, ctx_count, finish,
                )
            yield from push_reduce(
                copies, lambda d: merged.at[c, d], line_landing.at[c], count, line_total.at[c]
            )
            own_total[c] = line_total[c].astype(own_total.dtype)
            sent = []
            forwarded = []
            target = total.at[c, mine, columns(chip)]
            copy = copies.make(own_total.at[c], target, {"ctx": sibling})
            copy.start()
            forwarded.append(copy)
            for step in range(1, chips):
                copy = copies.make(
                    own_total.at[c], target, {"ctx": lax.rem(place + 2 * step, ctx_count)}
                )
                copy.start()
                sent.append(copy)
            total[c, mine, columns(chip)] = own_total[c]
            yield
            for step, copy in enumerate(sent, 1):
                copy.wait_recv()
                held = total.at[c, mine, columns(lax.rem(chip + chips - step, chips))]
                copy = copies.make(held, held, {"ctx": sibling})
                copy.start()
                forwarded.append(copy)
            yield
            for copy in sent:
                copy.wait_send()
            for copy in forwarded:
                copy.wait()

        together(
            line_reduce(
                copies, lambda d: given_rows.at[d], row_passing, row_landing, count, rows_total
            ),
            small_stream(),
            *[large_stream(c) for c in reversed(range(chunks))],
        )
        for copy in exchanged:
            copy.wait_send()
        for copy in exchanged[count:]:
            copy.wait_recv()

    kind = parts.dtype
    f32 = jnp.float32
    return remote_call(
        kernel, "totals",
        [
            struct((chunks, rows, width), kind),
            struct(small.shape, f32),
            struct(half_grads.shape, kind),
            struct(row_parts.shape[1:], f32),
        ],
        [*early, parts, small, half_grads, row_parts],
        [pltpu.VMEM] * len(early) + [pltpu.VMEM, pltpu.VMEM, pl.ANY, pltpu.VMEM],
        [pltpu.VMEM, pltpu.VMEM, pl.ANY, pltpu.VMEM],
        [
            pltpu.VMEM((2, count - 1) + row_parts.shape[1:], kind),
            pltpu.VMEM((2, count - 1) + row_parts.shape[1:], kind),
            pltpu.VMEM((count, half, width), kind),
            pltpu.VMEM((chips, count, half, share), kind),
            pltpu.VMEM((2, first, half, share), kind),
            pltpu.VMEM(lands, kind),
            pltpu.VMEM((chunks, count, half, share), kind),
            pltpu.VMEM((chunks, count - 1, half, share), kind),
            pltpu.VMEM((chunks, half, share), f32),
            pltpu.VMEM((chunks, half, share), kind),
            pltpu.VMEM(small.shape, f32),
            pltpu.VMEM(small.shape, f32),
            pltpu.VMEM((chips - 1,) + small.shape, f32),
            pltpu.VMEM(small.shape, f32),
            pltpu.VMEM((count - 1,) + small.shape, f32),
        ],
        8 + 8 * count + 6 * chips + own + chunks * (8 + 2 * count + 3 * chips), parts.size * 8,
    )


def local_call(kernel, name, grid, results, operands, in_specs, out_specs, scratch, flops, cost):
    return pl.pallas_call(
        kernel,
        grid=grid,
        out_shape=results,
        in_specs=in_specs,
        out_specs=out_specs,
        scratch_shapes=scratch,
        compiler_params=pltpu.CompilerParams(vmem_limit_bytes=60 * 1024 * 1024),
        cost_estimate=pl.CostEstimate(flops=flops, bytes_accessed=cost, transcendentals=0),
        name=name,
    )(*operands)


def whole_block(shape):
    return pl.BlockSpec(shape, lambda *_: (0,) * len(shape))


def product(left, right, left_dim=1, right_dim=0):
    return lax.dot_general(
        left, right, (((left_dim,), (right_dim,)), ((), ())), preferred_element_type=jnp.float32
    )


def expert_layers(routed_rows, block_rows, notes, weights):
    peers, piece_len, width = routed_rows.shape
    experts, _, units, _ = weights.shape
    capacity = piece_len // 4
    count = peers * capacity

    slots = experts * capacity

    def kernel(routed, block, note, w, out_parts, grad_parts, dots, hots, taken, blocks, outs, ins):
        expert = pl.program_id(0)
        low = jnp.bfloat16

        def chosen(g, first_slot, number):
            places = (
                lax.broadcasted_iota(jnp.int32, (number, piece_len), 0) + first_slot
            ).astype(jnp.float32)
            return note[g, 0:1, :] == places, note[g, 1:2, :] == places

        @pl.when(expert == 0)
        def _():
            dots[...] = jnp.zeros_like(dots)
            for g in range(peers):
                first, second = chosen(g, 0, slots)
                hots[g] = jnp.where(first | second, 1.0, 0.0).astype(low)
                taken[g] = product(hots[g], routed[g]).astype(low)
                blocks[g] = product(hots[g], block[g]).astype(low)

        span = pl.ds(pl.multiple_of(expert * capacity, 16), capacity)
        firsts, seconds, gates = [], [], []
        for g in range(peers):
            first, second = chosen(g, expert * capacity, capacity)
            gates.append(
                jnp.sum(
                    jnp.where(first, note[g, 2:3, :], jnp.where(second, note[g, 3:4, :], 0.0)),
                    axis=1,
                    keepdims=True,
                )
            )
            firsts.append(first)
            seconds.append(second)
        rows = jnp.concatenate([taken[g, span, :] for g in range(peers)], axis=0)
        block_part = jnp.concatenate(
            [blocks[g, span, :] for g in range(peers)], axis=0
        ).astype(jnp.float32)
        gate = jnp.concatenate(gates, axis=0)
        grad_out = (gate * block_part).astype(low)
        w_gate, w_up, w_down = w[0, 0], w[0, 1], w[0, 2]
        gate_proj = product(rows, w_gate, 1, 1)
        up_proj = product(rows, w_up, 1, 1)
        grad_hidden = product(grad_out, w_down, 1, 1)
        sigmoid = 1.0 / (1.0 + jnp.exp(-gate_proj))
        silu = gate_proj * sigmoid
        hidden = (silu * up_proj).astype(low)
        grad_gate_proj = (
            grad_hidden * up_proj * sigmoid * (1.0 + gate_proj * (1.0 - sigmoid))
        ).astype(low)
        grad_up_proj = (grad_hidden * silu).astype(low)
        expert_out = product(hidden, w_down)
        grad_in = (product(grad_gate_proj, w_gate) + product(grad_up_proj, w_up)).astype(low)
        row_dots = jnp.sum(block_part * expert_out, axis=1, keepdims=True)
        gated = (gate * expert_out).astype(low)
        for g in range(peers):
            part = slice(g * capacity, (g + 1) * capacity)
            outs[g, span, :] = gated[part]
            ins[g, span, :] = grad_in[part]
            for k, hit in enumerate((firsts[g], seconds[g])):
                dots[g, k : k + 1, :] += jnp.sum(
                    jnp.where(hit, row_dots[part], 0.0), axis=0, keepdims=True
                )

        @pl.when(expert == experts - 1)
        def _():
            for g in range(peers):
                out_parts[g] = product(hots[g], outs[g], 0, 0).astype(low)
                grad_parts[g] = product(hots[g], ins[g], 0, 0).astype(low)

    rows_shape = (peers, piece_len, width)
    low = jnp.bfloat16
    expert_block = pl.BlockSpec((1, 3, units, width), lambda e: (e, 0, 0, 0))
    return local_call(
        kernel, "experts", (experts,),
        [struct(rows_shape, low), struct(rows_shape, low),
         struct(notes.shape, jnp.float32)],
        [routed_rows, block_rows, notes, weights],
        [whole_block(rows_shape), whole_block(rows_shape), whole_block(notes.shape), expert_block],
        [whole_block(rows_shape), whole_block(rows_shape), whole_block(notes.shape)],
        [pltpu.VMEM((peers, slots, piece_len), low)]
        + [pltpu.VMEM((peers, slots, width), low)] * 4,
        12 * experts * count * units * width, 2 * weights.size,
    )


def expert_gradients(first, counts, routed_rows, block_rows, notes, weights):
    pieces, piece_len, width = routed_rows.shape
    experts, _, units, _ = weights.shape
    capacity = piece_len // 4
    own = experts // 2
    tile = 256
    room = pieces * capacity + tile
    batch = max(d for d in range(1, own + 1) if own % d == 0 and (d == 1 or d * room * width * 4 <= 30 << 20))
    low = jnp.bfloat16
    group = 4
    steps = pieces // group

    def kernel(start, count, routed, block, note, w, grads, final, rows, grad_rows, ends):
        turn, step = pl.program_id(0), pl.program_id(1)
        expert = start[0] + turn * batch

        @pl.when(step == 0)
        def _():
            for j in range(batch):
                ends[j] = 0

        for part in range(group):
            piece = jnp.minimum(step * group + part, pieces - 1)
            numbers = [count[piece * experts + expert + j] for j in range(batch)]

            @pl.when((step < steps) & (sum(numbers) > 0))
            def _():
                slots = (
                    lax.broadcasted_iota(jnp.int32, (batch * capacity, piece_len), 0)
                    + expert * capacity
                ).astype(jnp.float32)
                first = note[part, 0:1, :] == slots
                second = note[part, 1:2, :] == slots
                gate = jnp.sum(
                    jnp.where(first, note[part, 2:3, :], jnp.where(second, note[part, 3:4, :], 0.0)),
                    axis=1,
                    keepdims=True,
                )
                hot = jnp.where(first | second, 1.0, 0.0).astype(low)
                taken = product(hot, routed[part]).astype(low)
                grad_out = (gate * product(hot, block[part])).astype(low)
                for j in range(batch):
                    place = pl.ds(pl.multiple_of(ends[j], 16), capacity)
                    span = slice(j * capacity, (j + 1) * capacity)
                    rows[j, place, :] = taken[span]
                    grad_rows[j, place, :] = grad_out[span]
                    ends[j] += (numbers[j] + 15) // 16 * 16

        @pl.when(step >= steps)
        def _():
            j = jnp.maximum(step - steps, 0)
            end = pl.multiple_of(ends[j], 16)
            rest = pl.ds(end, tile)
            rows[j, rest, :] = jnp.zeros((tile, width), low)
            grad_rows[j, rest, :] = jnp.zeros((tile, width), low)
            def terms(index):
                place = pl.ds(pl.multiple_of(index * tile, tile), tile)
                x = rows[j, place, :]
                grad_out = grad_rows[j, place, :]
                gate_proj = product(x, w[0, 0], 1, 1)
                up_proj = product(x, w[0, 1], 1, 1)
                grad_hidden = product(grad_out, w[0, 2], 1, 1)
                sigmoid = 1.0 / (1.0 + jnp.exp(-gate_proj))
                silu = gate_proj * sigmoid
                hidden = (silu * up_proj).astype(low)
                grad_gate_proj = (
                    grad_hidden * up_proj * sigmoid * (1.0 + gate_proj * (1.0 - sigmoid))
                ).astype(low)
                grad_up_proj = (grad_hidden * silu).astype(low)
                return (
                    product(grad_gate_proj, x, 0, 0),
                    product(grad_up_proj, x, 0, 0),
                    product(hidden, grad_out, 0, 0),
                )

            for k, term in enumerate(terms(0)):
                final[0, k] = term

            def one_tile(index, _):
                for k, term in enumerate(terms(index)):
                    final[0, k] += term
                return 0

            lax.fori_loop(1, (end + tile - 1) // tile, one_tile, 0)
            grads[...] = final[...].astype(low)

    def piece_block(shape):
        return pl.BlockSpec(
            (group,) + shape[1:], lambda turn, step, *_: (jnp.minimum(step, steps - 1), 0, 0)
        )

    def local(turn, step):
        return turn * batch + jnp.maximum(step - steps, 0)

    return pl.pallas_call(
        kernel,
        grid_spec=pltpu.PrefetchScalarGridSpec(
            num_scalar_prefetch=2,
            grid=(own // batch, steps + batch),
            in_specs=[
                piece_block(routed_rows.shape),
                piece_block(block_rows.shape),
                piece_block(notes.shape),
                pl.BlockSpec(
                    (1, 3, units, width),
                    lambda turn, step, start, _: (start[0] + local(turn, step), 0, 0, 0),
                ),
            ],
            out_specs=[
                pl.BlockSpec(
                    (1, 3, units, width), lambda turn, step, *_: (local(turn, step), 0, 0, 0)
                ),
                pl.BlockSpec(
                    (1, 3, units, width),
                    lambda turn, step, start, _: (start[0] + local(turn, step), 0, 0, 0),
                ),
            ],
            scratch_shapes=[
                pltpu.VMEM((batch, room, width), low),
                pltpu.VMEM((batch, room, width), low),
                pltpu.SMEM((batch,), jnp.int32),
            ],
        ),
        out_shape=[
            struct((own, 3, units, width), low),
            struct((experts, 3, units, width), jnp.float32),
        ],
        compiler_params=pltpu.CompilerParams(vmem_limit_bytes=60 * 1024 * 1024),
        cost_estimate=pl.CostEstimate(
            flops=12 * own * pieces * capacity * units * width // 2,
            bytes_accessed=routed_rows.size * 4 + weights.size * 2,
            transcendentals=0,
        ),
        name="expert_gradients",
    )(first, counts, routed_rows, block_rows, notes, weights)


def last_results(first, received, final, weight_sums, small, base, live, ffn_sum, few):
    own, _, units, width = received.shape
    rows = weight_sums.shape[1]
    block = (1, 3, units, width)
    shapes = [(rows, 3 * width), (rows, width), base.shape, (few, width), (2, width)]
    shapes += [(width,), (width,), (1, width)]

    def kernel(start, given, _, sums, few_sums, base_ref, live_ref, ffn, result, qkv, out, output,
               router, const, gain_one, gain_two, mixing):
        result[...] = given[...].astype(jnp.float32)

        @pl.when(pl.program_id(0) == 0)
        def _():
            both = sums.shape[0] == 2
            first_part = sums[1] if both else sums[0, :, : 2 * width]
            second_part = sums[0] if both else sums[0, :, 2 * width :]
            qkv[:, :width] = first_part[:, :width].astype(jnp.float32)
            qkv[:, width:] = second_part.astype(jnp.float32)
            out[...] = first_part[:, width:].astype(jnp.float32)
            output[...] = (base_ref[...] + live_ref[...] * ffn[...]).astype(output.dtype)
            router[...] = few_sums[0:few, :]
            const[...] = few_sums[few : few + 2, :]
            gain_one[...] = few_sums[few + 2, :]
            gain_two[...] = few_sums[few + 3, :]
            mixing[...] = few_sums[few + 4 : few + 5, :]

    return pl.pallas_call(
        kernel,
        grid_spec=pltpu.PrefetchScalarGridSpec(
            num_scalar_prefetch=1,
            grid=(own,),
            in_specs=[
                pl.BlockSpec(block, lambda i, _: (i, 0, 0, 0)),
                pl.BlockSpec(memory_space=pl.ANY),
                whole_block(weight_sums.shape),
                whole_block(small.shape),
                whole_block(base.shape),
                whole_block(live.shape),
                whole_block(ffn_sum.shape),
            ],
            out_specs=[pl.BlockSpec(block, lambda i, start: (start[0] + i, 0, 0, 0))]
            + [whole_block(shape) for shape in shapes],
        ),
        out_shape=[
            struct(final.shape, jnp.float32),
            struct(shapes[0], jnp.float32),
            struct(shapes[1], jnp.float32),
            struct(shapes[2], jnp.bfloat16),
        ]
        + [struct(shape, jnp.float32) for shape in shapes[3:]],
        input_output_aliases={2: 0},
        compiler_params=pltpu.CompilerParams(vmem_limit_bytes=VMEM_LIMIT),
        name="last_results",
    )(first, received, final, weight_sums, small, base, live, ffn_sum)


def score_bias(length, first_row, rows, keys):
    key_place = lax.broadcasted_iota(jnp.int32, (keys, rows), 0)
    query_place = first_row + lax.broadcasted_iota(jnp.int32, (keys, rows), 1)
    return jnp.where(key_place <= jnp.minimum(query_place, length - 1), 0.0, MASKED)


def head_masks(shape):
    lane = lax.broadcasted_iota(jnp.int32, shape, 1)
    return [lane < HEAD_DIM, lane >= HEAD_DIM]


def turn_halves(values, cosines, sines):
    lane = lax.broadcasted_iota(jnp.int32, values.shape, 1)
    half = HEAD_DIM // 2
    swapped = jnp.where(
        lax.rem(lane, HEAD_DIM) < half,
        pltpu.roll(values, 2 * HEAD_DIM - half, 1),
        pltpu.roll(values, half, 1),
    )
    return values * cosines + swapped * sines


def project_keys(tokens, gain, weights, turns):
    rows, width = tokens.shape
    tile = 2 * HEAD_DIM

    def kernel(token, gain_row, weight, turn, normed, pairs):
        x = token[...].astype(jnp.float32)
        scaling = lax.rsqrt(jnp.mean(x * x, axis=1, keepdims=True) + EPSILON)
        normed[...] = (x * scaling * gain_row[...]).astype(jnp.bfloat16)
        for i in range(2 * width // tile):
            span = slice(i * tile, (i + 1) * tile)
            values = product(normed[...], weight[:, span])
            if i < width // tile:
                values = turn_halves(values, turn[0], turn[1])
            pairs[:, span] = values.astype(jnp.bfloat16)

    return pl.pallas_call(
        kernel,
        out_shape=[struct((rows, width), jnp.bfloat16), struct((rows, 2 * width), jnp.bfloat16)],
        compiler_params=pltpu.CompilerParams(vmem_limit_bytes=VMEM_LIMIT),
        name="project_keys",
    )(tokens, gain, weights, turns)


def projection_gradients(
    pair_grads, query_rows, normed, tokens, gain, turns, full_query, full_kv, grad_residual, number
):
    rows, width = tokens.shape
    below = (pair_grads[0].shape[0] - 2 * rows) // max(number, 1)
    tile = 2 * HEAD_DIM
    low = jnp.bfloat16

    def kernel(*refs):
        pairs = refs[: len(pair_grads)]
        (query, normed_ref, token, gain_row, turn, w_query, w_kv, residual, weight_grad, token_grad,
         gain_grad, *early, projected) = refs[len(pair_grads) :]

        def summed(kind, span):
            place = slice(kind * rows, (kind + 1) * rows)
            return sum(pair[place, span].astype(jnp.float32) for pair in pairs)

        for d in range(number):
            place = slice(2 * rows + d * below, 2 * rows + (d + 1) * below)
            value = sum(pair[place, :].astype(jnp.float32) for pair in pairs).astype(low)
            early[0][d, :below] = value[:, : width // 2]
            early[0][d, below:] = value[:, width // 2 :]

        for i in range(width // tile):
            span = slice(i * tile, (i + 1) * tile)
            projected[:, span] = turn_halves(summed(0, span), turn[0], -turn[1]).astype(low)
            projected[:, width + i * tile : width + (i + 1) * tile] = summed(1, span).astype(low)
        for i in range(2):
            span = slice(i * width, (i + 1) * width)
            weight_grad[:, span] = product(normed_ref[...], projected[:, span], 0, 0).astype(low)
        grad_normed = product(query[...], w_query[...], 1, 1) + product(
            projected[...], w_kv[...], 1, 1
        )
        x = token[...].astype(jnp.float32)
        scaling = lax.rsqrt(jnp.mean(x * x, axis=1, keepdims=True) + EPSILON)
        scaled = x * scaling
        gain_grad[...] = jnp.broadcast_to(
            jnp.sum(grad_normed * scaled, axis=0, keepdims=True), gain_grad.shape
        )
        grad_hat = grad_normed * gain_row[...]
        inner = jnp.mean(grad_hat * x, axis=1, keepdims=True)
        token_grad[...] = residual[...] + scaling * grad_hat - scaled * (scaling * scaling * inner)

    return pl.pallas_call(
        kernel,
        out_shape=[
            struct((width, 2 * width), low),
            struct((rows, width), jnp.float32),
            struct((8, width), jnp.float32),
        ]
        + ([struct((number, 2 * below, width // 2), low)] if number else []),
        scratch_shapes=[pltpu.VMEM((rows, 2 * width), low)],
        compiler_params=pltpu.CompilerParams(vmem_limit_bytes=VMEM_LIMIT),
        name="projection_gradients",
    )(*pair_grads, query_rows, normed, tokens, gain, turns, full_query, full_kv, grad_residual)


def attention_forward(places, normed, w_query, turns, pairs):
    rows, width = normed.shape
    keys = pairs.shape[0]
    chunk = min(keys, 1024)
    tile = 2 * HEAD_DIM
    tiles = width // tile

    def kernel(place, normed_ref, weight, turn, key, value, mixed, query, sums, bias):
        step = pl.program_id(0)

        @pl.when(step == 0)
        def _():
            bias[...] = score_bias(place[0], place[1], rows, keys)

        query[...] = turn_halves(
            product(normed_ref[...], weight[...]), turn[0], turn[1]
        ).astype(query.dtype)
        own_masks = head_masks((rows, tile))
        scaled = query[...] * HEAD_DIM**-0.5
        outs = []
        for head in range(2):
            chosen = jnp.where(own_masks[head], scaled, 0)
            parts = [
                product(key[place : place + chunk, :], chosen, 1, 1) + bias[place : place + chunk, :]
                for place in range(0, keys, chunk)
            ]
            top = parts[0]
            for part in parts[1:]:
                top = jnp.maximum(top, part)
            top = jnp.max(top, axis=0, keepdims=True)
            turned, total = 0.0, 0.0
            for i, part in enumerate(parts):
                weights = jnp.exp(part - top)
                total = total + jnp.sum(weights, axis=0, keepdims=True)
                turned = turned + product(
                    value[i * chunk : (i + 1) * chunk, :], weights.astype(jnp.bfloat16), 0, 0
                )
            span = slice(head * HEAD_DIM, (head + 1) * HEAD_DIM)
            outs.append(turned[span] * (1.0 / total))
            sums[0, head : head + 1, :] = top + jnp.log(total)
        mixed[...] = jnp.transpose(jnp.concatenate(outs, axis=0)).astype(mixed.dtype)

    return pl.pallas_call(
        kernel,
        grid_spec=pltpu.PrefetchScalarGridSpec(
            num_scalar_prefetch=1,
            grid=(tiles,),
            in_specs=[
                whole_block((rows, width)),
                pl.BlockSpec((width, tile), lambda i, _: (0, i)),
                whole_block(turns.shape),
                pl.BlockSpec((keys, tile), lambda i, _: (0, i)),
                pl.BlockSpec((keys, tile), lambda i, _: (0, i + tiles)),
            ],
            out_specs=[
                pl.BlockSpec((rows, tile), lambda i, _: (0, i)),
                pl.BlockSpec((rows, tile), lambda i, _: (0, i)),
                pl.BlockSpec((1, 8, rows), lambda i, _: (i, 0, 0)),
            ],
            scratch_shapes=[pltpu.VMEM((keys, rows), jnp.float32)],
        ),
        out_shape=[
            struct((rows, width), jnp.bfloat16),
            struct((rows, width), jnp.bfloat16),
            struct((tiles, 8, rows), jnp.float32),
        ],
        compiler_params=pltpu.CompilerParams(vmem_limit_bytes=60 * 1024 * 1024),
        cost_estimate=pl.CostEstimate(
            flops=4 * rows * keys * width, bytes_accessed=pairs.size * 2, transcendentals=0
        ),
        name="attention",
    )(places, normed, w_query, turns, pairs, pairs)


def attention_backward(
    places, queries, pairs, sums, mixed, grad_mixed, normed, turns, grad_attention
):
    rows, width = queries.shape
    keys = pairs.shape[0]
    pieces = keys // rows
    tile = 2 * HEAD_DIM
    tiles = width // tile
    scaling = HEAD_DIM**-0.5

    def kernel(place, query, key, value, total, out, grad_out, normed_ref, turn, all_out, attention,
               grad_query, grad_pair, weight_grad, bias):
        step = pl.program_id(0)

        @pl.when(step == 0)
        def _():
            bias[...] = score_bias(place[0], place[1], rows, keys)

        own_masks = head_masks((rows, tile))
        scaled = query[...] * scaling
        inner = out[...].astype(jnp.float32) * grad_out[...].astype(jnp.float32)
        grads, key_sum, value_sum = [], None, None
        for head in range(2):
            chosen = jnp.where(own_masks[head], scaled, 0)
            upstream = jnp.where(own_masks[head], grad_out[...], 0)
            ones = jnp.where(own_masks[head][:8], 1.0, 0.0)
            inner_row = lax.dot_general(
                ones, inner, (((1,), (1,)), ((), ())),
                precision=HIGHEST, preferred_element_type=jnp.float32,
            )[0:1]
            scores = product(key[...], chosen, 1, 1) + bias[...]
            probabilities = jnp.exp(scores - total[0, head : head + 1, :])
            grad_probs = product(value[...], upstream, 1, 1)
            grad_scores = (probabilities * (grad_probs - inner_row)).astype(jnp.bfloat16)
            key_part = product(grad_scores, chosen)
            value_part = product(probabilities.astype(jnp.bfloat16), upstream)
            key_sum = key_part if key_sum is None else key_sum + key_part
            value_sum = value_part if value_sum is None else value_sum + value_part
            span = slice(head * HEAD_DIM, (head + 1) * HEAD_DIM)
            grads.append(product(key[...], grad_scores, 0, 0)[span] * scaling)
        grad_query[...] = turn_halves(
            jnp.transpose(jnp.concatenate(grads, axis=0)), turn[0], -turn[1]
        ).astype(grad_query.dtype)
        weight_grad[0] = product(normed_ref[...], grad_query[...], 0, 0).astype(weight_grad.dtype)
        weight_grad[1] = product(all_out[...], attention[...], 0, 0).astype(weight_grad.dtype)
        grad_pair[:, 0] = key_sum.astype(grad_pair.dtype).reshape(pieces, rows, tile)
        grad_pair[:, 1] = value_sum.astype(grad_pair.dtype).reshape(pieces, rows, tile)

    own_block = pl.BlockSpec((rows, tile), lambda i, _: (0, i))
    key_block = pl.BlockSpec((keys, tile), lambda i, _: (0, i))
    low = jnp.bfloat16
    return pl.pallas_call(
        kernel,
        grid_spec=pltpu.PrefetchScalarGridSpec(
            num_scalar_prefetch=1,
            grid=(tiles,),
            in_specs=[
                own_block,
                key_block,
                pl.BlockSpec((keys, tile), lambda i, _: (0, i + tiles)),
                pl.BlockSpec((1, 8, rows), lambda i, _: (i, 0, 0)),
                own_block,
                own_block,
                whole_block((rows, width)),
                whole_block(turns.shape),
                whole_block((rows, width)),
                own_block,
            ],
            out_specs=[
                own_block,
                pl.BlockSpec((pieces, 2, rows, tile), lambda i, _: (0, 0, 0, i)),
                pl.BlockSpec((2, width, tile), lambda i, _: (0, 0, i)),
            ],
            scratch_shapes=[pltpu.VMEM((keys, rows), jnp.float32)],
        ),
        out_shape=[
            struct((rows, width), low),
            struct((pieces, 2, rows, width), low),
            struct((2, width, width), low),
        ],
        compiler_params=pltpu.CompilerParams(vmem_limit_bytes=60 * 1024 * 1024),
        cost_estimate=pl.CostEstimate(
            flops=10 * rows * keys * width, bytes_accessed=pairs.size * 2, transcendentals=0
        ),
        name="attention_back",
    )(places, queries, pairs, pairs, sums, mixed, grad_mixed, normed, turns, mixed, grad_attention)


def normalize_rows(values, gain_row):
    scaling = lax.rsqrt(jnp.mean(values * values, axis=-1, keepdims=True) + EPSILON)
    return (values * scaling * gain_row, scaling)


def normalize_back(values, scaling, gain_row, grad_out):
    grad_hat = grad_out * gain_row
    grad_gain = jnp.sum(grad_out * values * scaling, axis=(0, 1))
    grad_values = scaling * grad_hat - values * scaling**3 * jnp.mean(
        grad_hat * values, axis=-1, keepdims=True
    )
    return (grad_values, grad_gain)


def rope_angles(positions, head_size):
    half_dim = head_size // 2
    frequency = jnp.exp(
        jnp.arange(half_dim, dtype=jnp.float32) * (-2.0 * math.log(10000.0) / head_size)
    )
    return positions.astype(jnp.float32)[:, None] * frequency[None, :]


def per_device(
    tokens,
    prev_logits,
    routes,
    lengths,
    cotangent,
    w_qkv,
    w_out,
    gain_attn,
    gain_moe,
    w_router,
    w_residual,
    const_vec,
    w_expert,
):
    groups, piece_len, model_width = tokens.shape
    positions = lax.axis_index("ctx") * piece_len + jnp.arange(piece_len, dtype=jnp.int32)
    live_rows = (positions[None, :] < lengths[:, None]).astype(jnp.float32)[..., None]
    experts = w_expert.shape[0]
    capacity = piece_len // 4
    slot_count = experts * capacity
    fsdp_count, ctx_count = lax.axis_size("fsdp"), lax.axis_size("ctx")
    full_kv = gather_weights(w_qkv, model_width, fsdp_count, ctx_count)
    inputs = tokens.astype(jnp.float32)
    gain_one = gain_attn.astype(jnp.float32)
    gain_two = gain_moe.astype(jnp.float32)
    angles = rope_angles(positions, HEAD_DIM)
    cosines, sines = jnp.cos(angles), jnp.sin(angles)
    turns = jnp.stack(
        [jnp.tile(cosines, (1, 4)), jnp.concatenate([-sines, sines, -sines, sines], axis=1)]
    )
    normed_one_low, own_pairs = project_keys(tokens[0], gain_one[None], full_kv, turns)
    cotangent_low = live_rows.astype(jnp.bfloat16) * cotangent
    all_pairs, (full_query, full_out) = gather_keys(
        own_pairs, [w_qkv, w_out], model_width, fsdp_count, ctx_count
    )
    cotangent_rows = lax.all_gather(cotangent_low, "fsdp", axis=0, tiled=True)
    cotangent_rows, all_pairs = lax.optimization_barrier((cotangent_rows, all_pairs))
    slot_block = lax.all_gather(cotangent_rows, "ctx", axis=0, tiled=True)
    places = jnp.stack([lengths[0], lax.axis_index("ctx") * piece_len]).astype(jnp.int32)
    mixed_rows, query_rows, score_sums = attention_forward(
        places, normed_one_low, full_query, turns, all_pairs
    )
    mixed_low = mixed_rows[None]
    attention = jnp.einsum("gpd,de->gpe", mixed_low, full_out, preferred_element_type=jnp.float32)
    residual_sum = inputs + attention
    normed_two, scale_two = normalize_rows(residual_sum, gain_two)
    routed_low = normed_two.astype(jnp.bfloat16)
    routed = routed_low.astype(jnp.float32)
    logits = jnp.einsum("gpd,de->gpe", routed, w_router, precision=HIGHEST) + jnp.einsum(
        "gpi,ie->gpe", prev_logits, w_residual, precision=HIGHEST
    )
    id_range = jnp.arange(experts + 4, dtype=jnp.int32)
    route_hot = (routes[..., None] == id_range).astype(jnp.float32)
    chosen = jnp.sum(route_hot * logits[:, :, None, :], axis=-1)
    chosen_exp = jnp.exp(chosen - jnp.max(chosen, axis=-1, keepdims=True))
    gate_weights = chosen_exp / jnp.sum(chosen_exp, axis=-1, keepdims=True)
    assign_hot = route_hot[..., :experts].reshape(groups, 2 * piece_len, experts)
    earlier = jnp.cumsum(assign_hot, axis=1) - assign_hot
    order_in = jnp.sum(earlier * assign_hot, axis=-1)
    expert_of = jnp.sum(assign_hot * jnp.arange(experts, dtype=jnp.float32), axis=-1)
    is_ffn = jnp.sum(assign_hot, axis=-1)
    slot_of = jnp.where(is_ffn > 0.5, expert_of * capacity + order_in, -1.0).reshape(
        groups, piece_len, 2
    )
    live_counts = jnp.sum(
        assign_hot * jnp.repeat(live_rows[..., 0], 2, axis=1)[..., None], axis=(0, 1)
    )
    notes = jnp.concatenate(
        [
            slot_of[0].T,
            gate_weights[0].T,
            jnp.pad(live_counts[None], ((0, 3), (0, piece_len - experts))),
        ],
        axis=0,
    )
    routed_rows, all_notes = gather_rows(routed_low[0], notes, fsdp_count)
    expert_weights = w_expert.swapaxes(1, 2)
    out_parts, grad_parts, dot_notes = expert_layers(
        routed_rows, cotangent_rows, all_notes, expert_weights
    )
    slot_block, routed_rows, grad_parts = lax.optimization_barrier(
        (slot_block, routed_rows, grad_parts)
    )
    slot_routed = lax.all_gather(routed_rows, "ctx", axis=0, tiled=True)
    ffn_grad, dot_sums, slot_notes = reduce_rows(
        grad_parts, dot_notes, all_notes, fsdp_count, ctx_count
    )
    slot_notes = slot_notes.reshape((ctx_count * fsdp_count,) + notes.shape)
    ffn_grad = ffn_grad[None]
    copy_hot = route_hot[..., experts + 1]
    const_hot = route_hot[..., experts + 2 :]
    constants = const_vec.astype(jnp.float32)
    gate_const = jnp.sum(gate_weights[..., None] * const_hot, axis=2)
    copy_gate = jnp.sum(gate_weights * copy_hot, axis=2, keepdims=True)
    special_sum = copy_gate * routed + jnp.einsum(
        "gpj,jd->gpd", gate_const, constants, precision=HIGHEST
    )
    grad_block = live_rows * cotangent.astype(jnp.float32)
    copy_dot = jnp.sum(grad_block * routed, axis=-1)[..., None]
    const_dot = jnp.einsum("gpd,jd->gpj", grad_block, constants, precision=HIGHEST)
    grad_gate = (
        dot_sums[:2].T[None]
        + copy_hot * copy_dot
        + jnp.sum(const_hot * const_dot[:, :, None, :], axis=-1)
    )
    grad_chosen = gate_weights * (
        grad_gate - jnp.sum(gate_weights * grad_gate, axis=-1, keepdims=True)
    )
    grad_logits = jnp.sum(grad_chosen[..., None] * route_hot, axis=2)
    grad_router = jnp.einsum("gpd,gpe->de", routed, grad_logits, precision=HIGHEST)
    grad_mixing = jnp.einsum("gpi,gpe->ie", prev_logits, grad_logits, precision=HIGHEST)
    grad_previous = jnp.einsum("gpe,ie->gpi", grad_logits, w_residual, precision=HIGHEST)
    grad_const = jnp.einsum("gpd,gpj->jd", grad_block, gate_const, precision=HIGHEST)
    grad_routed = (
        jnp.einsum("gpe,de->gpd", grad_logits, w_router, precision=HIGHEST)
        + copy_gate * grad_block
        + ffn_grad
    )
    grad_norm_two, grad_gain_two = normalize_back(residual_sum, scale_two, gain_two, grad_routed)
    grad_residual = grad_block + grad_norm_two
    grad_attention = grad_residual.astype(jnp.bfloat16)
    grad_mixed = jnp.einsum(
        "gpe,de->gpd", grad_attention, full_out, preferred_element_type=jnp.float32
    ).astype(jnp.bfloat16)
    counts = slot_notes[:, 4, :experts].astype(jnp.int32).reshape(-1)
    first_expert = lax.rem(lax.axis_index("ctx"), 2) * (experts // 2)
    query_back, pair_grads, early_parts = attention_backward(
        places, query_rows, all_pairs, score_sums, mixed_rows, grad_mixed[0], normed_one_low, turns,
        grad_attention[0],
    )
    early_parts = early_parts.reshape(2, fsdp_count, -1, model_width)
    chips = ctx_count // 2
    split = chips == 4
    chip_grads = pair_sums(pair_grads, early_parts if split else None, ctx_count)
    counts, *chip_grads = lax.optimization_barrier((counts, *chip_grads))

    arrived = list(chip_grads[:1])
    for step, block in enumerate(chip_grads[1:], 1):
        ring = [(i, (i + 2 * step) % ctx_count) for i in range(ctx_count)]
        arrived.append(lax.ppermute(block, "ctx", ring))
    half_grads, expert_half = expert_gradients(
        first_expert.astype(jnp.int32)[None], counts, slot_routed, slot_block, slot_notes, expert_weights
    )
    half_grads, query_back = lax.optimization_barrier((half_grads, query_back))
    weight_parts, grad_inputs, grad_gain_one, *early_sums = projection_gradients(
        arrived,
        query_back,
        normed_one_low,
        tokens[0],
        gain_one[None],
        turns,
        full_query,
        full_kv,
        grad_residual[0],
        fsdp_count if split else 0,
    )
    grad_inputs = grad_inputs[None]
    weight_parts = weight_parts.reshape(fsdp_count, -1, 2 * model_width)
    if not split:
        weight_parts = jnp.concatenate([early_parts[0], early_parts[1], weight_parts], axis=-1)
    few = experts + 4
    mixing_row = jnp.pad(grad_mixing.reshape(1, -1), ((0, 0), (0, model_width - few * few)))
    small = jnp.concatenate(
        [grad_router.T, grad_const, grad_gain_one[:1], grad_gain_two[None], mixing_row], axis=0
    )
    small = jnp.pad(small, ((0, -small.shape[0] % 8), (0, 0)))
    weight_sum, small_sum, expert_grads, ffn_sum = reduce_weights(
        weight_parts, early_sums, small, half_grads, out_parts, fsdp_count, ctx_count
    )
    other_first = (experts // 2 - first_expert).astype(jnp.int32)[None]
    expert_sum, wqkv_sum, wout_sum, output, router_sum, const_sum, *rest = last_results(
        other_first, expert_grads, expert_half, weight_sum, small_sum,
        (live_rows * (residual_sum + special_sum))[0], live_rows[0], ffn_sum, few,
    )
    expert_sum, output, router_sum = expert_sum.swapaxes(1, 2), output[None], router_sum.T
    gain_one_sum, gain_two_sum, mixing_row = rest
    mixing_sum = mixing_row[0, : few * few].reshape(few, few)
    return (
        output,
        grad_inputs,
        grad_previous,
        wqkv_sum,
        wout_sum,
        gain_one_sum,
        gain_two_sum,
        router_sum,
        mixing_sum,
        const_sum,
        expert_sum,
    )


def solution(mesh):
    return jax.shard_map(
        per_device,
        mesh=mesh,
        in_specs=(
            P("fsdp", "ctx", None),
            P("fsdp", "ctx", None),
            P("fsdp", "ctx", None),
            P("fsdp"),
            P("fsdp", "ctx", None),
            P("fsdp", None),
            P("fsdp", None),
            P(),
            P(),
            P(),
            P(),
            P(),
            P(None, "fsdp", None, None),
        ),
        out_specs=(
            P("fsdp", "ctx", None),
            P("fsdp", "ctx", None),
            P("fsdp", "ctx", None),
            P("fsdp", None),
            P("fsdp", None),
            P(),
            P(),
            P(),
            P(),
            P(),
            P(None, "fsdp", None, None),
        ),
        check_vma=False,
    )
```

```python
import itertools
import math

import jax
import jax.numpy as jnp
from jax import lax
from jax.experimental import pallas as pl
from jax.experimental.pallas import tpu as pltpu

from jax.sharding import PartitionSpec as P

HEAD_DIM = 64


EPSILON = 1e-05
MASKED = -1e30
HIGHEST = lax.Precision.HIGHEST


LOGICAL = pl.DeviceIdType.MESH
VMEM_LIMIT = 56 * 1024 * 1024


class Copies:
    def __init__(self, send, recv):
        self.send, self.recv, self.used = send, recv, 0

    def make(self, source, target, peer):
        index = self.used
        self.used += 1
        return pltpu.make_async_remote_copy(
            source, target, self.send.at[index], self.recv.at[index],
            device_id=peer, device_id_type=LOGICAL,
        )


def meet(peers):
    barrier = pltpu.get_barrier_semaphore()
    for allowed, peer in peers:
        @pl.when(allowed)
        def _():
            pl.semaphore_signal(barrier, 1, device_id=peer, device_id_type=LOGICAL)
    awaited = sum(jnp.where(allowed, 1, 0) for allowed, _ in peers)
    pl.semaphore_wait(barrier, awaited)


def together(*streams):
    for _ in itertools.zip_longest(*streams):
        pass


def within(value, count):
    return (value >= 0) & (value < count)


def bounded(value, count):
    return jnp.minimum(jnp.maximum(value, 0), count - 1)


def line_peers(count):
    rank = lax.axis_index("fsdp")
    return [
        (within(rank + way, count), {"fsdp": bounded(rank + way, count)}) for way in (1, -1)
    ]


def ring_peers(axis, count, stride=1):
    rank = lax.axis_index(axis)
    return [
        (rank >= 0, {axis: lax.rem(rank + stride * step, count)})
        for step in range(1, count // stride)
    ]


def own_place(count):
    rank = lax.axis_index("ctx")
    core = lax.rem(rank, 2)
    return rank, core, rank // 2, count // 2, rank + 1 - 2 * core


def plane_peers(count):
    rank, core, chip, chips, sibling = own_place(count)
    peers = [(rank >= 0, {"ctx": sibling})]
    if chips == 4:
        across, along, _ = square(chip)
        return peers + [(rank >= 0, {"ctx": 2 * c + core}) for c in (across, along)]
    return peers + ring_peers("ctx", count, 2)


def square(chip):
    side, row = lax.rem(chip, 2), chip // 2
    across = chip + 1 - 2 * side
    along = chip + 2 - 4 * row
    return across, along, across + 2 - 4 * row


def line_gather(copies, own, slot, count, arrived=None):
    rank = lax.axis_index("fsdp")
    sent, latest = [], {}
    for hop in range(1, count + 1):
        for way in (1, -1):
            origin = rank - way * (hop - 1)
            held = slot(bounded(origin, count))
            if hop > 1:
                earlier = latest[way]

                @pl.when(within(origin, count))
                def _():
                    earlier.wait_recv()

                if arrived is not None:
                    arrived(within(origin, count), bounded(origin, count), held)
            if hop < count:
                copy = copies.make(
                    own if hop == 1 else held, held, {"fsdp": bounded(rank + way, count)}
                )
                allowed = within(origin, count) & within(rank + way, count)

                @pl.when(allowed)
                def _():
                    copy.start()

                sent.append((allowed, copy))
                latest[way] = copy
        yield
    for allowed, copy in sent:

        @pl.when(allowed)
        def _():
            copy.wait_send()


def line_reduce(copies, part, passing, landing, count, total):
    rank = lax.axis_index("fsdp")
    sent, arriving = [], {}
    for step in range(count - 1, 0, -1):
        for side, way in enumerate((1, -1)):
            goal = rank + way * step
            allowed = within(goal, count)
            copy = copies.make(
                passing.at[side, step - 1],
                landing.at[side, step - 1],
                {"fsdp": bounded(rank + way, count)},
            )
            arriving[side, step - 1] = copy
            own = part(bounded(goal, count))
            has_earlier = allowed & within(rank - way, count)
            if step < count - 1:
                earlier = arriving[side, step]

                @pl.when(has_earlier)
                def _():
                    earlier.wait_recv()
                    passing[side, step - 1] = (
                        own[...].astype(jnp.float32) + landing[side, step].astype(jnp.float32)
                    ).astype(passing.dtype)

                @pl.when(allowed & jnp.logical_not(within(rank - way, count)))
                def _():
                    passing[side, step - 1] = own[...]
            else:

                @pl.when(allowed)
                def _():
                    passing[side, step - 1] = own[...]

            @pl.when(allowed)
            def _():
                copy.start()

            sent.append((allowed, copy))
        yield
    total[...] = part(rank)[...].astype(jnp.float32)
    for side, way in enumerate((1, -1)):
        last = arriving[side, 0]

        @pl.when(within(rank - way, count))
        def _():
            last.wait_recv()
            total[...] += landing[side, 0].astype(jnp.float32)
    for allowed, copy in sent:

        @pl.when(allowed)
        def _():
            copy.wait_send()


def push_reduce(copies, part, landing, count, total):
    rank = lax.axis_index("fsdp")
    sent = []
    for step in range(1, count):
        peer = lax.rem(rank + step, count)
        copy = copies.make(part(peer), landing.at[step - 1], {"fsdp": peer})
        copy.start()
        sent.append(copy)
    yield
    value = part(rank)[...].astype(jnp.float32)
    for step, copy in enumerate(sent):
        copy.wait_recv()
        value = value + landing[step].astype(jnp.float32)
    total[...] = value
    for copy in sent:
        copy.wait_send()


def push_gather(copies, own, slot, axis, count, stride=1):
    rank = lax.axis_index(axis)
    sent = []
    for step in range(1, count // stride):
        copy = copies.make(own, slot(step), {axis: lax.rem(rank + stride * step, count)})
        copy.start()
        sent.append(copy)
    yield
    for copy in sent:
        copy.wait()


def plane_gather(copies, own, slot, count):
    rank, core, chip, chips, sibling = own_place(count)
    sent, forwarded = [], []

    def send(source, target, peer):
        copy = copies.make(source, target, {"ctx": peer})
        copy.start()
        sent.append(copy)
        return copy

    def forward(index, part):
        copy = copies.make(slot(index, part), slot(index, part), {"ctx": sibling})
        copy.start()
        forwarded.append(copy)

    if chips == 4:
        across, along, _ = square(chip)
        side_x, side_y = 2 * across + core, 2 * along + core
        corner = 2 * square(chip)[2] + core
        first_x = send(own(1), slot(rank, 1), side_x)
        second_y = send(own(2), slot(rank, 2), side_y)
        second_x = send(own(2), slot(rank, 2), side_x)
        first_y = send(own(1), slot(rank, 1), side_y)
        copy = copies.make(own(0), slot(rank, 0), {"ctx": sibling})
        copy.start()
        forwarded.append(copy)
        yield
        first_x.wait_recv()
        corner_first = send(slot(side_x, 1), slot(side_x, 1), side_y)
        forward(side_x, 1)
        second_y.wait_recv()
        corner_second = send(slot(side_y, 2), slot(side_y, 2), side_x)
        forward(side_y, 2)
        yield
        second_x.wait_recv()
        forward(side_x, 2)
        first_y.wait_recv()
        forward(side_y, 1)
        yield
        corner_first.wait_recv()
        forward(corner, 1)
        corner_second.wait_recv()
        forward(corner, 2)
        yield
    else:
        pending = []
        for step in range(1, chips):
            peer = lax.rem(rank + 2 * step, count)
            pending.append((lax.rem(rank + count - 2 * step, count), send(own(0), slot(rank, 0), peer)))
        copy = copies.make(own(0), slot(rank, 0), {"ctx": sibling})
        copy.start()
        forwarded.append(copy)
        yield
        for origin, copy in pending:
            copy.wait_recv()
            forward(origin, 0)
        yield
    for copy in sent:
        copy.wait_send()
    for copy in forwarded:
        copy.wait()


def plane_reduce(copies, paired, passing, landing, count, finish):
    rank, core, chip, chips, sibling = own_place(count)
    sent = []

    def send(source, target, peer_chip):
        copy = copies.make(source, target, {"ctx": 2 * peer_chip + core})
        copy.start()
        sent.append(copy)
        return copy

    if chips == 4:
        across, along, corner = square(chip)
        via_x = send(paired(corner, 1), landing.at[0], across)
        via_y = send(paired(corner, 2), landing.at[1], along)
        own_x = send(paired(across, 1), landing.at[2], across)
        own_y = send(paired(along, 2), landing.at[3], along)
        yield
        via_x.wait_recv()
        passing[0] = (
            paired(along, 1)[...].astype(jnp.float32) + landing[0].astype(jnp.float32)
        ).astype(passing.dtype)
        last_first = send(passing.at[0], landing.at[4], along)
        via_y.wait_recv()
        passing[1] = (
            paired(across, 2)[...].astype(jnp.float32) + landing[1].astype(jnp.float32)
        ).astype(passing.dtype)
        last_second = send(passing.at[1], landing.at[5], across)
        yield
        own_x.wait_recv()
        own_y.wait_recv()
        last_first.wait_recv()
        last_second.wait_recv()
        for half in (1, 2):
            total = paired(chip, half)[...].astype(jnp.float32)
            total = total + landing[1 + half].astype(jnp.float32)
            total = total + landing[3 + half].astype(jnp.float32)
            finish(half, total)
    else:
        for step in range(1, chips):
            send(paired(lax.rem(chip + step, chips), 0), landing.at[step - 1], lax.rem(chip + step, chips))
        yield
        total = paired(chip, 0)[...].astype(jnp.float32)
        for step, copy in enumerate(sent):
            copy.wait_recv()
            total = total + landing[step].astype(jnp.float32)
        finish(0, total)
    for copy in sent:
        copy.wait_send()


def remote_call(kernel, name, results, operands, in_spaces, out_spaces, scratch, copies, cost):
    ids = ("weights", "keys", "rows", "row_sums", "pair_sums", "totals")
    return pl.pallas_call(
        kernel,
        out_shape=results,
        in_specs=[pl.BlockSpec(memory_space=space) for space in in_spaces],
        out_specs=[pl.BlockSpec(memory_space=space) for space in out_spaces],
        scratch_shapes=list(scratch)
        + [pltpu.SemaphoreType.DMA((copies,)), pltpu.SemaphoreType.DMA((copies,))],
        compiler_params=pltpu.CompilerParams(
            collective_id=ids.index(name), has_side_effects=True, vmem_limit_bytes=VMEM_LIMIT
        ),
        cost_estimate=pl.CostEstimate(flops=0, bytes_accessed=cost, transcendentals=0),
        name=name,
    )(*operands)


def struct(shape, dtype):
    return jax.ShapeDtypeStruct(shape, dtype)


class SharedBlock:
    def __init__(self, copies, source, target, count, ctx_count):
        _, core, _, _, self.sibling = own_place(ctx_count)
        half = source.shape[0] // 2
        rows = pl.ds(pl.multiple_of(core * half, math.gcd(half, 256)), half)
        self.copies, self.forwarded = copies, []
        self.stream = line_gather(
            copies, source.at[rows], lambda i: target.at[i, rows], count, self.arrived
        )

    def arrived(self, allowed, _, held):
        copy = self.copies.make(held, held, {"ctx": self.sibling})

        @pl.when(allowed)
        def _():
            copy.start()

        self.forwarded.append((allowed, copy))

    def wait(self):
        for allowed, copy in self.forwarded:

            @pl.when(allowed)
            def _():
                copy.wait()


def gather_weights(weight, skip, count, ctx_count):
    rows, width = weight.shape[0], weight.shape[1] - skip
    chips = ctx_count // 2
    parts = chips if chips == 4 and width % (128 * chips) == 0 else 1
    half, share = rows // 2, width // parts

    def kernel(source, target, send, recv):
        copies = Copies(send, recv)
        rank = lax.axis_index("fsdp")
        place, core, chip, _, sibling = own_place(ctx_count)
        span = pl.ds(pl.multiple_of(core * half, math.gcd(half, 256)), half)
        meet(
            (ring_peers("fsdp", count) if parts > 1 else line_peers(count))
            + plane_peers(ctx_count)[:1]
            + (ring_peers("ctx", ctx_count, 2) if parts > 1 else [])
        )

        def held(origin, part):
            return target.at[origin, span, pl.ds(pl.multiple_of(part * share, 128), share)]

        mine = chip if parts > 1 else 0
        received, forwarded = [], []

        def hand(allowed, ref):
            copy = copies.make(ref, ref, {"ctx": sibling})

            @pl.when(allowed)
            def _():
                copy.start()

            forwarded.append((allowed, copy))

        def arrived(allowed, origin, ref):
            for step in range(1, parts):
                copy = copies.make(ref, ref, {"ctx": lax.rem(place + 2 * step, ctx_count)})

                @pl.when(allowed)
                def _():
                    copy.start()

                received.append((allowed, origin, lax.rem(chip + chips - step, chips), copy))
            hand(allowed, ref)

        if parts > 1:
            pushes = []
            for step in range(1, count):
                copy = copies.make(
                    source.at[span, pl.ds(pl.multiple_of(skip + mine * share, 128), share)],
                    held(rank, mine),
                    {"fsdp": lax.rem(rank + step, count)},
                )
                copy.start()
                pushes.append(copy)
            target[rank] = source[:, skip:]
            for step, copy in enumerate(pushes, 1):
                copy.wait()
                origin = lax.rem(rank + count - step, count)
                arrived(rank >= 0, origin, held(origin, mine))
        else:
            target[rank] = source[:, skip:]
            together(
                line_gather(copies, source.at[span, pl.ds(skip, width)], lambda i: held(i, mine), count, arrived)
            )
        for allowed, origin, part, copy in received:

            @pl.when(allowed)
            def _():
                copy.wait()

            hand(allowed, held(origin, part))
        for allowed, copy in forwarded:

            @pl.when(allowed)
            def _():
                copy.wait()

    (full,) = remote_call(
        kernel, "weights", [struct((count, rows, width), weight.dtype)], [weight],
        [pltpu.VMEM], [pltpu.VMEM], [], 2 * count + 4 * count * (2 * parts - 1),
        count * rows * width * 4,
    )
    return full.reshape(count * rows, width)


def gather_keys(block, weights, wide, count, ctx_count):
    rows, width = block.shape
    half = rows // 2

    def kernel(*refs):
        own, *sources = refs[: 1 + len(weights)]
        sources = [source.at[:, pl.ds(0, wide)] for source in sources]
        gathered, *targets = refs[1 + len(weights) : 2 + 2 * len(weights)]
        local, send, recv = refs[2 + 2 * len(weights) :]
        copies = Copies(send, recv)
        rank, place = lax.axis_index("fsdp"), lax.axis_index("ctx")
        spans = (pl.ds(0, rows), pl.ds(0, half), pl.ds(half, half))
        meet(line_peers(count) + plane_peers(ctx_count))
        kept = [pltpu.make_async_copy(own, gathered.at[place], local.at[0])]
        kept += [
            pltpu.make_async_copy(source, target.at[rank], local.at[1 + i])
            for i, (source, target) in enumerate(zip(sources, targets))
        ]
        for copy in kept:
            copy.start()
        blocks = [SharedBlock(copies, s, t, count, ctx_count) for s, t in zip(sources, targets)]
        together(
            plane_gather(
                copies,
                lambda part: own.at[spans[part]],
                lambda i, part: gathered.at[i, spans[part]],
                ctx_count,
            ),
            *[b.stream for b in blocks],
        )
        for b in blocks:
            b.wait()
        for copy in kept:
            copy.wait()

    results = [struct((ctx_count, rows, width), block.dtype)]
    results += [struct((count, w.shape[0], wide), w.dtype) for w in weights]
    gathered, *full = remote_call(
        kernel, "keys", results, [block, *weights],
        [pltpu.VMEM] * (1 + len(weights)), [pl.ANY] * (1 + len(weights)),
        [pltpu.SemaphoreType.DMA((1 + len(weights),))],
        16 + 2 * ctx_count + 4 * count * len(weights),
        ctx_count * rows * width * 4,
    )
    return gathered.reshape(ctx_count * rows, width), [
        f.reshape(count * f.shape[1], f.shape[2]) for f in full
    ]


def gather_rows(block, notes, count):
    def kernel(own, own_notes, gathered, all_notes, local, send, recv):
        copies = Copies(send, recv)
        half = own.shape[0] // 2
        parts = (pl.ds(0, half), pl.ds(half, half))
        rank = lax.axis_index("fsdp")
        meet(ring_peers("fsdp", count))
        kept = [
            pltpu.make_async_copy(own, gathered.at[rank], local.at[0]),
            pltpu.make_async_copy(own_notes, all_notes.at[rank], local.at[1]),
        ]
        for copy in kept:
            copy.start()
        together(
            push_gather(copies, own_notes, lambda step: all_notes.at[rank], "fsdp", count),
            *[
                line_gather(
                    copies, own.at[part], lambda i, part=part: gathered.at[i, part], count
                )
                for part in parts
            ],
        )
        for copy in kept:
            copy.wait()

    return remote_call(
        kernel, "rows",
        [struct((count,) + block.shape, block.dtype), struct((count,) + notes.shape, notes.dtype)],
        [block, notes], [pltpu.VMEM] * 2, [pl.ANY] * 2, [pltpu.SemaphoreType.DMA((2,))],
        6 * count, count * block.size * 4,
    )


def reduce_rows(parts, notes, shared, count, ctx_count):
    _, rows, width = parts.shape
    half = rows // 2

    def kernel(given, given_notes, own, total, notes_total, all_shared,
               passing, landing, noted, send, recv):
        copies = Copies(send, recv)
        rank, place = lax.axis_index("fsdp"), lax.axis_index("ctx")
        meet(ring_peers("fsdp", count) + ring_peers("ctx", ctx_count))
        pushes, spread = [], []
        for step in range(1, count):
            peer = lax.rem(rank + step, count)
            copy = copies.make(given_notes.at[peer], noted.at[step - 1], {"fsdp": peer})
            copy.start()
            pushes.append(copy)
        for step in range(1, ctx_count):
            copy = copies.make(own, all_shared.at[place], {"ctx": lax.rem(place + step, ctx_count)})
            copy.start()
            spread.append(copy)
        all_shared[place] = own[...]
        together(
            *[
                line_reduce(
                    copies,
                    lambda d, part=part: given.at[d, part],
                    passing.at[i],
                    landing.at[i],
                    count,
                    total.at[part],
                )
                for i, part in enumerate((pl.ds(0, half), pl.ds(half, half)))
            ]
        )
        sums = given_notes[rank]
        for step, copy in enumerate(pushes):
            copy.wait()
            sums = sums + noted[step]
        notes_total[...] = sums
        for copy in spread:
            copy.wait()

    return remote_call(
        kernel, "row_sums",
        [
            struct((rows, width), jnp.float32),
            struct(notes.shape[1:], notes.dtype),
            struct((ctx_count,) + shared.shape, shared.dtype),
        ],
        [parts, notes, shared], [pltpu.VMEM] * 3, [pltpu.VMEM] * 3,
        [
            pltpu.VMEM((2, 2, count - 1, half, width), parts.dtype),
            pltpu.VMEM((2, 2, count - 1, half, width), parts.dtype),
            pltpu.VMEM((count - 1,) + notes.shape[1:], notes.dtype),
        ],
        6 * count + ctx_count, count * rows * width * 4,
    )


def pair_sums(parts, early, ctx_count):
    chips = ctx_count // 2
    shape, kind = parts.shape[1:], parts.dtype
    _, rows, width = shape
    number = 0 if early is None else early.shape[1]
    if number:
        half, share = early.shape[2] // 2, width // 2
        low_half = half // 2
    else:
        low_half = 0

    def kernel(*refs):
        given, refs = refs[0], refs[1:]
        if number:
            given_early, refs = refs[0], refs[1:]
        totals, refs = refs[:chips], refs[chips:]
        met, *met_early, send, recv = refs
        copies = Copies(send, recv)
        _, core, chip, _, sibling = own_place(ctx_count)
        meet(plane_peers(ctx_count)[:1])
        exchanged = []
        for k in range(chips):
            q = lax.rem(chip + k, chips)
            copy = copies.make(given.at[2 * q + 1 - core], met.at[q], {"ctx": sibling})
            copy.start()
            exchanged.append(copy)
        if number:
            mine = pl.ds(pl.multiple_of(core * half, 16), half)
            theirs = pl.ds(pl.multiple_of((1 - core) * half, 16), half)
            for which in range(2):
                for d in range(number):
                    copy = copies.make(
                        given_early.at[which, d, theirs], met_early[0].at[which, d], {"ctx": sibling}
                    )
                    copy.start()
                    exchanged.append(copy)
        for k in range(chips):
            q = lax.rem(chip + k, chips)
            exchanged[k].wait_recv()
            for which in range(2):
                totals[k][which * rows : (which + 1) * rows, :] = (
                    given[2 * q + core, which].astype(jnp.float32)
                    + met[q, which].astype(jnp.float32)
                ).astype(kind)
        for copy in exchanged[chips:]:
            copy.wait_recv()
        if number:
            for k in range(chips):
                q = lax.rem(chip + k, chips)
                which = q // 2
                columns = pl.ds(pl.multiple_of(lax.rem(q, 2) * share, 128), share)
                for d in range(number):
                    value = (
                        given_early[which, d, mine, columns].astype(jnp.float32)
                        + met_early[0][which, d, :, columns].astype(jnp.float32)
                    ).astype(kind)
                    place = 2 * rows + d * low_half
                    totals[k][place : place + low_half, :share] = value[:low_half]
                    totals[k][place : place + low_half, share:] = value[low_half:]
        for copy in exchanged:
            copy.wait_send()

    results = [struct((2 * rows + number * low_half, width), kind)] * chips
    operands, scratch = [parts], [pltpu.VMEM((chips,) + shape, kind)]
    if number:
        operands = operands + [early]
        scratch = scratch + [pltpu.VMEM((2, number, half, width), kind)]
    return remote_call(
        kernel, "pair_sums", results, operands, [pltpu.VMEM] * len(operands),
        [pltpu.VMEM] * len(results), scratch, chips + 2 * number, parts.size * 4,
    )


def reduce_weights(parts, early, small, half_grads, row_parts, count, ctx_count):
    _, rows, width = parts.shape
    chips = ctx_count // 2
    half, share = rows // 2, width // chips
    chunks = 2 if early else 1
    row_unit = math.gcd(half, 256)
    first = max(count // 2, 1)
    lands = (6, first, half, share) if chips == 4 else (chips - 1, count, half, share)

    own = half_grads.shape[0]

    def kernel(*refs):
        early_refs, refs = refs[: len(early)], refs[len(early) :]
        (given, given_small, half_ref, given_rows, total, small_total, grads_ref, rows_total,
         row_passing, row_landing, met, paired, passing, landing, merged, line_landing, line_total,
         own_total, small_met, small_sum, small_plane, small_plane_sum, small_line, send, recv) = refs
        copies = Copies(send, recv)
        rank = lax.axis_index("fsdp")
        place, core, chip, _, sibling = own_place(ctx_count)
        spans = (pl.ds(0, count), pl.ds(0, first), pl.ds(first, count - first))
        mine = pl.ds(pl.multiple_of(core * half, row_unit), half)
        theirs = pl.ds(pl.multiple_of((1 - core) * half, row_unit), half)

        def columns(q):
            return pl.ds(pl.multiple_of(q * share, 128), share)

        meet(
            ring_peers("fsdp", count)
            + ring_peers("ctx", ctx_count, 2)
            + plane_peers(ctx_count)[:1]
        )
        small_pair = copies.make(given_small, small_met, {"ctx": sibling})
        small_pair.start()
        exchanged = []
        for d in range(count):
            copy = copies.make(given.at[d, theirs], met.at[d], {"ctx": sibling})
            copy.start()
            exchanged.append(copy)

        for i in range(own):
            copy = copies.make(half_ref.at[i], grads_ref.at[i], {"ctx": sibling})
            copy.start()
            exchanged.append(copy)

        def small_stream():
            small_pair.wait()
            small_sum[...] = given_small[...] + small_met[...]
            pushes = []
            for step in range(1, chips):
                copy = copies.make(
                    small_sum, small_plane.at[step - 1],
                    {"ctx": lax.rem(place + 2 * step, ctx_count)},
                )
                copy.start()
                pushes.append(copy)
            yield
            for copy in pushes:
                copy.wait()
            small_plane_sum[...] = small_sum[...] + jnp.sum(small_plane[...], axis=0)
            pushes = []
            for step in range(1, count):
                copy = copies.make(
                    small_plane_sum, small_line.at[step - 1],
                    {"fsdp": lax.rem(rank + step, count)},
                )
                copy.start()
                pushes.append(copy)
            yield
            yield
            for copy in pushes:
                copy.wait()
            small_total[...] = small_plane_sum[...] + jnp.sum(small_line[...], axis=0)

        def large_stream(c):
            def finish(part, value):
                merged[c, spans[part]] = value.astype(merged.dtype)

            if c > 0:
                merged[c] = early_refs[0][...]
            else:
                for d, copy in enumerate(exchanged[:count]):
                    copy.wait_recv()
                    for q in range(chips):
                        span = slice(q * share, (q + 1) * share)
                        paired[q, d] = (
                            given[d, mine, span].astype(jnp.float32)
                            + met[d, :, span].astype(jnp.float32)
                        ).astype(paired.dtype)
                yield from plane_reduce(
                    copies, lambda q, part: paired.at[q, spans[part]],
                    passing, landing, ctx_count, finish,
                )
            yield from push_reduce(
                copies, lambda d: merged.at[c, d], line_landing.at[c], count, line_total.at[c]
            )
            own_total[c] = line_total[c].astype(own_total.dtype)
            sent = []
            forwarded = []
            target = total.at[c, mine, columns(chip)]
            copy = copies.make(own_total.at[c], target, {"ctx": sibling})
            copy.start()
            forwarded.append(copy)
            for step in range(1, chips):
                copy = copies.make(
                    own_total.at[c], target, {"ctx": lax.rem(place + 2 * step, ctx_count)}
                )
                copy.start()
                sent.append(copy)
            total[c, mine, columns(chip)] = own_total[c]
            yield
            for step, copy in enumerate(sent, 1):
                copy.wait_recv()
                held = total.at[c, mine, columns(lax.rem(chip + chips - step, chips))]
                copy = copies.make(held, held, {"ctx": sibling})
                copy.start()
                forwarded.append(copy)
            yield
            for copy in sent:
                copy.wait_send()
            for copy in forwarded:
                copy.wait()

        together(
            line_reduce(
                copies, lambda d: given_rows.at[d], row_passing, row_landing, count, rows_total
            ),
            small_stream(),
            *[large_stream(c) for c in reversed(range(chunks))],
        )
        for copy in exchanged:
            copy.wait_send()
        for copy in exchanged[count:]:
            copy.wait_recv()

    kind = parts.dtype
    f32 = jnp.float32
    return remote_call(
        kernel, "totals",
        [
            struct((chunks, rows, width), kind),
            struct(small.shape, f32),
            struct(half_grads.shape, kind),
            struct(row_parts.shape[1:], f32),
        ],
        [*early, parts, small, half_grads, row_parts],
        [pltpu.VMEM] * len(early) + [pltpu.VMEM, pltpu.VMEM, pl.ANY, pltpu.VMEM],
        [pltpu.VMEM, pltpu.VMEM, pl.ANY, pltpu.VMEM],
        [
            pltpu.VMEM((2, count - 1) + row_parts.shape[1:], kind),
            pltpu.VMEM((2, count - 1) + row_parts.shape[1:], kind),
            pltpu.VMEM((count, half, width), kind),
            pltpu.VMEM((chips, count, half, share), kind),
            pltpu.VMEM((2, first, half, share), kind),
            pltpu.VMEM(lands, kind),
            pltpu.VMEM((chunks, count, half, share), kind),
            pltpu.VMEM((chunks, count - 1, half, share), kind),
            pltpu.VMEM((chunks, half, share), f32),
            pltpu.VMEM((chunks, half, share), kind),
            pltpu.VMEM(small.shape, f32),
            pltpu.VMEM(small.shape, f32),
            pltpu.VMEM((chips - 1,) + small.shape, f32),
            pltpu.VMEM(small.shape, f32),
            pltpu.VMEM((count - 1,) + small.shape, f32),
        ],
        8 + 8 * count + 6 * chips + own + chunks * (8 + 2 * count + 3 * chips), parts.size * 8,
    )


def local_call(kernel, name, grid, results, operands, in_specs, out_specs, scratch, flops, cost):
    return pl.pallas_call(
        kernel,
        grid=grid,
        out_shape=results,
        in_specs=in_specs,
        out_specs=out_specs,
        scratch_shapes=scratch,
        compiler_params=pltpu.CompilerParams(vmem_limit_bytes=60 * 1024 * 1024),
        cost_estimate=pl.CostEstimate(flops=flops, bytes_accessed=cost, transcendentals=0),
        name=name,
    )(*operands)


def whole_block(shape):
    return pl.BlockSpec(shape, lambda *_: (0,) * len(shape))


def product(left, right, left_dim=1, right_dim=0):
    return lax.dot_general(
        left, right, (((left_dim,), (right_dim,)), ((), ())), preferred_element_type=jnp.float32
    )


def expert_layers(routed_rows, block_rows, notes, weights):
    peers, piece_len, width = routed_rows.shape
    experts, _, units, _ = weights.shape
    capacity = piece_len // 4
    count = peers * capacity

    slots = experts * capacity

    def kernel(routed, block, note, w, out_parts, grad_parts, dots, hots, taken, blocks, outs, ins):
        expert = pl.program_id(0)
        low = jnp.bfloat16

        def chosen(g, first_slot, number):
            places = (
                lax.broadcasted_iota(jnp.int32, (number, piece_len), 0) + first_slot
            ).astype(jnp.float32)
            return note[g, 0:1, :] == places, note[g, 1:2, :] == places

        @pl.when(expert == 0)
        def _():
            dots[...] = jnp.zeros_like(dots)
            for g in range(peers):
                first, second = chosen(g, 0, slots)
                hots[g] = jnp.where(first | second, 1.0, 0.0).astype(low)
                taken[g] = product(hots[g], routed[g]).astype(low)
                blocks[g] = product(hots[g], block[g]).astype(low)

        span = pl.ds(pl.multiple_of(expert * capacity, 16), capacity)
        firsts, seconds, gates = [], [], []
        for g in range(peers):
            first, second = chosen(g, expert * capacity, capacity)
            gates.append(
                jnp.sum(
                    jnp.where(first, note[g, 2:3, :], jnp.where(second, note[g, 3:4, :], 0.0)),
                    axis=1,
                    keepdims=True,
                )
            )
            firsts.append(first)
            seconds.append(second)
        rows = jnp.concatenate([taken[g, span, :] for g in range(peers)], axis=0)
        block_part = jnp.concatenate(
            [blocks[g, span, :] for g in range(peers)], axis=0
        ).astype(jnp.float32)
        gate = jnp.concatenate(gates, axis=0)
        grad_out = (gate * block_part).astype(low)
        w_gate, w_up, w_down = w[0, 0], w[0, 1], w[0, 2]
        gate_proj = product(rows, w_gate, 1, 1)
        up_proj = product(rows, w_up, 1, 1)
        grad_hidden = product(grad_out, w_down, 1, 1)
        sigmoid = 1.0 / (1.0 + jnp.exp(-gate_proj))
        silu = gate_proj * sigmoid
        hidden = (silu * up_proj).astype(low)
        grad_gate_proj = (
            grad_hidden * up_proj * sigmoid * (1.0 + gate_proj * (1.0 - sigmoid))
        ).astype(low)
        grad_up_proj = (grad_hidden * silu).astype(low)
        expert_out = product(hidden, w_down)
        grad_in = (product(grad_gate_proj, w_gate) + product(grad_up_proj, w_up)).astype(low)
        row_dots = jnp.sum(block_part * expert_out, axis=1, keepdims=True)
        gated = (gate * expert_out).astype(low)
        for g in range(peers):
            part = slice(g * capacity, (g + 1) * capacity)
            outs[g, span, :] = gated[part]
            ins[g, span, :] = grad_in[part]
            for k, hit in enumerate((firsts[g], seconds[g])):
                dots[g, k : k + 1, :] += jnp.sum(
                    jnp.where(hit, row_dots[part], 0.0), axis=0, keepdims=True
                )

        @pl.when(expert == experts - 1)
        def _():
            for g in range(peers):
                out_parts[g] = product(hots[g], outs[g], 0, 0).astype(low)
                grad_parts[g] = product(hots[g], ins[g], 0, 0).astype(low)

    rows_shape = (peers, piece_len, width)
    low = jnp.bfloat16
    expert_block = pl.BlockSpec((1, 3, units, width), lambda e: (e, 0, 0, 0))
    return local_call(
        kernel, "experts", (experts,),
        [struct(rows_shape, low), struct(rows_shape, low),
         struct(notes.shape, jnp.float32)],
        [routed_rows, block_rows, notes, weights],
        [whole_block(rows_shape), whole_block(rows_shape), whole_block(notes.shape), expert_block],
        [whole_block(rows_shape), whole_block(rows_shape), whole_block(notes.shape)],
        [pltpu.VMEM((peers, slots, piece_len), low)]
        + [pltpu.VMEM((peers, slots, width), low)] * 4,
        12 * experts * count * units * width, 2 * weights.size,
    )


def expert_gradients(first, counts, routed_rows, block_rows, notes, weights):
    pieces, piece_len, width = routed_rows.shape
    experts, _, units, _ = weights.shape
    capacity = piece_len // 4
    own = experts // 2
    tile = 256
    room = pieces * capacity + tile
    batch = max(d for d in range(1, own + 1) if own % d == 0 and (d == 1 or d * room * width * 4 <= 30 << 20))
    low = jnp.bfloat16
    group = 4
    steps = pieces // group

    def kernel(start, count, routed, block, note, w, grads, final, rows, grad_rows, ends):
        turn, step = pl.program_id(0), pl.program_id(1)
        expert = start[0] + turn * batch

        @pl.when(step == 0)
        def _():
            for j in range(batch):
                ends[j] = 0

        for part in range(group):
            piece = jnp.minimum(step * group + part, pieces - 1)
            numbers = [count[piece * experts + expert + j] for j in range(batch)]

            @pl.when((step < steps) & (sum(numbers) > 0))
            def _():
                slots = (
                    lax.broadcasted_iota(jnp.int32, (batch * capacity, piece_len), 0)
                    + expert * capacity
                ).astype(jnp.float32)
                first = note[part, 0:1, :] == slots
                second = note[part, 1:2, :] == slots
                gate = jnp.sum(
                    jnp.where(first, note[part, 2:3, :], jnp.where(second, note[part, 3:4, :], 0.0)),
                    axis=1,
                    keepdims=True,
                )
                hot = jnp.where(first | second, 1.0, 0.0).astype(low)
                taken = product(hot, routed[part]).astype(low)
                grad_out = (gate * product(hot, block[part])).astype(low)
                for j in range(batch):
                    place = pl.ds(pl.multiple_of(ends[j], 16), capacity)
                    span = slice(j * capacity, (j + 1) * capacity)
                    rows[j, place, :] = taken[span]
                    grad_rows[j, place, :] = grad_out[span]
                    ends[j] += (numbers[j] + 15) // 16 * 16

        @pl.when(step >= steps)
        def _():
            j = jnp.maximum(step - steps, 0)
            end = pl.multiple_of(ends[j], 16)
            rest = pl.ds(end, tile)
            rows[j, rest, :] = jnp.zeros((tile, width), low)
            grad_rows[j, rest, :] = jnp.zeros((tile, width), low)
            def terms(index):
                place = pl.ds(pl.multiple_of(index * tile, tile), tile)
                x = rows[j, place, :]
                grad_out = grad_rows[j, place, :]
                gate_proj = product(x, w[0, 0], 1, 1)
                up_proj = product(x, w[0, 1], 1, 1)
                grad_hidden = product(grad_out, w[0, 2], 1, 1)
                sigmoid = 1.0 / (1.0 + jnp.exp(-gate_proj))
                silu = gate_proj * sigmoid
                hidden = (silu * up_proj).astype(low)
                grad_gate_proj = (
                    grad_hidden * up_proj * sigmoid * (1.0 + gate_proj * (1.0 - sigmoid))
                ).astype(low)
                grad_up_proj = (grad_hidden * silu).astype(low)
                return (
                    product(grad_gate_proj, x, 0, 0),
                    product(grad_up_proj, x, 0, 0),
                    product(hidden, grad_out, 0, 0),
                )

            for k, term in enumerate(terms(0)):
                final[0, k] = term

            def one_tile(index, _):
                for k, term in enumerate(terms(index)):
                    final[0, k] += term
                return 0

            lax.fori_loop(1, (end + tile - 1) // tile, one_tile, 0)
            grads[...] = final[...].astype(low)

    def piece_block(shape):
        return pl.BlockSpec(
            (group,) + shape[1:], lambda turn, step, *_: (jnp.minimum(step, steps - 1), 0, 0)
        )

    def local(turn, step):
        return turn * batch + jnp.maximum(step - steps, 0)

    return pl.pallas_call(
        kernel,
        grid_spec=pltpu.PrefetchScalarGridSpec(
            num_scalar_prefetch=2,
            grid=(own // batch, steps + batch),
            in_specs=[
                piece_block(routed_rows.shape),
                piece_block(block_rows.shape),
                piece_block(notes.shape),
                pl.BlockSpec(
                    (1, 3, units, width),
                    lambda turn, step, start, _: (start[0] + local(turn, step), 0, 0, 0),
                ),
            ],
            out_specs=[
                pl.BlockSpec(
                    (1, 3, units, width), lambda turn, step, *_: (local(turn, step), 0, 0, 0)
                ),
                pl.BlockSpec(
                    (1, 3, units, width),
                    lambda turn, step, start, _: (start[0] + local(turn, step), 0, 0, 0),
                ),
            ],
            scratch_shapes=[
                pltpu.VMEM((batch, room, width), low),
                pltpu.VMEM((batch, room, width), low),
                pltpu.SMEM((batch,), jnp.int32),
            ],
        ),
        out_shape=[
            struct((own, 3, units, width), low),
            struct((experts, 3, units, width), jnp.float32),
        ],
        compiler_params=pltpu.CompilerParams(vmem_limit_bytes=60 * 1024 * 1024),
        cost_estimate=pl.CostEstimate(
            flops=12 * own * pieces * capacity * units * width // 2,
            bytes_accessed=routed_rows.size * 4 + weights.size * 2,
            transcendentals=0,
        ),
        name="expert_gradients",
    )(first, counts, routed_rows, block_rows, notes, weights)


def last_results(first, received, final, weight_sums, small, base, live, ffn_sum, few):
    own, _, units, width = received.shape
    rows = weight_sums.shape[1]
    block = (1, 3, units, width)
    shapes = [(rows, 3 * width), (rows, width), base.shape, (few, width), (2, width)]
    shapes += [(width,), (width,), (1, width)]

    def kernel(start, given, _, sums, few_sums, base_ref, live_ref, ffn, result, qkv, out, output,
               router, const, gain_one, gain_two, mixing):
        result[...] = given[...].astype(jnp.float32)

        @pl.when(pl.program_id(0) == 0)
        def _():
            both = sums.shape[0] == 2
            first_part = sums[1] if both else sums[0, :, : 2 * width]
            second_part = sums[0] if both else sums[0, :, 2 * width :]
            qkv[:, :width] = first_part[:, :width].astype(jnp.float32)
            qkv[:, width:] = second_part.astype(jnp.float32)
            out[...] = first_part[:, width:].astype(jnp.float32)
            output[...] = (base_ref[...] + live_ref[...] * ffn[...]).astype(output.dtype)
            router[...] = few_sums[0:few, :]
            const[...] = few_sums[few : few + 2, :]
            gain_one[...] = few_sums[few + 2, :]
            gain_two[...] = few_sums[few + 3, :]
            mixing[...] = few_sums[few + 4 : few + 5, :]

    return pl.pallas_call(
        kernel,
        grid_spec=pltpu.PrefetchScalarGridSpec(
            num_scalar_prefetch=1,
            grid=(own,),
            in_specs=[
                pl.BlockSpec(block, lambda i, _: (i, 0, 0, 0)),
                pl.BlockSpec(memory_space=pl.ANY),
                whole_block(weight_sums.shape),
                whole_block(small.shape),
                whole_block(base.shape),
                whole_block(live.shape),
                whole_block(ffn_sum.shape),
            ],
            out_specs=[pl.BlockSpec(block, lambda i, start: (start[0] + i, 0, 0, 0))]
            + [whole_block(shape) for shape in shapes],
        ),
        out_shape=[
            struct(final.shape, jnp.float32),
            struct(shapes[0], jnp.float32),
            struct(shapes[1], jnp.float32),
            struct(shapes[2], jnp.bfloat16),
        ]
        + [struct(shape, jnp.float32) for shape in shapes[3:]],
        input_output_aliases={2: 0},
        compiler_params=pltpu.CompilerParams(vmem_limit_bytes=VMEM_LIMIT),
        name="last_results",
    )(first, received, final, weight_sums, small, base, live, ffn_sum)


def score_bias(length, first_row, rows, keys):
    key_place = lax.broadcasted_iota(jnp.int32, (keys, rows), 0)
    query_place = first_row + lax.broadcasted_iota(jnp.int32, (keys, rows), 1)
    return jnp.where(key_place <= jnp.minimum(query_place, length - 1), 0.0, MASKED)


def head_masks(shape):
    lane = lax.broadcasted_iota(jnp.int32, shape, 1)
    return [lane < HEAD_DIM, lane >= HEAD_DIM]


def turn_halves(values, cosines, sines):
    lane = lax.broadcasted_iota(jnp.int32, values.shape, 1)
    half = HEAD_DIM // 2
    swapped = jnp.where(
        lax.rem(lane, HEAD_DIM) < half,
        pltpu.roll(values, 2 * HEAD_DIM - half, 1),
        pltpu.roll(values, half, 1),
    )
    return values * cosines + swapped * sines


def project_keys(tokens, gain, weights, turns):
    rows, width = tokens.shape
    tile = 2 * HEAD_DIM

    def kernel(token, gain_row, weight, turn, normed, pairs):
        x = token[...].astype(jnp.float32)
        scaling = lax.rsqrt(jnp.mean(x * x, axis=1, keepdims=True) + EPSILON)
        normed[...] = (x * scaling * gain_row[...]).astype(jnp.bfloat16)
        for i in range(2 * width // tile):
            span = slice(i * tile, (i + 1) * tile)
            values = product(normed[...], weight[:, span])
            if i < width // tile:
                values = turn_halves(values, turn[0], turn[1])
            pairs[:, span] = values.astype(jnp.bfloat16)

    return pl.pallas_call(
        kernel,
        out_shape=[struct((rows, width), jnp.bfloat16), struct((rows, 2 * width), jnp.bfloat16)],
        compiler_params=pltpu.CompilerParams(vmem_limit_bytes=VMEM_LIMIT),
        name="project_keys",
    )(tokens, gain, weights, turns)


def projection_gradients(
    pair_grads, query_rows, normed, tokens, gain, turns, full_query, full_kv, grad_residual, number
):
    rows, width = tokens.shape
    below = (pair_grads[0].shape[0] - 2 * rows) // max(number, 1)
    tile = 2 * HEAD_DIM
    low = jnp.bfloat16

    def kernel(*refs):
        pairs = refs[: len(pair_grads)]
        (query, normed_ref, token, gain_row, turn, w_query, w_kv, residual, weight_grad, token_grad,
         gain_grad, *early, projected) = refs[len(pair_grads) :]

        def summed(kind, span):
            place = slice(kind * rows, (kind + 1) * rows)
            return sum(pair[place, span].astype(jnp.float32) for pair in pairs)

        for d in range(number):
            place = slice(2 * rows + d * below, 2 * rows + (d + 1) * below)
            value = sum(pair[place, :].astype(jnp.float32) for pair in pairs).astype(low)
            early[0][d, :below] = value[:, : width // 2]
            early[0][d, below:] = value[:, width // 2 :]

        for i in range(width // tile):
            span = slice(i * tile, (i + 1) * tile)
            projected[:, span] = turn_halves(summed(0, span), turn[0], -turn[1]).astype(low)
            projected[:, width + i * tile : width + (i + 1) * tile] = summed(1, span).astype(low)
        for i in range(2):
            span = slice(i * width, (i + 1) * width)
            weight_grad[:, span] = product(normed_ref[...], projected[:, span], 0, 0).astype(low)
        grad_normed = product(query[...], w_query[...], 1, 1) + product(
            projected[...], w_kv[...], 1, 1
        )
        x = token[...].astype(jnp.float32)
        scaling = lax.rsqrt(jnp.mean(x * x, axis=1, keepdims=True) + EPSILON)
        scaled = x * scaling
        gain_grad[...] = jnp.broadcast_to(
            jnp.sum(grad_normed * scaled, axis=0, keepdims=True), gain_grad.shape
        )
        grad_hat = grad_normed * gain_row[...]
        inner = jnp.mean(grad_hat * x, axis=1, keepdims=True)
        token_grad[...] = residual[...] + scaling * grad_hat - scaled * (scaling * scaling * inner)

    return pl.pallas_call(
        kernel,
        out_shape=[
            struct((width, 2 * width), low),
            struct((rows, width), jnp.float32),
            struct((8, width), jnp.float32),
        ]
        + ([struct((number, 2 * below, width // 2), low)] if number else []),
        scratch_shapes=[pltpu.VMEM((rows, 2 * width), low)],
        compiler_params=pltpu.CompilerParams(vmem_limit_bytes=VMEM_LIMIT),
        name="projection_gradients",
    )(*pair_grads, query_rows, normed, tokens, gain, turns, full_query, full_kv, grad_residual)


def attention_forward(places, normed, w_query, turns, pairs):
    rows, width = normed.shape
    keys = pairs.shape[0]
    chunk = min(keys, 1024)
    tile = 2 * HEAD_DIM
    tiles = width // tile

    def kernel(place, normed_ref, weight, turn, key, value, mixed, query, sums, bias):
        step = pl.program_id(0)

        @pl.when(step == 0)
        def _():
            bias[...] = score_bias(place[0], place[1], rows, keys)

        query[...] = turn_halves(
            product(normed_ref[...], weight[...]), turn[0], turn[1]
        ).astype(query.dtype)
        own_masks = head_masks((rows, tile))
        scaled = query[...] * HEAD_DIM**-0.5
        outs = []
        for head in range(2):
            chosen = jnp.where(own_masks[head], scaled, 0)
            parts = [
                product(key[place : place + chunk, :], chosen, 1, 1) + bias[place : place + chunk, :]
                for place in range(0, keys, chunk)
            ]
            top = parts[0]
            for part in parts[1:]:
                top = jnp.maximum(top, part)
            top = jnp.max(top, axis=0, keepdims=True)
            turned, total = 0.0, 0.0
            for i, part in enumerate(parts):
                weights = jnp.exp(part - top)
                total = total + jnp.sum(weights, axis=0, keepdims=True)
                turned = turned + product(
                    value[i * chunk : (i + 1) * chunk, :], weights.astype(jnp.bfloat16), 0, 0
                )
            span = slice(head * HEAD_DIM, (head + 1) * HEAD_DIM)
            outs.append(turned[span] * (1.0 / total))
            sums[0, head : head + 1, :] = top + jnp.log(total)
        mixed[...] = jnp.transpose(jnp.concatenate(outs, axis=0)).astype(mixed.dtype)

    return pl.pallas_call(
        kernel,
        grid_spec=pltpu.PrefetchScalarGridSpec(
            num_scalar_prefetch=1,
            grid=(tiles,),
            in_specs=[
                whole_block((rows, width)),
                pl.BlockSpec((width, tile), lambda i, _: (0, i)),
                whole_block(turns.shape),
                pl.BlockSpec((keys, tile), lambda i, _: (0, i)),
                pl.BlockSpec((keys, tile), lambda i, _: (0, i + tiles)),
            ],
            out_specs=[
                pl.BlockSpec((rows, tile), lambda i, _: (0, i)),
                pl.BlockSpec((rows, tile), lambda i, _: (0, i)),
                pl.BlockSpec((1, 8, rows), lambda i, _: (i, 0, 0)),
            ],
            scratch_shapes=[pltpu.VMEM((keys, rows), jnp.float32)],
        ),
        out_shape=[
            struct((rows, width), jnp.bfloat16),
            struct((rows, width), jnp.bfloat16),
            struct((tiles, 8, rows), jnp.float32),
        ],
        compiler_params=pltpu.CompilerParams(vmem_limit_bytes=60 * 1024 * 1024),
        cost_estimate=pl.CostEstimate(
            flops=4 * rows * keys * width, bytes_accessed=pairs.size * 2, transcendentals=0
        ),
        name="attention",
    )(places, normed, w_query, turns, pairs, pairs)


def attention_backward(
    places, queries, pairs, sums, mixed, grad_mixed, normed, turns, grad_attention
):
    rows, width = queries.shape
    keys = pairs.shape[0]
    pieces = keys // rows
    tile = 2 * HEAD_DIM
    tiles = width // tile
    scaling = HEAD_DIM**-0.5

    def kernel(place, query, key, value, total, out, grad_out, normed_ref, turn, all_out, attention,
               grad_query, grad_pair, weight_grad, bias):
        step = pl.program_id(0)

        @pl.when(step == 0)
        def _():
            bias[...] = score_bias(place[0], place[1], rows, keys)

        own_masks = head_masks((rows, tile))
        scaled = query[...] * scaling
        inner = out[...].astype(jnp.float32) * grad_out[...].astype(jnp.float32)
        grads, key_sum, value_sum = [], None, None
        for head in range(2):
            chosen = jnp.where(own_masks[head], scaled, 0)
            upstream = jnp.where(own_masks[head], grad_out[...], 0)
            ones = jnp.where(own_masks[head][:8], 1.0, 0.0)
            inner_row = lax.dot_general(
                ones, inner, (((1,), (1,)), ((), ())),
                precision=HIGHEST, preferred_element_type=jnp.float32,
            )[0:1]
            scores = product(key[...], chosen, 1, 1) + bias[...]
            probabilities = jnp.exp(scores - total[0, head : head + 1, :])
            grad_probs = product(value[...], upstream, 1, 1)
            grad_scores = (probabilities * (grad_probs - inner_row)).astype(jnp.bfloat16)
            key_part = product(grad_scores, chosen)
            value_part = product(probabilities.astype(jnp.bfloat16), upstream)
            key_sum = key_part if key_sum is None else key_sum + key_part
            value_sum = value_part if value_sum is None else value_sum + value_part
            span = slice(head * HEAD_DIM, (head + 1) * HEAD_DIM)
            grads.append(product(key[...], grad_scores, 0, 0)[span] * scaling)
        grad_query[...] = turn_halves(
            jnp.transpose(jnp.concatenate(grads, axis=0)), turn[0], -turn[1]
        ).astype(grad_query.dtype)
        weight_grad[0] = product(normed_ref[...], grad_query[...], 0, 0).astype(weight_grad.dtype)
        weight_grad[1] = product(all_out[...], attention[...], 0, 0).astype(weight_grad.dtype)
        grad_pair[:, 0] = key_sum.astype(grad_pair.dtype).reshape(pieces, rows, tile)
        grad_pair[:, 1] = value_sum.astype(grad_pair.dtype).reshape(pieces, rows, tile)

    own_block = pl.BlockSpec((rows, tile), lambda i, _: (0, i))
    key_block = pl.BlockSpec((keys, tile), lambda i, _: (0, i))
    low = jnp.bfloat16
    return pl.pallas_call(
        kernel,
        grid_spec=pltpu.PrefetchScalarGridSpec(
            num_scalar_prefetch=1,
            grid=(tiles,),
            in_specs=[
                own_block,
                key_block,
                pl.BlockSpec((keys, tile), lambda i, _: (0, i + tiles)),
                pl.BlockSpec((1, 8, rows), lambda i, _: (i, 0, 0)),
                own_block,
                own_block,
                whole_block((rows, width)),
                whole_block(turns.shape),
                whole_block((rows, width)),
                own_block,
            ],
            out_specs=[
                own_block,
                pl.BlockSpec((pieces, 2, rows, tile), lambda i, _: (0, 0, 0, i)),
                pl.BlockSpec((2, width, tile), lambda i, _: (0, 0, i)),
            ],
            scratch_shapes=[pltpu.VMEM((keys, rows), jnp.float32)],
        ),
        out_shape=[
            struct((rows, width), low),
            struct((pieces, 2, rows, width), low),
            struct((2, width, width), low),
        ],
        compiler_params=pltpu.CompilerParams(vmem_limit_bytes=60 * 1024 * 1024),
        cost_estimate=pl.CostEstimate(
            flops=10 * rows * keys * width, bytes_accessed=pairs.size * 2, transcendentals=0
        ),
        name="attention_back",
    )(places, queries, pairs, pairs, sums, mixed, grad_mixed, normed, turns, mixed, grad_attention)


def normalize_rows(values, gain_row):
    scaling = lax.rsqrt(jnp.mean(values * values, axis=-1, keepdims=True) + EPSILON)
    return (values * scaling * gain_row, scaling)


def normalize_back(values, scaling, gain_row, grad_out):
    grad_hat = grad_out * gain_row
    grad_gain = jnp.sum(grad_out * values * scaling, axis=(0, 1))
    grad_values = scaling * grad_hat - values * scaling**3 * jnp.mean(
        grad_hat * values, axis=-1, keepdims=True
    )
    return (grad_values, grad_gain)


def rope_angles(positions, head_size):
    half_dim = head_size // 2
    frequency = jnp.exp(
        jnp.arange(half_dim, dtype=jnp.float32) * (-2.0 * math.log(10000.0) / head_size)
    )
    return positions.astype(jnp.float32)[:, None] * frequency[None, :]


def per_device(
    tokens,
    prev_logits,
    routes,
    lengths,
    cotangent,
    w_qkv,
    w_out,
    gain_attn,
    gain_moe,
    w_router,
    w_residual,
    const_vec,
    w_expert,
):
    groups, piece_len, model_width = tokens.shape
    positions = lax.axis_index("ctx") * piece_len + jnp.arange(piece_len, dtype=jnp.int32)
    live_rows = (positions[None, :] < lengths[:, None]).astype(jnp.float32)[..., None]
    experts = w_expert.shape[0]
    capacity = piece_len // 4
    slot_count = experts * capacity
    fsdp_count, ctx_count = lax.axis_size("fsdp"), lax.axis_size("ctx")
    full_kv = gather_weights(w_qkv, model_width, fsdp_count, ctx_count)
    inputs = tokens.astype(jnp.float32)
    gain_one = gain_attn.astype(jnp.float32)
    gain_two = gain_moe.astype(jnp.float32)
    angles = rope_angles(positions, HEAD_DIM)
    cosines, sines = jnp.cos(angles), jnp.sin(angles)
    turns = jnp.stack(
        [jnp.tile(cosines, (1, 4)), jnp.concatenate([-sines, sines, -sines, sines], axis=1)]
    )
    normed_one_low, own_pairs = project_keys(tokens[0], gain_one[None], full_kv, turns)
    cotangent_low = live_rows.astype(jnp.bfloat16) * cotangent
    all_pairs, (full_query, full_out) = gather_keys(
        own_pairs, [w_qkv, w_out], model_width, fsdp_count, ctx_count
    )
    cotangent_rows = lax.all_gather(cotangent_low, "fsdp", axis=0, tiled=True)
    cotangent_rows, all_pairs = lax.optimization_barrier((cotangent_rows, all_pairs))
    slot_block = lax.all_gather(cotangent_rows, "ctx", axis=0, tiled=True)
    places = jnp.stack([lengths[0], lax.axis_index("ctx") * piece_len]).astype(jnp.int32)
    mixed_rows, query_rows, score_sums = attention_forward(
        places, normed_one_low, full_query, turns, all_pairs
    )
    mixed_low = mixed_rows[None]
    attention = jnp.einsum("gpd,de->gpe", mixed_low, full_out, preferred_element_type=jnp.float32)
    residual_sum = inputs + attention
    normed_two, scale_two = normalize_rows(residual_sum, gain_two)
    routed_low = normed_two.astype(jnp.bfloat16)
    routed = routed_low.astype(jnp.float32)
    logits = jnp.einsum("gpd,de->gpe", routed, w_router, precision=HIGHEST) + jnp.einsum(
        "gpi,ie->gpe", prev_logits, w_residual, precision=HIGHEST
    )
    id_range = jnp.arange(experts + 4, dtype=jnp.int32)
    route_hot = (routes[..., None] == id_range).astype(jnp.float32)
    chosen = jnp.sum(route_hot * logits[:, :, None, :], axis=-1)
    chosen_exp = jnp.exp(chosen - jnp.max(chosen, axis=-1, keepdims=True))
    gate_weights = chosen_exp / jnp.sum(chosen_exp, axis=-1, keepdims=True)
    assign_hot = route_hot[..., :experts].reshape(groups, 2 * piece_len, experts)
    earlier = jnp.cumsum(assign_hot, axis=1) - assign_hot
    order_in = jnp.sum(earlier * assign_hot, axis=-1)
    expert_of = jnp.sum(assign_hot * jnp.arange(experts, dtype=jnp.float32), axis=-1)
    is_ffn = jnp.sum(assign_hot, axis=-1)
    slot_of = jnp.where(is_ffn > 0.5, expert_of * capacity + order_in, -1.0).reshape(
        groups, piece_len, 2
    )
    live_counts = jnp.sum(
        assign_hot * jnp.repeat(live_rows[..., 0], 2, axis=1)[..., None], axis=(0, 1)
    )
    notes = jnp.concatenate(
        [
            slot_of[0].T,
            gate_weights[0].T,
            jnp.pad(live_counts[None], ((0, 3), (0, piece_len - experts))),
        ],
        axis=0,
    )
    routed_rows, all_notes = gather_rows(routed_low[0], notes, fsdp_count)
    expert_weights = w_expert.swapaxes(1, 2)
    out_parts, grad_parts, dot_notes = expert_layers(
        routed_rows, cotangent_rows, all_notes, expert_weights
    )
    slot_block, routed_rows, grad_parts = lax.optimization_barrier(
        (slot_block, routed_rows, grad_parts)
    )
    slot_routed = lax.all_gather(routed_rows, "ctx", axis=0, tiled=True)
    ffn_grad, dot_sums, slot_notes = reduce_rows(
        grad_parts, dot_notes, all_notes, fsdp_count, ctx_count
    )
    slot_notes = slot_notes.reshape((ctx_count * fsdp_count,) + notes.shape)
    ffn_grad = ffn_grad[None]
    copy_hot = route_hot[..., experts + 1]
    const_hot = route_hot[..., experts + 2 :]
    constants = const_vec.astype(jnp.float32)
    gate_const = jnp.sum(gate_weights[..., None] * const_hot, axis=2)
    copy_gate = jnp.sum(gate_weights * copy_hot, axis=2, keepdims=True)
    special_sum = copy_gate * routed + jnp.einsum(
        "gpj,jd->gpd", gate_const, constants, precision=HIGHEST
    )
    grad_block = live_rows * cotangent.astype(jnp.float32)
    copy_dot = jnp.sum(grad_block * routed, axis=-1)[..., None]
    const_dot = jnp.einsum("gpd,jd->gpj", grad_block, constants, precision=HIGHEST)
    grad_gate = (
        dot_sums[:2].T[None]
        + copy_hot * copy_dot
        + jnp.sum(const_hot * const_dot[:, :, None, :], axis=-1)
    )
    grad_chosen = gate_weights * (
        grad_gate - jnp.sum(gate_weights * grad_gate, axis=-1, keepdims=True)
    )
    grad_logits = jnp.sum(grad_chosen[..., None] * route_hot, axis=2)
    grad_router = jnp.einsum("gpd,gpe->de", routed, grad_logits, precision=HIGHEST)
    grad_mixing = jnp.einsum("gpi,gpe->ie", prev_logits, grad_logits, precision=HIGHEST)
    grad_previous = jnp.einsum("gpe,ie->gpi", grad_logits, w_residual, precision=HIGHEST)
    grad_const = jnp.einsum("gpd,gpj->jd", grad_block, gate_const, precision=HIGHEST)
    grad_routed = (
        jnp.einsum("gpe,de->gpd", grad_logits, w_router, precision=HIGHEST)
        + copy_gate * grad_block
        + ffn_grad
    )
    grad_norm_two, grad_gain_two = normalize_back(residual_sum, scale_two, gain_two, grad_routed)
    grad_residual = grad_block + grad_norm_two
    grad_attention = grad_residual.astype(jnp.bfloat16)
    grad_mixed = jnp.einsum(
        "gpe,de->gpd", grad_attention, full_out, preferred_element_type=jnp.float32
    ).astype(jnp.bfloat16)
    counts = slot_notes[:, 4, :experts].astype(jnp.int32).reshape(-1)
    first_expert = lax.rem(lax.axis_index("ctx"), 2) * (experts // 2)
    query_back, pair_grads, early_parts = attention_backward(
        places, query_rows, all_pairs, score_sums, mixed_rows, grad_mixed[0], normed_one_low, turns,
        grad_attention[0],
    )
    early_parts = early_parts.reshape(2, fsdp_count, -1, model_width)
    chips = ctx_count // 2
    split = chips == 4
    chip_grads = pair_sums(pair_grads, early_parts if split else None, ctx_count)
    counts, *chip_grads = lax.optimization_barrier((counts, *chip_grads))

    arrived = list(chip_grads[:1])
    for step, block in enumerate(chip_grads[1:], 1):
        ring = [(i, (i + 2 * step) % ctx_count) for i in range(ctx_count)]
        arrived.append(lax.ppermute(block, "ctx", ring))
    half_grads, expert_half = expert_gradients(
        first_expert.astype(jnp.int32)[None], counts, slot_routed, slot_block, slot_notes, expert_weights
    )
    half_grads, query_back = lax.optimization_barrier((half_grads, query_back))
    weight_parts, grad_inputs, grad_gain_one, *early_sums = projection_gradients(
        arrived,
        query_back,
        normed_one_low,
        tokens[0],
        gain_one[None],
        turns,
        full_query,
        full_kv,
        grad_residual[0],
        fsdp_count if split else 0,
    )
    grad_inputs = grad_inputs[None]
    weight_parts = weight_parts.reshape(fsdp_count, -1, 2 * model_width)
    if not split:
        weight_parts = jnp.concatenate([early_parts[0], early_parts[1], weight_parts], axis=-1)
    few = experts + 4
    mixing_row = jnp.pad(grad_mixing.reshape(1, -1), ((0, 0), (0, model_width - few * few)))
    small = jnp.concatenate(
        [grad_router.T, grad_const, grad_gain_one[:1], grad_gain_two[None], mixing_row], axis=0
    )
    small = jnp.pad(small, ((0, -small.shape[0] % 8), (0, 0)))
    weight_sum, small_sum, expert_grads, ffn_sum = reduce_weights(
        weight_parts, early_sums, small, half_grads, out_parts, fsdp_count, ctx_count
    )
    other_first = (experts // 2 - first_expert).astype(jnp.int32)[None]
    expert_sum, wqkv_sum, wout_sum, output, router_sum, const_sum, *rest = last_results(
        other_first, expert_grads, expert_half, weight_sum, small_sum,
        (live_rows * (residual_sum + special_sum))[0], live_rows[0], ffn_sum, few,
    )
    expert_sum, output, router_sum = expert_sum.swapaxes(1, 2), output[None], router_sum.T
    gain_one_sum, gain_two_sum, mixing_row = rest
    mixing_sum = mixing_row[0, : few * few].reshape(few, few)
    return (
        output,
        grad_inputs,
        grad_previous,
        wqkv_sum,
        wout_sum,
        gain_one_sum,
        gain_two_sum,
        router_sum,
        mixing_sum,
        const_sum,
        expert_sum,
    )


def solution(mesh):
    return jax.shard_map(
        per_device,
        mesh=mesh,
        in_specs=(
            P("fsdp", "ctx", None),
            P("fsdp", "ctx", None),
            P("fsdp", "ctx", None),
            P("fsdp"),
            P("fsdp", "ctx", None),
            P("fsdp", None),
            P("fsdp", None),
            P(),
            P(),
            P(),
            P(),
            P(),
            P(None, "fsdp", None, None),
        ),
        out_specs=(
            P("fsdp", "ctx", None),
            P("fsdp", "ctx", None),
            P("fsdp", "ctx", None),
            P("fsdp", None),
            P("fsdp", None),
            P(),
            P(),
            P(),
            P(),
            P(),
            P(None, "fsdp", None, None),
        ),
        check_vma=False,
    )
```
